32 devices in a mesh: outer: 16 (over z, y, core), inner: 2 (over x).
Axes of the slice: x: 2, y: 2, z: 4, core: 2. Of those that a mesh axis runs over, the one named last changes fastest.
Arguments:
- queries: bfloat16 [16384, 512], P(('outer', 'inner')), may hold values from -5 to 5
- key_matrix: bfloat16 [16384, 512], P(('outer', 'inner')), may hold values from -5 to 5
- value_matrix: bfloat16 [16384, 512], P(('outer', 'inner')), may hold values from -5 to 5
- cotangent: bfloat16 [16384, 512], P(('outer', 'inner')), may hold values from -6 to 6
Outputs:
- attended: bfloat16 [16384, 512], P(('outer', 'inner'))
- query_grad: bfloat16 [16384, 512], P(('outer', 'inner'))
- key_grad: bfloat16 [16384, 512], P(('outer', 'inner'))
- value_grad: bfloat16 [16384, 512], P(('outer', 'inner'))
The draws below stay inside these ranges and needn't reach their ends.
All inputs are finite; a program needn't handle non-finite values.
Results may differ from the reference program's by a relative error of at most 0.02.
Values may be sent and summed in bfloat16 or wider, within the bound.
No kernel may reach another device: no remote copies, remote signals or barrier semaphores. Data moves between devices by JAX's collectives and lax.ppermute only.
A program may use at most 128 MiB of HBM per device.

```python
import math
import jax
import jax.numpy as jnp
from jax import lax

HEAD = 128
BLOCK = 128
LEVELS = 3
D = 512
TOKENS = 16384


def textured(key, slow_scale, rough):
    key_slow, key_phase = jax.random.split(key)
    run_count = TOKENS // 8 + 1
    slow_part = jax.random.normal(key_slow, (run_count, D), jnp.float32) * slow_scale
    phase_shift = jax.random.randint(key_phase, (1, D), 0, 8)
    run_index = (jnp.arange(TOKENS, dtype=jnp.int32)[:, None] + phase_shift) // 8
    return jnp.take_along_axis(slow_part, run_index, axis=0) + rough


def draw_queries(key, part):
    key = jax.random.fold_in(key, 1)
    key_texture, key_rough = jax.random.split(key)
    rough = jax.random.normal(key_rough, (TOKENS, D), jnp.float32)
    values = textured(key_texture, 1.2, rough)
    return jnp.clip(values, -5.0, 5.0).astype(jnp.bfloat16)


def draw_key_matrix(key, part):
    key = jax.random.fold_in(key, 2)
    key_texture, key_rough = jax.random.split(key)
    rough = jax.random.normal(key_rough, (TOKENS, D), jnp.float32)
    values = textured(key_texture, 1.2, rough)
    return jnp.clip(values, -5.0, 5.0).astype(jnp.bfloat16)


def draw_value_matrix(key, part):
    key = jax.random.fold_in(key, 3)
    key_texture, key_rough = jax.random.split(key)
    rough = jax.random.normal(key_rough, (TOKENS, D), jnp.float32)
    values = textured(key_texture, 1.2, rough)
    return jnp.clip(values, -5.0, 5.0).astype(jnp.bfloat16)


def level_of(rng, shape, cuts, smallest, high):
    def one(dim, blocks):
        steps = jax.random.uniform(jax.random.fold_in(jax.random.fold_in(rng, 6), dim), (blocks,), jnp.float32, smallest / len(cuts), high / len(cuts))
        return jnp.repeat(jnp.exp(steps), shape[dim] // blocks).reshape((-1,) + (1,) * (len(shape) - dim - 1))

    gain = one(*cuts[0])
    for cut in cuts[1:]:
        gain = gain * one(*cut)
    return gain


def normal_values(stream_key, extent, width, most, cuts=(), kind=jnp.bfloat16):
    drawn = jax.random.normal(stream_key, extent, jnp.float32) * width
    if len(cuts) > 0:
        drawn = level_of(stream_key, extent, cuts, -0.22, 0.18) * drawn
    return jnp.clip(drawn, min=-most, max=most).astype(kind)


def setup_inputs(seed: int = 0) -> dict:
    splits = jax.random.split(jax.random.key(seed), 5)
    return {
        "queries": draw_queries(jax.random.fold_in(splits[4], 71), 0),
        "key_matrix": draw_key_matrix(jax.random.fold_in(splits[4], 71), 0),
        "value_matrix": draw_value_matrix(jax.random.fold_in(splits[4], 71), 0),
        "cotangent": normal_values(splits[3], (TOKENS, D), 1.0, 6.0, ((0, 32),)),
    }


def coarsen(matrix, degree):
    if degree == 0:
        return matrix
    renormalizing_multiplier = 2 ** degree
    grouped = matrix.reshape(matrix.shape[0] // renormalizing_multiplier, renormalizing_multiplier, matrix.shape[1])
    return (jnp.sum(grouped.astype(jnp.float32), axis=1) / renormalizing_multiplier).astype(jnp.bfloat16)


def windows(padded, pair_count):
    stride = 2 * BLOCK
    pieces = [padded[stride * tier_start_shift: stride * (tier_start_shift + pair_count)].reshape((pair_count, stride) + padded.shape[1:]) for tier_start_shift in range(3)]
    return jnp.concatenate(pieces, axis=1)


def unfold(windowed):
    stride = 2 * BLOCK
    pair_count = windowed.shape[0]
    trailing = windowed.shape[2:]
    pieces = windowed.reshape((pair_count, 3, stride) + trailing)
    summed = None
    for tier_start_shift in range(3):
        segment = pieces[:, tier_start_shift].reshape((pair_count * stride,) + trailing)
        widths = [(stride * tier_start_shift, stride * (2 - tier_start_shift))] + [(0, 0)] * len(trailing)
        placed = jnp.pad(segment, widths)
        summed = placed if summed is None else summed + placed
    return summed


def allowed_pairs(query_index, key_index, degree, length):
    allowed = (key_index >= 0) & (key_index < length)
    allowed = jnp.broadcast_to(allowed[:, None, :], (query_index.shape[0], query_index.shape[1], key_index.shape[1]))
    if degree > 0:
        query_block = query_index // BLOCK
        key_block = key_index // BLOCK
        allowed = allowed & (jnp.abs(query_block[:, :, None] - key_block[:, None, :]) >= 2)
    return allowed[:, None]


def masked_scores(query_block, key_block, query_index, key_index, degree, length):
    inverse_root = HEAD ** -0.5
    scores = jnp.einsum('nqhe,nkhe->nhqk', query_block.astype(jnp.float32), key_block.astype(jnp.float32)) * inverse_root
    return jnp.where(allowed_pairs(query_index, key_index, degree, length), scores, -jnp.inf)


def forward_block(query_block, key_block, value_block, query_index, key_index, degree, length):
    scores = masked_scores(query_block, key_block, query_index, key_index, degree, length)
    maxima = jnp.max(scores, axis=-1)
    weights = jnp.exp(scores - maxima[..., None])
    totals = jnp.sum(weights, axis=-1)
    rounded = lax.optimization_barrier(weights.astype(jnp.bfloat16))
    blended = jnp.einsum('nhqk,nkhe->nqhe', rounded.astype(jnp.float32), value_block.astype(jnp.float32))
    return jnp.swapaxes(maxima, 1, 2), jnp.swapaxes(totals, 1, 2), blended


def backward_block(query_block, key_block, value_block, grad_block, dot_block, lowest_block, query_index, key_index, degree, length):
    inverse_root = HEAD ** -0.5
    scores = masked_scores(query_block, key_block, query_index, key_index, degree, length)
    weights = (2.0 ** degree) * jnp.exp(scores - jnp.swapaxes(lowest_block, 1, 2)[..., None])
    rounded = lax.optimization_barrier(weights.astype(jnp.bfloat16))
    grad_wide = grad_block.astype(jnp.float32)
    value_part = jnp.einsum('nhqk,nqhe->nkhe', rounded.astype(jnp.float32), grad_wide)
    products = jnp.einsum('nqhe,nkhe->nhqk', grad_wide, value_block.astype(jnp.float32))
    slopes = lax.optimization_barrier((weights * (products - jnp.swapaxes(dot_block, 1, 2)[..., None])).astype(jnp.bfloat16))
    slopes_wide = slopes.astype(jnp.float32)
    query_part = jnp.einsum('nhqk,nkhe->nqhe', slopes_wide, key_block.astype(jnp.float32)) * inverse_root
    key_part = jnp.einsum('nhqk,nqhe->nkhe', slopes_wide, query_block.astype(jnp.float32)) * inverse_root
    return query_part, key_part, value_part


def level_forward(coarse_q, coarse_k, coarse_v, degree):
    length = coarse_q.shape[0]
    stride = 2 * BLOCK
    pair_count = length // stride
    batch_pairs = math.gcd(pair_count, 8)
    group_count = pair_count // batch_pairs
    head_count = coarse_q.shape[1] // HEAD
    shaped_q = coarse_q.reshape(group_count, batch_pairs, stride, head_count, HEAD)
    padded_k = jnp.pad(coarse_k.reshape(length, head_count, HEAD), ((stride, stride), (0, 0), (0, 0)))
    padded_v = jnp.pad(coarse_v.reshape(length, head_count, HEAD), ((stride, stride), (0, 0), (0, 0)))
    span_rows = batch_pairs * stride + 2 * stride

    def one_group(position):
        first_row = position * (batch_pairs * stride)
        window_k = windows(lax.dynamic_slice_in_dim(padded_k, first_row, span_rows, 0), batch_pairs)
        window_v = windows(lax.dynamic_slice_in_dim(padded_v, first_row, span_rows, 0), batch_pairs)
        query_index = first_row + jnp.arange(batch_pairs * stride, dtype=jnp.int32).reshape(batch_pairs, stride)
        key_index = first_row - stride + stride * jnp.arange(batch_pairs, dtype=jnp.int32)[:, None] + jnp.arange(3 * stride, dtype=jnp.int32)[None, :]
        return forward_block(shaped_q[position], window_k, window_v, query_index, key_index, degree, length)

    maxima, totals, blended = lax.map(one_group, jnp.arange(group_count, dtype=jnp.int32))
    return maxima.reshape(length, head_count), totals.reshape(length, head_count), blended.reshape(length, head_count, HEAD)


def level_backward(coarse_q, coarse_k, coarse_v, coarse_g, pooled_query_key_scores, coarse_low, degree):
    length = coarse_q.shape[0]
    stride = 2 * BLOCK
    pair_count = length // stride
    batch_pairs = math.gcd(pair_count, 8)
    group_count = pair_count // batch_pairs
    head_count = coarse_q.shape[1] // HEAD
    shaped_q = coarse_q.reshape(group_count, batch_pairs, stride, head_count, HEAD)
    shaped_g = coarse_g.reshape(group_count, batch_pairs, stride, head_count, HEAD)
    shaped_dot = pooled_query_key_scores.reshape(group_count, batch_pairs, stride, head_count)
    shaped_low = coarse_low.reshape(group_count, batch_pairs, stride, head_count)
    padded_k = jnp.pad(coarse_k.reshape(length, head_count, HEAD), ((stride, stride), (0, 0), (0, 0)))
    padded_v = jnp.pad(coarse_v.reshape(length, head_count, HEAD), ((stride, stride), (0, 0), (0, 0)))
    span_rows = batch_pairs * stride + 2 * stride

    def one_group(running, position):
        running_k, running_v = running
        first_row = position * (batch_pairs * stride)
        window_k = windows(lax.dynamic_slice_in_dim(padded_k, first_row, span_rows, 0), batch_pairs)
        window_v = windows(lax.dynamic_slice_in_dim(padded_v, first_row, span_rows, 0), batch_pairs)
        query_index = first_row + jnp.arange(batch_pairs * stride, dtype=jnp.int32).reshape(batch_pairs, stride)
        key_index = first_row - stride + stride * jnp.arange(batch_pairs, dtype=jnp.int32)[:, None] + jnp.arange(3 * stride, dtype=jnp.int32)[None, :]
        query_part, key_part, value_part = backward_block(shaped_q[position], window_k, window_v, shaped_g[position], shaped_dot[position], shaped_low[position], query_index, key_index, degree, length)
        running_k = lax.dynamic_update_slice_in_dim(running_k, lax.dynamic_slice_in_dim(running_k, first_row, span_rows, 0) + unfold(key_part), first_row, 0)
        running_v = lax.dynamic_update_slice_in_dim(running_v, lax.dynamic_slice_in_dim(running_v, first_row, span_rows, 0) + unfold(value_part), first_row, 0)
        return (running_k, running_v), query_part

    initial = (jnp.zeros((length + 2 * stride, head_count, HEAD), jnp.float32), jnp.zeros((length + 2 * stride, head_count, HEAD), jnp.float32))
    (grad_k, grad_v), query_parts = lax.scan(one_group, initial, jnp.arange(group_count, dtype=jnp.int32))
    return query_parts.reshape(length, head_count, HEAD), grad_k[stride:length + stride], grad_v[stride:length + stride]


def reference(queries, key_matrix, value_matrix, cotangent):
    tokens, columns = queries.shape
    head_count = columns // HEAD
    coarse = [(coarsen(queries, degree), coarsen(key_matrix, degree), coarsen(value_matrix, degree)) for degree in range(LEVELS)]
    forward = [level_forward(coarse[degree][0], coarse[degree][1], coarse[degree][2], degree) for degree in range(LEVELS)]
    row_peak = None
    for degree in range(LEVELS):
        expanded = jnp.repeat(forward[degree][0], 2 ** degree, axis=0)
        row_peak = expanded if row_peak is None else jnp.maximum(row_peak, expanded)
    numerator = jnp.zeros((tokens, head_count, HEAD), jnp.float32)
    denominator = jnp.zeros((tokens, head_count), jnp.float32)
    for degree in range(LEVELS):
        renormalizing_multiplier = 2 ** degree
        maxima, totals, blended = forward[degree]
        scale_rows = renormalizing_multiplier * jnp.exp(jnp.repeat(maxima, renormalizing_multiplier, axis=0) - row_peak)
        denominator = denominator + scale_rows * jnp.repeat(totals, renormalizing_multiplier, axis=0)
        numerator = numerator + scale_rows[..., None] * jnp.repeat(blended, renormalizing_multiplier, axis=0)
    attended = (numerator / denominator[..., None]).astype(jnp.bfloat16)
    log_norm = row_peak + jnp.log(denominator)
    shaped_g = cotangent.reshape(tokens, head_count, HEAD).astype(jnp.float32)
    query_key_inner = jnp.sum(attended.astype(jnp.float32).reshape(tokens, head_count, HEAD) * shaped_g, axis=-1)
    query_total = jnp.zeros((tokens, head_count, HEAD), jnp.float32)
    key_total = jnp.zeros((tokens, head_count, HEAD), jnp.float32)
    value_total = jnp.zeros((tokens, head_count, HEAD), jnp.float32)
    for degree in range(LEVELS):
        renormalizing_multiplier = 2 ** degree
        level_rows = tokens // renormalizing_multiplier
        grouped_log = log_norm.reshape(level_rows, renormalizing_multiplier, head_count)
        lowest_level = jnp.min(grouped_log, axis=1)
        scaling = jnp.exp(lowest_level[:, None] - grouped_log)
        coarse_g = jnp.sum(scaling[..., None] * shaped_g.reshape(level_rows, renormalizing_multiplier, head_count, HEAD), axis=1).astype(jnp.bfloat16)
        pooled_query_key_scores = jnp.sum(scaling * query_key_inner.reshape(level_rows, renormalizing_multiplier, head_count), axis=1)
        query_part, key_part, value_part = level_backward(coarse[degree][0], coarse[degree][1], coarse[degree][2], coarse_g, pooled_query_key_scores, lowest_level, degree)
        query_total = query_total + jnp.repeat(query_part, renormalizing_multiplier, axis=0) / renormalizing_multiplier
        key_total = key_total + jnp.repeat(key_part, renormalizing_multiplier, axis=0) / renormalizing_multiplier
        value_total = value_total + jnp.repeat(value_part, renormalizing_multiplier, axis=0) / renormalizing_multiplier
    return (attended.reshape(tokens, columns),
            query_total.reshape(tokens, columns).astype(jnp.bfloat16),
            key_total.reshape(tokens, columns).astype(jnp.bfloat16),
            value_total.reshape(tokens, columns).astype(jnp.bfloat16))
```

```python
import functools
import math

import jax
import jax.numpy as jnp
from jax import lax
from jax.experimental import pallas as pl
from jax.experimental.pallas import tpu as pltpu
from jax.sharding import PartitionSpec as P

HEAD = 128
BLOCK = 128
PARENT = 256
LEVELS = 3
CHUNKS = 2
INV_ROOT = HEAD**-0.5
TO_LOG2 = INV_ROOT * math.log2(math.e)
MASKED = -1e30
BF = jnp.bfloat16
F32 = jnp.float32


def dot_nt(a, b):
    return lax.dot_general(a, b, (((1,), (1,)), ((), ())), preferred_element_type=F32)


def dot_nn(a, b):
    return jnp.dot(a, b, preferred_element_type=F32)


def order_matrix(inverse):
    row = lax.broadcasted_iota(jnp.int32, (PARENT, PARENT), 0)
    col = lax.broadcasted_iota(jnp.int32, (PARENT, PARENT), 1)
    place, token = (col, row) if inverse else (row, col)
    slab = place // 64
    source = 4 * (place % 64) + 2 * (slab % 2) + slab // 2
    return jnp.where(source == token, 1.0, 0.0).astype(BF)


def pool1(x):
    return ((x[:BLOCK].astype(F32) + x[BLOCK:].astype(F32)) * 0.5).astype(BF)


def pool2(x):
    half = x[:BLOCK].astype(F32) + x[BLOCK:].astype(F32)
    return ((half[:64] + half[64:]) * 0.25).astype(BF)


def pool12(x):
    return ((x[:64].astype(F32) + x[64:].astype(F32)) * 0.5).astype(BF)


def twice(x, axis=0):
    return jnp.concatenate([x, x], axis=axis)


def pack_kernel(where, a_own, a_far, b_own, b_far, own, far):
    width = a_own.shape[1]
    order = order_matrix(False)
    for i in range(a_own.shape[0] // PARENT):
        rows = slice(i * PARENT, (i + 1) * PARENT)
        own[rows, :width] = dot_nn(order, a_own[rows, :]).astype(BF)
        own[rows, width:] = dot_nn(order, b_own[rows, :]).astype(BF)
        far[rows, :width] = dot_nn(order, a_far[rows, :]).astype(BF)
        far[rows, width:] = dot_nn(order, b_far[rows, :]).astype(BF)


def pack(where, a, b, chunk):
    rows, columns = a.shape
    width = columns // 2 // CHUNKS
    near = pl.BlockSpec((rows, width), lambda i, w: (0, w[0] * CHUNKS + chunk))
    away = pl.BlockSpec((rows, width), lambda i, w: (0, (1 - w[0]) * CHUNKS + chunk))
    out = pl.BlockSpec((rows, 2 * width), lambda i, w: (0, 0))
    return pl.pallas_call(
        pack_kernel,
        grid_spec=pltpu.PrefetchScalarGridSpec(
            num_scalar_prefetch=1,
            grid=(1,),
            in_specs=[near, away, near, away],
            out_specs=[out, out],
        ),
        out_shape=[jax.ShapeDtypeStruct((rows, 2 * width), BF)] * 2,
        cost_estimate=pl.CostEstimate(flops=0, bytes_accessed=8 * rows * width * 2, transcendentals=0),
    )(where, a, a, b, b)


def halo_kernel(where, own, got, to_right, to_left):
    def fill(first, second):
        to_right[0:256, :] = second[256:512, :]
        to_right[256:384, :] = pool1(second[0:256, :])
        to_right[384:448, :] = pool2(first[0:256, :])
        to_right[448:512, :] = pool2(first[256:512, :])
        to_left[0:256, :] = first[0:256, :]
        to_left[256:384, :] = pool1(first[256:512, :])
        to_left[384:448, :] = pool2(second[0:256, :])
        to_left[448:512, :] = pool2(second[256:512, :])

    @pl.when(where[0] == 0)
    def _():
        fill(own, got)

    @pl.when(where[0] == 1)
    def _():
        fill(got, own)


def smem():
    return pl.BlockSpec(memory_space=pltpu.SMEM)


def vmem():
    return pl.BlockSpec(memory_space=pltpu.VMEM)


def halo(where, own, got):
    shape = jax.ShapeDtypeStruct(own.shape, BF)
    return pl.pallas_call(
        halo_kernel,
        in_specs=[smem(), vmem(), vmem()],
        out_specs=[vmem(), vmem()],
        out_shape=[shape, shape],
        cost_estimate=pl.CostEstimate(flops=0, bytes_accessed=4 * own.size * 2, transcendentals=0),
    )(where, own, got)


def swap64(x):
    return pltpu.roll(x, 64, 1)


def low_lanes(shape):
    return lax.broadcasted_iota(jnp.int32, shape, 1) < 64


def spread64(x, half):
    other = swap64(x)
    low = low_lanes(x.shape)
    return jnp.where(low, x, other) if half == 0 else jnp.where(low, other, x)


def far_forward(k, v_t, q, bias, p_ref):
    k0, k1, k2, k3 = k
    v0, v1, v2, v3 = v_t
    left, right = bias
    outer = dot_nt(jnp.concatenate([k0, k3], axis=0), q)
    first, last = outer[:BLOCK], outer[BLOCK:]
    mid_low = dot_nt(k2, q[:BLOCK])
    mid_high = dot_nt(k1, q[BLOCK:])
    if left is not None:
        first = first + left
        mid_high = mid_high + left
    if right is not None:
        last = last + right
        mid_low = mid_low + right
    mid = jnp.concatenate([mid_low, mid_high], axis=1)
    peak = jnp.max(jnp.maximum(jnp.maximum(first, last), mid), axis=0, keepdims=True)
    parts = [jnp.exp2((x - peak) * TO_LOG2) for x in (first, last, mid)]
    for n, x in enumerate(parts):
        p_ref[n * BLOCK : (n + 1) * BLOCK, :] = x
    total = jnp.sum(parts[0] + parts[1] + parts[2], axis=0, keepdims=True)
    pb = [x.astype(BF) for x in parts]
    mixed = dot_nn(
        jnp.concatenate([v0, v3], axis=1), jnp.concatenate(pb[:2], axis=0)
    ) + jnp.concatenate([dot_nn(v2, pb[2][:, :BLOCK]), dot_nn(v1, pb[2][:, BLOCK:])], axis=1)
    return peak, total, mixed


def far_backward(k_t, v, q, p_ref, factor, g, ec):
    k0, k1, k2, k3 = k_t
    v0, v1, v2, v3 = v
    e_out = p_ref[: 2 * BLOCK, :] * factor
    e_mid = p_ref[2 * BLOCK :, :] * factor
    eb_out, eb_mid = e_out.astype(BF), e_mid.astype(BF)
    p_out = dot_nt(jnp.concatenate([v0, v3], axis=0), g)
    p_mid = jnp.concatenate([dot_nt(v2, g[:BLOCK]), dot_nt(v1, g[BLOCK:])], axis=1)
    r_out = (e_out * (p_out - ec)).astype(BF)
    r_mid = (e_mid * (p_mid - ec)).astype(BF)
    dv03 = dot_nn(eb_out, g)
    dv2 = dot_nn(eb_mid[:, :BLOCK], g[:BLOCK])
    dv1 = dot_nn(eb_mid[:, BLOCK:], g[BLOCK:])
    dk03 = dot_nn(r_out, q)
    dk2 = dot_nn(r_mid[:, :BLOCK], q[:BLOCK])
    dk1 = dot_nn(r_mid[:, BLOCK:], q[BLOCK:])
    dq_t = dot_nn(jnp.concatenate([k0, k3], axis=1), r_out) + jnp.concatenate(
        [dot_nn(k2, r_mid[:, :BLOCK]), dot_nn(k1, r_mid[:, BLOCK:])], axis=1
    )
    return (dk03[:BLOCK], dk1, dk2, dk03[BLOCK:]), (dv03[:BLOCK], dv1, dv2, dv03[BLOCK:]), dq_t


def main_kernel(
    where, kv_own, kv_got, qg_own, qg_got, from_left, from_right,
    oq_own, oq_far, grad, to_left, to_right,
    raw, raw_t, one, one_t, two, two_t, qs, gs, p0, p1, p2, acc0, acc1, acc2, oq,
):
    side = where[0]
    width = kv_own.shape[1] // 2
    left_bias = (1 - where[1]).astype(F32) * MASKED
    right_bias = (1 - where[2]).astype(F32) * MASKED
    own_at = pl.multiple_of(side * 512, 512)
    got_at = pl.multiple_of((1 - side) * 512, 512)
    for h in range(width // HEAD):
        kc = slice(h * HEAD, (h + 1) * HEAD)
        vc = slice(width + h * HEAD, width + (h + 1) * HEAD)
        for n, cols in ((0, kc), (1, vc)):
            raw[n, 0:256, :] = from_left[0:256, cols]
            raw[n, pl.ds(256 + own_at, 512), :] = kv_own[:, cols]
            raw[n, pl.ds(256 + got_at, 512), :] = kv_got[:, cols]
            raw[n, 1280:1536, :] = from_right[0:256, cols]
            one[n, 0:128, :] = from_left[256:384, cols]
            for i in range(6):
                block = pool1(raw[n, i * PARENT : (i + 1) * PARENT, :])
                at = (i + 1) * BLOCK
                one[n, at : at + BLOCK, :] = block
            one[n, 896:1024, :] = from_right[256:384, cols]
            two[n, 0:128, :] = from_left[384:512, cols]
            two[n, 128:192, :] = pool12(one[n, 0:128, :])
            two[n, 192:256, :] = pool2(raw[n, 0:256, :])
            two[n, 256:320, :] = pool2(raw[n, 1280:1536, :])
            two[n, 320:384, :] = pool12(one[n, 896:1024, :])
            two[n, 384:512, :] = from_right[384:512, cols]
            for i in range(6):
                rows = slice(i * PARENT, (i + 1) * PARENT)
                raw_t[n, :, rows] = raw[n, rows, :].T
            for i in range(8):
                rows = slice(i * BLOCK, (i + 1) * BLOCK)
                one_t[n, :, rows] = one[n, rows, :].T
            for i in range(4):
                rows = slice(i * BLOCK, (i + 1) * BLOCK)
                two_t[n, :, rows] = two[n, rows, :].T
        qs[pl.ds(own_at, 512), :] = qg_own[:, kc]
        qs[pl.ds(got_at, 512), :] = qg_got[:, kc]
        gs[pl.ds(own_at, 512), :] = qg_own[:, vc]
        gs[pl.ds(got_at, 512), :] = qg_got[:, vc]

        def blocks(ref, n, which):
            return [ref[n, b * BLOCK : (b + 1) * BLOCK, :] for b in which]

        def blocks_t(ref, n, which):
            return [ref[n, :, b * BLOCK : (b + 1) * BLOCK] for b in which]

        q_parents = [qs[i * PARENT : (i + 1) * PARENT, :] for i in range(4)]
        q1 = [
            jnp.concatenate([pool1(q_parents[2 * j]), pool1(q_parents[2 * j + 1])], axis=0)
            for j in range(2)
        ]
        q2 = jnp.concatenate([pool2(x) for x in q_parents], axis=0)
        which1 = [(0, 1, 4, 5), (2, 3, 6, 7)]
        bias1 = [(left_bias, None), (None, right_bias)]
        which2 = (0, 1, 2, 3)
        far1 = [
            far_forward(
                blocks(one, 0, which1[j]), blocks_t(one_t, 1, which1[j]), q1[j], bias1[j], p1.at[j]
            )
            for j in range(2)
        ]
        far2 = far_forward(
            blocks(two, 0, which2), blocks_t(two_t, 1, which2), q2, (left_bias, right_bias), p2
        )
        acc0[...] = jnp.zeros_like(acc0)
        g1_t, ec1, f1 = [], [], []
        g2_t, ec2, low2 = [], [], []
        dq0 = []
        for i in range(4):
            rows = slice(i * PARENT, i * PARENT + 3 * PARENT)
            q = q_parents[i]
            g = gs[i * PARENT : (i + 1) * PARENT, :]
            s = dot_nt(raw[0, rows, :], q)
            pieces = [s[:PARENT], s[PARENT : 2 * PARENT], s[2 * PARENT :]]
            if i == 0:
                pieces[0] = pieces[0] + left_bias
            if i == 3:
                pieces[2] = pieces[2] + right_bias
            m0 = jnp.max(
                jnp.maximum(jnp.maximum(pieces[0], pieces[1]), pieces[2]), axis=0, keepdims=True
            )
            e = [jnp.exp2((x - m0) * TO_LOG2) for x in pieces]
            for n in range(3):
                p0[n * PARENT : (n + 1) * PARENT, :] = e[n]
            z0 = jnp.sum(e[0] + e[1] + e[2], axis=0, keepdims=True)
            u0 = dot_nn(raw_t[1, :, rows], jnp.concatenate([x.astype(BF) for x in e], axis=0))
            j, half = i // 2, i % 2
            lanes = slice(half * BLOCK, (half + 1) * BLOCK)
            m1, z1, u1 = (x[:, lanes] for x in far1[j])
            lanes2 = slice(j * BLOCK, (j + 1) * BLOCK)
            m2, z2, u2 = (spread64(x[:, lanes2], half) for x in far2)
            m1w, m2w = twice(m1, 1), twice(m2, 1)
            m = jnp.maximum(jnp.maximum(m0, m1w), m2w)
            a0 = jnp.exp2((m0 - m) * TO_LOG2)
            a1 = 2.0 * jnp.exp2((m1w - m) * TO_LOG2)
            a2 = 4.0 * jnp.exp2((m2w - m) * TO_LOG2)
            z = a0 * z0 + a1 * twice(z1, 1) + a2 * twice(z2, 1)
            inv = 1.0 / z
            o = ((a0 * inv) * u0 + (a1 * inv) * twice(u1, 1) + (a2 * inv) * twice(u2, 1)).astype(BF)
            oq[i, 0, h * HEAD : (h + 1) * HEAD, :] = o
            lg = m * TO_LOG2 + jnp.log2(z)
            g_t = g.astype(F32).T
            dr = jnp.sum(o.astype(F32) * g_t, axis=0, keepdims=True)
            lg_a, lg_b = lg[:, :BLOCK], lg[:, BLOCK:]
            g_a, g_b = g_t[:, :BLOCK], g_t[:, BLOCK:]
            dr_a, dr_b = dr[:, :BLOCK], dr[:, BLOCK:]
            low = jnp.minimum(lg_a, lg_b)
            w_a, w_b = jnp.exp2(low - lg_a), jnp.exp2(low - lg_b)
            g1_t.append((w_a * g_a + w_b * g_b).astype(BF))
            ec1.append(w_a * dr_a + w_b * dr_b)
            f1.append(2.0 * jnp.exp2(m1 * TO_LOG2 - low))
            lower = jnp.minimum(low, swap64(low))
            w_a, w_b = jnp.exp2(lower - lg_a), jnp.exp2(lower - lg_b)
            part = w_a * g_a + w_b * g_b
            g2_t.append(part + swap64(part))
            part = w_a * dr_a + w_b * dr_b
            ec2.append(part + swap64(part))
            low2.append(lower)
            f0 = jnp.exp2(m0 * TO_LOG2 - lg)
            products = dot_nt(raw[1, rows, :], g)
            weights = p0[...] * f0
            eb = weights.astype(BF)
            r = (weights * (products - dr)).astype(BF)
            acc0[1, rows, :] += dot_nn(eb, g)
            acc0[0, rows, :] += dot_nn(r, q)
            dq0.append(dot_nn(raw_t[0, :, rows], r))
        acc1[...] = jnp.zeros_like(acc1)
        dq1 = []
        for j in range(2):
            pair = slice(2 * j, 2 * j + 2)
            g1 = jnp.concatenate([x.astype(F32).T.astype(BF) for x in g1_t[pair]], axis=0)
            dk, dv, dq = far_backward(
                blocks_t(one_t, 0, which1[j]), blocks(one, 1, which1[j]), q1[j], p1.at[j],
                jnp.concatenate(f1[pair], axis=1), g1, jnp.concatenate(ec1[pair], axis=1),
            )
            for n, b in enumerate(which1[j]):
                acc1[0, b * BLOCK : (b + 1) * BLOCK, :] += dk[n]
                acc1[1, b * BLOCK : (b + 1) * BLOCK, :] += dv[n]
            dq1.append(dq)

        def joined(parts):
            return jnp.concatenate(
                [
                    jnp.where(low_lanes(parts[0].shape), parts[2 * j], parts[2 * j + 1])
                    for j in range(2)
                ],
                axis=1,
            )

        g2 = joined(g2_t).T.astype(BF)
        f2 = 4.0 * jnp.exp2(far2[0] * TO_LOG2 - joined(low2))
        dk, dv, dq2 = far_backward(
            blocks_t(two_t, 0, which2), blocks(two, 1, which2), q2, p2, f2, g2, joined(ec2)
        )
        for n in range(4):
            acc2[0, n * BLOCK : (n + 1) * BLOCK, :] = dk[n]
            acc2[1, n * BLOCK : (n + 1) * BLOCK, :] = dv[n]
        for i in range(4):
            j, half = i // 2, i % 2
            d1 = dq1[j][:, half * BLOCK : (half + 1) * BLOCK]
            d2 = spread64(dq2[:, j * BLOCK : (j + 1) * BLOCK], half)
            coarse = 0.5 * d1 + 0.25 * d2
            oq[i, 1, h * HEAD : (h + 1) * HEAD, :] = ((dq0[i] + twice(coarse, 1)) * INV_ROOT).astype(BF)
        for n, cols, scale in ((0, kc, INV_ROOT), (1, vc, 1.0)):
            for i in range(4):
                rows = slice((i + 1) * PARENT, (i + 2) * PARENT)
                coarse = acc1[n, (i + 2) * BLOCK : (i + 3) * BLOCK, :] * (0.5 * scale)
                grad[i * PARENT : (i + 1) * PARENT, cols] = acc0[n, rows, :] * scale + twice(coarse)
            far = acc2[n, 128:256, :] * (0.25 * scale)
            mid = acc1[n, 0:256, :] * (0.5 * scale)
            near = acc0[n, 0:256, :] * scale
            to_left[0:256, cols] = (near + twice(mid[128:] + twice(far[64:]))).astype(BF)
            to_left[256:384, cols] = (mid[:128] + twice(far[:64])).astype(BF)
            to_left[384:512, cols] = (acc2[n, 0:128, :] * (0.25 * scale)).astype(BF)
            far = acc2[n, 256:384, :] * (0.25 * scale)
            mid = acc1[n, 768:1024, :] * (0.5 * scale)
            near = acc0[n, 1280:1536, :] * scale
            to_right[0:256, cols] = (near + twice(mid[:128] + twice(far[:64]))).astype(BF)
            to_right[256:384, cols] = (mid[128:] + twice(far[64:])).astype(BF)
            to_right[384:512, cols] = (acc2[n, 384:512, :] * (0.25 * scale)).astype(BF)
    oq_own[...] = oq[pl.ds(side * 2, 2)]
    oq_far[...] = oq[pl.ds((1 - side) * 2, 2)]


def main(where, kv_own, kv_got, qg_own, qg_got, from_left, from_right):
    rows, both = kv_own.shape
    width = both // 2
    oq_shape = jax.ShapeDtypeStruct((2, 2, width, PARENT), BF)
    halo_shape = jax.ShapeDtypeStruct((512, both), BF)
    return pl.pallas_call(
        main_kernel,
        in_specs=[smem()] + [vmem()] * 6,
        out_specs=[vmem()] * 5,
        out_shape=[
            oq_shape,
            oq_shape,
            jax.ShapeDtypeStruct((2 * rows, both), F32),
            halo_shape,
            halo_shape,
        ],
        scratch_shapes=[
            pltpu.VMEM((2, 1536, HEAD), BF),
            pltpu.VMEM((2, HEAD, 1536), BF),
            pltpu.VMEM((2, 1024, HEAD), BF),
            pltpu.VMEM((2, HEAD, 1024), BF),
            pltpu.VMEM((2, 512, HEAD), BF),
            pltpu.VMEM((2, HEAD, 512), BF),
            pltpu.VMEM((1024, HEAD), BF),
            pltpu.VMEM((1024, HEAD), BF),
            pltpu.VMEM((768, PARENT), F32),
            pltpu.VMEM((2, 384, PARENT), F32),
            pltpu.VMEM((384, PARENT), F32),
            pltpu.VMEM((2, 1536, HEAD), F32),
            pltpu.VMEM((2, 1024, HEAD), F32),
            pltpu.VMEM((2, 512, HEAD), F32),
            pltpu.VMEM((4, 2, width, PARENT), BF),
        ],
        compiler_params=pltpu.CompilerParams(vmem_limit_bytes=32 * 1024 * 1024),
        cost_estimate=pl.CostEstimate(
            flops=4_000_000_000 // CHUNKS, bytes_accessed=6 * 512 * both * 2, transcendentals=1_000_000
        ),
    )(where, kv_own, kv_got, qg_own, qg_got, from_left, from_right)


def join_kernel(where, grad, from_left, from_right, own, far):
    def part(i, ref):
        x = grad[i * PARENT : (i + 1) * PARENT, :]
        tail = ref[384:512, :].astype(F32)
        return x, tail

    def value(i):
        x = grad[i * PARENT : (i + 1) * PARENT, :]
        if i == 0:
            return x + from_left[0:256, :].astype(F32) + twice(twice(from_right[384:448, :].astype(F32)))
        if i == 1:
            return x + twice(
                from_left[256:384, :].astype(F32) + twice(from_right[448:512, :].astype(F32))
            )
        if i == 2:
            return x + twice(
                from_right[256:384, :].astype(F32) + twice(from_left[384:448, :].astype(F32))
            )
        return x + from_right[0:256, :].astype(F32) + twice(twice(from_left[448:512, :].astype(F32)))

    def fill(first, second):
        first[0:256, :] = value(0).astype(BF)
        first[256:512, :] = value(1).astype(BF)
        second[0:256, :] = value(2).astype(BF)
        second[256:512, :] = value(3).astype(BF)

    @pl.when(where[0] == 0)
    def _():
        fill(own, far)

    @pl.when(where[0] == 1)
    def _():
        fill(far, own)


def join(where, grad, from_left, from_right):
    shape = jax.ShapeDtypeStruct(from_left.shape, BF)
    return pl.pallas_call(
        join_kernel,
        in_specs=[smem(), vmem(), vmem(), vmem()],
        out_specs=[vmem(), vmem()],
        out_shape=[shape, shape],
        cost_estimate=pl.CostEstimate(flops=0, bytes_accessed=grad.size * 8, transcendentals=0),
    )(where, grad, from_left, from_right)


def unpack_rows_kernel(where, *refs):
    ins, (first, second) = refs[:-2], refs[-2:]
    order = order_matrix(True)
    width = ins[0].shape[1] // 2
    for c in range(CHUNKS):
        for ref, side in ((ins[c], where[0]), (ins[CHUNKS + c], 1 - where[0])):
            at = pl.ds(pl.multiple_of((side * CHUNKS + c) * width, width), width)
            for i in range(2):
                rows = slice(i * PARENT, (i + 1) * PARENT)
                first[rows, at] = dot_nn(order, ref[rows, :width]).astype(BF)
                second[rows, at] = dot_nn(order, ref[rows, width:]).astype(BF)


def unpack_columns_kernel(where, *refs):
    ins, (first, second) = refs[:-2], refs[-2:]
    order = order_matrix(True)
    width = ins[0].shape[2]
    for c in range(CHUNKS):
        for ref, side in ((ins[c], where[0]), (ins[CHUNKS + c], 1 - where[0])):
            at = pl.ds(pl.multiple_of((side * CHUNKS + c) * width, width), width)
            for i in range(2):
                rows = slice(i * PARENT, (i + 1) * PARENT)
                first[rows, at] = dot_nt(order, ref[i, 0]).astype(BF)
                second[rows, at] = dot_nt(order, ref[i, 1]).astype(BF)


def unpack(kernel, where, own, got, shape):
    out = jax.ShapeDtypeStruct(shape, BF)
    return pl.pallas_call(
        kernel,
        in_specs=[smem()] + [vmem()] * (2 * CHUNKS),
        out_specs=[vmem(), vmem()],
        out_shape=[out, out],
        cost_estimate=pl.CostEstimate(flops=0, bytes_accessed=shape[0] * shape[1] * 8, transcendentals=0),
    )(where, *own, *got)


def on_device(queries, key_matrix, value_matrix, cotangent):
    axes = ("outer", "inner")
    count = lax.axis_size("outer") * lax.axis_size("inner")
    device = lax.axis_index("outer") * lax.axis_size("inner") + lax.axis_index("inner")
    where = jnp.stack(
        [device % 2, (device >= 2).astype(jnp.int32), (device < count - 2).astype(jnp.int32)]
    ).astype(jnp.int32)
    across = [(i, i ^ 1) for i in range(count)]
    rightward = [(i, i + 2) for i in range(count - 2)]
    leftward = [(i + 2, i) for i in range(count - 2)]

    def swap(x):
        return lax.ppermute(x, axes, across)

    kv = [pack(where, key_matrix, value_matrix, c) for c in range(CHUNKS)]
    qg = [pack(where, queries, cotangent, c) for c in range(CHUNKS)]
    oq_own, oq_got, kv_own, kv_got = [], [], [], []
    for c in range(CHUNKS):
        got_kv = swap(kv[c][1])
        got_qg = swap(qg[c][1])
        to_right, to_left = halo(where, kv[c][0], got_kv)
        from_left = lax.ppermute(to_right, axes, rightward)
        from_right = lax.ppermute(to_left, axes, leftward)
        own, far, grad, to_left, to_right = main(
            where, kv[c][0], got_kv, qg[c][0], got_qg, from_left, from_right
        )
        from_left = lax.ppermute(to_right, axes, rightward)
        from_right = lax.ppermute(to_left, axes, leftward)
        oq_own.append(own)
        oq_got.append(swap(far))
        own, far = join(where, grad, from_left, from_right)
        kv_own.append(own)
        kv_got.append(swap(far))
    attended, query_grad = unpack(unpack_columns_kernel, where, oq_own, oq_got, queries.shape)
    key_grad, value_grad = unpack(unpack_rows_kernel, where, kv_own, kv_got, queries.shape)
    return attended, query_grad, key_grad, value_grad


def solution(mesh):
    spec = P(("outer", "inner"), None)
    return jax.shard_map(
        on_device,
        mesh=mesh,
        in_specs=(spec,) * 4,
        out_specs=(spec,) * 4,
        check_vma=False,
    )
```

```python
import functools
import math

import jax
import jax.numpy as jnp
from jax import lax
from jax.experimental import pallas as pl
from jax.experimental.pallas import tpu as pltpu
from jax.sharding import PartitionSpec as P

HEAD = 128
BLOCK = 128
PARENT = 256
LEVELS = 3
CHUNKS = 2
INV_ROOT = HEAD**-0.5
TO_LOG2 = INV_ROOT * math.log2(math.e)
MASKED = -1e30
BF = jnp.bfloat16
F32 = jnp.float32


def dot_nt(a, b):
    return lax.dot_general(a, b, (((1,), (1,)), ((), ())), preferred_element_type=F32)


def dot_nn(a, b):
    return jnp.dot(a, b, preferred_element_type=F32)


def order_matrix(inverse):
    row = lax.broadcasted_iota(jnp.int32, (PARENT, PARENT), 0)
    col = lax.broadcasted_iota(jnp.int32, (PARENT, PARENT), 1)
    place, token = (col, row) if inverse else (row, col)
    slab = place // 64
    source = 4 * (place % 64) + 2 * (slab % 2) + slab // 2
    return jnp.where(source == token, 1.0, 0.0).astype(BF)


def pool1(x):
    return ((x[:BLOCK].astype(F32) + x[BLOCK:].astype(F32)) * 0.5).astype(BF)


def pool2(x):
    half = x[:BLOCK].astype(F32) + x[BLOCK:].astype(F32)
    return ((half[:64] + half[64:]) * 0.25).astype(BF)


def pool12(x):
    return ((x[:64].astype(F32) + x[64:].astype(F32)) * 0.5).astype(BF)


def twice(x, axis=0):
    return jnp.concatenate([x, x], axis=axis)


def pack_kernel(where, a, b, *refs):
    outs, held, sems = refs[: 2 * CHUNKS], refs[2 * CHUNKS], refs[2 * CHUNKS + 1]
    rows, columns = a.shape
    half = columns // 2
    width = half // CHUNKS
    copies = []
    for n, side in enumerate((1 - where[0], where[0])):
        at = pl.ds(pl.multiple_of(side * half, half), half)
        for m, ref in enumerate((a, b)):
            copies.append(
                pltpu.make_async_copy(ref.at[:, at], held.at[2 * n + m], sems.at[2 * n + m])
            )
            copies[-1].start()
    order = order_matrix(False)
    for n in range(2):
        own = n == 1
        for m in range(2):
            copies[2 * n + m].wait()
            for i in range(rows // PARENT):
                at = slice(i * PARENT, (i + 1) * PARENT)
                x = dot_nn(order, held[2 * n + m, at, :]).astype(BF)
                for c in range(CHUNKS):
                    ref = outs[c] if own else outs[CHUNKS + c]
                    ref[at, m * width : (m + 1) * width] = x[:, c * width : (c + 1) * width]


def pack(where, a, b):
    rows, columns = a.shape
    out = jax.ShapeDtypeStruct((rows, columns // CHUNKS), BF)
    outs = pl.pallas_call(
        pack_kernel,
        in_specs=[smem(), pl.BlockSpec(memory_space=pl.ANY), pl.BlockSpec(memory_space=pl.ANY)],
        out_specs=[vmem()] * (2 * CHUNKS),
        out_shape=[out] * (2 * CHUNKS),
        scratch_shapes=[
            pltpu.VMEM((4, rows, columns // 2), BF),
            pltpu.SemaphoreType.DMA((4,)),
        ],
        compiler_params=small(),
        cost_estimate=light(),
    )(where, a, b)
    return outs[:CHUNKS], outs[CHUNKS:]


def smem():
    return pl.BlockSpec(memory_space=pltpu.SMEM)


def vmem():
    return pl.BlockSpec(memory_space=pltpu.VMEM)


def small():
    return pltpu.CompilerParams(vmem_limit_bytes=8 * 1024 * 1024)


def light():
    return pl.CostEstimate(flops=1000, bytes_accessed=1000, transcendentals=0)


def halo_kernel(where, own, got, to_right, to_left):
    def fill(first, second):
        to_right[0:256, :] = second[256:512, :]
        to_right[256:384, :] = pool1(second[0:256, :])
        to_right[384:448, :] = pool2(first[0:256, :])
        to_right[448:512, :] = pool2(first[256:512, :])
        to_left[0:256, :] = first[0:256, :]
        to_left[256:384, :] = pool1(first[256:512, :])
        to_left[384:448, :] = pool2(second[0:256, :])
        to_left[448:512, :] = pool2(second[256:512, :])

    @pl.when(where[0] == 0)
    def _():
        fill(own, got)

    @pl.when(where[0] == 1)
    def _():
        fill(got, own)


def halo(where, own, got):
    shape = jax.ShapeDtypeStruct(own.shape, BF)
    return pl.pallas_call(
        halo_kernel,
        in_specs=[smem(), vmem(), vmem()],
        out_specs=[vmem(), vmem()],
        out_shape=[shape, shape],
        compiler_params=small(),
        cost_estimate=light(),
    )(where, own, got)


def swap64(x):
    return pltpu.roll(x, 64, 1)


def low_lanes(shape):
    return lax.broadcasted_iota(jnp.int32, shape, 1) < 64


def spread64(x, half):
    other = swap64(x)
    low = low_lanes(x.shape)
    return jnp.where(low, x, other) if half == 0 else jnp.where(low, other, x)


def far_forward(k, v_t, q, bias, p_ref):
    k0, k1, k2, k3 = k
    v0, v1, v2, v3 = v_t
    left, right = bias
    outer = dot_nt(jnp.concatenate([k0, k3], axis=0), q)
    first, last = outer[:BLOCK], outer[BLOCK:]
    mid_low = dot_nt(k2, q[:BLOCK])
    mid_high = dot_nt(k1, q[BLOCK:])
    if left is not None:
        first = first + left
        mid_high = mid_high + left
    if right is not None:
        last = last + right
        mid_low = mid_low + right
    mid = jnp.concatenate([mid_low, mid_high], axis=1)
    peak = jnp.max(jnp.maximum(jnp.maximum(first, last), mid), axis=0, keepdims=True)
    parts = [jnp.exp2((x - peak) * TO_LOG2) for x in (first, last, mid)]
    for n, x in enumerate(parts):
        p_ref[n * BLOCK : (n + 1) * BLOCK, :] = x
    total = jnp.sum(parts[0] + parts[1] + parts[2], axis=0, keepdims=True)
    pb = [x.astype(BF) for x in parts]
    mixed = dot_nn(
        jnp.concatenate([v0, v3], axis=1), jnp.concatenate(pb[:2], axis=0)
    ) + jnp.concatenate([dot_nn(v2, pb[2][:, :BLOCK]), dot_nn(v1, pb[2][:, BLOCK:])], axis=1)
    return peak, total, mixed


def far_backward(k_t, v, q, p_ref, factor, g, ec):
    k0, k1, k2, k3 = k_t
    v0, v1, v2, v3 = v
    e_out = p_ref[: 2 * BLOCK, :] * factor
    e_mid = p_ref[2 * BLOCK :, :] * factor
    eb_out, eb_mid = e_out.astype(BF), e_mid.astype(BF)
    p_out = dot_nt(jnp.concatenate([v0, v3], axis=0), g)
    p_mid = jnp.concatenate([dot_nt(v2, g[:BLOCK]), dot_nt(v1, g[BLOCK:])], axis=1)
    r_out = (e_out * (p_out - ec)).astype(BF)
    r_mid = (e_mid * (p_mid - ec)).astype(BF)
    dv03 = dot_nn(eb_out, g)
    dv2 = dot_nn(eb_mid[:, :BLOCK], g[:BLOCK])
    dv1 = dot_nn(eb_mid[:, BLOCK:], g[BLOCK:])
    dk03 = dot_nn(r_out, q)
    dk2 = dot_nn(r_mid[:, :BLOCK], q[:BLOCK])
    dk1 = dot_nn(r_mid[:, BLOCK:], q[BLOCK:])
    dq_t = dot_nn(jnp.concatenate([k0, k3], axis=1), r_out) + jnp.concatenate(
        [dot_nn(k2, r_mid[:, :BLOCK]), dot_nn(k1, r_mid[:, BLOCK:])], axis=1
    )
    return (dk03[:BLOCK], dk1, dk2, dk03[BLOCK:]), (dv03[:BLOCK], dv1, dv2, dv03[BLOCK:]), dq_t


def main_kernel(
    where, kv_own, kv_got, qg_own, qg_got, from_left, from_right,
    oq_own, oq_far, grad, to_left, to_right,
    raw, raw_t, one, one_t, two, two_t, qs, gs, p0, p1, p2, acc0, acc1, acc2, oq,
):
    side = where[0]
    width = kv_own.shape[1] // 2
    left_bias = (1 - where[1]).astype(F32) * MASKED
    right_bias = (1 - where[2]).astype(F32) * MASKED
    own_at = pl.multiple_of(side * 512, 512)
    got_at = pl.multiple_of((1 - side) * 512, 512)
    for h in range(width // HEAD):
        kc = slice(h * HEAD, (h + 1) * HEAD)
        vc = slice(width + h * HEAD, width + (h + 1) * HEAD)
        for n, cols in ((0, kc), (1, vc)):
            raw[n, 0:256, :] = from_left[0:256, cols]
            raw[n, pl.ds(256 + own_at, 512), :] = kv_own[:, cols]
            raw[n, pl.ds(256 + got_at, 512), :] = kv_got[:, cols]
            raw[n, 1280:1536, :] = from_right[0:256, cols]
            one[n, 0:128, :] = from_left[256:384, cols]
            for i in range(6):
                block = pool1(raw[n, i * PARENT : (i + 1) * PARENT, :])
                at = (i + 1) * BLOCK
                one[n, at : at + BLOCK, :] = block
            one[n, 896:1024, :] = from_right[256:384, cols]
            two[n, 0:128, :] = from_left[384:512, cols]
            two[n, 128:192, :] = pool12(one[n, 0:128, :])
            two[n, 192:256, :] = pool2(raw[n, 0:256, :])
            two[n, 256:320, :] = pool2(raw[n, 1280:1536, :])
            two[n, 320:384, :] = pool12(one[n, 896:1024, :])
            two[n, 384:512, :] = from_right[384:512, cols]
            for i in range(6):
                rows = slice(i * PARENT, (i + 1) * PARENT)
                raw_t[n, :, rows] = raw[n, rows, :].T
            for i in range(8):
                rows = slice(i * BLOCK, (i + 1) * BLOCK)
                one_t[n, :, rows] = one[n, rows, :].T
            for i in range(4):
                rows = slice(i * BLOCK, (i + 1) * BLOCK)
                two_t[n, :, rows] = two[n, rows, :].T
        qs[pl.ds(own_at, 512), :] = qg_own[:, kc]
        qs[pl.ds(got_at, 512), :] = qg_got[:, kc]
        gs[pl.ds(own_at, 512), :] = qg_own[:, vc]
        gs[pl.ds(got_at, 512), :] = qg_got[:, vc]

        def blocks(ref, n, which):
            return [ref[n, b * BLOCK : (b + 1) * BLOCK, :] for b in which]

        def blocks_t(ref, n, which):
            return [ref[n, :, b * BLOCK : (b + 1) * BLOCK] for b in which]

        q_parents = [qs[i * PARENT : (i + 1) * PARENT, :] for i in range(4)]
        q1 = [
            jnp.concatenate([pool1(q_parents[2 * j]), pool1(q_parents[2 * j + 1])], axis=0)
            for j in range(2)
        ]
        q2 = jnp.concatenate([pool2(x) for x in q_parents], axis=0)
        which1 = [(0, 1, 4, 5), (2, 3, 6, 7)]
        bias1 = [(left_bias, None), (None, right_bias)]
        which2 = (0, 1, 2, 3)
        far1 = [
            far_forward(
                blocks(one, 0, which1[j]), blocks_t(one_t, 1, which1[j]), q1[j], bias1[j], p1.at[j]
            )
            for j in range(2)
        ]
        far2 = far_forward(
            blocks(two, 0, which2), blocks_t(two_t, 1, which2), q2, (left_bias, right_bias), p2
        )
        acc0[...] = jnp.zeros_like(acc0)
        g1_t, ec1, f1 = [], [], []
        g2_t, ec2, low2 = [], [], []
        dq0 = []
        for i in range(4):
            rows = slice(i * PARENT, i * PARENT + 3 * PARENT)
            q = q_parents[i]
            g = gs[i * PARENT : (i + 1) * PARENT, :]
            s = dot_nt(raw[0, rows, :], q)
            pieces = [s[:PARENT], s[PARENT : 2 * PARENT], s[2 * PARENT :]]
            if i == 0:
                pieces[0] = pieces[0] + left_bias
            if i == 3:
                pieces[2] = pieces[2] + right_bias
            m0 = jnp.max(
                jnp.maximum(jnp.maximum(pieces[0], pieces[1]), pieces[2]), axis=0, keepdims=True
            )
            e = [jnp.exp2((x - m0) * TO_LOG2) for x in pieces]
            for n in range(3):
                p0[n * PARENT : (n + 1) * PARENT, :] = e[n]
            z0 = jnp.sum(e[0] + e[1] + e[2], axis=0, keepdims=True)
            u0 = dot_nn(raw_t[1, :, rows], jnp.concatenate([x.astype(BF) for x in e], axis=0))
            j, half = i // 2, i % 2
            lanes = slice(half * BLOCK, (half + 1) * BLOCK)
            m1, z1, u1 = (x[:, lanes] for x in far1[j])
            lanes2 = slice(j * BLOCK, (j + 1) * BLOCK)
            m2, z2, u2 = (spread64(x[:, lanes2], half) for x in far2)
            m1w, m2w = twice(m1, 1), twice(m2, 1)
            m = jnp.maximum(jnp.maximum(m0, m1w), m2w)
            a0 = jnp.exp2((m0 - m) * TO_LOG2)
            a1 = 2.0 * jnp.exp2((m1w - m) * TO_LOG2)
            a2 = 4.0 * jnp.exp2((m2w - m) * TO_LOG2)
            z = a0 * z0 + a1 * twice(z1, 1) + a2 * twice(z2, 1)
            inv = 1.0 / z
            o = ((a0 * inv) * u0 + (a1 * inv) * twice(u1, 1) + (a2 * inv) * twice(u2, 1)).astype(BF)
            oq[i, 0, h * HEAD : (h + 1) * HEAD, :] = o
            lg = m * TO_LOG2 + jnp.log2(z)
            g_t = g.astype(F32).T
            dr = jnp.sum(o.astype(F32) * g_t, axis=0, keepdims=True)
            lg_a, lg_b = lg[:, :BLOCK], lg[:, BLOCK:]
            g_a, g_b = g_t[:, :BLOCK], g_t[:, BLOCK:]
            dr_a, dr_b = dr[:, :BLOCK], dr[:, BLOCK:]
            low = jnp.minimum(lg_a, lg_b)
            w_a, w_b = jnp.exp2(low - lg_a), jnp.exp2(low - lg_b)
            g1_t.append((w_a * g_a + w_b * g_b).astype(BF))
            ec1.append(w_a * dr_a + w_b * dr_b)
            f1.append(2.0 * jnp.exp2(m1 * TO_LOG2 - low))
            lower = jnp.minimum(low, swap64(low))
            w_a, w_b = jnp.exp2(lower - lg_a), jnp.exp2(lower - lg_b)
            part = w_a * g_a + w_b * g_b
            g2_t.append(part + swap64(part))
            part = w_a * dr_a + w_b * dr_b
            ec2.append(part + swap64(part))
            low2.append(lower)
            f0 = jnp.exp2(m0 * TO_LOG2 - lg)
            products = dot_nt(raw[1, rows, :], g)
            weights = p0[...] * f0
            eb = weights.astype(BF)
            r = (weights * (products - dr)).astype(BF)
            acc0[1, rows, :] += dot_nn(eb, g)
            acc0[0, rows, :] += dot_nn(r, q)
            dq0.append(dot_nn(raw_t[0, :, rows], r))
        acc1[...] = jnp.zeros_like(acc1)
        dq1 = []
        for j in range(2):
            pair = slice(2 * j, 2 * j + 2)
            g1 = jnp.concatenate([x.astype(F32).T.astype(BF) for x in g1_t[pair]], axis=0)
            dk, dv, dq = far_backward(
                blocks_t(one_t, 0, which1[j]), blocks(one, 1, which1[j]), q1[j], p1.at[j],
                jnp.concatenate(f1[pair], axis=1), g1, jnp.concatenate(ec1[pair], axis=1),
            )
            for n, b in enumerate(which1[j]):
                acc1[0, b * BLOCK : (b + 1) * BLOCK, :] += dk[n]
                acc1[1, b * BLOCK : (b + 1) * BLOCK, :] += dv[n]
            dq1.append(dq)

        def joined(parts):
            return jnp.concatenate(
                [
                    jnp.where(low_lanes(parts[0].shape), parts[2 * j], parts[2 * j + 1])
                    for j in range(2)
                ],
                axis=1,
            )

        g2 = joined(g2_t).T.astype(BF)
        f2 = 4.0 * jnp.exp2(far2[0] * TO_LOG2 - joined(low2))
        dk, dv, dq2 = far_backward(
            blocks_t(two_t, 0, which2), blocks(two, 1, which2), q2, p2, f2, g2, joined(ec2)
        )
        for n in range(4):
            acc2[0, n * BLOCK : (n + 1) * BLOCK, :] = dk[n]
            acc2[1, n * BLOCK : (n + 1) * BLOCK, :] = dv[n]
        for i in range(4):
            j, half = i // 2, i % 2
            d1 = dq1[j][:, half * BLOCK : (half + 1) * BLOCK]
            d2 = spread64(dq2[:, j * BLOCK : (j + 1) * BLOCK], half)
            coarse = 0.5 * d1 + 0.25 * d2
            oq[i, 1, h * HEAD : (h + 1) * HEAD, :] = ((dq0[i] + twice(coarse, 1)) * INV_ROOT).astype(BF)
        for n, cols, scale in ((0, kc, INV_ROOT), (1, vc, 1.0)):
            for i in range(4):
                rows = slice((i + 1) * PARENT, (i + 2) * PARENT)
                coarse = acc1[n, (i + 2) * BLOCK : (i + 3) * BLOCK, :] * (0.5 * scale)
                grad[i * PARENT : (i + 1) * PARENT, cols] = acc0[n, rows, :] * scale + twice(coarse)
            far = acc2[n, 128:256, :] * (0.25 * scale)
            mid = acc1[n, 0:256, :] * (0.5 * scale)
            near = acc0[n, 0:256, :] * scale
            to_left[0:256, cols] = (near + twice(mid[128:] + twice(far[64:]))).astype(BF)
            to_left[256:384, cols] = (mid[:128] + twice(far[:64])).astype(BF)
            to_left[384:512, cols] = (acc2[n, 0:128, :] * (0.25 * scale)).astype(BF)
            far = acc2[n, 256:384, :] * (0.25 * scale)
            mid = acc1[n, 768:1024, :] * (0.5 * scale)
            near = acc0[n, 1280:1536, :] * scale
            to_right[0:256, cols] = (near + twice(mid[:128] + twice(far[:64]))).astype(BF)
            to_right[256:384, cols] = (mid[128:] + twice(far[64:])).astype(BF)
            to_right[384:512, cols] = (acc2[n, 384:512, :] * (0.25 * scale)).astype(BF)
    oq_own[...] = oq[pl.ds(side * 2, 2)]
    oq_far[...] = oq[pl.ds((1 - side) * 2, 2)]


def main(where, kv_own, kv_got, qg_own, qg_got, from_left, from_right):
    rows, both = kv_own.shape
    width = both // 2
    oq_shape = jax.ShapeDtypeStruct((2, 2, width, PARENT), BF)
    halo_shape = jax.ShapeDtypeStruct((512, both), BF)
    return pl.pallas_call(
        main_kernel,
        in_specs=[smem()] + [vmem()] * 6,
        out_specs=[vmem()] * 5,
        out_shape=[
            oq_shape,
            oq_shape,
            jax.ShapeDtypeStruct((2 * rows, both), F32),
            halo_shape,
            halo_shape,
        ],
        scratch_shapes=[
            pltpu.VMEM((2, 1536, HEAD), BF),
            pltpu.VMEM((2, HEAD, 1536), BF),
            pltpu.VMEM((2, 1024, HEAD), BF),
            pltpu.VMEM((2, HEAD, 1024), BF),
            pltpu.VMEM((2, 512, HEAD), BF),
            pltpu.VMEM((2, HEAD, 512), BF),
            pltpu.VMEM((1024, HEAD), BF),
            pltpu.VMEM((1024, HEAD), BF),
            pltpu.VMEM((768, PARENT), F32),
            pltpu.VMEM((2, 384, PARENT), F32),
            pltpu.VMEM((384, PARENT), F32),
            pltpu.VMEM((2, 1536, HEAD), F32),
            pltpu.VMEM((2, 1024, HEAD), F32),
            pltpu.VMEM((2, 512, HEAD), F32),
            pltpu.VMEM((4, 2, width, PARENT), BF),
        ],
        compiler_params=pltpu.CompilerParams(vmem_limit_bytes=24 * 1024 * 1024),
        cost_estimate=light(),
    )(where, kv_own, kv_got, qg_own, qg_got, from_left, from_right)


def join_kernel(where, grad, from_left, from_right, own, far):
    def part(i, ref):
        x = grad[i * PARENT : (i + 1) * PARENT, :]
        tail = ref[384:512, :].astype(F32)
        return x, tail

    def value(i):
        x = grad[i * PARENT : (i + 1) * PARENT, :]
        if i == 0:
            return x + from_left[0:256, :].astype(F32) + twice(twice(from_right[384:448, :].astype(F32)))
        if i == 1:
            return x + twice(
                from_left[256:384, :].astype(F32) + twice(from_right[448:512, :].astype(F32))
            )
        if i == 2:
            return x + twice(
                from_right[256:384, :].astype(F32) + twice(from_left[384:448, :].astype(F32))
            )
        return x + from_right[0:256, :].astype(F32) + twice(twice(from_left[448:512, :].astype(F32)))

    def fill(first, second):
        first[0:256, :] = value(0).astype(BF)
        first[256:512, :] = value(1).astype(BF)
        second[0:256, :] = value(2).astype(BF)
        second[256:512, :] = value(3).astype(BF)

    @pl.when(where[0] == 0)
    def _():
        fill(own, far)

    @pl.when(where[0] == 1)
    def _():
        fill(far, own)


def join(where, grad, from_left, from_right):
    shape = jax.ShapeDtypeStruct(from_left.shape, BF)
    return pl.pallas_call(
        join_kernel,
        in_specs=[smem(), vmem(), vmem(), vmem()],
        out_specs=[vmem(), vmem()],
        out_shape=[shape, shape],
        compiler_params=small(),
        cost_estimate=light(),
    )(where, grad, from_left, from_right)


def unpack_rows_kernel(where, *refs):
    ins, (first, second) = refs[:-2], refs[-2:]
    order = order_matrix(True)
    width = ins[0].shape[1] // 2
    for c in range(CHUNKS):
        for ref, side in ((ins[c], where[0]), (ins[CHUNKS + c], 1 - where[0])):
            at = pl.ds(pl.multiple_of((side * CHUNKS + c) * width, width), width)
            for i in range(2):
                rows = slice(i * PARENT, (i + 1) * PARENT)
                first[rows, at] = dot_nn(order, ref[rows, :width]).astype(BF)
                second[rows, at] = dot_nn(order, ref[rows, width:]).astype(BF)


def unpack_columns_kernel(where, *refs):
    ins, (first, second) = refs[:-2], refs[-2:]
    order = order_matrix(True)
    width = ins[0].shape[2]
    for c in range(CHUNKS):
        for ref, side in ((ins[c], where[0]), (ins[CHUNKS + c], 1 - where[0])):
            at = pl.ds(pl.multiple_of((side * CHUNKS + c) * width, width), width)
            for i in range(2):
                rows = slice(i * PARENT, (i + 1) * PARENT)
                first[rows, at] = dot_nt(order, ref[i, 0]).astype(BF)
                second[rows, at] = dot_nt(order, ref[i, 1]).astype(BF)


def unpack(kernel, where, own, got, shape):
    out = jax.ShapeDtypeStruct(shape, BF)
    return pl.pallas_call(
        kernel,
        in_specs=[smem()] + [vmem()] * (2 * CHUNKS),
        out_specs=[vmem(), vmem()],
        out_shape=[out, out],
        compiler_params=small(),
        cost_estimate=light(),
    )(where, *own, *got)


def on_device(queries, key_matrix, value_matrix, cotangent):
    axes = ("outer", "inner")
    count = lax.axis_size("outer") * lax.axis_size("inner")
    device = lax.axis_index("outer") * lax.axis_size("inner") + lax.axis_index("inner")
    where = jnp.stack(
        [device % 2, (device >= 2).astype(jnp.int32), (device < count - 2).astype(jnp.int32)]
    ).astype(jnp.int32)
    across = [(i, i ^ 1) for i in range(count)]
    rightward = [(i, i + 2) for i in range(count - 2)]
    leftward = [(i + 2, i) for i in range(count - 2)]

    def swap(x):
        return lax.ppermute(x, axes, across)

    kv, kv_far = pack(where, key_matrix, value_matrix)
    qg, qg_far = pack(where, queries, cotangent)
    oq_own, oq_got, kv_own, kv_got = [], [], [], []
    back = []
    for c in range(CHUNKS):
        got_kv = swap(kv_far[c])
        got_qg = swap(qg_far[c])
        to_right, to_left = halo(where, kv[c], got_kv)
        from_left = lax.ppermute(to_right, axes, rightward)
        from_right = lax.ppermute(to_left, axes, leftward)
        inputs = (kv[c], got_kv, qg[c], got_qg, from_left, from_right)
        if c > 0:
            oq_got[c - 1], inputs = lax.optimization_barrier((oq_got[c - 1], inputs))
        own, far, grad, to_left, to_right = main(where, *inputs)
        oq_own.append(own)
        oq_got.append(swap(far))
        from_left = lax.ppermute(to_right, axes, rightward)
        from_right = lax.ppermute(to_left, axes, leftward)
        back.append((grad, from_left, from_right))
    for c in range(CHUNKS):
        own, far = join(where, *back[c])
        kv_own.append(own)
        kv_got.append(swap(far))
    attended, query_grad = unpack(unpack_columns_kernel, where, oq_own, oq_got, queries.shape)
    key_grad, value_grad = unpack(unpack_rows_kernel, where, kv_own, kv_got, queries.shape)
    return attended, query_grad, key_grad, value_grad


def solution(mesh):
    spec = P(("outer", "inner"), None)
    return jax.shard_map(
        on_device,
        mesh=mesh,
        in_specs=(spec,) * 4,
        out_specs=(spec,) * 4,
        check_vma=False,
    )
```

```python
import functools
import math

import jax
import jax.numpy as jnp
from jax import lax
from jax.experimental import pallas as pl
from jax.experimental.pallas import tpu as pltpu
from jax.sharding import PartitionSpec as P

HEAD = 128
BLOCK = 128
PARENT = 256
LEVELS = 3
CHUNKS = 2
INV_ROOT = HEAD**-0.5
TO_LOG2 = INV_ROOT * math.log2(math.e)
MASKED = -1e30
BF = jnp.bfloat16
F32 = jnp.float32


def dot_nt(a, b):
    return lax.dot_general(a, b, (((1,), (1,)), ((), ())), preferred_element_type=F32)


def dot_nn(a, b):
    return jnp.dot(a, b, preferred_element_type=F32)


def order_matrix(inverse):
    row = lax.broadcasted_iota(jnp.int32, (PARENT, PARENT), 0)
    col = lax.broadcasted_iota(jnp.int32, (PARENT, PARENT), 1)
    place, token = (col, row) if inverse else (row, col)
    slab = place // 64
    source = 4 * (place % 64) + 2 * (slab % 2) + slab // 2
    return jnp.where(source == token, 1.0, 0.0).astype(BF)


def pool1(x):
    return ((x[:BLOCK].astype(F32) + x[BLOCK:].astype(F32)) * 0.5).astype(BF)


def pool2(x):
    half = x[:BLOCK].astype(F32) + x[BLOCK:].astype(F32)
    return ((half[:64] + half[64:]) * 0.25).astype(BF)


def pool12(x):
    return ((x[:64].astype(F32) + x[64:].astype(F32)) * 0.5).astype(BF)


def twice(x, axis=0):
    return jnp.concatenate([x, x], axis=axis)


def pack_kernel(where, a, b, *refs):
    outs, held, sems = refs[: 2 * CHUNKS], refs[2 * CHUNKS], refs[2 * CHUNKS + 1]
    rows, columns = a.shape
    half = columns // 2
    width = half // CHUNKS
    copies = []
    for n, side in enumerate((1 - where[0], where[0])):
        at = pl.ds(pl.multiple_of(side * half, half), half)
        for m, ref in enumerate((a, b)):
            copies.append(
                pltpu.make_async_copy(ref.at[:, at], held.at[2 * n + m], sems.at[2 * n + m])
            )
            copies[-1].start()
    order = order_matrix(False)
    for n in range(2):
        own = n == 1
        for m in range(2):
            copies[2 * n + m].wait()
            for i in range(rows // PARENT):
                at = slice(i * PARENT, (i + 1) * PARENT)
                x = dot_nn(order, held[2 * n + m, at, :]).astype(BF)
                for c in range(CHUNKS):
                    ref = outs[c] if own else outs[CHUNKS + c]
                    ref[at, m * width : (m + 1) * width] = x[:, c * width : (c + 1) * width]


def pack(where, a, b):
    rows, columns = a.shape
    out = jax.ShapeDtypeStruct((rows, columns // CHUNKS), BF)
    outs = pl.pallas_call(
        pack_kernel,
        in_specs=[smem(), pl.BlockSpec(memory_space=pl.ANY), pl.BlockSpec(memory_space=pl.ANY)],
        out_specs=[vmem()] * (2 * CHUNKS),
        out_shape=[out] * (2 * CHUNKS),
        scratch_shapes=[
            pltpu.VMEM((4, rows, columns // 2), BF),
            pltpu.SemaphoreType.DMA((4,)),
        ],
        compiler_params=small(),
        cost_estimate=light(),
    )(where, a, b)
    return outs[:CHUNKS], outs[CHUNKS:]


def smem():
    return pl.BlockSpec(memory_space=pltpu.SMEM)


def vmem():
    return pl.BlockSpec(memory_space=pltpu.VMEM)


def small():
    return pltpu.CompilerParams(vmem_limit_bytes=8 * 1024 * 1024)


def light():
    return pl.CostEstimate(flops=1000, bytes_accessed=1000, transcendentals=0)


def halo_kernel(where, own, got, to_right, to_left):
    def fill(first, second):
        to_right[0:256, :] = second[256:512, :]
        to_right[256:384, :] = pool1(second[0:256, :])
        to_right[384:448, :] = pool2(first[0:256, :])
        to_right[448:512, :] = pool2(first[256:512, :])
        to_left[0:256, :] = first[0:256, :]
        to_left[256:384, :] = pool1(first[256:512, :])
        to_left[384:448, :] = pool2(second[0:256, :])
        to_left[448:512, :] = pool2(second[256:512, :])

    @pl.when(where[0] == 0)
    def _():
        fill(own, got.at[1])

    @pl.when(where[0] == 1)
    def _():
        fill(got.at[0], own)


def halo(where, own, got):
    shape = jax.ShapeDtypeStruct(own.shape, BF)
    return pl.pallas_call(
        halo_kernel,
        in_specs=[smem(), vmem(), vmem()],
        out_specs=[vmem(), vmem()],
        out_shape=[shape, shape],
        compiler_params=small(),
        cost_estimate=light(),
    )(where, own, got)


def swap64(x):
    return pltpu.roll(x, 64, 1)


def low_lanes(shape):
    return lax.broadcasted_iota(jnp.int32, shape, 1) < 64


def spread64(x, half):
    other = swap64(x)
    low = low_lanes(x.shape)
    return jnp.where(low, x, other) if half == 0 else jnp.where(low, other, x)


def far_forward(k, v_t, q, bias, p_ref):
    k0, k1, k2, k3 = k
    v0, v1, v2, v3 = v_t
    left, right = bias
    outer = dot_nt(jnp.concatenate([k0, k3], axis=0), q)
    first, last = outer[:BLOCK], outer[BLOCK:]
    mid_low = dot_nt(k2, q[:BLOCK])
    mid_high = dot_nt(k1, q[BLOCK:])
    if left is not None:
        first = first + left
        mid_high = mid_high + left
    if right is not None:
        last = last + right
        mid_low = mid_low + right
    mid = jnp.concatenate([mid_low, mid_high], axis=1)
    peak = jnp.max(jnp.maximum(jnp.maximum(first, last), mid), axis=0, keepdims=True)
    parts = [jnp.exp2((x - peak) * TO_LOG2) for x in (first, last, mid)]
    for n, x in enumerate(parts):
        p_ref[n * BLOCK : (n + 1) * BLOCK, :] = x
    total = jnp.sum(parts[0] + parts[1] + parts[2], axis=0, keepdims=True)
    pb = [x.astype(BF) for x in parts]
    mixed = dot_nn(
        jnp.concatenate([v0, v3], axis=1), jnp.concatenate(pb[:2], axis=0)
    ) + jnp.concatenate([dot_nn(v2, pb[2][:, :BLOCK]), dot_nn(v1, pb[2][:, BLOCK:])], axis=1)
    return peak, total, mixed


def far_backward(k_t, v, q, p_ref, factor, g, ec):
    k0, k1, k2, k3 = k_t
    v0, v1, v2, v3 = v
    e_out = p_ref[: 2 * BLOCK, :] * factor
    e_mid = p_ref[2 * BLOCK :, :] * factor
    eb_out, eb_mid = e_out.astype(BF), e_mid.astype(BF)
    p_out = dot_nt(jnp.concatenate([v0, v3], axis=0), g)
    p_mid = jnp.concatenate([dot_nt(v2, g[:BLOCK]), dot_nt(v1, g[BLOCK:])], axis=1)
    r_out = (e_out * (p_out - ec)).astype(BF)
    r_mid = (e_mid * (p_mid - ec)).astype(BF)
    dv03 = dot_nn(eb_out, g)
    dv2 = dot_nn(eb_mid[:, :BLOCK], g[:BLOCK])
    dv1 = dot_nn(eb_mid[:, BLOCK:], g[BLOCK:])
    dk03 = dot_nn(r_out, q)
    dk2 = dot_nn(r_mid[:, :BLOCK], q[:BLOCK])
    dk1 = dot_nn(r_mid[:, BLOCK:], q[BLOCK:])
    dq_t = dot_nn(jnp.concatenate([k0, k3], axis=1), r_out) + jnp.concatenate(
        [dot_nn(k2, r_mid[:, :BLOCK]), dot_nn(k1, r_mid[:, BLOCK:])], axis=1
    )
    return (dk03[:BLOCK], dk1, dk2, dk03[BLOCK:]), (dv03[:BLOCK], dv1, dv2, dv03[BLOCK:]), dq_t


def main_kernel(
    where, kv_own, kv_got, qg_own, qg_got, from_left, from_right,
    oq_own, oq_far, grad, to_left, to_right,
    raw, raw_t, one, one_t, two, two_t, qs, gs, p0, p1, p2, acc0, acc1, acc2, oq,
):
    side = where[0]
    width = kv_own.shape[1] // 2
    left_bias = (1 - where[1]).astype(F32) * MASKED
    right_bias = (1 - where[2]).astype(F32) * MASKED
    own_at = pl.multiple_of(side * 512, 512)
    got_at = pl.multiple_of((1 - side) * 512, 512)
    for h in range(width // HEAD):
        kc = slice(h * HEAD, (h + 1) * HEAD)
        vc = slice(width + h * HEAD, width + (h + 1) * HEAD)
        for n, cols in ((0, kc), (1, vc)):
            raw[n, 0:256, :] = from_left[0:256, cols]
            raw[n, pl.ds(256 + own_at, 512), :] = kv_own[:, cols]
            raw[n, pl.ds(256 + got_at, 512), :] = kv_got[1 - side, :, cols]
            raw[n, 1280:1536, :] = from_right[0:256, cols]
            one[n, 0:128, :] = from_left[256:384, cols]
            for i in range(6):
                block = pool1(raw[n, i * PARENT : (i + 1) * PARENT, :])
                at = (i + 1) * BLOCK
                one[n, at : at + BLOCK, :] = block
            one[n, 896:1024, :] = from_right[256:384, cols]
            two[n, 0:128, :] = from_left[384:512, cols]
            two[n, 128:192, :] = pool12(one[n, 0:128, :])
            two[n, 192:256, :] = pool2(raw[n, 0:256, :])
            two[n, 256:320, :] = pool2(raw[n, 1280:1536, :])
            two[n, 320:384, :] = pool12(one[n, 896:1024, :])
            two[n, 384:512, :] = from_right[384:512, cols]
            for i in range(6):
                rows = slice(i * PARENT, (i + 1) * PARENT)
                raw_t[n, :, rows] = raw[n, rows, :].T
            for i in range(8):
                rows = slice(i * BLOCK, (i + 1) * BLOCK)
                one_t[n, :, rows] = one[n, rows, :].T
            for i in range(4):
                rows = slice(i * BLOCK, (i + 1) * BLOCK)
                two_t[n, :, rows] = two[n, rows, :].T
        qs[pl.ds(own_at, 512), :] = qg_own[:, kc]
        qs[pl.ds(got_at, 512), :] = qg_got[1 - side, :, kc]
        gs[pl.ds(own_at, 512), :] = qg_own[:, vc]
        gs[pl.ds(got_at, 512), :] = qg_got[1 - side, :, vc]

        def blocks(ref, n, which):
            return [ref[n, b * BLOCK : (b + 1) * BLOCK, :] for b in which]

        def blocks_t(ref, n, which):
            return [ref[n, :, b * BLOCK : (b + 1) * BLOCK] for b in which]

        q_parents = [qs[i * PARENT : (i + 1) * PARENT, :] for i in range(4)]
        q1 = [
            jnp.concatenate([pool1(q_parents[2 * j]), pool1(q_parents[2 * j + 1])], axis=0)
            for j in range(2)
        ]
        q2 = jnp.concatenate([pool2(x) for x in q_parents], axis=0)
        which1 = [(0, 1, 4, 5), (2, 3, 6, 7)]
        bias1 = [(left_bias, None), (None, right_bias)]
        which2 = (0, 1, 2, 3)
        far1 = [
            far_forward(
                blocks(one, 0, which1[j]), blocks_t(one_t, 1, which1[j]), q1[j], bias1[j], p1.at[j]
            )
            for j in range(2)
        ]
        far2 = far_forward(
            blocks(two, 0, which2), blocks_t(two_t, 1, which2), q2, (left_bias, right_bias), p2
        )
        acc0[...] = jnp.zeros_like(acc0)
        g1_t, ec1, f1 = [], [], []
        g2_t, ec2, low2 = [], [], []
        dq0 = []
        for i in range(4):
            rows = slice(i * PARENT, i * PARENT + 3 * PARENT)
            q = q_parents[i]
            g = gs[i * PARENT : (i + 1) * PARENT, :]
            s = dot_nt(raw[0, rows, :], q)
            pieces = [s[:PARENT], s[PARENT : 2 * PARENT], s[2 * PARENT :]]
            if i == 0:
                pieces[0] = pieces[0] + left_bias
            if i == 3:
                pieces[2] = pieces[2] + right_bias
            m0 = jnp.max(
                jnp.maximum(jnp.maximum(pieces[0], pieces[1]), pieces[2]), axis=0, keepdims=True
            )
            e = [jnp.exp2((x - m0) * TO_LOG2) for x in pieces]
            for n in range(3):
                p0[n * PARENT : (n + 1) * PARENT, :] = e[n]
            z0 = jnp.sum(e[0] + e[1] + e[2], axis=0, keepdims=True)
            u0 = dot_nn(raw_t[1, :, rows], jnp.concatenate([x.astype(BF) for x in e], axis=0))
            j, half = i // 2, i % 2
            lanes = slice(half * BLOCK, (half + 1) * BLOCK)
            m1, z1, u1 = (x[:, lanes] for x in far1[j])
            lanes2 = slice(j * BLOCK, (j + 1) * BLOCK)
            m2, z2, u2 = (spread64(x[:, lanes2], half) for x in far2)
            m1w, m2w = twice(m1, 1), twice(m2, 1)
            m = jnp.maximum(jnp.maximum(m0, m1w), m2w)
            a0 = jnp.exp2((m0 - m) * TO_LOG2)
            a1 = 2.0 * jnp.exp2((m1w - m) * TO_LOG2)
            a2 = 4.0 * jnp.exp2((m2w - m) * TO_LOG2)
            z = a0 * z0 + a1 * twice(z1, 1) + a2 * twice(z2, 1)
            inv = 1.0 / z
            o = ((a0 * inv) * u0 + (a1 * inv) * twice(u1, 1) + (a2 * inv) * twice(u2, 1)).astype(BF)
            oq[i, 0, h * HEAD : (h + 1) * HEAD, :] = o
            lg = m * TO_LOG2 + jnp.log2(z)
            g_t = g.astype(F32).T
            dr = jnp.sum(o.astype(F32) * g_t, axis=0, keepdims=True)
            lg_a, lg_b = lg[:, :BLOCK], lg[:, BLOCK:]
            g_a, g_b = g_t[:, :BLOCK], g_t[:, BLOCK:]
            dr_a, dr_b = dr[:, :BLOCK], dr[:, BLOCK:]
            low = jnp.minimum(lg_a, lg_b)
            w_a, w_b = jnp.exp2(low - lg_a), jnp.exp2(low - lg_b)
            g1_t.append((w_a * g_a + w_b * g_b).astype(BF))
            ec1.append(w_a * dr_a + w_b * dr_b)
            f1.append(2.0 * jnp.exp2(m1 * TO_LOG2 - low))
            lower = jnp.minimum(low, swap64(low))
            w_a, w_b = jnp.exp2(lower - lg_a), jnp.exp2(lower - lg_b)
            part = w_a * g_a + w_b * g_b
            g2_t.append(part + swap64(part))
            part = w_a * dr_a + w_b * dr_b
            ec2.append(part + swap64(part))
            low2.append(lower)
            f0 = jnp.exp2(m0 * TO_LOG2 - lg)
            products = dot_nt(raw[1, rows, :], g)
            weights = p0[...] * f0
            eb = weights.astype(BF)
            r = (weights * (products - dr)).astype(BF)
            acc0[1, rows, :] += dot_nn(eb, g)
            acc0[0, rows, :] += dot_nn(r, q)
            dq0.append(dot_nn(raw_t[0, :, rows], r))
        acc1[...] = jnp.zeros_like(acc1)
        dq1 = []
        for j in range(2):
            pair = slice(2 * j, 2 * j + 2)
            g1 = jnp.concatenate([x.astype(F32).T.astype(BF) for x in g1_t[pair]], axis=0)
            dk, dv, dq = far_backward(
                blocks_t(one_t, 0, which1[j]), blocks(one, 1, which1[j]), q1[j], p1.at[j],
                jnp.concatenate(f1[pair], axis=1), g1, jnp.concatenate(ec1[pair], axis=1),
            )
            for n, b in enumerate(which1[j]):
                acc1[0, b * BLOCK : (b + 1) * BLOCK, :] += dk[n]
                acc1[1, b * BLOCK : (b + 1) * BLOCK, :] += dv[n]
            dq1.append(dq)

        def joined(parts):
            return jnp.concatenate(
                [
                    jnp.where(low_lanes(parts[0].shape), parts[2 * j], parts[2 * j + 1])
                    for j in range(2)
                ],
                axis=1,
            )

        g2 = joined(g2_t).T.astype(BF)
        f2 = 4.0 * jnp.exp2(far2[0] * TO_LOG2 - joined(low2))
        dk, dv, dq2 = far_backward(
            blocks_t(two_t, 0, which2), blocks(two, 1, which2), q2, p2, f2, g2, joined(ec2)
        )
        for n in range(4):
            acc2[0, n * BLOCK : (n + 1) * BLOCK, :] = dk[n]
            acc2[1, n * BLOCK : (n + 1) * BLOCK, :] = dv[n]
        for i in range(4):
            j, half = i // 2, i % 2
            d1 = dq1[j][:, half * BLOCK : (half + 1) * BLOCK]
            d2 = spread64(dq2[:, j * BLOCK : (j + 1) * BLOCK], half)
            coarse = 0.5 * d1 + 0.25 * d2
            oq[i, 1, h * HEAD : (h + 1) * HEAD, :] = ((dq0[i] + twice(coarse, 1)) * INV_ROOT).astype(BF)
        for n, cols, scale in ((0, kc, INV_ROOT), (1, vc, 1.0)):
            for i in range(4):
                rows = slice((i + 1) * PARENT, (i + 2) * PARENT)
                coarse = acc1[n, (i + 2) * BLOCK : (i + 3) * BLOCK, :] * (0.5 * scale)
                grad[i * PARENT : (i + 1) * PARENT, cols] = acc0[n, rows, :] * scale + twice(coarse)
            far = acc2[n, 128:256, :] * (0.25 * scale)
            mid = acc1[n, 0:256, :] * (0.5 * scale)
            near = acc0[n, 0:256, :] * scale
            to_left[0:256, cols] = (near + twice(mid[128:] + twice(far[64:]))).astype(BF)
            to_left[256:384, cols] = (mid[:128] + twice(far[:64])).astype(BF)
            to_left[384:512, cols] = (acc2[n, 0:128, :] * (0.25 * scale)).astype(BF)
            far = acc2[n, 256:384, :] * (0.25 * scale)
            mid = acc1[n, 768:1024, :] * (0.5 * scale)
            near = acc0[n, 1280:1536, :] * scale
            to_right[0:256, cols] = (near + twice(mid[:128] + twice(far[:64]))).astype(BF)
            to_right[256:384, cols] = (mid[128:] + twice(far[64:])).astype(BF)
            to_right[384:512, cols] = (acc2[n, 384:512, :] * (0.25 * scale)).astype(BF)
    oq_own[...] = oq[pl.ds(side * 2, 2)]
    oq_far[...] = oq[pl.ds((1 - side) * 2, 2)]


def main(where, kv_own, kv_got, qg_own, qg_got, from_left, from_right):
    rows, both = kv_own.shape
    width = both // 2
    oq_shape = jax.ShapeDtypeStruct((2, 2, width, PARENT), BF)
    halo_shape = jax.ShapeDtypeStruct((512, both), BF)
    return pl.pallas_call(
        main_kernel,
        in_specs=[smem()] + [vmem()] * 6,
        out_specs=[vmem()] * 5,
        out_shape=[
            oq_shape,
            oq_shape,
            jax.ShapeDtypeStruct((2 * rows, both), F32),
            halo_shape,
            halo_shape,
        ],
        scratch_shapes=[
            pltpu.VMEM((2, 1536, HEAD), BF),
            pltpu.VMEM((2, HEAD, 1536), BF),
            pltpu.VMEM((2, 1024, HEAD), BF),
            pltpu.VMEM((2, HEAD, 1024), BF),
            pltpu.VMEM((2, 512, HEAD), BF),
            pltpu.VMEM((2, HEAD, 512), BF),
            pltpu.VMEM((1024, HEAD), BF),
            pltpu.VMEM((1024, HEAD), BF),
            pltpu.VMEM((768, PARENT), F32),
            pltpu.VMEM((2, 384, PARENT), F32),
            pltpu.VMEM((384, PARENT), F32),
            pltpu.VMEM((2, 1536, HEAD), F32),
            pltpu.VMEM((2, 1024, HEAD), F32),
            pltpu.VMEM((2, 512, HEAD), F32),
            pltpu.VMEM((4, 2, width, PARENT), BF),
        ],
        compiler_params=pltpu.CompilerParams(vmem_limit_bytes=24 * 1024 * 1024),
        cost_estimate=light(),
    )(where, kv_own, kv_got, qg_own, qg_got, from_left, from_right)


def join_kernel(where, grad, from_left, from_right, own, far):
    def part(i, ref):
        x = grad[i * PARENT : (i + 1) * PARENT, :]
        tail = ref[384:512, :].astype(F32)
        return x, tail

    def value(i):
        x = grad[i * PARENT : (i + 1) * PARENT, :]
        if i == 0:
            return x + from_left[0:256, :].astype(F32) + twice(twice(from_right[384:448, :].astype(F32)))
        if i == 1:
            return x + twice(
                from_left[256:384, :].astype(F32) + twice(from_right[448:512, :].astype(F32))
            )
        if i == 2:
            return x + twice(
                from_right[256:384, :].astype(F32) + twice(from_left[384:448, :].astype(F32))
            )
        return x + from_right[0:256, :].astype(F32) + twice(twice(from_left[448:512, :].astype(F32)))

    def fill(first, second):
        first[0:256, :] = value(0).astype(BF)
        first[256:512, :] = value(1).astype(BF)
        second[0:256, :] = value(2).astype(BF)
        second[256:512, :] = value(3).astype(BF)

    @pl.when(where[0] == 0)
    def _():
        fill(own, far)

    @pl.when(where[0] == 1)
    def _():
        fill(far, own)


def join(where, grad, from_left, from_right):
    shape = jax.ShapeDtypeStruct(from_left.shape, BF)
    return pl.pallas_call(
        join_kernel,
        in_specs=[smem(), vmem(), vmem(), vmem()],
        out_specs=[vmem(), vmem()],
        out_shape=[shape, shape],
        compiler_params=small(),
        cost_estimate=light(),
    )(where, grad, from_left, from_right)


def unpack_rows_kernel(where, *refs):
    ins, (first, second) = refs[:-2], refs[-2:]
    order = order_matrix(True)
    width = ins[0].shape[1] // 2
    for c in range(CHUNKS):
        got = ins[CHUNKS + c].at[1 - where[0]]
        for ref, side in ((ins[c], where[0]), (got, 1 - where[0])):
            at = pl.ds(pl.multiple_of((side * CHUNKS + c) * width, width), width)
            for i in range(2):
                rows = slice(i * PARENT, (i + 1) * PARENT)
                first[rows, at] = dot_nn(order, ref[rows, :width]).astype(BF)
                second[rows, at] = dot_nn(order, ref[rows, width:]).astype(BF)


def unpack_columns_kernel(where, *refs):
    ins, (first, second) = refs[:-2], refs[-2:]
    order = order_matrix(True)
    width = ins[0].shape[2]
    for c in range(CHUNKS):
        got = ins[CHUNKS + c].at[1 - where[0]]
        for ref, side in ((ins[c], where[0]), (got, 1 - where[0])):
            at = pl.ds(pl.multiple_of((side * CHUNKS + c) * width, width), width)
            for i in range(2):
                rows = slice(i * PARENT, (i + 1) * PARENT)
                first[rows, at] = dot_nt(order, ref[i, 0]).astype(BF)
                second[rows, at] = dot_nt(order, ref[i, 1]).astype(BF)


def unpack(kernel, where, own, got, shape):
    out = jax.ShapeDtypeStruct(shape, BF)
    return pl.pallas_call(
        kernel,
        in_specs=[smem()] + [vmem()] * (2 * CHUNKS),
        out_specs=[vmem(), vmem()],
        out_shape=[out, out],
        compiler_params=small(),
        cost_estimate=light(),
    )(where, *own, *got)


def on_device(queries, key_matrix, value_matrix, cotangent):
    axes = ("outer", "inner")
    count = lax.axis_size("outer") * lax.axis_size("inner")
    device = lax.axis_index("outer") * lax.axis_size("inner") + lax.axis_index("inner")
    where = jnp.stack(
        [device % 2, (device >= 2).astype(jnp.int32), (device < count - 2).astype(jnp.int32)]
    ).astype(jnp.int32)
    rightward = [(i, i + 2) for i in range(count - 2)]
    leftward = [(i + 2, i) for i in range(count - 2)]

    inner = lax.axis_size("inner")
    pairs = None if inner == 2 else [[i, i + 1] for i in range(0, inner, 2)]

    def swap(x):
        return lax.all_gather(x, "inner", axis_index_groups=pairs)

    kv, kv_far = pack(where, key_matrix, value_matrix)
    qg, qg_far = pack(where, queries, cotangent)
    oq_own, oq_got, kv_own, kv_got = [], [], [], []
    back = []
    for c in range(CHUNKS):
        got_kv = swap(kv_far[c])
        got_qg = swap(qg_far[c])
        to_right, to_left = halo(where, kv[c], got_kv)
        from_left = lax.ppermute(to_right, axes, rightward)
        from_right = lax.ppermute(to_left, axes, leftward)
        inputs = (kv[c], got_kv, qg[c], got_qg, from_left, from_right)
        if c > 0:
            oq_got[c - 1], inputs = lax.optimization_barrier((oq_got[c - 1], inputs))
        own, far, grad, to_left, to_right = main(where, *inputs)
        oq_own.append(own)
        oq_got.append(swap(far))
        from_left = lax.ppermute(to_right, axes, rightward)
        from_right = lax.ppermute(to_left, axes, leftward)
        back.append((grad, from_left, from_right))
    for c in range(CHUNKS):
        own, far = join(where, *back[c])
        kv_own.append(own)
        kv_got.append(swap(far))
    attended, query_grad = unpack(unpack_columns_kernel, where, oq_own, oq_got, queries.shape)
    key_grad, value_grad = unpack(unpack_rows_kernel, where, kv_own, kv_got, queries.shape)
    return attended, query_grad, key_grad, value_grad


def solution(mesh):
    spec = P(("outer", "inner"), None)
    return jax.shard_map(
        on_device,
        mesh=mesh,
        in_specs=(spec,) * 4,
        out_specs=(spec,) * 4,
        check_vma=False,
    )
```

```python
import functools
import math

import jax
import jax.numpy as jnp
from jax import lax
from jax.experimental import pallas as pl
from jax.experimental.pallas import tpu as pltpu
from jax.sharding import PartitionSpec as P

HEAD = 128
BLOCK = 128
PARENT = 256
LEVELS = 3
CHUNKS = 2
INV_ROOT = HEAD**-0.5
TO_LOG2 = INV_ROOT * math.log2(math.e)
MASKED = -1e30
BF = jnp.bfloat16
F32 = jnp.float32


def dot_nt(a, b):
    return lax.dot_general(a, b, (((1,), (1,)), ((), ())), preferred_element_type=F32)


def dot_nn(a, b):
    return jnp.dot(a, b, preferred_element_type=F32)


def order_matrix(inverse):
    row = lax.broadcasted_iota(jnp.int32, (PARENT, PARENT), 0)
    col = lax.broadcasted_iota(jnp.int32, (PARENT, PARENT), 1)
    place, token = (col, row) if inverse else (row, col)
    slab = place // 64
    source = 4 * (place % 64) + 2 * (slab % 2) + slab // 2
    return jnp.where(source == token, 1.0, 0.0).astype(BF)


def pool1(x):
    return ((x[:BLOCK].astype(F32) + x[BLOCK:].astype(F32)) * 0.5).astype(BF)


def pool2(x):
    half = x[:BLOCK].astype(F32) + x[BLOCK:].astype(F32)
    return ((half[:64] + half[64:]) * 0.25).astype(BF)


def pool12(x):
    return ((x[:64].astype(F32) + x[64:].astype(F32)) * 0.5).astype(BF)


def twice(x, axis=0):
    return jnp.concatenate([x, x], axis=axis)


def pack_kernel(where, a, b, *refs):
    outs, held, sems = refs[: 2 * CHUNKS], refs[2 * CHUNKS], refs[2 * CHUNKS + 1]
    rows, columns = a.shape
    half = columns // 2
    width = half // CHUNKS
    copies = []
    for n, side in enumerate((1 - where[0], where[0])):
        at = pl.ds(pl.multiple_of(side * half, half), half)
        for m, ref in enumerate((a, b)):
            copies.append(
                pltpu.make_async_copy(ref.at[:, at], held.at[2 * n + m], sems.at[2 * n + m])
            )
            copies[-1].start()
    order = order_matrix(False)
    for n in range(2):
        own = n == 1
        for m in range(2):
            copies[2 * n + m].wait()
            for i in range(rows // PARENT):
                at = slice(i * PARENT, (i + 1) * PARENT)
                x = dot_nn(order, held[2 * n + m, at, :]).astype(BF)
                for c in range(CHUNKS):
                    ref = outs[c] if own else outs[CHUNKS + c]
                    ref[at, m * width : (m + 1) * width] = x[:, c * width : (c + 1) * width]


def pack(where, a, b):
    rows, columns = a.shape
    out = jax.ShapeDtypeStruct((rows, columns // CHUNKS), BF)
    outs = pl.pallas_call(
        pack_kernel,
        in_specs=[smem(), pl.BlockSpec(memory_space=pltpu.HBM), pl.BlockSpec(memory_space=pltpu.HBM)],
        out_specs=[vmem()] * (2 * CHUNKS),
        out_shape=[out] * (2 * CHUNKS),
        scratch_shapes=[
            pltpu.VMEM((4, rows, columns // 2), BF),
            pltpu.SemaphoreType.DMA((4,)),
        ],
        compiler_params=small(),
        cost_estimate=light(),
    )(where, a, b)
    return outs[:CHUNKS], outs[CHUNKS:]


def smem():
    return pl.BlockSpec(memory_space=pltpu.SMEM)


def vmem():
    return pl.BlockSpec(memory_space=pltpu.VMEM)


def small():
    return pltpu.CompilerParams(vmem_limit_bytes=8 * 1024 * 1024)


def light():
    return pl.CostEstimate(flops=1000, bytes_accessed=1000, transcendentals=0)


def halo_kernel(where, own, got, near, wide):
    def fill(first, second, to_right, to_left):
        to_right[0:256, :] = second[256:512, :]
        to_right[256:384, :] = pool1(second[0:256, :])
        to_right[384:448, :] = pool2(first[0:256, :])
        to_right[448:512, :] = pool2(first[256:512, :])
        to_left[0:256, :] = first[0:256, :]
        to_left[256:384, :] = pool1(first[256:512, :])
        to_left[384:448, :] = pool2(second[0:256, :])
        to_left[448:512, :] = pool2(second[256:512, :])

    for side in range(2):
        for odd in range(2):

            @pl.when((where[0] == side) & (where[3] == odd))
            def _(side=side, odd=odd):
                halves = (own, got) if side == 0 else (got, own)
                fill(*halves, *((near, wide) if odd == 0 else (wide, near)))


def halo(where, own, got):
    shape = jax.ShapeDtypeStruct(own.shape, BF)
    return pl.pallas_call(
        halo_kernel,
        in_specs=[smem(), vmem(), vmem()],
        out_specs=[vmem(), vmem()],
        out_shape=[shape, shape],
        compiler_params=small(),
        cost_estimate=light(),
    )(where, own, got)


def swap64(x):
    return pltpu.roll(x, 64, 1)


def low_lanes(shape):
    return lax.broadcasted_iota(jnp.int32, shape, 1) < 64


def spread64(x, half):
    other = swap64(x)
    low = low_lanes(x.shape)
    return jnp.where(low, x, other) if half == 0 else jnp.where(low, other, x)


def far_forward(k, v_t, q, bias, p_ref):
    k0, k1, k2, k3 = k
    v0, v1, v2, v3 = v_t
    left, right = bias
    outer = dot_nt(jnp.concatenate([k0, k3], axis=0), q)
    first, last = outer[:BLOCK], outer[BLOCK:]
    mid_low = dot_nt(k2, q[:BLOCK])
    mid_high = dot_nt(k1, q[BLOCK:])
    if left is not None:
        first = first + left
        mid_high = mid_high + left
    if right is not None:
        last = last + right
        mid_low = mid_low + right
    mid = jnp.concatenate([mid_low, mid_high], axis=1)
    peak = jnp.max(jnp.maximum(jnp.maximum(first, last), mid), axis=0, keepdims=True)
    parts = [jnp.exp2((x - peak) * TO_LOG2) for x in (first, last, mid)]
    for n, x in enumerate(parts):
        p_ref[n * BLOCK : (n + 1) * BLOCK, :] = x
    total = jnp.sum(parts[0] + parts[1] + parts[2], axis=0, keepdims=True)
    pb = [x.astype(BF) for x in parts]
    mixed = dot_nn(
        jnp.concatenate([v0, v3], axis=1), jnp.concatenate(pb[:2], axis=0)
    ) + jnp.concatenate([dot_nn(v2, pb[2][:, :BLOCK]), dot_nn(v1, pb[2][:, BLOCK:])], axis=1)
    return peak, total, mixed


def far_backward(k_t, v, q, p_ref, factor, g, ec):
    k0, k1, k2, k3 = k_t
    v0, v1, v2, v3 = v
    e_out = p_ref[: 2 * BLOCK, :] * factor
    e_mid = p_ref[2 * BLOCK :, :] * factor
    eb_out, eb_mid = e_out.astype(BF), e_mid.astype(BF)
    p_out = dot_nt(jnp.concatenate([v0, v3], axis=0), g)
    p_mid = jnp.concatenate([dot_nt(v2, g[:BLOCK]), dot_nt(v1, g[BLOCK:])], axis=1)
    r_out = (e_out * (p_out - ec)).astype(BF)
    r_mid = (e_mid * (p_mid - ec)).astype(BF)
    dv03 = dot_nn(eb_out, g)
    dv2 = dot_nn(eb_mid[:, :BLOCK], g[:BLOCK])
    dv1 = dot_nn(eb_mid[:, BLOCK:], g[BLOCK:])
    dk03 = dot_nn(r_out, q)
    dk2 = dot_nn(r_mid[:, :BLOCK], q[:BLOCK])
    dk1 = dot_nn(r_mid[:, BLOCK:], q[BLOCK:])
    dq_t = dot_nn(jnp.concatenate([k0, k3], axis=1), r_out) + jnp.concatenate(
        [dot_nn(k2, r_mid[:, :BLOCK]), dot_nn(k1, r_mid[:, BLOCK:])], axis=1
    )
    return (dk03[:BLOCK], dk1, dk2, dk03[BLOCK:]), (dv03[:BLOCK], dv1, dv2, dv03[BLOCK:]), dq_t


def main_kernel(
    where, kv_own, kv_got, qg_own, qg_got, near_got, wide_got,
    oq_own, oq_far, grad, near_out, wide_out,
    raw, raw_t, one, one_t, two, two_t, qs, gs, p0, p1, p2, acc0, acc1, acc2, oq, halos,
):
    side = where[0]
    odd = where[3]
    halos[1 - odd] = near_got[...]
    halos[odd] = wide_got[...]
    from_left, from_right = halos.at[0], halos.at[1]
    to_left, to_right = halos.at[0], halos.at[1]
    width = kv_own.shape[1] // 2
    left_bias = (1 - where[1]).astype(F32) * MASKED
    right_bias = (1 - where[2]).astype(F32) * MASKED
    own_at = pl.multiple_of(side * 512, 512)
    got_at = pl.multiple_of((1 - side) * 512, 512)
    for h in range(width // HEAD):
        kc = slice(h * HEAD, (h + 1) * HEAD)
        vc = slice(width + h * HEAD, width + (h + 1) * HEAD)
        for n, cols in ((0, kc), (1, vc)):
            raw[n, 0:256, :] = from_left[0:256, cols]
            raw[n, pl.ds(256 + own_at, 512), :] = kv_own[:, cols]
            raw[n, pl.ds(256 + got_at, 512), :] = kv_got[:, cols]
            raw[n, 1280:1536, :] = from_right[0:256, cols]
            one[n, 0:128, :] = from_left[256:384, cols]
            for i in range(6):
                block = pool1(raw[n, i * PARENT : (i + 1) * PARENT, :])
                at = (i + 1) * BLOCK
                one[n, at : at + BLOCK, :] = block
            one[n, 896:1024, :] = from_right[256:384, cols]
            two[n, 0:128, :] = from_left[384:512, cols]
            two[n, 128:192, :] = pool12(one[n, 0:128, :])
            two[n, 192:256, :] = pool2(raw[n, 0:256, :])
            two[n, 256:320, :] = pool2(raw[n, 1280:1536, :])
            two[n, 320:384, :] = pool12(one[n, 896:1024, :])
            two[n, 384:512, :] = from_right[384:512, cols]
            for i in range(6):
                rows = slice(i * PARENT, (i + 1) * PARENT)
                raw_t[n, :, rows] = raw[n, rows, :].T
            for i in range(8):
                rows = slice(i * BLOCK, (i + 1) * BLOCK)
                one_t[n, :, rows] = one[n, rows, :].T
            for i in range(4):
                rows = slice(i * BLOCK, (i + 1) * BLOCK)
                two_t[n, :, rows] = two[n, rows, :].T
        qs[pl.ds(own_at, 512), :] = qg_own[:, kc]
        qs[pl.ds(got_at, 512), :] = qg_got[:, kc]
        gs[pl.ds(own_at, 512), :] = qg_own[:, vc]
        gs[pl.ds(got_at, 512), :] = qg_got[:, vc]

        def blocks(ref, n, which):
            return [ref[n, b * BLOCK : (b + 1) * BLOCK, :] for b in which]

        def blocks_t(ref, n, which):
            return [ref[n, :, b * BLOCK : (b + 1) * BLOCK] for b in which]

        q_parents = [qs[i * PARENT : (i + 1) * PARENT, :] for i in range(4)]
        q1 = [
            jnp.concatenate([pool1(q_parents[2 * j]), pool1(q_parents[2 * j + 1])], axis=0)
            for j in range(2)
        ]
        q2 = jnp.concatenate([pool2(x) for x in q_parents], axis=0)
        which1 = [(0, 1, 4, 5), (2, 3, 6, 7)]
        bias1 = [(left_bias, None), (None, right_bias)]
        which2 = (0, 1, 2, 3)
        far1 = [
            far_forward(
                blocks(one, 0, which1[j]), blocks_t(one_t, 1, which1[j]), q1[j], bias1[j], p1.at[j]
            )
            for j in range(2)
        ]
        far2 = far_forward(
            blocks(two, 0, which2), blocks_t(two_t, 1, which2), q2, (left_bias, right_bias), p2
        )
        acc0[...] = jnp.zeros_like(acc0)
        g1_t, ec1, f1 = [], [], []
        g2_t, ec2, low2 = [], [], []
        dq0 = []
        for i in range(4):
            rows = slice(i * PARENT, i * PARENT + 3 * PARENT)
            q = q_parents[i]
            g = gs[i * PARENT : (i + 1) * PARENT, :]
            s = dot_nt(raw[0, rows, :], q)
            pieces = [s[:PARENT], s[PARENT : 2 * PARENT], s[2 * PARENT :]]
            if i == 0:
                pieces[0] = pieces[0] + left_bias
            if i == 3:
                pieces[2] = pieces[2] + right_bias
            m0 = jnp.max(
                jnp.maximum(jnp.maximum(pieces[0], pieces[1]), pieces[2]), axis=0, keepdims=True
            )
            e = [jnp.exp2((x - m0) * TO_LOG2) for x in pieces]
            for n in range(3):
                p0[n * PARENT : (n + 1) * PARENT, :] = e[n]
            z0 = jnp.sum(e[0] + e[1] + e[2], axis=0, keepdims=True)
            u0 = dot_nn(raw_t[1, :, rows], jnp.concatenate([x.astype(BF) for x in e], axis=0))
            j, half = i // 2, i % 2
            lanes = slice(half * BLOCK, (half + 1) * BLOCK)
            m1, z1, u1 = (x[:, lanes] for x in far1[j])
            lanes2 = slice(j * BLOCK, (j + 1) * BLOCK)
            m2, z2, u2 = (spread64(x[:, lanes2], half) for x in far2)
            m1w, m2w = twice(m1, 1), twice(m2, 1)
            m = jnp.maximum(jnp.maximum(m0, m1w), m2w)
            a0 = jnp.exp2((m0 - m) * TO_LOG2)
            a1 = 2.0 * jnp.exp2((m1w - m) * TO_LOG2)
            a2 = 4.0 * jnp.exp2((m2w - m) * TO_LOG2)
            z = a0 * z0 + a1 * twice(z1, 1) + a2 * twice(z2, 1)
            inv = 1.0 / z
            o = ((a0 * inv) * u0 + (a1 * inv) * twice(u1, 1) + (a2 * inv) * twice(u2, 1)).astype(BF)
            oq[i, 0, h * HEAD : (h + 1) * HEAD, :] = o
            lg = m * TO_LOG2 + jnp.log2(z)
            g_t = g.astype(F32).T
            dr = jnp.sum(o.astype(F32) * g_t, axis=0, keepdims=True)
            lg_a, lg_b = lg[:, :BLOCK], lg[:, BLOCK:]
            g_a, g_b = g_t[:, :BLOCK], g_t[:, BLOCK:]
            dr_a, dr_b = dr[:, :BLOCK], dr[:, BLOCK:]
            low = jnp.minimum(lg_a, lg_b)
            w_a, w_b = jnp.exp2(low - lg_a), jnp.exp2(low - lg_b)
            g1_t.append((w_a * g_a + w_b * g_b).astype(BF))
            ec1.append(w_a * dr_a + w_b * dr_b)
            f1.append(2.0 * jnp.exp2(m1 * TO_LOG2 - low))
            lower = jnp.minimum(low, swap64(low))
            w_a, w_b = jnp.exp2(lower - lg_a), jnp.exp2(lower - lg_b)
            part = w_a * g_a + w_b * g_b
            g2_t.append(part + swap64(part))
            part = w_a * dr_a + w_b * dr_b
            ec2.append(part + swap64(part))
            low2.append(lower)
            f0 = jnp.exp2(m0 * TO_LOG2 - lg)
            products = dot_nt(raw[1, rows, :], g)
            weights = p0[...] * f0
            eb = weights.astype(BF)
            r = (weights * (products - dr)).astype(BF)
            acc0[1, rows, :] += dot_nn(eb, g)
            acc0[0, rows, :] += dot_nn(r, q)
            dq0.append(dot_nn(raw_t[0, :, rows], r))
        acc1[...] = jnp.zeros_like(acc1)
        dq1 = []
        for j in range(2):
            pair = slice(2 * j, 2 * j + 2)
            g1 = jnp.concatenate([x.astype(F32).T.astype(BF) for x in g1_t[pair]], axis=0)
            dk, dv, dq = far_backward(
                blocks_t(one_t, 0, which1[j]), blocks(one, 1, which1[j]), q1[j], p1.at[j],
                jnp.concatenate(f1[pair], axis=1), g1, jnp.concatenate(ec1[pair], axis=1),
            )
            for n, b in enumerate(which1[j]):
                acc1[0, b * BLOCK : (b + 1) * BLOCK, :] += dk[n]
                acc1[1, b * BLOCK : (b + 1) * BLOCK, :] += dv[n]
            dq1.append(dq)

        def joined(parts):
            return jnp.concatenate(
                [
                    jnp.where(low_lanes(parts[0].shape), parts[2 * j], parts[2 * j + 1])
                    for j in range(2)
                ],
                axis=1,
            )

        g2 = joined(g2_t).T.astype(BF)
        f2 = 4.0 * jnp.exp2(far2[0] * TO_LOG2 - joined(low2))
        dk, dv, dq2 = far_backward(
            blocks_t(two_t, 0, which2), blocks(two, 1, which2), q2, p2, f2, g2, joined(ec2)
        )
        for n in range(4):
            acc2[0, n * BLOCK : (n + 1) * BLOCK, :] = dk[n]
            acc2[1, n * BLOCK : (n + 1) * BLOCK, :] = dv[n]
        for i in range(4):
            j, half = i // 2, i % 2
            d1 = dq1[j][:, half * BLOCK : (half + 1) * BLOCK]
            d2 = spread64(dq2[:, j * BLOCK : (j + 1) * BLOCK], half)
            coarse = 0.5 * d1 + 0.25 * d2
            oq[i, 1, h * HEAD : (h + 1) * HEAD, :] = ((dq0[i] + twice(coarse, 1)) * INV_ROOT).astype(BF)
        for n, cols, scale in ((0, kc, INV_ROOT), (1, vc, 1.0)):
            for i in range(4):
                rows = slice((i + 1) * PARENT, (i + 2) * PARENT)
                coarse = acc1[n, (i + 2) * BLOCK : (i + 3) * BLOCK, :] * (0.5 * scale)
                grad[i * PARENT : (i + 1) * PARENT, cols] = acc0[n, rows, :] * scale + twice(coarse)
            far = acc2[n, 128:256, :] * (0.25 * scale)
            mid = acc1[n, 0:256, :] * (0.5 * scale)
            near = acc0[n, 0:256, :] * scale
            to_left[0:256, cols] = (near + twice(mid[128:] + twice(far[64:]))).astype(BF)
            to_left[256:384, cols] = (mid[:128] + twice(far[:64])).astype(BF)
            to_left[384:512, cols] = (acc2[n, 0:128, :] * (0.25 * scale)).astype(BF)
            far = acc2[n, 256:384, :] * (0.25 * scale)
            mid = acc1[n, 768:1024, :] * (0.5 * scale)
            near = acc0[n, 1280:1536, :] * scale
            to_right[0:256, cols] = (near + twice(mid[:128] + twice(far[:64]))).astype(BF)
            to_right[256:384, cols] = (mid[128:] + twice(far[64:])).astype(BF)
            to_right[384:512, cols] = (acc2[n, 384:512, :] * (0.25 * scale)).astype(BF)
    oq_own[...] = oq[pl.ds(side * 2, 2)]
    oq_far[...] = oq[pl.ds((1 - side) * 2, 2)]
    near_out[...] = halos[1 - odd]
    wide_out[...] = halos[odd]


def main(where, kv_own, kv_got, qg_own, qg_got, near_got, wide_got):
    rows, both = kv_own.shape
    width = both // 2
    oq_shape = jax.ShapeDtypeStruct((2, 2, width, PARENT), BF)
    halo_shape = jax.ShapeDtypeStruct((512, both), BF)
    return pl.pallas_call(
        main_kernel,
        in_specs=[smem()] + [vmem()] * 6,
        out_specs=[vmem()] * 5,
        out_shape=[
            oq_shape,
            oq_shape,
            jax.ShapeDtypeStruct((2 * rows, both), F32),
            halo_shape,
            halo_shape,
        ],
        scratch_shapes=[
            pltpu.VMEM((2, 1536, HEAD), BF),
            pltpu.VMEM((2, HEAD, 1536), BF),
            pltpu.VMEM((2, 1024, HEAD), BF),
            pltpu.VMEM((2, HEAD, 1024), BF),
            pltpu.VMEM((2, 512, HEAD), BF),
            pltpu.VMEM((2, HEAD, 512), BF),
            pltpu.VMEM((1024, HEAD), BF),
            pltpu.VMEM((1024, HEAD), BF),
            pltpu.VMEM((768, PARENT), F32),
            pltpu.VMEM((2, 384, PARENT), F32),
            pltpu.VMEM((384, PARENT), F32),
            pltpu.VMEM((2, 1536, HEAD), F32),
            pltpu.VMEM((2, 1024, HEAD), F32),
            pltpu.VMEM((2, 512, HEAD), F32),
            pltpu.VMEM((4, 2, width, PARENT), BF),
            pltpu.VMEM((2, 512, both), BF),
        ],
        compiler_params=pltpu.CompilerParams(vmem_limit_bytes=24 * 1024 * 1024),
        cost_estimate=light(),
    )(where, kv_own, kv_got, qg_own, qg_got, near_got, wide_got)


def join_kernel(where, grad, near_got, wide_got, own, far):
    def fill(first, second, from_left, from_right):
        def parent(i):
            return grad[i * PARENT : (i + 1) * PARENT, :]

        def part(ref, start, stop):
            return ref[start:stop, :].astype(F32)

        first[0:256, :] = (
            parent(0) + part(from_left, 0, 256) + twice(twice(part(from_right, 384, 448)))
        ).astype(BF)
        first[256:512, :] = (
            parent(1) + twice(part(from_left, 256, 384) + twice(part(from_right, 448, 512)))
        ).astype(BF)
        second[0:256, :] = (
            parent(2) + twice(part(from_right, 256, 384) + twice(part(from_left, 384, 448)))
        ).astype(BF)
        second[256:512, :] = (
            parent(3) + part(from_right, 0, 256) + twice(twice(part(from_left, 448, 512)))
        ).astype(BF)

    for side in range(2):
        for odd in range(2):

            @pl.when((where[0] == side) & (where[3] == odd))
            def _(side=side, odd=odd):
                halves = (own, far) if side == 0 else (far, own)
                fill(*halves, *((wide_got, near_got) if odd == 0 else (near_got, wide_got)))


def join(where, grad, near_got, wide_got):
    shape = jax.ShapeDtypeStruct(near_got.shape, BF)
    return pl.pallas_call(
        join_kernel,
        in_specs=[smem(), vmem(), vmem(), vmem()],
        out_specs=[vmem(), vmem()],
        out_shape=[shape, shape],
        compiler_params=small(),
        cost_estimate=light(),
    )(where, grad, near_got, wide_got)


def unpack_rows_kernel(where, *refs):
    ins, (first, second) = refs[:-2], refs[-2:]
    order = order_matrix(True)
    width = ins[0].shape[1] // 2
    for c in range(CHUNKS):
        for ref, side in ((ins[c], where[0]), (ins[CHUNKS + c], 1 - where[0])):
            at = pl.ds(pl.multiple_of((side * CHUNKS + c) * width, width), width)
            for i in range(2):
                rows = slice(i * PARENT, (i + 1) * PARENT)
                first[rows, at] = dot_nn(order, ref[rows, :width]).astype(BF)
                second[rows, at] = dot_nn(order, ref[rows, width:]).astype(BF)


def unpack_columns_kernel(where, *refs):
    ins, (first, second) = refs[:-2], refs[-2:]
    order = order_matrix(True)
    width = ins[0].shape[2]
    for c in range(CHUNKS):
        for ref, side in ((ins[c], where[0]), (ins[CHUNKS + c], 1 - where[0])):
            at = pl.ds(pl.multiple_of((side * CHUNKS + c) * width, width), width)
            for i in range(2):
                rows = slice(i * PARENT, (i + 1) * PARENT)
                first[rows, at] = dot_nt(order, ref[i, 0]).astype(BF)
                second[rows, at] = dot_nt(order, ref[i, 1]).astype(BF)


def unpack(kernel, where, own, got, shape):
    out = jax.ShapeDtypeStruct(shape, BF)
    return pl.pallas_call(
        kernel,
        in_specs=[smem()] + [vmem()] * (2 * CHUNKS),
        out_specs=[vmem(), vmem()],
        out_shape=[out, out],
        compiler_params=small(),
        cost_estimate=light(),
    )(where, *own, *got)


def on_device(queries, key_matrix, value_matrix, cotangent):
    axes = ("outer", "inner")
    count = lax.axis_size("outer") * lax.axis_size("inner")
    device = lax.axis_index("outer") * lax.axis_size("inner") + lax.axis_index("inner")
    pair = device // 2
    where = jnp.stack([device % 2, pair > 0, pair < count // 2 - 1, pair % 2]).astype(jnp.int32)
    across = [(i, i ^ 1) for i in range(count)]
    near_edges = [(i, i ^ 2) for i in range(count) if i ^ 2 < count]
    wide_edges = [(i, i + 2 if i // 2 % 2 else i - 2) for i in range(count)]
    wide_edges = [(i, j) for i, j in wide_edges if 0 <= j < count]

    def swap(x):
        return lax.ppermute(x, axes, across)

    def beside(near, wide):
        wide = lax.ppermute(wide, axes, wide_edges)
        return lax.ppermute(near, axes, near_edges), wide

    kv, kv_far = pack(where, key_matrix, value_matrix)
    qg, qg_far = pack(where, queries, cotangent)
    oq_own, oq_got, kv_own, kv_got = [], [], [], []
    back = []
    for c in range(CHUNKS):
        got_kv = swap(kv_far[c])
        got_qg = swap(qg_far[c])
        inputs = (kv[c], got_kv, qg[c], got_qg, *beside(*halo(where, kv[c], got_kv)))
        if c > 0:
            oq_got[c - 1], inputs = lax.optimization_barrier((oq_got[c - 1], inputs))
        own, far, grad, near, wide = main(where, *inputs)
        oq_own.append(own)
        oq_got.append(swap(far))
        back.append((grad, *beside(near, wide)))
    for c in range(CHUNKS):
        own, far = join(where, *back[c])
        kv_own.append(own)
        kv_got.append(swap(far))
    attended, query_grad = unpack(unpack_columns_kernel, where, oq_own, oq_got, queries.shape)
    key_grad, value_grad = unpack(unpack_rows_kernel, where, kv_own, kv_got, queries.shape)
    return attended, query_grad, key_grad, value_grad


def solution(mesh):
    spec = P(("outer", "inner"), None)
    return jax.shard_map(
        on_device,
        mesh=mesh,
        in_specs=(spec,) * 4,
        out_specs=(spec,) * 4,
        check_vma=False,
    )
```

```python
import functools
import math

import jax
import jax.numpy as jnp
from jax import lax
from jax.experimental import pallas as pl
from jax.experimental.pallas import tpu as pltpu
from jax.sharding import PartitionSpec as P

HEAD = 128
BLOCK = 128
PARENT = 256
LEVELS = 3
CHUNKS = 2
INV_ROOT = HEAD**-0.5
TO_LOG2 = INV_ROOT * math.log2(math.e)
MASKED = -1e30
BF = jnp.bfloat16
F32 = jnp.float32


def dot_nt(a, b):
    return lax.dot_general(a, b, (((1,), (1,)), ((), ())), preferred_element_type=F32)


def dot_nn(a, b):
    return jnp.dot(a, b, preferred_element_type=F32)


def order_matrix(inverse):
    row = lax.broadcasted_iota(jnp.int32, (PARENT, PARENT), 0)
    col = lax.broadcasted_iota(jnp.int32, (PARENT, PARENT), 1)
    place, token = (col, row) if inverse else (row, col)
    slab = place // 64
    source = 4 * (place % 64) + 2 * (slab % 2) + slab // 2
    return jnp.where(source == token, 1.0, 0.0).astype(BF)


def pool1(x):
    return ((x[:BLOCK].astype(F32) + x[BLOCK:].astype(F32)) * 0.5).astype(BF)


def pool2(x):
    half = x[:BLOCK].astype(F32) + x[BLOCK:].astype(F32)
    return ((half[:64] + half[64:]) * 0.25).astype(BF)


def pool12(x):
    return ((x[:64].astype(F32) + x[64:].astype(F32)) * 0.5).astype(BF)


def twice(x, axis=0):
    return jnp.concatenate([x, x], axis=axis)


def pack_kernel(where, a, b, *refs):
    outs, held, sems = refs[: 2 * CHUNKS], refs[2 * CHUNKS], refs[2 * CHUNKS + 1]
    rows, columns = a.shape
    half = columns // 2
    width = half // CHUNKS
    copies = []
    for n, side in enumerate((1 - where[0], where[0])):
        at = pl.ds(pl.multiple_of(side * half, half), half)
        for m, ref in enumerate((a, b)):
            copies.append(
                pltpu.make_async_copy(ref.at[:, at], held.at[2 * n + m], sems.at[2 * n + m])
            )
            copies[-1].start()
    order = order_matrix(False)
    for n in range(2):
        own = n == 1
        for m in range(2):
            copies[2 * n + m].wait()
            for i in range(rows // PARENT):
                at = slice(i * PARENT, (i + 1) * PARENT)
                x = dot_nn(order, held[2 * n + m, at, :]).astype(BF)
                for c in range(CHUNKS):
                    ref = outs[c] if own else outs[CHUNKS + c]
                    ref[at, m * width : (m + 1) * width] = x[:, c * width : (c + 1) * width]


def pack(where, a, b):
    rows, columns = a.shape
    out = jax.ShapeDtypeStruct((rows, columns // CHUNKS), BF)
    outs = pl.pallas_call(
        pack_kernel,
        in_specs=[smem(), pl.BlockSpec(memory_space=pltpu.HBM), pl.BlockSpec(memory_space=pltpu.HBM)],
        out_specs=[vmem()] * (2 * CHUNKS),
        out_shape=[out] * (2 * CHUNKS),
        scratch_shapes=[
            pltpu.VMEM((4, rows, columns // 2), BF),
            pltpu.SemaphoreType.DMA((4,)),
        ],
        compiler_params=small(),
        cost_estimate=light(),
    )(where, a, b)
    return outs[:CHUNKS], outs[CHUNKS:]


def smem():
    return pl.BlockSpec(memory_space=pltpu.SMEM)


def vmem():
    return pl.BlockSpec(memory_space=pltpu.VMEM)


def small():
    return pltpu.CompilerParams(vmem_limit_bytes=8 * 1024 * 1024)


def light():
    return pl.CostEstimate(flops=1000, bytes_accessed=1000, transcendentals=0)


def halo_kernel(where, own, got, near, wide):
    def fill(first, second, to_right, to_left):
        to_right[0:256, :] = second[256:512, :]
        to_right[256:384, :] = pool1(second[0:256, :])
        to_right[384:448, :] = pool2(first[0:256, :])
        to_right[448:512, :] = pool2(first[256:512, :])
        to_left[0:256, :] = first[0:256, :]
        to_left[256:384, :] = pool1(first[256:512, :])
        to_left[384:448, :] = pool2(second[0:256, :])
        to_left[448:512, :] = pool2(second[256:512, :])

    for side in range(2):
        for odd in range(2):

            @pl.when((where[0] == side) & (where[3] == odd))
            def _(side=side, odd=odd):
                halves = (own, got) if side == 0 else (got, own)
                fill(*halves, *((near, wide) if odd == 0 else (wide, near)))


def halo(where, own, got):
    shape = jax.ShapeDtypeStruct(own.shape, BF)
    return pl.pallas_call(
        halo_kernel,
        in_specs=[smem(), vmem(), vmem()],
        out_specs=[vmem(), vmem()],
        out_shape=[shape, shape],
        compiler_params=small(),
        cost_estimate=light(),
    )(where, own, got)


def swap64(x):
    return pltpu.roll(x, 64, 1)


def low_lanes(shape):
    return lax.broadcasted_iota(jnp.int32, shape, 1) < 64


def spread64(x, half):
    other = swap64(x)
    low = low_lanes(x.shape)
    return jnp.where(low, x, other) if half == 0 else jnp.where(low, other, x)


def far_forward(k, v_t, q, bias, p_ref):
    k0, k1, k2, k3 = k
    v0, v1, v2, v3 = v_t
    left, right = bias
    outer = dot_nt(jnp.concatenate([k0, k3], axis=0), q)
    first, last = outer[:BLOCK], outer[BLOCK:]
    mid_low = dot_nt(k2, q[:BLOCK])
    mid_high = dot_nt(k1, q[BLOCK:])
    if left is not None:
        first = first + left
        mid_high = mid_high + left
    if right is not None:
        last = last + right
        mid_low = mid_low + right
    mid = jnp.concatenate([mid_low, mid_high], axis=1)
    peak = jnp.max(jnp.maximum(jnp.maximum(first, last), mid), axis=0, keepdims=True)
    parts = [jnp.exp2((x - peak) * TO_LOG2) for x in (first, last, mid)]
    for n, x in enumerate(parts):
        p_ref[n * BLOCK : (n + 1) * BLOCK, :] = x
    total = jnp.sum(parts[0] + parts[1] + parts[2], axis=0, keepdims=True)
    pb = [x.astype(BF) for x in parts]
    mixed = dot_nn(
        jnp.concatenate([v0, v3], axis=1), jnp.concatenate(pb[:2], axis=0)
    ) + jnp.concatenate([dot_nn(v2, pb[2][:, :BLOCK]), dot_nn(v1, pb[2][:, BLOCK:])], axis=1)
    return peak, total, mixed


def far_backward(k_t, v, q, p_ref, factor, g, ec):
    k0, k1, k2, k3 = k_t
    v0, v1, v2, v3 = v
    e_out = p_ref[: 2 * BLOCK, :] * factor
    e_mid = p_ref[2 * BLOCK :, :] * factor
    eb_out, eb_mid = e_out.astype(BF), e_mid.astype(BF)
    p_out = dot_nt(jnp.concatenate([v0, v3], axis=0), g)
    p_mid = jnp.concatenate([dot_nt(v2, g[:BLOCK]), dot_nt(v1, g[BLOCK:])], axis=1)
    r_out = (e_out * (p_out - ec)).astype(BF)
    r_mid = (e_mid * (p_mid - ec)).astype(BF)
    dv03 = dot_nn(eb_out, g)
    dv2 = dot_nn(eb_mid[:, :BLOCK], g[:BLOCK])
    dv1 = dot_nn(eb_mid[:, BLOCK:], g[BLOCK:])
    dk03 = dot_nn(r_out, q)
    dk2 = dot_nn(r_mid[:, :BLOCK], q[:BLOCK])
    dk1 = dot_nn(r_mid[:, BLOCK:], q[BLOCK:])
    dq_t = dot_nn(jnp.concatenate([k0, k3], axis=1), r_out) + jnp.concatenate(
        [dot_nn(k2, r_mid[:, :BLOCK]), dot_nn(k1, r_mid[:, BLOCK:])], axis=1
    )
    return (dk03[:BLOCK], dk1, dk2, dk03[BLOCK:]), (dv03[:BLOCK], dv1, dv2, dv03[BLOCK:]), dq_t


def main_kernel(
    where, kv_own, kv_got, qg_own, qg_got, near_got, wide_got,
    oq_own, oq_far, grad, near_out, wide_out,
    raw, raw_t, one, one_t, two, two_t, qs, gs, p0, p1, p2, acc0, acc1, acc2, oq, halos,
):
    side = where[0]
    odd = where[3]
    halos[1 - odd] = near_got[...]
    halos[odd] = wide_got[...]
    from_left, from_right = halos.at[0], halos.at[1]
    to_left, to_right = halos.at[0], halos.at[1]
    width = kv_own.shape[1] // 2
    left_bias = (1 - where[1]).astype(F32) * MASKED
    right_bias = (1 - where[2]).astype(F32) * MASKED
    own_at = pl.multiple_of(side * 512, 512)
    got_at = pl.multiple_of((1 - side) * 512, 512)
    for h in range(width // HEAD):
        kc = slice(h * HEAD, (h + 1) * HEAD)
        vc = slice(width + h * HEAD, width + (h + 1) * HEAD)
        for n, cols in ((0, kc), (1, vc)):
            raw[n, 0:256, :] = from_left[0:256, cols]
            raw[n, pl.ds(256 + own_at, 512), :] = kv_own[:, cols]
            raw[n, pl.ds(256 + got_at, 512), :] = kv_got[:, cols]
            raw[n, 1280:1536, :] = from_right[0:256, cols]
            one[n, 0:128, :] = from_left[256:384, cols]
            for i in range(6):
                block = pool1(raw[n, i * PARENT : (i + 1) * PARENT, :])
                at = (i + 1) * BLOCK
                one[n, at : at + BLOCK, :] = block
            one[n, 896:1024, :] = from_right[256:384, cols]
            two[n, 0:128, :] = from_left[384:512, cols]
            two[n, 128:192, :] = pool12(one[n, 0:128, :])
            two[n, 192:256, :] = pool2(raw[n, 0:256, :])
            two[n, 256:320, :] = pool2(raw[n, 1280:1536, :])
            two[n, 320:384, :] = pool12(one[n, 896:1024, :])
            two[n, 384:512, :] = from_right[384:512, cols]
            for i in range(6):
                rows = slice(i * PARENT, (i + 1) * PARENT)
                raw_t[n, :, rows] = raw[n, rows, :].T
            for i in range(8):
                rows = slice(i * BLOCK, (i + 1) * BLOCK)
                one_t[n, :, rows] = one[n, rows, :].T
            for i in range(4):
                rows = slice(i * BLOCK, (i + 1) * BLOCK)
                two_t[n, :, rows] = two[n, rows, :].T
        qs[pl.ds(own_at, 512), :] = qg_own[:, kc]
        qs[pl.ds(got_at, 512), :] = qg_got[:, kc]
        gs[pl.ds(own_at, 512), :] = qg_own[:, vc]
        gs[pl.ds(got_at, 512), :] = qg_got[:, vc]

        def blocks(ref, n, which):
            return [ref[n, b * BLOCK : (b + 1) * BLOCK, :] for b in which]

        def blocks_t(ref, n, which):
            return [ref[n, :, b * BLOCK : (b + 1) * BLOCK] for b in which]

        q_parents = [qs[i * PARENT : (i + 1) * PARENT, :] for i in range(4)]
        q1 = [
            jnp.concatenate([pool1(q_parents[2 * j]), pool1(q_parents[2 * j + 1])], axis=0)
            for j in range(2)
        ]
        q2 = jnp.concatenate([pool2(x) for x in q_parents], axis=0)
        which1 = [(0, 1, 4, 5), (2, 3, 6, 7)]
        bias1 = [(left_bias, None), (None, right_bias)]
        which2 = (0, 1, 2, 3)
        far1 = [
            far_forward(
                blocks(one, 0, which1[j]), blocks_t(one_t, 1, which1[j]), q1[j], bias1[j], p1.at[j]
            )
            for j in range(2)
        ]
        far2 = far_forward(
            blocks(two, 0, which2), blocks_t(two_t, 1, which2), q2, (left_bias, right_bias), p2
        )
        acc0[...] = jnp.zeros_like(acc0)
        g1_t, ec1, f1 = [], [], []
        g2_t, ec2, low2 = [], [], []
        dq0 = []
        for i in range(4):
            rows = slice(i * PARENT, i * PARENT + 3 * PARENT)
            q = q_parents[i]
            g = gs[i * PARENT : (i + 1) * PARENT, :]
            s = dot_nt(raw[0, rows, :], q)
            pieces = [s[:PARENT], s[PARENT : 2 * PARENT], s[2 * PARENT :]]
            if i == 0:
                pieces[0] = pieces[0] + left_bias
            if i == 3:
                pieces[2] = pieces[2] + right_bias
            m0 = jnp.max(
                jnp.maximum(jnp.maximum(pieces[0], pieces[1]), pieces[2]), axis=0, keepdims=True
            )
            e = [jnp.exp2((x - m0) * TO_LOG2) for x in pieces]
            for n in range(3):
                p0[n * PARENT : (n + 1) * PARENT, :] = e[n]
            z0 = jnp.sum(e[0] + e[1] + e[2], axis=0, keepdims=True)
            u0 = dot_nn(raw_t[1, :, rows], jnp.concatenate([x.astype(BF) for x in e], axis=0))
            j, half = i // 2, i % 2
            lanes = slice(half * BLOCK, (half + 1) * BLOCK)
            m1, z1, u1 = (x[:, lanes] for x in far1[j])
            lanes2 = slice(j * BLOCK, (j + 1) * BLOCK)
            m2, z2, u2 = (spread64(x[:, lanes2], half) for x in far2)
            m1w, m2w = twice(m1, 1), twice(m2, 1)
            m = jnp.maximum(jnp.maximum(m0, m1w), m2w)
            a0 = jnp.exp2((m0 - m) * TO_LOG2)
            a1 = 2.0 * jnp.exp2((m1w - m) * TO_LOG2)
            a2 = 4.0 * jnp.exp2((m2w - m) * TO_LOG2)
            z = a0 * z0 + a1 * twice(z1, 1) + a2 * twice(z2, 1)
            inv = 1.0 / z
            o = ((a0 * inv) * u0 + (a1 * inv) * twice(u1, 1) + (a2 * inv) * twice(u2, 1)).astype(BF)
            oq[i, 0, h * HEAD : (h + 1) * HEAD, :] = o
            lg = m * TO_LOG2 + jnp.log2(z)
            g_t = g.astype(F32).T
            dr = jnp.sum(o.astype(F32) * g_t, axis=0, keepdims=True)
            lg_a, lg_b = lg[:, :BLOCK], lg[:, BLOCK:]
            g_a, g_b = g_t[:, :BLOCK], g_t[:, BLOCK:]
            dr_a, dr_b = dr[:, :BLOCK], dr[:, BLOCK:]
            low = jnp.minimum(lg_a, lg_b)
            w_a, w_b = jnp.exp2(low - lg_a), jnp.exp2(low - lg_b)
            g1_t.append((w_a * g_a + w_b * g_b).astype(BF))
            ec1.append(w_a * dr_a + w_b * dr_b)
            f1.append(2.0 * jnp.exp2(m1 * TO_LOG2 - low))
            lower = jnp.minimum(low, swap64(low))
            w_a, w_b = jnp.exp2(lower - lg_a), jnp.exp2(lower - lg_b)
            part = w_a * g_a + w_b * g_b
            g2_t.append(part + swap64(part))
            part = w_a * dr_a + w_b * dr_b
            ec2.append(part + swap64(part))
            low2.append(lower)
            f0 = jnp.exp2(m0 * TO_LOG2 - lg)
            products = dot_nt(raw[1, rows, :], g)
            weights = p0[...] * f0
            eb = weights.astype(BF)
            r = (weights * (products - dr)).astype(BF)
            acc0[1, rows, :] += dot_nn(eb, g)
            acc0[0, rows, :] += dot_nn(r, q)
            dq0.append(dot_nn(raw_t[0, :, rows], r))
        acc1[...] = jnp.zeros_like(acc1)
        dq1 = []
        for j in range(2):
            pair = slice(2 * j, 2 * j + 2)
            g1 = jnp.concatenate([x.astype(F32).T.astype(BF) for x in g1_t[pair]], axis=0)
            dk, dv, dq = far_backward(
                blocks_t(one_t, 0, which1[j]), blocks(one, 1, which1[j]), q1[j], p1.at[j],
                jnp.concatenate(f1[pair], axis=1), g1, jnp.concatenate(ec1[pair], axis=1),
            )
            for n, b in enumerate(which1[j]):
                acc1[0, b * BLOCK : (b + 1) * BLOCK, :] += dk[n]
                acc1[1, b * BLOCK : (b + 1) * BLOCK, :] += dv[n]
            dq1.append(dq)

        def joined(parts):
            return jnp.concatenate(
                [
                    jnp.where(low_lanes(parts[0].shape), parts[2 * j], parts[2 * j + 1])
                    for j in range(2)
                ],
                axis=1,
            )

        g2 = joined(g2_t).T.astype(BF)
        f2 = 4.0 * jnp.exp2(far2[0] * TO_LOG2 - joined(low2))
        dk, dv, dq2 = far_backward(
            blocks_t(two_t, 0, which2), blocks(two, 1, which2), q2, p2, f2, g2, joined(ec2)
        )
        for n in range(4):
            acc2[0, n * BLOCK : (n + 1) * BLOCK, :] = dk[n]
            acc2[1, n * BLOCK : (n + 1) * BLOCK, :] = dv[n]
        for i in range(4):
            j, half = i // 2, i % 2
            d1 = dq1[j][:, half * BLOCK : (half + 1) * BLOCK]
            d2 = spread64(dq2[:, j * BLOCK : (j + 1) * BLOCK], half)
            coarse = 0.5 * d1 + 0.25 * d2
            oq[i, 1, h * HEAD : (h + 1) * HEAD, :] = ((dq0[i] + twice(coarse, 1)) * INV_ROOT).astype(BF)
        for n, cols, scale in ((0, kc, INV_ROOT), (1, vc, 1.0)):
            for i in range(4):
                rows = slice((i + 1) * PARENT, (i + 2) * PARENT)
                coarse = acc1[n, (i + 2) * BLOCK : (i + 3) * BLOCK, :] * (0.5 * scale)
                grad[i * PARENT : (i + 1) * PARENT, cols] = acc0[n, rows, :] * scale + twice(coarse)
            far = acc2[n, 128:256, :] * (0.25 * scale)
            mid = acc1[n, 0:256, :] * (0.5 * scale)
            near = acc0[n, 0:256, :] * scale
            to_left[0:256, cols] = (near + twice(mid[128:] + twice(far[64:]))).astype(BF)
            to_left[256:384, cols] = (mid[:128] + twice(far[:64])).astype(BF)
            to_left[384:512, cols] = (acc2[n, 0:128, :] * (0.25 * scale)).astype(BF)
            far = acc2[n, 256:384, :] * (0.25 * scale)
            mid = acc1[n, 768:1024, :] * (0.5 * scale)
            near = acc0[n, 1280:1536, :] * scale
            to_right[0:256, cols] = (near + twice(mid[:128] + twice(far[:64]))).astype(BF)
            to_right[256:384, cols] = (mid[128:] + twice(far[64:])).astype(BF)
            to_right[384:512, cols] = (acc2[n, 384:512, :] * (0.25 * scale)).astype(BF)
    oq_own[...] = oq[pl.ds(side * 2, 2)]
    oq_far[...] = oq[pl.ds((1 - side) * 2, 2)]
    near_out[...] = halos[1 - odd]
    wide_out[...] = halos[odd]


def main(where, kv_own, kv_got, qg_own, qg_got, near_got, wide_got):
    rows, both = kv_own.shape
    width = both // 2
    oq_shape = jax.ShapeDtypeStruct((2, 2, width, PARENT), BF)
    halo_shape = jax.ShapeDtypeStruct((512, both), BF)
    return pl.pallas_call(
        main_kernel,
        in_specs=[smem()] + [vmem()] * 6,
        out_specs=[vmem()] * 5,
        out_shape=[
            oq_shape,
            oq_shape,
            jax.ShapeDtypeStruct((2 * rows, both), F32),
            halo_shape,
            halo_shape,
        ],
        scratch_shapes=[
            pltpu.VMEM((2, 1536, HEAD), BF),
            pltpu.VMEM((2, HEAD, 1536), BF),
            pltpu.VMEM((2, 1024, HEAD), BF),
            pltpu.VMEM((2, HEAD, 1024), BF),
            pltpu.VMEM((2, 512, HEAD), BF),
            pltpu.VMEM((2, HEAD, 512), BF),
            pltpu.VMEM((1024, HEAD), BF),
            pltpu.VMEM((1024, HEAD), BF),
            pltpu.VMEM((768, PARENT), F32),
            pltpu.VMEM((2, 384, PARENT), F32),
            pltpu.VMEM((384, PARENT), F32),
            pltpu.VMEM((2, 1536, HEAD), F32),
            pltpu.VMEM((2, 1024, HEAD), F32),
            pltpu.VMEM((2, 512, HEAD), F32),
            pltpu.VMEM((4, 2, width, PARENT), BF),
            pltpu.VMEM((2, 512, both), BF),
        ],
        compiler_params=pltpu.CompilerParams(vmem_limit_bytes=24 * 1024 * 1024),
        cost_estimate=light(),
    )(where, kv_own, kv_got, qg_own, qg_got, near_got, wide_got)


def join_kernel(where, grad, near_got, wide_got, own, far):
    def fill(first, second, from_left, from_right):
        def parent(i):
            return grad[i * PARENT : (i + 1) * PARENT, :]

        def part(ref, start, stop):
            return ref[start:stop, :].astype(F32)

        first[0:256, :] = (
            parent(0) + part(from_left, 0, 256) + twice(twice(part(from_right, 384, 448)))
        ).astype(BF)
        first[256:512, :] = (
            parent(1) + twice(part(from_left, 256, 384) + twice(part(from_right, 448, 512)))
        ).astype(BF)
        second[0:256, :] = (
            parent(2) + twice(part(from_right, 256, 384) + twice(part(from_left, 384, 448)))
        ).astype(BF)
        second[256:512, :] = (
            parent(3) + part(from_right, 0, 256) + twice(twice(part(from_left, 448, 512)))
        ).astype(BF)

    for side in range(2):
        for odd in range(2):

            @pl.when((where[0] == side) & (where[3] == odd))
            def _(side=side, odd=odd):
                halves = (own, far) if side == 0 else (far, own)
                fill(*halves, *((wide_got, near_got) if odd == 0 else (near_got, wide_got)))


def join(where, grad, near_got, wide_got):
    shape = jax.ShapeDtypeStruct(near_got.shape, BF)
    return pl.pallas_call(
        join_kernel,
        in_specs=[smem(), vmem(), vmem(), vmem()],
        out_specs=[vmem(), vmem()],
        out_shape=[shape, shape],
        compiler_params=small(),
        cost_estimate=light(),
    )(where, grad, near_got, wide_got)


def unpack_rows_kernel(where, *refs):
    ins, (first, second) = refs[:-2], refs[-2:]
    order = order_matrix(True)
    width = ins[0].shape[1] // 2
    for c in range(CHUNKS):
        for ref, side in ((ins[c], where[0]), (ins[CHUNKS + c], 1 - where[0])):
            at = pl.ds(pl.multiple_of((side * CHUNKS + c) * width, width), width)
            for i in range(2):
                rows = slice(i * PARENT, (i + 1) * PARENT)
                first[rows, at] = dot_nn(order, ref[rows, :width]).astype(BF)
                second[rows, at] = dot_nn(order, ref[rows, width:]).astype(BF)


def unpack_columns_kernel(where, *refs):
    ins, (first, second) = refs[:-2], refs[-2:]
    order = order_matrix(True)
    width = ins[0].shape[2]
    for c in range(CHUNKS):
        for ref, side in ((ins[c], where[0]), (ins[CHUNKS + c], 1 - where[0])):
            at = pl.ds(pl.multiple_of((side * CHUNKS + c) * width, width), width)
            for i in range(2):
                rows = slice(i * PARENT, (i + 1) * PARENT)
                first[rows, at] = dot_nt(order, ref[i, 0]).astype(BF)
                second[rows, at] = dot_nt(order, ref[i, 1]).astype(BF)


def unpack(kernel, where, own, got, shape):
    out = jax.ShapeDtypeStruct(shape, BF)
    return pl.pallas_call(
        kernel,
        in_specs=[smem()] + [vmem()] * (2 * CHUNKS),
        out_specs=[vmem(), vmem()],
        out_shape=[out, out],
        compiler_params=small(),
        cost_estimate=light(),
    )(where, *own, *got)


def on_device(queries, key_matrix, value_matrix, cotangent):
    axes = ("outer", "inner")
    count = lax.axis_size("outer") * lax.axis_size("inner")
    device = lax.axis_index("outer") * lax.axis_size("inner") + lax.axis_index("inner")
    pair = device // 2
    where = jnp.stack([device % 2, pair > 0, pair < count // 2 - 1, pair % 2]).astype(jnp.int32)
    across = [(i, i ^ 1) for i in range(count)]
    near_edges = [(i, i ^ 2) for i in range(count) if i ^ 2 < count]
    wide_edges = [(i, i + 2 if i // 2 % 2 else i - 2) for i in range(count)]
    wide_edges = [(i, j) for i, j in wide_edges if 0 <= j < count]

    def swap(x):
        return lax.ppermute(x, axes, across)

    def beside(near, wide):
        wide = lax.ppermute(wide, axes, wide_edges)
        return lax.ppermute(near, axes, near_edges), wide

    kv, kv_far = pack(where, key_matrix, value_matrix)
    qg, qg_far = pack(where, queries, cotangent)
    oq_own, oq_got, kv_own, kv_got = [], [], [], []
    back = []
    for c in range(CHUNKS):
        got_kv = swap(kv_far[c])
        got_qg = swap(qg_far[c])
        halos = beside(*halo(where, kv[c], got_kv))
        own, far, grad, near, wide = main(where, kv[c], got_kv, qg[c], got_qg, *halos)
        oq_own.append(own)
        oq_got.append(swap(far))
        if c + 1 < CHUNKS:
            oq_got[c], near, wide = lax.optimization_barrier((oq_got[c], near, wide))
        back.append((grad, *beside(near, wide)))
    for c in range(CHUNKS):
        own, far = join(where, *back[c])
        kv_own.append(own)
        kv_got.append(swap(far))
    attended, query_grad = unpack(unpack_columns_kernel, where, oq_own, oq_got, queries.shape)
    key_grad, value_grad = unpack(unpack_rows_kernel, where, kv_own, kv_got, queries.shape)
    return attended, query_grad, key_grad, value_grad


def solution(mesh):
    spec = P(("outer", "inner"), None)
    return jax.shard_map(
        on_device,
        mesh=mesh,
        in_specs=(spec,) * 4,
        out_specs=(spec,) * 4,
        check_vma=False,
    )
```

```python
import functools
import math

import jax
import jax.numpy as jnp
from jax import lax
from jax.experimental import pallas as pl
from jax.experimental.pallas import tpu as pltpu
from jax.sharding import PartitionSpec as P

HEAD = 128
BLOCK = 128
PARENT = 256
LEVELS = 3
CHUNKS = 2
LATE_CHUNK = 0
INV_ROOT = HEAD**-0.5
TO_LOG2 = INV_ROOT * math.log2(math.e)
MASKED = -1e30
BF = jnp.bfloat16
F32 = jnp.float32


def dot_nt(a, b):
    return lax.dot_general(a, b, (((1,), (1,)), ((), ())), preferred_element_type=F32)


def dot_nn(a, b):
    return jnp.dot(a, b, preferred_element_type=F32)


def order_matrix(inverse):
    row = lax.broadcasted_iota(jnp.int32, (PARENT, PARENT), 0)
    col = lax.broadcasted_iota(jnp.int32, (PARENT, PARENT), 1)
    place, token = (col, row) if inverse else (row, col)
    slab = place // 64
    source = 4 * (place % 64) + 2 * (slab % 2) + slab // 2
    return jnp.where(source == token, 1.0, 0.0).astype(BF)


def pool1(x):
    return ((x[:BLOCK].astype(F32) + x[BLOCK:].astype(F32)) * 0.5).astype(BF)


def pool2(x):
    half = x[:BLOCK].astype(F32) + x[BLOCK:].astype(F32)
    return ((half[:64] + half[64:]) * 0.25).astype(BF)


def pool12(x):
    return ((x[:64].astype(F32) + x[64:].astype(F32)) * 0.5).astype(BF)


def twice(x, axis=0):
    return jnp.concatenate([x, x], axis=axis)


def pack_kernel(own, where, *refs):
    count = 4 if own else 2
    arrays, outs, (held, sems) = refs[:count], refs[count:-2], refs[-2:]
    rows, columns = arrays[0].shape
    half = columns // 2
    width = half // CHUNKS
    side = where[0] if own else 1 - where[0]
    at = pl.ds(pl.multiple_of(side * half, half), half)
    copies = [
        pltpu.make_async_copy(ref.at[:, at], held.at[m], sems.at[m]) for m, ref in enumerate(arrays)
    ]
    for copy in copies:
        copy.start()
    order = order_matrix(False)
    for m in range(count):
        copies[m].wait()
        first = m % 2 * width
        for i in range(rows // PARENT):
            at = slice(i * PARENT, (i + 1) * PARENT)
            x = dot_nn(order, held[m, at, :]).astype(BF)
            for c in range(CHUNKS):
                out = outs[m // 2 * CHUNKS + c]
                out[at, first : first + width] = x[:, c * width : (c + 1) * width]


def pack(own, where, *arrays):
    rows, columns = arrays[0].shape
    count = len(arrays)
    return pl.pallas_call(
        functools.partial(pack_kernel, own),
        in_specs=[smem()] + [pl.BlockSpec(memory_space=pltpu.HBM)] * count,
        out_specs=[vmem()] * (count // 2 * CHUNKS),
        out_shape=[jax.ShapeDtypeStruct((rows, columns // CHUNKS), BF)] * (count // 2 * CHUNKS),
        scratch_shapes=[
            pltpu.VMEM((count, rows, columns // 2), BF),
            pltpu.SemaphoreType.DMA((count,)),
        ],
        compiler_params=small(),
        cost_estimate=light(),
    )(where, *arrays)


def smem():
    return pl.BlockSpec(memory_space=pltpu.SMEM)


def vmem():
    return pl.BlockSpec(memory_space=pltpu.VMEM)


def small():
    return pltpu.CompilerParams(vmem_limit_bytes=8 * 1024 * 1024)


def light():
    return pl.CostEstimate(flops=1000, bytes_accessed=1000, transcendentals=0)


def halo_kernel(where, own, got, near, wide):
    def fill(first, second, to_right, to_left):
        to_right[0:256, :] = second[256:512, :]
        to_right[256:384, :] = pool1(second[0:256, :])
        to_right[384:448, :] = pool2(first[0:256, :])
        to_right[448:512, :] = pool2(first[256:512, :])
        to_left[0:256, :] = first[0:256, :]
        to_left[256:384, :] = pool1(first[256:512, :])
        to_left[384:448, :] = pool2(second[0:256, :])
        to_left[448:512, :] = pool2(second[256:512, :])

    for side in range(2):
        for odd in range(2):

            @pl.when((where[0] == side) & (where[3] == odd))
            def _(side=side, odd=odd):
                halves = (own, got) if side == 0 else (got, own)
                fill(*halves, *((near, wide) if odd == 0 else (wide, near)))


def halo(where, own, got):
    shape = jax.ShapeDtypeStruct(own.shape, BF)
    return pl.pallas_call(
        halo_kernel,
        in_specs=[smem(), vmem(), vmem()],
        out_specs=[vmem(), vmem()],
        out_shape=[shape, shape],
        compiler_params=small(),
        cost_estimate=light(),
    )(where, own, got)


def swap64(x):
    return pltpu.roll(x, 64, 1)


def low_lanes(shape):
    return lax.broadcasted_iota(jnp.int32, shape, 1) < 64


def spread64(x, half):
    other = swap64(x)
    low = low_lanes(x.shape)
    return jnp.where(low, x, other) if half == 0 else jnp.where(low, other, x)


def far_forward(k, v_t, q, bias, p_ref):
    k0, k1, k2, k3 = k
    v0, v1, v2, v3 = v_t
    left, right = bias
    outer = dot_nt(jnp.concatenate([k0, k3], axis=0), q)
    first, last = outer[:BLOCK], outer[BLOCK:]
    mid_low = dot_nt(k2, q[:BLOCK])
    mid_high = dot_nt(k1, q[BLOCK:])
    if left is not None:
        first = first + left
        mid_high = mid_high + left
    if right is not None:
        last = last + right
        mid_low = mid_low + right
    mid = jnp.concatenate([mid_low, mid_high], axis=1)
    peak = jnp.max(jnp.maximum(jnp.maximum(first, last), mid), axis=0, keepdims=True)
    parts = [jnp.exp2((x - peak) * TO_LOG2) for x in (first, last, mid)]
    for n, x in enumerate(parts):
        p_ref[n * BLOCK : (n + 1) * BLOCK, :] = x
    total = jnp.sum(parts[0] + parts[1] + parts[2], axis=0, keepdims=True)
    pb = [x.astype(BF) for x in parts]
    mixed = dot_nn(
        jnp.concatenate([v0, v3], axis=1), jnp.concatenate(pb[:2], axis=0)
    ) + jnp.concatenate([dot_nn(v2, pb[2][:, :BLOCK]), dot_nn(v1, pb[2][:, BLOCK:])], axis=1)
    return peak, total, mixed


def far_backward(k_t, v, q, p_ref, factor, g, ec):
    k0, k1, k2, k3 = k_t
    v0, v1, v2, v3 = v
    e_out = p_ref[: 2 * BLOCK, :] * factor
    e_mid = p_ref[2 * BLOCK :, :] * factor
    eb_out, eb_mid = e_out.astype(BF), e_mid.astype(BF)
    p_out = dot_nt(jnp.concatenate([v0, v3], axis=0), g)
    p_mid = jnp.concatenate([dot_nt(v2, g[:BLOCK]), dot_nt(v1, g[BLOCK:])], axis=1)
    r_out = (e_out * (p_out - ec)).astype(BF)
    r_mid = (e_mid * (p_mid - ec)).astype(BF)
    dv03 = dot_nn(eb_out, g)
    dv2 = dot_nn(eb_mid[:, :BLOCK], g[:BLOCK])
    dv1 = dot_nn(eb_mid[:, BLOCK:], g[BLOCK:])
    dk03 = dot_nn(r_out, q)
    dk2 = dot_nn(r_mid[:, :BLOCK], q[:BLOCK])
    dk1 = dot_nn(r_mid[:, BLOCK:], q[BLOCK:])
    dq_t = dot_nn(jnp.concatenate([k0, k3], axis=1), r_out) + jnp.concatenate(
        [dot_nn(k2, r_mid[:, :BLOCK]), dot_nn(k1, r_mid[:, BLOCK:])], axis=1
    )
    return (dk03[:BLOCK], dk1, dk2, dk03[BLOCK:]), (dv03[:BLOCK], dv1, dv2, dv03[BLOCK:]), dq_t


def main_kernel(
    where, kv_own, kv_got, qg_own, qg_got, near_got, wide_got,
    oq_own, oq_far, grad, near_out, wide_out,
    raw, raw_t, one, one_t, two, two_t, qs, gs, p0, p1, p2, acc0, acc1, acc2, oq, halos,
):
    side = where[0]
    odd = where[3]
    halos[1 - odd] = near_got[...]
    halos[odd] = wide_got[...]
    from_left, from_right = halos.at[0], halos.at[1]
    to_left, to_right = halos.at[0], halos.at[1]
    width = kv_own.shape[1] // 2
    left_bias = (1 - where[1]).astype(F32) * MASKED
    right_bias = (1 - where[2]).astype(F32) * MASKED
    own_at = pl.multiple_of(side * 512, 512)
    got_at = pl.multiple_of((1 - side) * 512, 512)
    for h in range(width // HEAD):
        kc = slice(h * HEAD, (h + 1) * HEAD)
        vc = slice(width + h * HEAD, width + (h + 1) * HEAD)
        for n, cols in ((0, kc), (1, vc)):
            raw[n, 0:256, :] = from_left[0:256, cols]
            raw[n, pl.ds(256 + own_at, 512), :] = kv_own[:, cols]
            raw[n, pl.ds(256 + got_at, 512), :] = kv_got[:, cols]
            raw[n, 1280:1536, :] = from_right[0:256, cols]
            one[n, 0:128, :] = from_left[256:384, cols]
            for i in range(6):
                rows = slice(i * PARENT, (i + 1) * PARENT)
                at = slice((i + 1) * BLOCK, (i + 2) * BLOCK)
                one[n, at, :] = pool1(raw[n, rows, :])
                flipped = raw[n, rows, :].T
                raw_t[n, :, rows] = flipped
                one_t[n, :, at] = (
                    (flipped[:, :BLOCK].astype(F32) + flipped[:, BLOCK:].astype(F32)) * 0.5
                ).astype(BF)
            one[n, 896:1024, :] = from_right[256:384, cols]
            for at in (slice(0, 128), slice(896, 1024)):
                one_t[n, :, at] = one[n, at, :].T
            two[n, 0:128, :] = from_left[384:512, cols]
            two[n, 128:192, :] = pool12(one[n, 0:128, :])
            two[n, 192:256, :] = pool2(raw[n, 0:256, :])
            two[n, 256:320, :] = pool2(raw[n, 1280:1536, :])
            two[n, 320:384, :] = pool12(one[n, 896:1024, :])
            two[n, 384:512, :] = from_right[384:512, cols]
            for i in range(4):
                rows = slice(i * BLOCK, (i + 1) * BLOCK)
                two_t[n, :, rows] = two[n, rows, :].T
        qs[pl.ds(own_at, 512), :] = qg_own[:, kc]
        qs[pl.ds(got_at, 512), :] = qg_got[:, kc]
        gs[pl.ds(own_at, 512), :] = qg_own[:, vc]
        gs[pl.ds(got_at, 512), :] = qg_got[:, vc]

        def blocks(ref, n, which):
            return [ref[n, b * BLOCK : (b + 1) * BLOCK, :] for b in which]

        def blocks_t(ref, n, which):
            return [ref[n, :, b * BLOCK : (b + 1) * BLOCK] for b in which]

        q_parents = [qs[i * PARENT : (i + 1) * PARENT, :] for i in range(4)]
        q1 = [
            jnp.concatenate([pool1(q_parents[2 * j]), pool1(q_parents[2 * j + 1])], axis=0)
            for j in range(2)
        ]
        q2 = jnp.concatenate([pool2(x) for x in q_parents], axis=0)
        which1 = [(0, 1, 4, 5), (2, 3, 6, 7)]
        bias1 = [(left_bias, None), (None, right_bias)]
        which2 = (0, 1, 2, 3)
        far1 = [
            far_forward(
                blocks(one, 0, which1[j]), blocks_t(one_t, 1, which1[j]), q1[j], bias1[j], p1.at[j]
            )
            for j in range(2)
        ]
        far2 = far_forward(
            blocks(two, 0, which2), blocks_t(two_t, 1, which2), q2, (left_bias, right_bias), p2
        )
        near0 = []
        for i in range(4):
            rows = slice(i * PARENT, i * PARENT + 3 * PARENT)
            s = dot_nt(raw[0, rows, :], q_parents[i])
            pieces = [s[:PARENT], s[PARENT : 2 * PARENT], s[2 * PARENT :]]
            if i == 0:
                pieces[0] = pieces[0] + left_bias
            if i == 3:
                pieces[2] = pieces[2] + right_bias
            m0 = jnp.max(
                jnp.maximum(jnp.maximum(pieces[0], pieces[1]), pieces[2]), axis=0, keepdims=True
            )
            e = [jnp.exp2((x - m0) * TO_LOG2) for x in pieces]
            for n in range(3):
                p0[i, n * PARENT : (n + 1) * PARENT, :] = e[n]
            z0 = jnp.sum(e[0] + e[1] + e[2], axis=0, keepdims=True)
            u0 = dot_nn(raw_t[1, :, rows], jnp.concatenate([x.astype(BF) for x in e], axis=0))
            near0.append((m0, z0, u0))
        acc0[...] = jnp.zeros_like(acc0)
        g1_t, ec1, f1 = [], [], []
        g2_t, ec2, low2 = [], [], []
        dq0 = []
        for i in range(4):
            rows = slice(i * PARENT, i * PARENT + 3 * PARENT)
            q = q_parents[i]
            g = gs[i * PARENT : (i + 1) * PARENT, :]
            m0, z0, u0 = near0[i]
            j, half = i // 2, i % 2
            lanes = slice(half * BLOCK, (half + 1) * BLOCK)
            m1, z1, u1 = (x[:, lanes] for x in far1[j])
            lanes2 = slice(j * BLOCK, (j + 1) * BLOCK)
            m2, z2, u2 = (spread64(x[:, lanes2], half) for x in far2)
            m1w, m2w = twice(m1, 1), twice(m2, 1)
            m = jnp.maximum(jnp.maximum(m0, m1w), m2w)
            a0 = jnp.exp2((m0 - m) * TO_LOG2)
            a1 = 2.0 * jnp.exp2((m1w - m) * TO_LOG2)
            a2 = 4.0 * jnp.exp2((m2w - m) * TO_LOG2)
            z = a0 * z0 + a1 * twice(z1, 1) + a2 * twice(z2, 1)
            inv = 1.0 / z
            o = ((a0 * inv) * u0 + (a1 * inv) * twice(u1, 1) + (a2 * inv) * twice(u2, 1)).astype(BF)
            oq[i, 0, h * HEAD : (h + 1) * HEAD, :] = o
            lg = m * TO_LOG2 + jnp.log2(z)
            g_t = g.astype(F32).T
            dr = jnp.sum(o.astype(F32) * g_t, axis=0, keepdims=True)
            lg_a, lg_b = lg[:, :BLOCK], lg[:, BLOCK:]
            g_a, g_b = g_t[:, :BLOCK], g_t[:, BLOCK:]
            dr_a, dr_b = dr[:, :BLOCK], dr[:, BLOCK:]
            low = jnp.minimum(lg_a, lg_b)
            w_a, w_b = jnp.exp2(low - lg_a), jnp.exp2(low - lg_b)
            g1_t.append((w_a * g_a + w_b * g_b).astype(BF))
            ec1.append(w_a * dr_a + w_b * dr_b)
            f1.append(2.0 * jnp.exp2(m1 * TO_LOG2 - low))
            lower = jnp.minimum(low, swap64(low))
            w_a, w_b = jnp.exp2(lower - lg_a), jnp.exp2(lower - lg_b)
            part = w_a * g_a + w_b * g_b
            g2_t.append(part + swap64(part))
            part = w_a * dr_a + w_b * dr_b
            ec2.append(part + swap64(part))
            low2.append(lower)
            f0 = jnp.exp2(m0 * TO_LOG2 - lg)
            products = dot_nt(raw[1, rows, :], g)
            weights = p0[i] * f0
            eb = weights.astype(BF)
            r = (weights * (products - dr)).astype(BF)
            acc0[1, rows, :] += dot_nn(eb, g)
            acc0[0, rows, :] += dot_nn(r, q)
            dq0.append(dot_nn(raw_t[0, :, rows], r))
        acc1[...] = jnp.zeros_like(acc1)
        dq1 = []
        for j in range(2):
            pair = slice(2 * j, 2 * j + 2)
            g1 = jnp.concatenate([x.astype(F32).T.astype(BF) for x in g1_t[pair]], axis=0)
            dk, dv, dq = far_backward(
                blocks_t(one_t, 0, which1[j]), blocks(one, 1, which1[j]), q1[j], p1.at[j],
                jnp.concatenate(f1[pair], axis=1), g1, jnp.concatenate(ec1[pair], axis=1),
            )
            for n, b in enumerate(which1[j]):
                acc1[0, b * BLOCK : (b + 1) * BLOCK, :] += dk[n]
                acc1[1, b * BLOCK : (b + 1) * BLOCK, :] += dv[n]
            dq1.append(dq)

        def joined(parts):
            return jnp.concatenate(
                [
                    jnp.where(low_lanes(parts[0].shape), parts[2 * j], parts[2 * j + 1])
                    for j in range(2)
                ],
                axis=1,
            )

        g2 = joined(g2_t).T.astype(BF)
        f2 = 4.0 * jnp.exp2(far2[0] * TO_LOG2 - joined(low2))
        dk, dv, dq2 = far_backward(
            blocks_t(two_t, 0, which2), blocks(two, 1, which2), q2, p2, f2, g2, joined(ec2)
        )
        for n in range(4):
            acc2[0, n * BLOCK : (n + 1) * BLOCK, :] = dk[n]
            acc2[1, n * BLOCK : (n + 1) * BLOCK, :] = dv[n]
        for i in range(4):
            j, half = i // 2, i % 2
            d1 = dq1[j][:, half * BLOCK : (half + 1) * BLOCK]
            d2 = spread64(dq2[:, j * BLOCK : (j + 1) * BLOCK], half)
            coarse = 0.5 * d1 + 0.25 * d2
            oq[i, 1, h * HEAD : (h + 1) * HEAD, :] = ((dq0[i] + twice(coarse, 1)) * INV_ROOT).astype(BF)
        for n, cols, scale in ((0, kc, INV_ROOT), (1, vc, 1.0)):
            for i in range(4):
                rows = slice((i + 1) * PARENT, (i + 2) * PARENT)
                coarse = acc1[n, (i + 2) * BLOCK : (i + 3) * BLOCK, :] * (0.5 * scale)
                grad[i * PARENT : (i + 1) * PARENT, cols] = acc0[n, rows, :] * scale + twice(coarse)
            far = acc2[n, 128:256, :] * (0.25 * scale)
            mid = acc1[n, 0:256, :] * (0.5 * scale)
            near = acc0[n, 0:256, :] * scale
            to_left[0:256, cols] = (near + twice(mid[128:] + twice(far[64:]))).astype(BF)
            to_left[256:384, cols] = (mid[:128] + twice(far[:64])).astype(BF)
            to_left[384:512, cols] = (acc2[n, 0:128, :] * (0.25 * scale)).astype(BF)
            far = acc2[n, 256:384, :] * (0.25 * scale)
            mid = acc1[n, 768:1024, :] * (0.5 * scale)
            near = acc0[n, 1280:1536, :] * scale
            to_right[0:256, cols] = (near + twice(mid[:128] + twice(far[:64]))).astype(BF)
            to_right[256:384, cols] = (mid[128:] + twice(far[64:])).astype(BF)
            to_right[384:512, cols] = (acc2[n, 384:512, :] * (0.25 * scale)).astype(BF)
    oq_own[...] = oq[pl.ds(side * 2, 2)]
    oq_far[...] = oq[pl.ds((1 - side) * 2, 2)]
    near_out[...] = halos[1 - odd]
    wide_out[...] = halos[odd]


def main(where, kv_own, kv_got, qg_own, qg_got, near_got, wide_got):
    rows, both = kv_own.shape
    width = both // 2
    oq_shape = jax.ShapeDtypeStruct((2, 2, width, PARENT), BF)
    halo_shape = jax.ShapeDtypeStruct((512, both), BF)
    return pl.pallas_call(
        main_kernel,
        in_specs=[smem()] + [vmem()] * 6,
        out_specs=[vmem()] * 5,
        out_shape=[
            oq_shape,
            oq_shape,
            jax.ShapeDtypeStruct((2 * rows, both), F32),
            halo_shape,
            halo_shape,
        ],
        scratch_shapes=[
            pltpu.VMEM((2, 1536, HEAD), BF),
            pltpu.VMEM((2, HEAD, 1536), BF),
            pltpu.VMEM((2, 1024, HEAD), BF),
            pltpu.VMEM((2, HEAD, 1024), BF),
            pltpu.VMEM((2, 512, HEAD), BF),
            pltpu.VMEM((2, HEAD, 512), BF),
            pltpu.VMEM((1024, HEAD), BF),
            pltpu.VMEM((1024, HEAD), BF),
            pltpu.VMEM((4, 768, PARENT), F32),
            pltpu.VMEM((2, 384, PARENT), F32),
            pltpu.VMEM((384, PARENT), F32),
            pltpu.VMEM((2, 1536, HEAD), F32),
            pltpu.VMEM((2, 1024, HEAD), F32),
            pltpu.VMEM((2, 512, HEAD), F32),
            pltpu.VMEM((4, 2, width, PARENT), BF),
            pltpu.VMEM((2, 512, both), BF),
        ],
        compiler_params=pltpu.CompilerParams(vmem_limit_bytes=24 * 1024 * 1024),
        cost_estimate=light(),
    )(where, kv_own, kv_got, qg_own, qg_got, near_got, wide_got)


def join_kernel(where, grad, near_got, wide_got, own, far):
    def fill(first, second, from_left, from_right):
        def parent(i):
            return grad[i * PARENT : (i + 1) * PARENT, :]

        def part(ref, start, stop):
            return ref[start:stop, :].astype(F32)

        first[0:256, :] = (
            parent(0) + part(from_left, 0, 256) + twice(twice(part(from_right, 384, 448)))
        ).astype(BF)
        first[256:512, :] = (
            parent(1) + twice(part(from_left, 256, 384) + twice(part(from_right, 448, 512)))
        ).astype(BF)
        second[0:256, :] = (
            parent(2) + twice(part(from_right, 256, 384) + twice(part(from_left, 384, 448)))
        ).astype(BF)
        second[256:512, :] = (
            parent(3) + part(from_right, 0, 256) + twice(twice(part(from_left, 448, 512)))
        ).astype(BF)

    for side in range(2):
        for odd in range(2):

            @pl.when((where[0] == side) & (where[3] == odd))
            def _(side=side, odd=odd):
                halves = (own, far) if side == 0 else (far, own)
                fill(*halves, *((wide_got, near_got) if odd == 0 else (near_got, wide_got)))


def join(where, grad, near_got, wide_got):
    shape = jax.ShapeDtypeStruct(near_got.shape, BF)
    return pl.pallas_call(
        join_kernel,
        in_specs=[smem(), vmem(), vmem(), vmem()],
        out_specs=[vmem(), vmem()],
        out_shape=[shape, shape],
        compiler_params=small(),
        cost_estimate=light(),
    )(where, grad, near_got, wide_got)


def unpack_rows_kernel(where, *refs):
    ins, (first, second) = refs[:-2], refs[-2:]
    order = order_matrix(True)
    width = ins[0].shape[1] // 2
    side = where[0]
    blocks = [(side * CHUNKS + c, ins[c]) for c in range(CHUNKS)]
    blocks += [((1 - side) * CHUNKS + 1 - LATE_CHUNK, ins[CHUNKS])]
    for block, ref in blocks:
        at = pl.ds(pl.multiple_of(block * width, width), width)
        for i in range(2):
            rows = slice(i * PARENT, (i + 1) * PARENT)
            first[rows, at] = dot_nn(order, ref[rows, :width]).astype(BF)
            second[rows, at] = dot_nn(order, ref[rows, width:]).astype(BF)


def unpack_rows(where, own, got, shape):
    out = jax.ShapeDtypeStruct(shape, BF)
    return pl.pallas_call(
        unpack_rows_kernel,
        in_specs=[smem()] + [vmem()] * (CHUNKS + 1),
        out_specs=[vmem(), vmem()],
        out_shape=[out, out],
        compiler_params=small(),
        cost_estimate=light(),
    )(where, *own, got)


def unpack_last_kernel(where, got, first_in, second_in, first, second, held, sems):
    del first_in, second_in
    order = order_matrix(True)
    width = got.shape[1] // 2
    block = (1 - where[0]) * CHUNKS + LATE_CHUNK
    at = pl.ds(pl.multiple_of(block * width, width), width)
    copies = []
    for m, ref in enumerate((first, second)):
        for i in range(2):
            rows = slice(i * PARENT, (i + 1) * PARENT)
            held[m, rows, :] = dot_nn(order, got[rows, m * width : (m + 1) * width]).astype(BF)
        copies.append(pltpu.make_async_copy(held.at[m], ref.at[:, at], sems.at[m]))
        copies[-1].start()
    for copy in copies:
        copy.wait()


def unpack_last(where, got, first, second):
    out = jax.ShapeDtypeStruct(first.shape, BF)
    hbm = pl.BlockSpec(memory_space=pltpu.HBM)
    return pl.pallas_call(
        unpack_last_kernel,
        in_specs=[smem(), vmem(), hbm, hbm],
        out_specs=[hbm, hbm],
        out_shape=[out, out],
        input_output_aliases={2: 0, 3: 1},
        scratch_shapes=[
            pltpu.VMEM((2, got.shape[0], got.shape[1] // 2), BF),
            pltpu.SemaphoreType.DMA((2,)),
        ],
        compiler_params=small(),
        cost_estimate=light(),
    )(where, got, first, second)


def unpack_columns_kernel(where, *refs):
    ins, (first, second) = refs[:-2], refs[-2:]
    order = order_matrix(True)
    width = ins[0].shape[2]
    for c in range(CHUNKS):
        for ref, side in ((ins[c], where[0]), (ins[CHUNKS + c], 1 - where[0])):
            at = pl.ds(pl.multiple_of((side * CHUNKS + c) * width, width), width)
            for i in range(2):
                rows = slice(i * PARENT, (i + 1) * PARENT)
                first[rows, at] = dot_nt(order, ref[i, 0]).astype(BF)
                second[rows, at] = dot_nt(order, ref[i, 1]).astype(BF)


def unpack_columns(where, own, got, shape):
    out = jax.ShapeDtypeStruct(shape, BF)
    return pl.pallas_call(
        unpack_columns_kernel,
        in_specs=[smem()] + [vmem()] * (2 * CHUNKS),
        out_specs=[vmem(), vmem()],
        out_shape=[out, out],
        compiler_params=small(),
        cost_estimate=light(),
    )(where, *own, *got)


def on_device(queries, key_matrix, value_matrix, cotangent):
    axes = ("outer", "inner")
    count = lax.axis_size("outer") * lax.axis_size("inner")
    device = lax.axis_index("outer") * lax.axis_size("inner") + lax.axis_index("inner")
    pair = device // 2
    where = jnp.stack([device % 2, pair > 0, pair < count // 2 - 1, pair % 2]).astype(jnp.int32)
    across = [(i, i ^ 1) for i in range(count)]
    near_edges = [(i, i ^ 2) for i in range(count) if i ^ 2 < count]
    wide_edges = [(i, i + 2 if i // 2 % 2 else i - 2) for i in range(count)]
    wide_edges = [(i, j) for i, j in wide_edges if 0 <= j < count]

    def swap(x):
        return lax.ppermute(x, axes, across)

    def beside(near, wide):
        near = lax.ppermute(near, axes, near_edges)
        return near, lax.ppermute(wide, axes, wide_edges)

    kv_far = pack(False, where, key_matrix, value_matrix)
    qg_far = pack(False, where, queries, cotangent)
    packed = pack(True, where, key_matrix, value_matrix, queries, cotangent)
    kv, qg = packed[:CHUNKS], packed[CHUNKS:]
    oq_own, oq_got, kv_own, kv_got = [], [], [], []
    back = []
    for c in range(CHUNKS):
        got_kv = swap(kv_far[c])
        got_qg = swap(qg_far[c])
        halos = beside(*halo(where, kv[c], got_kv))
        own, far, grad, near, wide = main(where, kv[c], got_kv, qg[c], got_qg, *halos)
        oq_own.append(own)
        oq_got.append(swap(far))
        if c + 1 < CHUNKS:
            oq_got[c], near, wide = lax.optimization_barrier((oq_got[c], near, wide))
        back.append((grad, *beside(near, wide)))
    for c in range(CHUNKS):
        own, far = join(where, *back[c])
        kv_own.append(own)
        kv_got.append(swap(far))
    attended, query_grad = unpack_columns(where, oq_own, oq_got, queries.shape)
    key_grad, value_grad = unpack_rows(where, kv_own, kv_got[1 - LATE_CHUNK], queries.shape)
    key_grad, value_grad = unpack_last(where, kv_got[LATE_CHUNK], key_grad, value_grad)
    return attended, query_grad, key_grad, value_grad


def solution(mesh):
    spec = P(("outer", "inner"), None)
    return jax.shard_map(
        on_device,
        mesh=mesh,
        in_specs=(spec,) * 4,
        out_specs=(spec,) * 4,
        check_vma=False,
    )
```

```python
import functools
import math

import jax
import jax.numpy as jnp
from jax import lax
from jax.experimental import pallas as pl
from jax.experimental.pallas import tpu as pltpu
from jax.sharding import PartitionSpec as P

HEAD = 128
BLOCK = 128
PARENT = 256
LEVELS = 3
CHUNKS = 2
LATE_CHUNK = 0
INV_ROOT = HEAD**-0.5
TO_LOG2 = INV_ROOT * math.log2(math.e)
MASKED = -1e30
BF = jnp.bfloat16
F32 = jnp.float32


def dot_nt(a, b):
    return lax.dot_general(a, b, (((1,), (1,)), ((), ())), preferred_element_type=F32)


def dot_nn(a, b):
    return jnp.dot(a, b, preferred_element_type=F32)


def order_matrix(inverse):
    row = lax.broadcasted_iota(jnp.int32, (PARENT, PARENT), 0)
    col = lax.broadcasted_iota(jnp.int32, (PARENT, PARENT), 1)
    place, token = (col, row) if inverse else (row, col)
    slab = place // 64
    source = 4 * (place % 64) + 2 * (slab % 2) + slab // 2
    return jnp.where(source == token, 1.0, 0.0).astype(BF)


def pool1(x):
    return ((x[:BLOCK].astype(F32) + x[BLOCK:].astype(F32)) * 0.5).astype(BF)


def pool2(x):
    half = x[:BLOCK].astype(F32) + x[BLOCK:].astype(F32)
    return ((half[:64] + half[64:]) * 0.25).astype(BF)


def pool12(x):
    return ((x[:64].astype(F32) + x[64:].astype(F32)) * 0.5).astype(BF)


def twice(x, axis=0):
    return jnp.concatenate([x, x], axis=axis)


def pack_kernel(own, where, *refs):
    count = 4 if own else 2
    arrays, outs, (held, sems) = refs[:count], refs[count:-2], refs[-2:]
    rows, columns = arrays[0].shape
    half = columns // 2
    width = half // CHUNKS
    side = where[0] if own else 1 - where[0]
    at = pl.ds(pl.multiple_of(side * half, half), half)
    copies = [
        pltpu.make_async_copy(ref.at[:, at], held.at[m], sems.at[m]) for m, ref in enumerate(arrays)
    ]
    for copy in copies:
        copy.start()
    order = order_matrix(False)
    for m in range(count):
        copies[m].wait()
        first = m % 2 * width
        for i in range(rows // PARENT):
            at = slice(i * PARENT, (i + 1) * PARENT)
            x = dot_nn(order, held[m, at, :]).astype(BF)
            for c in range(CHUNKS):
                out = outs[m // 2 * CHUNKS + c]
                out[at, first : first + width] = x[:, c * width : (c + 1) * width]


def pack(own, where, *arrays):
    rows, columns = arrays[0].shape
    count = len(arrays)
    return pl.pallas_call(
        functools.partial(pack_kernel, own),
        in_specs=[smem()] + [pl.BlockSpec(memory_space=pltpu.HBM)] * count,
        out_specs=[vmem()] * (count // 2 * CHUNKS),
        out_shape=[jax.ShapeDtypeStruct((rows, columns // CHUNKS), BF)] * (count // 2 * CHUNKS),
        scratch_shapes=[
            pltpu.VMEM((count, rows, columns // 2), BF),
            pltpu.SemaphoreType.DMA((count,)),
        ],
        compiler_params=small(),
        cost_estimate=light(),
    )(where, *arrays)


def smem():
    return pl.BlockSpec(memory_space=pltpu.SMEM)


def vmem():
    return pl.BlockSpec(memory_space=pltpu.VMEM)


def small():
    return pltpu.CompilerParams(vmem_limit_bytes=8 * 1024 * 1024)


def light():
    return pl.CostEstimate(flops=1000, bytes_accessed=1000, transcendentals=0)


def halo_kernel(where, own, got, near, wide):
    def fill(first, second, to_right, to_left):
        to_right[0:256, :] = second[256:512, :]
        to_right[256:384, :] = pool1(second[0:256, :])
        to_right[384:448, :] = pool2(first[0:256, :])
        to_right[448:512, :] = pool2(first[256:512, :])
        to_left[0:256, :] = first[0:256, :]
        to_left[256:384, :] = pool1(first[256:512, :])
        to_left[384:448, :] = pool2(second[0:256, :])
        to_left[448:512, :] = pool2(second[256:512, :])

    for side in range(2):
        for odd in range(2):

            @pl.when((where[0] == side) & (where[3] == odd))
            def _(side=side, odd=odd):
                halves = (own, got) if side == 0 else (got, own)
                fill(*halves, *((near, wide) if odd == 0 else (wide, near)))


def halo(where, own, got):
    shape = jax.ShapeDtypeStruct(own.shape, BF)
    return pl.pallas_call(
        halo_kernel,
        in_specs=[smem(), vmem(), vmem()],
        out_specs=[vmem(), vmem()],
        out_shape=[shape, shape],
        compiler_params=small(),
        cost_estimate=light(),
    )(where, own, got)


def swap64(x):
    return pltpu.roll(x, 64, 1)


def low_lanes(shape):
    return lax.broadcasted_iota(jnp.int32, shape, 1) < 64


def spread64(x, half):
    other = swap64(x)
    low = low_lanes(x.shape)
    return jnp.where(low, x, other) if half == 0 else jnp.where(low, other, x)


def far_forward(k, v_t, q, bias, p_ref):
    k0, k1, k2, k3 = k
    v0, v1, v2, v3 = v_t
    left, right = bias
    outer = dot_nt(jnp.concatenate([k0, k3], axis=0), q)
    first, last = outer[:BLOCK], outer[BLOCK:]
    mid_low = dot_nt(k2, q[:BLOCK])
    mid_high = dot_nt(k1, q[BLOCK:])
    if left is not None:
        first = first + left
        mid_high = mid_high + left
    if right is not None:
        last = last + right
        mid_low = mid_low + right
    mid = jnp.concatenate([mid_low, mid_high], axis=1)
    peak = jnp.max(jnp.maximum(jnp.maximum(first, last), mid), axis=0, keepdims=True)
    parts = [jnp.exp2((x - peak) * TO_LOG2) for x in (first, last, mid)]
    for n, x in enumerate(parts):
        p_ref[n * BLOCK : (n + 1) * BLOCK, :] = x
    total = jnp.sum(parts[0] + parts[1] + parts[2], axis=0, keepdims=True)
    pb = [x.astype(BF) for x in parts]
    mixed = dot_nn(
        jnp.concatenate([v0, v3], axis=1), jnp.concatenate(pb[:2], axis=0)
    ) + jnp.concatenate([dot_nn(v2, pb[2][:, :BLOCK]), dot_nn(v1, pb[2][:, BLOCK:])], axis=1)
    return peak, total, mixed


def far_backward(k_t, v, q, p_ref, factor, g, ec):
    k0, k1, k2, k3 = k_t
    v0, v1, v2, v3 = v
    e_out = p_ref[: 2 * BLOCK, :] * factor
    e_mid = p_ref[2 * BLOCK :, :] * factor
    eb_out, eb_mid = e_out.astype(BF), e_mid.astype(BF)
    p_out = dot_nt(jnp.concatenate([v0, v3], axis=0), g)
    p_mid = jnp.concatenate([dot_nt(v2, g[:BLOCK]), dot_nt(v1, g[BLOCK:])], axis=1)
    r_out = (e_out * (p_out - ec)).astype(BF)
    r_mid = (e_mid * (p_mid - ec)).astype(BF)
    dv03 = dot_nn(eb_out, g)
    dv2 = dot_nn(eb_mid[:, :BLOCK], g[:BLOCK])
    dv1 = dot_nn(eb_mid[:, BLOCK:], g[BLOCK:])
    dk03 = dot_nn(r_out, q)
    dk2 = dot_nn(r_mid[:, :BLOCK], q[:BLOCK])
    dk1 = dot_nn(r_mid[:, BLOCK:], q[BLOCK:])
    dq_t = dot_nn(jnp.concatenate([k0, k3], axis=1), r_out) + jnp.concatenate(
        [dot_nn(k2, r_mid[:, :BLOCK]), dot_nn(k1, r_mid[:, BLOCK:])], axis=1
    )
    return (dk03[:BLOCK], dk1, dk2, dk03[BLOCK:]), (dv03[:BLOCK], dv1, dv2, dv03[BLOCK:]), dq_t


def main_kernel(
    where, kv_own, kv_got, near_got, wide_got, qg_own, qg_got,
    oq_own, oq_far, grad, near_out, wide_out,
    raw, raw_t, one, one_t, two, two_t, qs, gs, p0, p1, p2, acc0, acc1, acc2, oq, halos,
):
    side = where[0]
    odd = where[3]
    halos[1 - odd] = near_got[...]
    halos[odd] = wide_got[...]
    from_left, from_right = halos.at[0], halos.at[1]
    to_left, to_right = halos.at[0], halos.at[1]
    width = kv_own.shape[1] // 2
    left_bias = (1 - where[1]).astype(F32) * MASKED
    right_bias = (1 - where[2]).astype(F32) * MASKED
    own_at = pl.multiple_of(side * 512, 512)
    got_at = pl.multiple_of((1 - side) * 512, 512)
    for h in range(width // HEAD):
        kc = slice(h * HEAD, (h + 1) * HEAD)
        vc = slice(width + h * HEAD, width + (h + 1) * HEAD)
        for n, cols in ((0, kc), (1, vc)):
            raw[n, 0:256, :] = from_left[0:256, cols]
            raw[n, pl.ds(256 + own_at, 512), :] = kv_own[:, cols]
            raw[n, pl.ds(256 + got_at, 512), :] = kv_got[:, cols]
            raw[n, 1280:1536, :] = from_right[0:256, cols]
            one[n, 0:128, :] = from_left[256:384, cols]
            for i in range(6):
                rows = slice(i * PARENT, (i + 1) * PARENT)
                at = slice((i + 1) * BLOCK, (i + 2) * BLOCK)
                one[n, at, :] = pool1(raw[n, rows, :])
                flipped = raw[n, rows, :].T
                raw_t[n, :, rows] = flipped
                one_t[n, :, at] = (
                    (flipped[:, :BLOCK].astype(F32) + flipped[:, BLOCK:].astype(F32)) * 0.5
                ).astype(BF)
            one[n, 896:1024, :] = from_right[256:384, cols]
            for at in (slice(0, 128), slice(896, 1024)):
                one_t[n, :, at] = one[n, at, :].T
            two[n, 0:128, :] = from_left[384:512, cols]
            two[n, 128:192, :] = pool12(one[n, 0:128, :])
            two[n, 192:256, :] = pool2(raw[n, 0:256, :])
            two[n, 256:320, :] = pool2(raw[n, 1280:1536, :])
            two[n, 320:384, :] = pool12(one[n, 896:1024, :])
            two[n, 384:512, :] = from_right[384:512, cols]
            for i in range(4):
                rows = slice(i * BLOCK, (i + 1) * BLOCK)
                two_t[n, :, rows] = two[n, rows, :].T
        qs[pl.ds(own_at, 512), :] = qg_own[:, kc]
        qs[pl.ds(got_at, 512), :] = qg_got[:, kc]
        gs[pl.ds(own_at, 512), :] = qg_own[:, vc]
        gs[pl.ds(got_at, 512), :] = qg_got[:, vc]

        def blocks(ref, n, which):
            return [ref[n, b * BLOCK : (b + 1) * BLOCK, :] for b in which]

        def blocks_t(ref, n, which):
            return [ref[n, :, b * BLOCK : (b + 1) * BLOCK] for b in which]

        q_parents = [qs[i * PARENT : (i + 1) * PARENT, :] for i in range(4)]
        q1 = [
            jnp.concatenate([pool1(q_parents[2 * j]), pool1(q_parents[2 * j + 1])], axis=0)
            for j in range(2)
        ]
        q2 = jnp.concatenate([pool2(x) for x in q_parents], axis=0)
        which1 = [(0, 1, 4, 5), (2, 3, 6, 7)]
        bias1 = [(left_bias, None), (None, right_bias)]
        which2 = (0, 1, 2, 3)
        far1 = [
            far_forward(
                blocks(one, 0, which1[j]), blocks_t(one_t, 1, which1[j]), q1[j], bias1[j], p1.at[j]
            )
            for j in range(2)
        ]
        far2 = far_forward(
            blocks(two, 0, which2), blocks_t(two_t, 1, which2), q2, (left_bias, right_bias), p2
        )
        acc0[...] = jnp.zeros_like(acc0)
        g1_t, ec1, f1 = [], [], []
        g2_t, ec2, low2 = [], [], []
        dq0 = []
        for i in range(4):
            rows = slice(i * PARENT, i * PARENT + 3 * PARENT)
            q = q_parents[i]
            g = gs[i * PARENT : (i + 1) * PARENT, :]
            s = dot_nt(raw[0, rows, :], q)
            pieces = [s[:PARENT], s[PARENT : 2 * PARENT], s[2 * PARENT :]]
            if i == 0:
                pieces[0] = pieces[0] + left_bias
            if i == 3:
                pieces[2] = pieces[2] + right_bias
            m0 = jnp.max(
                jnp.maximum(jnp.maximum(pieces[0], pieces[1]), pieces[2]), axis=0, keepdims=True
            )
            e = [jnp.exp2((x - m0) * TO_LOG2) for x in pieces]
            for n in range(3):
                p0[n * PARENT : (n + 1) * PARENT, :] = e[n]
            z0 = jnp.sum(e[0] + e[1] + e[2], axis=0, keepdims=True)
            u0 = dot_nn(raw_t[1, :, rows], jnp.concatenate([x.astype(BF) for x in e], axis=0))
            j, half = i // 2, i % 2
            lanes = slice(half * BLOCK, (half + 1) * BLOCK)
            m1, z1, u1 = (x[:, lanes] for x in far1[j])
            lanes2 = slice(j * BLOCK, (j + 1) * BLOCK)
            m2, z2, u2 = (spread64(x[:, lanes2], half) for x in far2)
            m1w, m2w = twice(m1, 1), twice(m2, 1)
            m = jnp.maximum(jnp.maximum(m0, m1w), m2w)
            a0 = jnp.exp2((m0 - m) * TO_LOG2)
            a1 = 2.0 * jnp.exp2((m1w - m) * TO_LOG2)
            a2 = 4.0 * jnp.exp2((m2w - m) * TO_LOG2)
            z = a0 * z0 + a1 * twice(z1, 1) + a2 * twice(z2, 1)
            inv = 1.0 / z
            o = ((a0 * inv) * u0 + (a1 * inv) * twice(u1, 1) + (a2 * inv) * twice(u2, 1)).astype(BF)
            oq[i, 0, h * HEAD : (h + 1) * HEAD, :] = o
            lg = m * TO_LOG2 + jnp.log2(z)
            g_t = g.astype(F32).T
            dr = jnp.sum(o.astype(F32) * g_t, axis=0, keepdims=True)
            lg_a, lg_b = lg[:, :BLOCK], lg[:, BLOCK:]
            g_a, g_b = g_t[:, :BLOCK], g_t[:, BLOCK:]
            dr_a, dr_b = dr[:, :BLOCK], dr[:, BLOCK:]
            low = jnp.minimum(lg_a, lg_b)
            w_a, w_b = jnp.exp2(low - lg_a), jnp.exp2(low - lg_b)
            g1_t.append((w_a * g_a + w_b * g_b).astype(BF))
            ec1.append(w_a * dr_a + w_b * dr_b)
            f1.append(2.0 * jnp.exp2(m1 * TO_LOG2 - low))
            lower = jnp.minimum(low, swap64(low))
            w_a, w_b = jnp.exp2(lower - lg_a), jnp.exp2(lower - lg_b)
            part = w_a * g_a + w_b * g_b
            g2_t.append(part + swap64(part))
            part = w_a * dr_a + w_b * dr_b
            ec2.append(part + swap64(part))
            low2.append(lower)
            f0 = jnp.exp2(m0 * TO_LOG2 - lg)
            products = dot_nt(raw[1, rows, :], g)
            weights = p0[...] * f0
            eb = weights.astype(BF)
            r = (weights * (products - dr)).astype(BF)
            acc0[1, rows, :] += dot_nn(eb, g)
            acc0[0, rows, :] += dot_nn(r, q)
            dq0.append(dot_nn(raw_t[0, :, rows], r))
        acc1[...] = jnp.zeros_like(acc1)
        dq1 = []
        for j in range(2):
            pair = slice(2 * j, 2 * j + 2)
            g1 = jnp.concatenate([x.astype(F32).T.astype(BF) for x in g1_t[pair]], axis=0)
            dk, dv, dq = far_backward(
                blocks_t(one_t, 0, which1[j]), blocks(one, 1, which1[j]), q1[j], p1.at[j],
                jnp.concatenate(f1[pair], axis=1), g1, jnp.concatenate(ec1[pair], axis=1),
            )
            for n, b in enumerate(which1[j]):
                acc1[0, b * BLOCK : (b + 1) * BLOCK, :] += dk[n]
                acc1[1, b * BLOCK : (b + 1) * BLOCK, :] += dv[n]
            dq1.append(dq)

        def joined(parts):
            return jnp.concatenate(
                [
                    jnp.where(low_lanes(parts[0].shape), parts[2 * j], parts[2 * j + 1])
                    for j in range(2)
                ],
                axis=1,
            )

        g2 = joined(g2_t).T.astype(BF)
        f2 = 4.0 * jnp.exp2(far2[0] * TO_LOG2 - joined(low2))
        dk, dv, dq2 = far_backward(
            blocks_t(two_t, 0, which2), blocks(two, 1, which2), q2, p2, f2, g2, joined(ec2)
        )
        for n in range(4):
            acc2[0, n * BLOCK : (n + 1) * BLOCK, :] = dk[n]
            acc2[1, n * BLOCK : (n + 1) * BLOCK, :] = dv[n]
        for i in range(4):
            j, half = i // 2, i % 2
            d1 = dq1[j][:, half * BLOCK : (half + 1) * BLOCK]
            d2 = spread64(dq2[:, j * BLOCK : (j + 1) * BLOCK], half)
            coarse = 0.5 * d1 + 0.25 * d2
            oq[i, 1, h * HEAD : (h + 1) * HEAD, :] = ((dq0[i] + twice(coarse, 1)) * INV_ROOT).astype(BF)
        for n, cols, scale in ((0, kc, INV_ROOT), (1, vc, 1.0)):
            for i in range(4):
                rows = slice((i + 1) * PARENT, (i + 2) * PARENT)
                coarse = acc1[n, (i + 2) * BLOCK : (i + 3) * BLOCK, :] * (0.5 * scale)
                grad[i * PARENT : (i + 1) * PARENT, cols] = acc0[n, rows, :] * scale + twice(coarse)
            far = acc2[n, 128:256, :] * (0.25 * scale)
            mid = acc1[n, 0:256, :] * (0.5 * scale)
            near = acc0[n, 0:256, :] * scale
            to_left[0:256, cols] = (near + twice(mid[128:] + twice(far[64:]))).astype(BF)
            to_left[256:384, cols] = (mid[:128] + twice(far[:64])).astype(BF)
            to_left[384:512, cols] = (acc2[n, 0:128, :] * (0.25 * scale)).astype(BF)
            far = acc2[n, 256:384, :] * (0.25 * scale)
            mid = acc1[n, 768:1024, :] * (0.5 * scale)
            near = acc0[n, 1280:1536, :] * scale
            to_right[0:256, cols] = (near + twice(mid[:128] + twice(far[:64]))).astype(BF)
            to_right[256:384, cols] = (mid[128:] + twice(far[64:])).astype(BF)
            to_right[384:512, cols] = (acc2[n, 384:512, :] * (0.25 * scale)).astype(BF)
    oq_own[...] = oq[pl.ds(side * 2, 2)]
    oq_far[...] = oq[pl.ds((1 - side) * 2, 2)]
    near_out[...] = halos[1 - odd]
    wide_out[...] = halos[odd]


def main(where, kv_own, kv_got, near_got, wide_got, qg_own, qg_got):
    rows, both = kv_own.shape
    width = both // 2
    oq_shape = jax.ShapeDtypeStruct((2, 2, width, PARENT), BF)
    halo_shape = jax.ShapeDtypeStruct((512, both), BF)
    return pl.pallas_call(
        main_kernel,
        in_specs=[smem()] + [vmem()] * 6,
        out_specs=[vmem()] * 5,
        out_shape=[
            oq_shape,
            oq_shape,
            jax.ShapeDtypeStruct((2 * rows, both), F32),
            halo_shape,
            halo_shape,
        ],
        scratch_shapes=[
            pltpu.VMEM((2, 1536, HEAD), BF),
            pltpu.VMEM((2, HEAD, 1536), BF),
            pltpu.VMEM((2, 1024, HEAD), BF),
            pltpu.VMEM((2, HEAD, 1024), BF),
            pltpu.VMEM((2, 512, HEAD), BF),
            pltpu.VMEM((2, HEAD, 512), BF),
            pltpu.VMEM((1024, HEAD), BF),
            pltpu.VMEM((1024, HEAD), BF),
            pltpu.VMEM((768, PARENT), F32),
            pltpu.VMEM((2, 384, PARENT), F32),
            pltpu.VMEM((384, PARENT), F32),
            pltpu.VMEM((2, 1536, HEAD), F32),
            pltpu.VMEM((2, 1024, HEAD), F32),
            pltpu.VMEM((2, 512, HEAD), F32),
            pltpu.VMEM((4, 2, width, PARENT), BF),
            pltpu.VMEM((2, 512, both), BF),
        ],
        compiler_params=pltpu.CompilerParams(vmem_limit_bytes=24 * 1024 * 1024),
        cost_estimate=light(),
    )(where, kv_own, kv_got, near_got, wide_got, qg_own, qg_got)


def join_kernel(where, grad, near_got, wide_got, own, far):
    def fill(first, second, from_left, from_right):
        def parent(i):
            return grad[i * PARENT : (i + 1) * PARENT, :]

        def part(ref, start, stop):
            return ref[start:stop, :].astype(F32)

        first[0:256, :] = (
            parent(0) + part(from_left, 0, 256) + twice(twice(part(from_right, 384, 448)))
        ).astype(BF)
        first[256:512, :] = (
            parent(1) + twice(part(from_left, 256, 384) + twice(part(from_right, 448, 512)))
        ).astype(BF)
        second[0:256, :] = (
            parent(2) + twice(part(from_right, 256, 384) + twice(part(from_left, 384, 448)))
        ).astype(BF)
        second[256:512, :] = (
            parent(3) + part(from_right, 0, 256) + twice(twice(part(from_left, 448, 512)))
        ).astype(BF)

    for side in range(2):
        for odd in range(2):

            @pl.when((where[0] == side) & (where[3] == odd))
            def _(side=side, odd=odd):
                halves = (own, far) if side == 0 else (far, own)
                fill(*halves, *((wide_got, near_got) if odd == 0 else (near_got, wide_got)))


def join(where, grad, near_got, wide_got):
    shape = jax.ShapeDtypeStruct(near_got.shape, BF)
    return pl.pallas_call(
        join_kernel,
        in_specs=[smem(), vmem(), vmem(), vmem()],
        out_specs=[vmem(), vmem()],
        out_shape=[shape, shape],
        compiler_params=small(),
        cost_estimate=light(),
    )(where, grad, near_got, wide_got)


def unpack_rows_kernel(where, *refs):
    ins, (first, second) = refs[:-2], refs[-2:]
    order = order_matrix(True)
    width = ins[0].shape[1] // 2
    side = where[0]
    blocks = [(side * CHUNKS + c, ins[c]) for c in range(CHUNKS)]
    blocks += [((1 - side) * CHUNKS + 1 - LATE_CHUNK, ins[CHUNKS])]
    for block, ref in blocks:
        at = pl.ds(pl.multiple_of(block * width, width), width)
        for i in range(2):
            rows = slice(i * PARENT, (i + 1) * PARENT)
            first[rows, at] = dot_nn(order, ref[rows, :width]).astype(BF)
            second[rows, at] = dot_nn(order, ref[rows, width:]).astype(BF)


def unpack_rows(where, own, got, shape):
    out = jax.ShapeDtypeStruct(shape, BF)
    return pl.pallas_call(
        unpack_rows_kernel,
        in_specs=[smem()] + [vmem()] * (CHUNKS + 1),
        out_specs=[vmem(), vmem()],
        out_shape=[out, out],
        compiler_params=small(),
        cost_estimate=light(),
    )(where, *own, got)


def unpack_last_kernel(where, got, first_in, second_in, first, second, held, sems):
    del first_in, second_in
    order = order_matrix(True)
    width = got.shape[1] // 2
    block = (1 - where[0]) * CHUNKS + LATE_CHUNK
    at = pl.ds(pl.multiple_of(block * width, width), width)
    copies = []
    for m, ref in enumerate((first, second)):
        for i in range(2):
            rows = slice(i * PARENT, (i + 1) * PARENT)
            held[m, rows, :] = dot_nn(order, got[rows, m * width : (m + 1) * width]).astype(BF)
        copies.append(pltpu.make_async_copy(held.at[m], ref.at[:, at], sems.at[m]))
        copies[-1].start()
    for copy in copies:
        copy.wait()


def unpack_last(where, got, first, second):
    out = jax.ShapeDtypeStruct(first.shape, BF)
    hbm = pl.BlockSpec(memory_space=pltpu.HBM)
    return pl.pallas_call(
        unpack_last_kernel,
        in_specs=[smem(), vmem(), hbm, hbm],
        out_specs=[hbm, hbm],
        out_shape=[out, out],
        input_output_aliases={2: 0, 3: 1},
        scratch_shapes=[
            pltpu.VMEM((2, got.shape[0], got.shape[1] // 2), BF),
            pltpu.SemaphoreType.DMA((2,)),
        ],
        compiler_params=small(),
        cost_estimate=light(),
    )(where, got, first, second)


def unpack_columns_kernel(where, *refs):
    ins, (first, second) = refs[:-2], refs[-2:]
    order = order_matrix(True)
    width = ins[0].shape[2]
    for c in range(CHUNKS):
        for ref, side in ((ins[c], where[0]), (ins[CHUNKS + c], 1 - where[0])):
            at = pl.ds(pl.multiple_of((side * CHUNKS + c) * width, width), width)
            for i in range(2):
                rows = slice(i * PARENT, (i + 1) * PARENT)
                first[rows, at] = dot_nt(order, ref[i, 0]).astype(BF)
                second[rows, at] = dot_nt(order, ref[i, 1]).astype(BF)


def unpack_columns(where, own, got, shape):
    out = jax.ShapeDtypeStruct(shape, BF)
    return pl.pallas_call(
        unpack_columns_kernel,
        in_specs=[smem()] + [vmem()] * (2 * CHUNKS),
        out_specs=[vmem(), vmem()],
        out_shape=[out, out],
        compiler_params=small(),
        cost_estimate=light(),
    )(where, *own, *got)


def on_device(queries, key_matrix, value_matrix, cotangent):
    axes = ("outer", "inner")
    count = lax.axis_size("outer") * lax.axis_size("inner")
    device = lax.axis_index("outer") * lax.axis_size("inner") + lax.axis_index("inner")
    pair = device // 2
    where = jnp.stack([device % 2, pair > 0, pair < count // 2 - 1, pair % 2]).astype(jnp.int32)
    across = [(i, i ^ 1) for i in range(count)]
    near_edges = [(i, i ^ 2) for i in range(count) if i ^ 2 < count]
    wide_edges = [(i, i + 2 if i // 2 % 2 else i - 2) for i in range(count)]
    wide_edges = [(i, j) for i, j in wide_edges if 0 <= j < count]

    def swap(x):
        return lax.ppermute(x, axes, across)

    def beside(near, wide):
        near = lax.ppermute(near, axes, near_edges)
        return near, lax.ppermute(wide, axes, wide_edges)

    kv_far = pack(False, where, key_matrix, value_matrix)
    qg_far = pack(False, where, queries, cotangent)
    packed = pack(True, where, key_matrix, value_matrix, queries, cotangent)
    kv, qg = packed[:CHUNKS], packed[CHUNKS:]
    oq_own, oq_got, kv_own, kv_got = [], [], [], []
    back = []
    for c in range(CHUNKS):
        got_kv = swap(kv_far[c])
        near, wide, far = lax.optimization_barrier((*halo(where, kv[c], got_kv), qg_far[c]))
        near, wide = beside(near, wide)
        own, far, grad, near, wide = main(where, kv[c], got_kv, near, wide, qg[c], swap(far))
        oq_own.append(own)
        oq_got.append(swap(far))
        if c + 1 < CHUNKS:
            oq_got[c], near, wide = lax.optimization_barrier((oq_got[c], near, wide))
        back.append((grad, *beside(near, wide)))
    for c in range(CHUNKS):
        own, far = join(where, *back[c])
        kv_own.append(own)
        kv_got.append(swap(far))
    attended, query_grad = unpack_columns(where, oq_own, oq_got, queries.shape)
    key_grad, value_grad = unpack_rows(where, kv_own, kv_got[1 - LATE_CHUNK], queries.shape)
    key_grad, value_grad = unpack_last(where, kv_got[LATE_CHUNK], key_grad, value_grad)
    return attended, query_grad, key_grad, value_grad


def solution(mesh):
    spec = P(("outer", "inner"), None)
    return jax.shard_map(
        on_device,
        mesh=mesh,
        in_specs=(spec,) * 4,
        out_specs=(spec,) * 4,
        check_vma=False,
    )
```

```python
import functools
import math

import jax
import jax.numpy as jnp
from jax import lax
from jax.experimental import pallas as pl
from jax.experimental.pallas import tpu as pltpu
from jax.sharding import PartitionSpec as P

HEAD = 128
BLOCK = 128
PARENT = 256
LEVELS = 3
CHUNKS = 2
LATE_CHUNK = 0
INV_ROOT = HEAD**-0.5
TO_LOG2 = INV_ROOT * math.log2(math.e)
MASKED = -1e30
BF = jnp.bfloat16
F32 = jnp.float32


def dot_nt(a, b):
    return lax.dot_general(a, b, (((1,), (1,)), ((), ())), preferred_element_type=F32)


def dot_nn(a, b):
    return jnp.dot(a, b, preferred_element_type=F32)


def order_matrix(inverse):
    row = lax.broadcasted_iota(jnp.int32, (PARENT, PARENT), 0)
    col = lax.broadcasted_iota(jnp.int32, (PARENT, PARENT), 1)
    place, token = (col, row) if inverse else (row, col)
    slab = place // 64
    source = 4 * (place % 64) + 2 * (slab % 2) + slab // 2
    return jnp.where(source == token, 1.0, 0.0).astype(BF)


def pool1(x):
    return ((x[:BLOCK].astype(F32) + x[BLOCK:].astype(F32)) * 0.5).astype(BF)


def pool2(x):
    half = x[:BLOCK].astype(F32) + x[BLOCK:].astype(F32)
    return ((half[:64] + half[64:]) * 0.25).astype(BF)


def pool12(x):
    return ((x[:64].astype(F32) + x[64:].astype(F32)) * 0.5).astype(BF)


def twice(x, axis=0):
    return jnp.concatenate([x, x], axis=axis)


def pack_kernel(own, where, *refs):
    count = 4 if own else 2
    arrays, outs, (held, sems) = refs[:count], refs[count:-2], refs[-2:]
    rows, columns = arrays[0].shape
    half = columns // 2
    width = half // CHUNKS
    side = where[0] if own else 1 - where[0]
    at = pl.ds(pl.multiple_of(side * half, half), half)
    copies = [
        pltpu.make_async_copy(ref.at[:, at], held.at[m], sems.at[m]) for m, ref in enumerate(arrays)
    ]
    for copy in copies:
        copy.start()
    order = order_matrix(False)
    for m in range(count):
        copies[m].wait()
        first = m % 2 * width
        for i in range(rows // PARENT):
            at = slice(i * PARENT, (i + 1) * PARENT)
            x = dot_nn(order, held[m, at, :]).astype(BF)
            for c in range(CHUNKS):
                out = outs[m // 2 * CHUNKS + c]
                out[at, first : first + width] = x[:, c * width : (c + 1) * width]


def pack(own, where, *arrays):
    rows, columns = arrays[0].shape
    count = len(arrays)
    return pl.pallas_call(
        functools.partial(pack_kernel, own),
        in_specs=[smem()] + [pl.BlockSpec(memory_space=pltpu.HBM)] * count,
        out_specs=[vmem()] * (count // 2 * CHUNKS),
        out_shape=[jax.ShapeDtypeStruct((rows, columns // CHUNKS), BF)] * (count // 2 * CHUNKS),
        scratch_shapes=[
            pltpu.VMEM((count, rows, columns // 2), BF),
            pltpu.SemaphoreType.DMA((count,)),
        ],
        compiler_params=small(),
        cost_estimate=light(),
    )(where, *arrays)


def smem():
    return pl.BlockSpec(memory_space=pltpu.SMEM)


def vmem():
    return pl.BlockSpec(memory_space=pltpu.VMEM)


def small():
    return pltpu.CompilerParams(vmem_limit_bytes=8 * 1024 * 1024)


def light():
    return pl.CostEstimate(flops=1000, bytes_accessed=1000, transcendentals=0)


def halo_kernel(where, own, got, near, wide):
    def fill(first, second, to_right, to_left):
        to_right[0:256, :] = second[256:512, :]
        to_right[256:384, :] = pool1(second[0:256, :])
        to_right[384:448, :] = pool2(first[0:256, :])
        to_right[448:512, :] = pool2(first[256:512, :])
        to_left[0:256, :] = first[0:256, :]
        to_left[256:384, :] = pool1(first[256:512, :])
        to_left[384:448, :] = pool2(second[0:256, :])
        to_left[448:512, :] = pool2(second[256:512, :])

    for side in range(2):
        for odd in range(2):

            @pl.when((where[0] == side) & (where[3] == odd))
            def _(side=side, odd=odd):
                halves = (own, got) if side == 0 else (got, own)
                fill(*halves, *((near, wide) if odd == 0 else (wide, near)))


def halo(where, own, got):
    shape = jax.ShapeDtypeStruct(own.shape, BF)
    return pl.pallas_call(
        halo_kernel,
        in_specs=[smem(), vmem(), vmem()],
        out_specs=[vmem(), vmem()],
        out_shape=[shape, shape],
        compiler_params=small(),
        cost_estimate=light(),
    )(where, own, got)


def swap64(x):
    return pltpu.roll(x, 64, 1)


def low_lanes(shape):
    return lax.broadcasted_iota(jnp.int32, shape, 1) < 64


def spread64(x, half):
    other = swap64(x)
    low = low_lanes(x.shape)
    return jnp.where(low, x, other) if half == 0 else jnp.where(low, other, x)


def far_forward(k, v_t, q, bias, p_ref):
    k0, k1, k2, k3 = k
    v0, v1, v2, v3 = v_t
    left, right = bias
    outer = dot_nt(jnp.concatenate([k0, k3], axis=0), q)
    first, last = outer[:BLOCK], outer[BLOCK:]
    mid_low = dot_nt(k2, q[:BLOCK])
    mid_high = dot_nt(k1, q[BLOCK:])
    if left is not None:
        first = first + left
        mid_high = mid_high + left
    if right is not None:
        last = last + right
        mid_low = mid_low + right
    mid = jnp.concatenate([mid_low, mid_high], axis=1)
    peak = jnp.max(jnp.maximum(jnp.maximum(first, last), mid), axis=0, keepdims=True)
    parts = [jnp.exp2((x - peak) * TO_LOG2) for x in (first, last, mid)]
    for n, x in enumerate(parts):
        p_ref[n * BLOCK : (n + 1) * BLOCK, :] = x
    total = jnp.sum(parts[0] + parts[1] + parts[2], axis=0, keepdims=True)
    pb = [x.astype(BF) for x in parts]
    mixed = dot_nn(
        jnp.concatenate([v0, v3], axis=1), jnp.concatenate(pb[:2], axis=0)
    ) + jnp.concatenate([dot_nn(v2, pb[2][:, :BLOCK]), dot_nn(v1, pb[2][:, BLOCK:])], axis=1)
    return peak, total, mixed


def far_backward(k_t, v, q, p_ref, factor, g, ec):
    k0, k1, k2, k3 = k_t
    v0, v1, v2, v3 = v
    e_out = p_ref[: 2 * BLOCK, :] * factor
    e_mid = p_ref[2 * BLOCK :, :] * factor
    eb_out, eb_mid = e_out.astype(BF), e_mid.astype(BF)
    p_out = dot_nt(jnp.concatenate([v0, v3], axis=0), g)
    p_mid = jnp.concatenate([dot_nt(v2, g[:BLOCK]), dot_nt(v1, g[BLOCK:])], axis=1)
    r_out = (e_out * (p_out - ec)).astype(BF)
    r_mid = (e_mid * (p_mid - ec)).astype(BF)
    dv03 = dot_nn(eb_out, g)
    dv2 = dot_nn(eb_mid[:, :BLOCK], g[:BLOCK])
    dv1 = dot_nn(eb_mid[:, BLOCK:], g[BLOCK:])
    dk03 = dot_nn(r_out, q)
    dk2 = dot_nn(r_mid[:, :BLOCK], q[:BLOCK])
    dk1 = dot_nn(r_mid[:, BLOCK:], q[BLOCK:])
    dq_t = dot_nn(jnp.concatenate([k0, k3], axis=1), r_out) + jnp.concatenate(
        [dot_nn(k2, r_mid[:, :BLOCK]), dot_nn(k1, r_mid[:, BLOCK:])], axis=1
    )
    return (dk03[:BLOCK], dk1, dk2, dk03[BLOCK:]), (dv03[:BLOCK], dv1, dv2, dv03[BLOCK:]), dq_t


def main_kernel(
    where, kv_own, kv_got, near_got, wide_got, qg_own, qg_got,
    oq_own, oq_far, grad, near_out, wide_out,
    raw, raw_t, one, one_t, two, two_t, qs, gs, p0, p1, p2, acc0, acc1, acc2, oq, halos,
):
    side = where[0]
    odd = where[3]
    halos[1 - odd] = near_got[...]
    halos[odd] = wide_got[...]
    from_left, from_right = halos.at[0], halos.at[1]
    to_left, to_right = halos.at[0], halos.at[1]
    width = kv_own.shape[1] // 2
    left_bias = (1 - where[1]).astype(F32) * MASKED
    right_bias = (1 - where[2]).astype(F32) * MASKED
    own_at = pl.multiple_of(side * 512, 512)
    got_at = pl.multiple_of((1 - side) * 512, 512)
    for h in range(width // HEAD):
        kc = slice(h * HEAD, (h + 1) * HEAD)
        vc = slice(width + h * HEAD, width + (h + 1) * HEAD)
        for n, cols in ((0, kc), (1, vc)):
            raw[n, 0:256, :] = from_left[0:256, cols]
            raw[n, pl.ds(256 + own_at, 512), :] = kv_own[:, cols]
            raw[n, pl.ds(256 + got_at, 512), :] = kv_got[:, cols]
            raw[n, 1280:1536, :] = from_right[0:256, cols]
            one[n, 0:128, :] = from_left[256:384, cols]
            for i in range(6):
                rows = slice(i * PARENT, (i + 1) * PARENT)
                at = slice((i + 1) * BLOCK, (i + 2) * BLOCK)
                one[n, at, :] = pool1(raw[n, rows, :])
                flipped = raw[n, rows, :].T
                raw_t[n, :, rows] = flipped
                one_t[n, :, at] = (
                    (flipped[:, :BLOCK].astype(F32) + flipped[:, BLOCK:].astype(F32)) * 0.5
                ).astype(BF)
            one[n, 896:1024, :] = from_right[256:384, cols]
            for at in (slice(0, 128), slice(896, 1024)):
                one_t[n, :, at] = one[n, at, :].T
            two[n, 0:128, :] = from_left[384:512, cols]
            two[n, 128:192, :] = pool12(one[n, 0:128, :])
            two[n, 192:256, :] = pool2(raw[n, 0:256, :])
            two[n, 256:320, :] = pool2(raw[n, 1280:1536, :])
            two[n, 320:384, :] = pool12(one[n, 896:1024, :])
            two[n, 384:512, :] = from_right[384:512, cols]
            for i in range(4):
                rows = slice(i * BLOCK, (i + 1) * BLOCK)
                two_t[n, :, rows] = two[n, rows, :].T
        qs[pl.ds(own_at, 512), :] = qg_own[:, kc]
        qs[pl.ds(got_at, 512), :] = qg_got[:, kc]
        gs[pl.ds(own_at, 512), :] = qg_own[:, vc]
        gs[pl.ds(got_at, 512), :] = qg_got[:, vc]

        def blocks(ref, n, which):
            return [ref[n, b * BLOCK : (b + 1) * BLOCK, :] for b in which]

        def blocks_t(ref, n, which):
            return [ref[n, :, b * BLOCK : (b + 1) * BLOCK] for b in which]

        q_parents = [qs[i * PARENT : (i + 1) * PARENT, :] for i in range(4)]
        q1 = [
            jnp.concatenate([pool1(q_parents[2 * j]), pool1(q_parents[2 * j + 1])], axis=0)
            for j in range(2)
        ]
        q2 = jnp.concatenate([pool2(x) for x in q_parents], axis=0)
        which1 = [(0, 1, 4, 5), (2, 3, 6, 7)]
        bias1 = [(left_bias, None), (None, right_bias)]
        which2 = (0, 1, 2, 3)
        far1 = [
            far_forward(
                blocks(one, 0, which1[j]), blocks_t(one_t, 1, which1[j]), q1[j], bias1[j], p1.at[j]
            )
            for j in range(2)
        ]
        far2 = far_forward(
            blocks(two, 0, which2), blocks_t(two_t, 1, which2), q2, (left_bias, right_bias), p2
        )
        acc0[...] = jnp.zeros_like(acc0)
        g1_t, ec1, f1 = [], [], []
        g2_t, ec2, low2 = [], [], []
        dq0 = []
        for i in range(4):
            q = q_parents[i]
            g = gs[i * PARENT : (i + 1) * PARENT, :]
            parents = [slice(n * PARENT, (n + 1) * PARENT) for n in range(i, i + 3)]
            pieces = [dot_nt(raw[0, at, :], q) for at in parents]
            if i == 0:
                pieces[0] = pieces[0] + left_bias
            if i == 3:
                pieces[2] = pieces[2] + right_bias
            m0 = jnp.max(
                jnp.maximum(jnp.maximum(pieces[0], pieces[1]), pieces[2]), axis=0, keepdims=True
            )
            e = [jnp.exp2((x - m0) * TO_LOG2) for x in pieces]
            for n in range(3):
                p0[n * PARENT : (n + 1) * PARENT, :] = e[n]
            z0 = jnp.sum(e[0] + e[1] + e[2], axis=0, keepdims=True)
            u0 = sum(dot_nn(raw_t[1, :, at], x.astype(BF)) for at, x in zip(parents, e))
            j, half = i // 2, i % 2
            lanes = slice(half * BLOCK, (half + 1) * BLOCK)
            m1, z1, u1 = (x[:, lanes] for x in far1[j])
            lanes2 = slice(j * BLOCK, (j + 1) * BLOCK)
            m2, z2, u2 = (spread64(x[:, lanes2], half) for x in far2)
            m1w, m2w = twice(m1, 1), twice(m2, 1)
            m = jnp.maximum(jnp.maximum(m0, m1w), m2w)
            a0 = jnp.exp2((m0 - m) * TO_LOG2)
            a1 = 2.0 * jnp.exp2((m1w - m) * TO_LOG2)
            a2 = 4.0 * jnp.exp2((m2w - m) * TO_LOG2)
            z = a0 * z0 + a1 * twice(z1, 1) + a2 * twice(z2, 1)
            inv = 1.0 / z
            o = ((a0 * inv) * u0 + (a1 * inv) * twice(u1, 1) + (a2 * inv) * twice(u2, 1)).astype(BF)
            oq[i, 0, h * HEAD : (h + 1) * HEAD, :] = o
            lg = m * TO_LOG2 + jnp.log2(z)
            g_t = g.astype(F32).T
            dr = jnp.sum(o.astype(F32) * g_t, axis=0, keepdims=True)
            lg_a, lg_b = lg[:, :BLOCK], lg[:, BLOCK:]
            g_a, g_b = g_t[:, :BLOCK], g_t[:, BLOCK:]
            dr_a, dr_b = dr[:, :BLOCK], dr[:, BLOCK:]
            low = jnp.minimum(lg_a, lg_b)
            w_a, w_b = jnp.exp2(low - lg_a), jnp.exp2(low - lg_b)
            g1_t.append((w_a * g_a + w_b * g_b).astype(BF))
            ec1.append(w_a * dr_a + w_b * dr_b)
            f1.append(2.0 * jnp.exp2(m1 * TO_LOG2 - low))
            lower = jnp.minimum(low, swap64(low))
            w_a, w_b = jnp.exp2(lower - lg_a), jnp.exp2(lower - lg_b)
            part = w_a * g_a + w_b * g_b
            g2_t.append(part + swap64(part))
            part = w_a * dr_a + w_b * dr_b
            ec2.append(part + swap64(part))
            low2.append(lower)
            f0 = jnp.exp2(m0 * TO_LOG2 - lg)
            dq = None
            for n, at in enumerate(parents):
                products = dot_nt(raw[1, at, :], g)
                weights = p0[n * PARENT : (n + 1) * PARENT, :] * f0
                r = (weights * (products - dr)).astype(BF)
                acc0[1, at, :] += dot_nn(weights.astype(BF), g)
                acc0[0, at, :] += dot_nn(r, q)
                part = dot_nn(raw_t[0, :, at], r)
                dq = part if dq is None else dq + part
            dq0.append(dq)
        acc1[...] = jnp.zeros_like(acc1)
        dq1 = []
        for j in range(2):
            pair = slice(2 * j, 2 * j + 2)
            g1 = jnp.concatenate([x.astype(F32).T.astype(BF) for x in g1_t[pair]], axis=0)
            dk, dv, dq = far_backward(
                blocks_t(one_t, 0, which1[j]), blocks(one, 1, which1[j]), q1[j], p1.at[j],
                jnp.concatenate(f1[pair], axis=1), g1, jnp.concatenate(ec1[pair], axis=1),
            )
            for n, b in enumerate(which1[j]):
                acc1[0, b * BLOCK : (b + 1) * BLOCK, :] += dk[n]
                acc1[1, b * BLOCK : (b + 1) * BLOCK, :] += dv[n]
            dq1.append(dq)

        def joined(parts):
            return jnp.concatenate(
                [
                    jnp.where(low_lanes(parts[0].shape), parts[2 * j], parts[2 * j + 1])
                    for j in range(2)
                ],
                axis=1,
            )

        g2 = joined(g2_t).T.astype(BF)
        f2 = 4.0 * jnp.exp2(far2[0] * TO_LOG2 - joined(low2))
        dk, dv, dq2 = far_backward(
            blocks_t(two_t, 0, which2), blocks(two, 1, which2), q2, p2, f2, g2, joined(ec2)
        )
        for n in range(4):
            acc2[0, n * BLOCK : (n + 1) * BLOCK, :] = dk[n]
            acc2[1, n * BLOCK : (n + 1) * BLOCK, :] = dv[n]
        for i in range(4):
            j, half = i // 2, i % 2
            d1 = dq1[j][:, half * BLOCK : (half + 1) * BLOCK]
            d2 = spread64(dq2[:, j * BLOCK : (j + 1) * BLOCK], half)
            coarse = 0.5 * d1 + 0.25 * d2
            oq[i, 1, h * HEAD : (h + 1) * HEAD, :] = ((dq0[i] + twice(coarse, 1)) * INV_ROOT).astype(BF)
        for n, cols, scale in ((0, kc, INV_ROOT), (1, vc, 1.0)):
            for i in range(4):
                rows = slice((i + 1) * PARENT, (i + 2) * PARENT)
                coarse = acc1[n, (i + 2) * BLOCK : (i + 3) * BLOCK, :] * (0.5 * scale)
                grad[i * PARENT : (i + 1) * PARENT, cols] = acc0[n, rows, :] * scale + twice(coarse)
            far = acc2[n, 128:256, :] * (0.25 * scale)
            mid = acc1[n, 0:256, :] * (0.5 * scale)
            near = acc0[n, 0:256, :] * scale
            to_left[0:256, cols] = (near + twice(mid[128:] + twice(far[64:]))).astype(BF)
            to_left[256:384, cols] = (mid[:128] + twice(far[:64])).astype(BF)
            to_left[384:512, cols] = (acc2[n, 0:128, :] * (0.25 * scale)).astype(BF)
            far = acc2[n, 256:384, :] * (0.25 * scale)
            mid = acc1[n, 768:1024, :] * (0.5 * scale)
            near = acc0[n, 1280:1536, :] * scale
            to_right[0:256, cols] = (near + twice(mid[:128] + twice(far[:64]))).astype(BF)
            to_right[256:384, cols] = (mid[128:] + twice(far[64:])).astype(BF)
            to_right[384:512, cols] = (acc2[n, 384:512, :] * (0.25 * scale)).astype(BF)
    oq_own[...] = oq[pl.ds(side * 2, 2)]
    oq_far[...] = oq[pl.ds((1 - side) * 2, 2)]
    near_out[...] = halos[1 - odd]
    wide_out[...] = halos[odd]


def main(where, kv_own, kv_got, near_got, wide_got, qg_own, qg_got):
    rows, both = kv_own.shape
    width = both // 2
    oq_shape = jax.ShapeDtypeStruct((2, 2, width, PARENT), BF)
    halo_shape = jax.ShapeDtypeStruct((512, both), BF)
    return pl.pallas_call(
        main_kernel,
        in_specs=[smem()] + [vmem()] * 6,
        out_specs=[vmem()] * 5,
        out_shape=[
            oq_shape,
            oq_shape,
            jax.ShapeDtypeStruct((2 * rows, both), F32),
            halo_shape,
            halo_shape,
        ],
        scratch_shapes=[
            pltpu.VMEM((2, 1536, HEAD), BF),
            pltpu.VMEM((2, HEAD, 1536), BF),
            pltpu.VMEM((2, 1024, HEAD), BF),
            pltpu.VMEM((2, HEAD, 1024), BF),
            pltpu.VMEM((2, 512, HEAD), BF),
            pltpu.VMEM((2, HEAD, 512), BF),
            pltpu.VMEM((1024, HEAD), BF),
            pltpu.VMEM((1024, HEAD), BF),
            pltpu.VMEM((768, PARENT), F32),
            pltpu.VMEM((2, 384, PARENT), F32),
            pltpu.VMEM((384, PARENT), F32),
            pltpu.VMEM((2, 1536, HEAD), F32),
            pltpu.VMEM((2, 1024, HEAD), F32),
            pltpu.VMEM((2, 512, HEAD), F32),
            pltpu.VMEM((4, 2, width, PARENT), BF),
            pltpu.VMEM((2, 512, both), BF),
        ],
        compiler_params=pltpu.CompilerParams(vmem_limit_bytes=24 * 1024 * 1024),
        cost_estimate=light(),
    )(where, kv_own, kv_got, near_got, wide_got, qg_own, qg_got)


def join_kernel(where, grad, near_got, wide_got, own, far):
    def fill(first, second, from_left, from_right):
        def parent(i):
            return grad[i * PARENT : (i + 1) * PARENT, :]

        def part(ref, start, stop):
            return ref[start:stop, :].astype(F32)

        first[0:256, :] = (
            parent(0) + part(from_left, 0, 256) + twice(twice(part(from_right, 384, 448)))
        ).astype(BF)
        first[256:512, :] = (
            parent(1) + twice(part(from_left, 256, 384) + twice(part(from_right, 448, 512)))
        ).astype(BF)
        second[0:256, :] = (
            parent(2) + twice(part(from_right, 256, 384) + twice(part(from_left, 384, 448)))
        ).astype(BF)
        second[256:512, :] = (
            parent(3) + part(from_right, 0, 256) + twice(twice(part(from_left, 448, 512)))
        ).astype(BF)

    for side in range(2):
        for odd in range(2):

            @pl.when((where[0] == side) & (where[3] == odd))
            def _(side=side, odd=odd):
                halves = (own, far) if side == 0 else (far, own)
                fill(*halves, *((wide_got, near_got) if odd == 0 else (near_got, wide_got)))


def join(where, grad, near_got, wide_got):
    shape = jax.ShapeDtypeStruct(near_got.shape, BF)
    return pl.pallas_call(
        join_kernel,
        in_specs=[smem(), vmem(), vmem(), vmem()],
        out_specs=[vmem(), vmem()],
        out_shape=[shape, shape],
        compiler_params=small(),
        cost_estimate=light(),
    )(where, grad, near_got, wide_got)


def unpack_rows_kernel(where, *refs):
    ins, (first, second) = refs[:-2], refs[-2:]
    order = order_matrix(True)
    width = ins[0].shape[1] // 2
    side = where[0]
    blocks = [(side * CHUNKS + c, ins[c]) for c in range(CHUNKS)]
    blocks += [((1 - side) * CHUNKS + 1 - LATE_CHUNK, ins[CHUNKS])]
    for block, ref in blocks:
        at = pl.ds(pl.multiple_of(block * width, width), width)
        for i in range(2):
            rows = slice(i * PARENT, (i + 1) * PARENT)
            first[rows, at] = dot_nn(order, ref[rows, :width]).astype(BF)
            second[rows, at] = dot_nn(order, ref[rows, width:]).astype(BF)


def unpack_rows(where, own, got, shape):
    out = jax.ShapeDtypeStruct(shape, BF)
    return pl.pallas_call(
        unpack_rows_kernel,
        in_specs=[smem()] + [vmem()] * (CHUNKS + 1),
        out_specs=[vmem(), vmem()],
        out_shape=[out, out],
        compiler_params=small(),
        cost_estimate=light(),
    )(where, *own, got)


def unpack_last_kernel(where, got, first_in, second_in, first, second, held, sems):
    del first_in, second_in
    order = order_matrix(True)
    width = got.shape[1] // 2
    block = (1 - where[0]) * CHUNKS + LATE_CHUNK
    at = pl.ds(pl.multiple_of(block * width, width), width)
    copies = []
    for m, ref in enumerate((first, second)):
        for i in range(2):
            rows = slice(i * PARENT, (i + 1) * PARENT)
            held[m, rows, :] = dot_nn(order, got[rows, m * width : (m + 1) * width]).astype(BF)
        copies.append(pltpu.make_async_copy(held.at[m], ref.at[:, at], sems.at[m]))
        copies[-1].start()
    for copy in copies:
        copy.wait()


def unpack_last(where, got, first, second):
    out = jax.ShapeDtypeStruct(first.shape, BF)
    hbm = pl.BlockSpec(memory_space=pltpu.HBM)
    return pl.pallas_call(
        unpack_last_kernel,
        in_specs=[smem(), vmem(), hbm, hbm],
        out_specs=[hbm, hbm],
        out_shape=[out, out],
        input_output_aliases={2: 0, 3: 1},
        scratch_shapes=[
            pltpu.VMEM((2, got.shape[0], got.shape[1] // 2), BF),
            pltpu.SemaphoreType.DMA((2,)),
        ],
        compiler_params=small(),
        cost_estimate=light(),
    )(where, got, first, second)


def unpack_columns_kernel(where, *refs):
    ins, (first, second) = refs[:-2], refs[-2:]
    order = order_matrix(True)
    width = ins[0].shape[2]
    for c in range(CHUNKS):
        for ref, side in ((ins[c], where[0]), (ins[CHUNKS + c], 1 - where[0])):
            at = pl.ds(pl.multiple_of((side * CHUNKS + c) * width, width), width)
            for i in range(2):
                rows = slice(i * PARENT, (i + 1) * PARENT)
                first[rows, at] = dot_nt(order, ref[i, 0]).astype(BF)
                second[rows, at] = dot_nt(order, ref[i, 1]).astype(BF)


def unpack_columns(where, own, got, shape):
    out = jax.ShapeDtypeStruct(shape, BF)
    return pl.pallas_call(
        unpack_columns_kernel,
        in_specs=[smem()] + [vmem()] * (2 * CHUNKS),
        out_specs=[vmem(), vmem()],
        out_shape=[out, out],
        compiler_params=small(),
        cost_estimate=light(),
    )(where, *own, *got)


def on_device(queries, key_matrix, value_matrix, cotangent):
    axes = ("outer", "inner")
    count = lax.axis_size("outer") * lax.axis_size("inner")
    device = lax.axis_index("outer") * lax.axis_size("inner") + lax.axis_index("inner")
    pair = device // 2
    where = jnp.stack([device % 2, pair > 0, pair < count // 2 - 1, pair % 2]).astype(jnp.int32)
    across = [(i, i ^ 1) for i in range(count)]
    near_edges = [(i, i ^ 2) for i in range(count) if i ^ 2 < count]
    wide_edges = [(i, i + 2 if i // 2 % 2 else i - 2) for i in range(count)]
    wide_edges = [(i, j) for i, j in wide_edges if 0 <= j < count]

    def swap(x):
        return lax.ppermute(x, axes, across)

    def beside(near, wide):
        near = lax.ppermute(near, axes, near_edges)
        return near, lax.ppermute(wide, axes, wide_edges)

    kv_far = pack(False, where, key_matrix, value_matrix)
    qg_far = pack(False, where, queries, cotangent)
    packed = pack(True, where, key_matrix, value_matrix, queries, cotangent)
    kv, qg = packed[:CHUNKS], packed[CHUNKS:]
    oq_own, oq_got, back = [], [], []
    for c in range(CHUNKS):
        got_kv = swap(kv_far[c])
        near, wide, far = lax.optimization_barrier((*halo(where, kv[c], got_kv), qg_far[c]))
        near, wide = beside(near, wide)
        own, far, grad, near, wide = main(where, kv[c], got_kv, near, wide, qg[c], swap(far))
        oq_own.append(own)
        oq_got.append(swap(far))
        if c + 1 < CHUNKS:
            oq_got[c], near, wide = lax.optimization_barrier((oq_got[c], near, wide))
        back.append([grad, *beside(near, wide)])
    kv_own, kv_got = [None] * CHUNKS, [None] * CHUNKS
    oq_got[-1], back[-1] = lax.optimization_barrier((oq_got[-1], back[-1]))
    for c in reversed(range(CHUNKS)):
        kv_own[c], far = join(where, *back[c])
        kv_got[c] = swap(far)
    attended, query_grad = unpack_columns(where, oq_own, oq_got, queries.shape)
    key_grad, value_grad = unpack_rows(where, kv_own, kv_got[1 - LATE_CHUNK], queries.shape)
    key_grad, value_grad = unpack_last(where, kv_got[LATE_CHUNK], key_grad, value_grad)
    return attended, query_grad, key_grad, value_grad


def solution(mesh):
    spec = P(("outer", "inner"), None)
    return jax.shard_map(
        on_device,
        mesh=mesh,
        in_specs=(spec,) * 4,
        out_specs=(spec,) * 4,
        check_vma=False,
    )
```

```python
import functools
import math

import jax
import jax.numpy as jnp
from jax import lax
from jax.experimental import pallas as pl
from jax.experimental.pallas import tpu as pltpu
from jax.sharding import PartitionSpec as P

HEAD = 128
BLOCK = 128
PARENT = 256
LEVELS = 3
CHUNKS = 2
LATE_CHUNK = 0
INV_ROOT = HEAD**-0.5
TO_LOG2 = INV_ROOT * math.log2(math.e)
MASKED = -1e30
BF = jnp.bfloat16
F32 = jnp.float32


def dot_nt(a, b):
    return lax.dot_general(a, b, (((1,), (1,)), ((), ())), preferred_element_type=F32)


def dot_nn(a, b):
    return jnp.dot(a, b, preferred_element_type=F32)


def order_matrix(inverse):
    row = lax.broadcasted_iota(jnp.int32, (PARENT, PARENT), 0)
    col = lax.broadcasted_iota(jnp.int32, (PARENT, PARENT), 1)
    place, token = (col, row) if inverse else (row, col)
    slab = place // 64
    source = 4 * (place % 64) + 2 * (slab % 2) + slab // 2
    return jnp.where(source == token, 1.0, 0.0).astype(BF)


def pool1(x):
    return ((x[:BLOCK].astype(F32) + x[BLOCK:].astype(F32)) * 0.5).astype(BF)


def pool2(x):
    half = x[:BLOCK].astype(F32) + x[BLOCK:].astype(F32)
    return ((half[:64] + half[64:]) * 0.25).astype(BF)


def pool12(x):
    return ((x[:64].astype(F32) + x[64:].astype(F32)) * 0.5).astype(BF)


def twice(x, axis=0):
    return jnp.concatenate([x, x], axis=axis)


def pack_kernel(own, where, *refs):
    count = 4 if own else 2
    arrays, outs, (held, sems) = refs[:count], refs[count:-2], refs[-2:]
    rows, columns = arrays[0].shape
    half = columns // 2
    width = half // CHUNKS
    side = where[0] if own else 1 - where[0]
    at = pl.ds(pl.multiple_of(side * half, half), half)
    copies = [
        pltpu.make_async_copy(ref.at[:, at], held.at[m], sems.at[m]) for m, ref in enumerate(arrays)
    ]
    for copy in copies:
        copy.start()
    order = order_matrix(False)
    for m in range(count):
        copies[m].wait()
        first = m % 2 * width
        for i in range(rows // PARENT):
            at = slice(i * PARENT, (i + 1) * PARENT)
            x = dot_nn(order, held[m, at, :]).astype(BF)
            for c in range(CHUNKS):
                out = outs[m // 2 * CHUNKS + c]
                out[at, first : first + width] = x[:, c * width : (c + 1) * width]


def pack(own, where, *arrays):
    rows, columns = arrays[0].shape
    count = len(arrays)
    return pl.pallas_call(
        functools.partial(pack_kernel, own),
        in_specs=[smem()] + [pl.BlockSpec(memory_space=pltpu.HBM)] * count,
        out_specs=[vmem()] * (count // 2 * CHUNKS),
        out_shape=[jax.ShapeDtypeStruct((rows, columns // CHUNKS), BF)] * (count // 2 * CHUNKS),
        scratch_shapes=[
            pltpu.VMEM((count, rows, columns // 2), BF),
            pltpu.SemaphoreType.DMA((count,)),
        ],
        compiler_params=small(),
        cost_estimate=light(),
    )(where, *arrays)


def smem():
    return pl.BlockSpec(memory_space=pltpu.SMEM)


def vmem():
    return pl.BlockSpec(memory_space=pltpu.VMEM)


def small():
    return pltpu.CompilerParams(vmem_limit_bytes=8 * 1024 * 1024)


def light():
    return pl.CostEstimate(flops=1000, bytes_accessed=1000, transcendentals=0)


def halo_kernel(where, own, got, near, wide):
    def fill(first, second, to_right, to_left):
        to_right[0:256, :] = second[256:512, :]
        to_right[256:384, :] = pool1(second[0:256, :])
        to_right[384:448, :] = pool2(first[0:256, :])
        to_right[448:512, :] = pool2(first[256:512, :])
        to_left[0:256, :] = first[0:256, :]
        to_left[256:384, :] = pool1(first[256:512, :])
        to_left[384:448, :] = pool2(second[0:256, :])
        to_left[448:512, :] = pool2(second[256:512, :])

    for side in range(2):
        for odd in range(2):

            @pl.when((where[0] == side) & (where[3] == odd))
            def _(side=side, odd=odd):
                halves = (own, got) if side == 0 else (got, own)
                fill(*halves, *((near, wide) if odd == 0 else (wide, near)))


def halo(where, own, got):
    shape = jax.ShapeDtypeStruct(own.shape, BF)
    return pl.pallas_call(
        halo_kernel,
        in_specs=[smem(), vmem(), vmem()],
        out_specs=[vmem(), vmem()],
        out_shape=[shape, shape],
        compiler_params=small(),
        cost_estimate=light(),
    )(where, own, got)


def swap64(x):
    return pltpu.roll(x, 64, 1)


def low_lanes(shape):
    return lax.broadcasted_iota(jnp.int32, shape, 1) < 64


def spread64(x, half):
    other = swap64(x)
    low = low_lanes(x.shape)
    return jnp.where(low, x, other) if half == 0 else jnp.where(low, other, x)


def far_forward(k, v_t, q, bias, p_ref):
    k0, k1, k2, k3 = k
    v0, v1, v2, v3 = v_t
    left, right = bias
    outer = dot_nt(jnp.concatenate([k0, k3], axis=0), q)
    first, last = outer[:BLOCK], outer[BLOCK:]
    mid_low = dot_nt(k2, q[:BLOCK])
    mid_high = dot_nt(k1, q[BLOCK:])
    if left is not None:
        first = first + left
        mid_high = mid_high + left
    if right is not None:
        last = last + right
        mid_low = mid_low + right
    mid = jnp.concatenate([mid_low, mid_high], axis=1)
    peak = jnp.max(jnp.maximum(jnp.maximum(first, last), mid), axis=0, keepdims=True)
    parts = [jnp.exp2((x - peak) * TO_LOG2) for x in (first, last, mid)]
    for n, x in enumerate(parts):
        p_ref[n * BLOCK : (n + 1) * BLOCK, :] = x
    total = jnp.sum(parts[0] + parts[1] + parts[2], axis=0, keepdims=True)
    pb = [x.astype(BF) for x in parts]
    mixed = dot_nn(
        jnp.concatenate([v0, v3], axis=1), jnp.concatenate(pb[:2], axis=0)
    ) + jnp.concatenate([dot_nn(v2, pb[2][:, :BLOCK]), dot_nn(v1, pb[2][:, BLOCK:])], axis=1)
    return peak, total, mixed


def far_backward(k_t, v, q, p_ref, factor, g, ec):
    k0, k1, k2, k3 = k_t
    v0, v1, v2, v3 = v
    e_out = p_ref[: 2 * BLOCK, :] * factor
    e_mid = p_ref[2 * BLOCK :, :] * factor
    eb_out, eb_mid = e_out.astype(BF), e_mid.astype(BF)
    p_out = dot_nt(jnp.concatenate([v0, v3], axis=0), g)
    p_mid = jnp.concatenate([dot_nt(v2, g[:BLOCK]), dot_nt(v1, g[BLOCK:])], axis=1)
    r_out = (e_out * (p_out - ec)).astype(BF)
    r_mid = (e_mid * (p_mid - ec)).astype(BF)
    dv03 = dot_nn(eb_out, g)
    dv2 = dot_nn(eb_mid[:, :BLOCK], g[:BLOCK])
    dv1 = dot_nn(eb_mid[:, BLOCK:], g[BLOCK:])
    dk03 = dot_nn(r_out, q)
    dk2 = dot_nn(r_mid[:, :BLOCK], q[:BLOCK])
    dk1 = dot_nn(r_mid[:, BLOCK:], q[BLOCK:])
    dq_t = dot_nn(jnp.concatenate([k0, k3], axis=1), r_out) + jnp.concatenate(
        [dot_nn(k2, r_mid[:, :BLOCK]), dot_nn(k1, r_mid[:, BLOCK:])], axis=1
    )
    return (dk03[:BLOCK], dk1, dk2, dk03[BLOCK:]), (dv03[:BLOCK], dv1, dv2, dv03[BLOCK:]), dq_t


def main_kernel(
    where, kv_own, kv_got, near_got, wide_got, qg_own, qg_got,
    oq_own, oq_far, grad, near_out, wide_out,
    raw, raw_t, one, one_t, two, two_t, qs, gs, p0, p1, p2, acc0, acc1, acc2, oq, halos,
):
    side = where[0]
    odd = where[3]
    halos[1 - odd] = near_got[...]
    halos[odd] = wide_got[...]
    from_left, from_right = halos.at[0], halos.at[1]
    to_left, to_right = halos.at[0], halos.at[1]
    width = kv_own.shape[1] // 2
    left_bias = (1 - where[1]).astype(F32) * MASKED
    right_bias = (1 - where[2]).astype(F32) * MASKED
    own_at = pl.multiple_of(side * 512, 512)
    got_at = pl.multiple_of((1 - side) * 512, 512)
    for h in range(width // HEAD):
        kc = slice(h * HEAD, (h + 1) * HEAD)
        vc = slice(width + h * HEAD, width + (h + 1) * HEAD)
        for n, cols in ((0, kc), (1, vc)):
            raw[n, 0:256, :] = from_left[0:256, cols]
            raw[n, pl.ds(256 + own_at, 512), :] = kv_own[:, cols]
            raw[n, pl.ds(256 + got_at, 512), :] = kv_got[:, cols]
            raw[n, 1280:1536, :] = from_right[0:256, cols]
            one[n, 0:128, :] = from_left[256:384, cols]
            for i in range(6):
                block = pool1(raw[n, i * PARENT : (i + 1) * PARENT, :])
                at = (i + 1) * BLOCK
                one[n, at : at + BLOCK, :] = block
            one[n, 896:1024, :] = from_right[256:384, cols]
            two[n, 0:128, :] = from_left[384:512, cols]
            two[n, 128:192, :] = pool12(one[n, 0:128, :])
            two[n, 192:256, :] = pool2(raw[n, 0:256, :])
            two[n, 256:320, :] = pool2(raw[n, 1280:1536, :])
            two[n, 320:384, :] = pool12(one[n, 896:1024, :])
            two[n, 384:512, :] = from_right[384:512, cols]
            for i in range(6):
                rows = slice(i * PARENT, (i + 1) * PARENT)
                raw_t[n, :, rows] = raw[n, rows, :].T
            for i in range(8):
                rows = slice(i * BLOCK, (i + 1) * BLOCK)
                one_t[n, :, rows] = one[n, rows, :].T
            for i in range(4):
                rows = slice(i * BLOCK, (i + 1) * BLOCK)
                two_t[n, :, rows] = two[n, rows, :].T
        qs[pl.ds(own_at, 512), :] = qg_own[:, kc]
        qs[pl.ds(got_at, 512), :] = qg_got[:, kc]
        gs[pl.ds(own_at, 512), :] = qg_own[:, vc]
        gs[pl.ds(got_at, 512), :] = qg_got[:, vc]

        def blocks(ref, n, which):
            return [ref[n, b * BLOCK : (b + 1) * BLOCK, :] for b in which]

        def blocks_t(ref, n, which):
            return [ref[n, :, b * BLOCK : (b + 1) * BLOCK] for b in which]

        q_parents = [qs[i * PARENT : (i + 1) * PARENT, :] for i in range(4)]
        q1 = [
            jnp.concatenate([pool1(q_parents[2 * j]), pool1(q_parents[2 * j + 1])], axis=0)
            for j in range(2)
        ]
        q2 = jnp.concatenate([pool2(x) for x in q_parents], axis=0)
        which1 = [(0, 1, 4, 5), (2, 3, 6, 7)]
        bias1 = [(left_bias, None), (None, right_bias)]
        which2 = (0, 1, 2, 3)
        far1 = [
            far_forward(
                blocks(one, 0, which1[j]), blocks_t(one_t, 1, which1[j]), q1[j], bias1[j], p1.at[j]
            )
            for j in range(2)
        ]
        far2 = far_forward(
            blocks(two, 0, which2), blocks_t(two_t, 1, which2), q2, (left_bias, right_bias), p2
        )
        acc0[...] = jnp.zeros_like(acc0)
        g1_t, ec1, f1 = [], [], []
        g2_t, ec2, low2 = [], [], []
        dq0 = []
        for i in range(4):
            rows = slice(i * PARENT, i * PARENT + 3 * PARENT)
            q = q_parents[i]
            g = gs[i * PARENT : (i + 1) * PARENT, :]
            s = dot_nt(raw[0, rows, :], q)
            pieces = [s[:PARENT], s[PARENT : 2 * PARENT], s[2 * PARENT :]]
            if i == 0:
                pieces[0] = pieces[0] + left_bias
            if i == 3:
                pieces[2] = pieces[2] + right_bias
            m0 = jnp.max(
                jnp.maximum(jnp.maximum(pieces[0], pieces[1]), pieces[2]), axis=0, keepdims=True
            )
            e = [jnp.exp2((x - m0) * TO_LOG2) for x in pieces]
            for n in range(3):
                p0[n * PARENT : (n + 1) * PARENT, :] = e[n]
            z0 = jnp.sum(e[0] + e[1] + e[2], axis=0, keepdims=True)
            u0 = dot_nn(raw_t[1, :, rows], jnp.concatenate([x.astype(BF) for x in e], axis=0))
            j, half = i // 2, i % 2
            lanes = slice(half * BLOCK, (half + 1) * BLOCK)
            m1, z1, u1 = (x[:, lanes] for x in far1[j])
            lanes2 = slice(j * BLOCK, (j + 1) * BLOCK)
            m2, z2, u2 = (spread64(x[:, lanes2], half) for x in far2)
            m1w, m2w = twice(m1, 1), twice(m2, 1)
            m = jnp.maximum(jnp.maximum(m0, m1w), m2w)
            a0 = jnp.exp2((m0 - m) * TO_LOG2)
            a1 = 2.0 * jnp.exp2((m1w - m) * TO_LOG2)
            a2 = 4.0 * jnp.exp2((m2w - m) * TO_LOG2)
            z = a0 * z0 + a1 * twice(z1, 1) + a2 * twice(z2, 1)
            inv = 1.0 / z
            o = ((a0 * inv) * u0 + (a1 * inv) * twice(u1, 1) + (a2 * inv) * twice(u2, 1)).astype(BF)
            oq[i, 0, h * HEAD : (h + 1) * HEAD, :] = o
            lg = m * TO_LOG2 + jnp.log2(z)
            g_t = g.astype(F32).T
            dr = jnp.sum(o.astype(F32) * g_t, axis=0, keepdims=True)
            lg_a, lg_b = lg[:, :BLOCK], lg[:, BLOCK:]
            g_a, g_b = g_t[:, :BLOCK], g_t[:, BLOCK:]
            dr_a, dr_b = dr[:, :BLOCK], dr[:, BLOCK:]
            low = jnp.minimum(lg_a, lg_b)
            w_a, w_b = jnp.exp2(low - lg_a), jnp.exp2(low - lg_b)
            g1_t.append((w_a * g_a + w_b * g_b).astype(BF))
            ec1.append(w_a * dr_a + w_b * dr_b)
            f1.append(2.0 * jnp.exp2(m1 * TO_LOG2 - low))
            lower = jnp.minimum(low, swap64(low))
            w_a, w_b = jnp.exp2(lower - lg_a), jnp.exp2(lower - lg_b)
            part = w_a * g_a + w_b * g_b
            g2_t.append(part + swap64(part))
            part = w_a * dr_a + w_b * dr_b
            ec2.append(part + swap64(part))
            low2.append(lower)
            f0 = jnp.exp2(m0 * TO_LOG2 - lg)
            products = dot_nt(raw[1, rows, :], g)
            weights = p0[...] * f0
            eb = weights.astype(BF)
            r = (weights * (products - dr)).astype(BF)
            acc0[1, rows, :] += dot_nn(eb, g)
            acc0[0, rows, :] += dot_nn(r, q)
            dq0.append(dot_nn(raw_t[0, :, rows], r))
        acc1[...] = jnp.zeros_like(acc1)
        dq1 = []
        for j in range(2):
            pair = slice(2 * j, 2 * j + 2)
            g1 = jnp.concatenate([x.astype(F32).T.astype(BF) for x in g1_t[pair]], axis=0)
            dk, dv, dq = far_backward(
                blocks_t(one_t, 0, which1[j]), blocks(one, 1, which1[j]), q1[j], p1.at[j],
                jnp.concatenate(f1[pair], axis=1), g1, jnp.concatenate(ec1[pair], axis=1),
            )
            for n, b in enumerate(which1[j]):
                acc1[0, b * BLOCK : (b + 1) * BLOCK, :] += dk[n]
                acc1[1, b * BLOCK : (b + 1) * BLOCK, :] += dv[n]
            dq1.append(dq)

        def joined(parts):
            return jnp.concatenate(
                [
                    jnp.where(low_lanes(parts[0].shape), parts[2 * j], parts[2 * j + 1])
                    for j in range(2)
                ],
                axis=1,
            )

        g2 = joined(g2_t).T.astype(BF)
        f2 = 4.0 * jnp.exp2(far2[0] * TO_LOG2 - joined(low2))
        dk, dv, dq2 = far_backward(
            blocks_t(two_t, 0, which2), blocks(two, 1, which2), q2, p2, f2, g2, joined(ec2)
        )
        for n in range(4):
            acc2[0, n * BLOCK : (n + 1) * BLOCK, :] = dk[n]
            acc2[1, n * BLOCK : (n + 1) * BLOCK, :] = dv[n]
        for i in range(4):
            j, half = i // 2, i % 2
            d1 = dq1[j][:, half * BLOCK : (half + 1) * BLOCK]
            d2 = spread64(dq2[:, j * BLOCK : (j + 1) * BLOCK], half)
            coarse = 0.5 * d1 + 0.25 * d2
            oq[i, 1, h * HEAD : (h + 1) * HEAD, :] = ((dq0[i] + twice(coarse, 1)) * INV_ROOT).astype(BF)
        for n, cols, scale in ((0, kc, INV_ROOT), (1, vc, 1.0)):
            for i in range(4):
                rows = slice((i + 1) * PARENT, (i + 2) * PARENT)
                coarse = acc1[n, (i + 2) * BLOCK : (i + 3) * BLOCK, :] * (0.5 * scale)
                grad[i * PARENT : (i + 1) * PARENT, cols] = acc0[n, rows, :] * scale + twice(coarse)
            far = acc2[n, 128:256, :] * (0.25 * scale)
            mid = acc1[n, 0:256, :] * (0.5 * scale)
            near = acc0[n, 0:256, :] * scale
            to_left[0:256, cols] = (near + twice(mid[128:] + twice(far[64:]))).astype(BF)
            to_left[256:384, cols] = (mid[:128] + twice(far[:64])).astype(BF)
            to_left[384:512, cols] = (acc2[n, 0:128, :] * (0.25 * scale)).astype(BF)
            far = acc2[n, 256:384, :] * (0.25 * scale)
            mid = acc1[n, 768:1024, :] * (0.5 * scale)
            near = acc0[n, 1280:1536, :] * scale
            to_right[0:256, cols] = (near + twice(mid[:128] + twice(far[:64]))).astype(BF)
            to_right[256:384, cols] = (mid[128:] + twice(far[64:])).astype(BF)
            to_right[384:512, cols] = (acc2[n, 384:512, :] * (0.25 * scale)).astype(BF)
    oq_own[...] = oq[pl.ds(side * 2, 2)]
    oq_far[...] = oq[pl.ds((1 - side) * 2, 2)]
    near_out[...] = halos[1 - odd]
    wide_out[...] = halos[odd]


def main(where, kv_own, kv_got, near_got, wide_got, qg_own, qg_got):
    rows, both = kv_own.shape
    width = both // 2
    oq_shape = jax.ShapeDtypeStruct((2, 2, width, PARENT), BF)
    halo_shape = jax.ShapeDtypeStruct((512, both), BF)
    return pl.pallas_call(
        main_kernel,
        in_specs=[smem()] + [vmem()] * 6,
        out_specs=[vmem()] * 5,
        out_shape=[
            oq_shape,
            oq_shape,
            jax.ShapeDtypeStruct((2 * rows, both), F32),
            halo_shape,
            halo_shape,
        ],
        scratch_shapes=[
            pltpu.VMEM((2, 1536, HEAD), BF),
            pltpu.VMEM((2, HEAD, 1536), BF),
            pltpu.VMEM((2, 1024, HEAD), BF),
            pltpu.VMEM((2, HEAD, 1024), BF),
            pltpu.VMEM((2, 512, HEAD), BF),
            pltpu.VMEM((2, HEAD, 512), BF),
            pltpu.VMEM((1024, HEAD), BF),
            pltpu.VMEM((1024, HEAD), BF),
            pltpu.VMEM((768, PARENT), F32),
            pltpu.VMEM((2, 384, PARENT), F32),
            pltpu.VMEM((384, PARENT), F32),
            pltpu.VMEM((2, 1536, HEAD), F32),
            pltpu.VMEM((2, 1024, HEAD), F32),
            pltpu.VMEM((2, 512, HEAD), F32),
            pltpu.VMEM((4, 2, width, PARENT), BF),
            pltpu.VMEM((2, 512, both), BF),
        ],
        compiler_params=pltpu.CompilerParams(vmem_limit_bytes=24 * 1024 * 1024),
        cost_estimate=light(),
    )(where, kv_own, kv_got, near_got, wide_got, qg_own, qg_got)


def join_kernel(where, grad, near_got, wide_got, own, far):
    def fill(first, second, from_left, from_right):
        def parent(i):
            return grad[i * PARENT : (i + 1) * PARENT, :]

        def part(ref, start, stop):
            return ref[start:stop, :].astype(F32)

        first[0:256, :] = (
            parent(0) + part(from_left, 0, 256) + twice(twice(part(from_right, 384, 448)))
        ).astype(BF)
        first[256:512, :] = (
            parent(1) + twice(part(from_left, 256, 384) + twice(part(from_right, 448, 512)))
        ).astype(BF)
        second[0:256, :] = (
            parent(2) + twice(part(from_right, 256, 384) + twice(part(from_left, 384, 448)))
        ).astype(BF)
        second[256:512, :] = (
            parent(3) + part(from_right, 0, 256) + twice(twice(part(from_left, 448, 512)))
        ).astype(BF)

    for side in range(2):
        for odd in range(2):

            @pl.when((where[0] == side) & (where[3] == odd))
            def _(side=side, odd=odd):
                halves = (own, far) if side == 0 else (far, own)
                fill(*halves, *((wide_got, near_got) if odd == 0 else (near_got, wide_got)))


def join(where, grad, near_got, wide_got):
    shape = jax.ShapeDtypeStruct(near_got.shape, BF)
    return pl.pallas_call(
        join_kernel,
        in_specs=[smem(), vmem(), vmem(), vmem()],
        out_specs=[vmem(), vmem()],
        out_shape=[shape, shape],
        compiler_params=small(),
        cost_estimate=light(),
    )(where, grad, near_got, wide_got)


def unpack_rows_kernel(where, *refs):
    ins, (first, second) = refs[:-2], refs[-2:]
    order = order_matrix(True)
    width = ins[0].shape[1] // 2
    side = where[0]
    blocks = [(side * CHUNKS + c, ins[c]) for c in range(CHUNKS)]
    blocks += [((1 - side) * CHUNKS + 1 - LATE_CHUNK, ins[CHUNKS])]
    for block, ref in blocks:
        at = pl.ds(pl.multiple_of(block * width, width), width)
        for i in range(2):
            rows = slice(i * PARENT, (i + 1) * PARENT)
            first[rows, at] = dot_nn(order, ref[rows, :width]).astype(BF)
            second[rows, at] = dot_nn(order, ref[rows, width:]).astype(BF)


def unpack_rows(where, own, got, shape):
    out = jax.ShapeDtypeStruct(shape, BF)
    return pl.pallas_call(
        unpack_rows_kernel,
        in_specs=[smem()] + [vmem()] * (CHUNKS + 1),
        out_specs=[vmem(), vmem()],
        out_shape=[out, out],
        compiler_params=small(),
        cost_estimate=light(),
    )(where, *own, got)


def unpack_last_kernel(where, got, first_in, second_in, first, second, held, sems):
    del first_in, second_in
    order = order_matrix(True)
    width = got.shape[1] // 2
    block = (1 - where[0]) * CHUNKS + LATE_CHUNK
    at = pl.ds(pl.multiple_of(block * width, width), width)
    copies = []
    for m, ref in enumerate((first, second)):
        for i in range(2):
            rows = slice(i * PARENT, (i + 1) * PARENT)
            held[m, rows, :] = dot_nn(order, got[rows, m * width : (m + 1) * width]).astype(BF)
        copies.append(pltpu.make_async_copy(held.at[m], ref.at[:, at], sems.at[m]))
        copies[-1].start()
    for copy in copies:
        copy.wait()


def unpack_last(where, got, first, second):
    out = jax.ShapeDtypeStruct(first.shape, BF)
    hbm = pl.BlockSpec(memory_space=pltpu.HBM)
    return pl.pallas_call(
        unpack_last_kernel,
        in_specs=[smem(), vmem(), hbm, hbm],
        out_specs=[hbm, hbm],
        out_shape=[out, out],
        input_output_aliases={2: 0, 3: 1},
        scratch_shapes=[
            pltpu.VMEM((2, got.shape[0], got.shape[1] // 2), BF),
            pltpu.SemaphoreType.DMA((2,)),
        ],
        compiler_params=small(),
        cost_estimate=light(),
    )(where, got, first, second)


def unpack_columns_kernel(where, *refs):
    ins, (first, second) = refs[:-2], refs[-2:]
    order = order_matrix(True)
    width = ins[0].shape[2]
    for c in range(CHUNKS):
        for ref, side in ((ins[c], where[0]), (ins[CHUNKS + c], 1 - where[0])):
            at = pl.ds(pl.multiple_of((side * CHUNKS + c) * width, width), width)
            for i in range(2):
                rows = slice(i * PARENT, (i + 1) * PARENT)
                first[rows, at] = dot_nt(order, ref[i, 0]).astype(BF)
                second[rows, at] = dot_nt(order, ref[i, 1]).astype(BF)


def unpack_columns(where, own, got, shape):
    out = jax.ShapeDtypeStruct(shape, BF)
    return pl.pallas_call(
        unpack_columns_kernel,
        in_specs=[smem()] + [vmem()] * (2 * CHUNKS),
        out_specs=[vmem(), vmem()],
        out_shape=[out, out],
        compiler_params=small(),
        cost_estimate=light(),
    )(where, *own, *got)


def on_device(queries, key_matrix, value_matrix, cotangent):
    axes = ("outer", "inner")
    count = lax.axis_size("outer") * lax.axis_size("inner")
    device = lax.axis_index("outer") * lax.axis_size("inner") + lax.axis_index("inner")
    pair = device // 2
    where = jnp.stack([device % 2, pair > 0, pair < count // 2 - 1, pair % 2]).astype(jnp.int32)
    across = [(i, i ^ 1) for i in range(count)]
    near_edges = [(i, i ^ 2) for i in range(count) if i ^ 2 < count]
    wide_edges = [(i, i + 2 if i // 2 % 2 else i - 2) for i in range(count)]
    wide_edges = [(i, j) for i, j in wide_edges if 0 <= j < count]

    def swap(x):
        return lax.ppermute(x, axes, across)

    def beside(near, wide):
        near = lax.ppermute(near, axes, near_edges)
        return near, lax.ppermute(wide, axes, wide_edges)

    kv_far = pack(False, where, key_matrix, value_matrix)
    qg_far = pack(False, where, queries, cotangent)
    packed = pack(True, where, key_matrix, value_matrix, queries, cotangent)
    kv, qg = packed[:CHUNKS], packed[CHUNKS:]
    oq_own, oq_got, back = [], [], []
    for c in range(CHUNKS):
        got_kv = swap(kv_far[c])
        near, wide = halo(where, kv[c], got_kv)
        far = qg_far[c]
        if c > 0:
            near, wide, far = lax.optimization_barrier((near, wide, far))
        near, wide = beside(near, wide)
        own, far, grad, near, wide = main(where, kv[c], got_kv, near, wide, qg[c], swap(far))
        oq_own.append(own)
        oq_got.append(swap(far))
        if c + 1 < CHUNKS:
            oq_got[c], near, wide = lax.optimization_barrier((oq_got[c], near, wide))
        back.append([grad, *beside(near, wide)])
    kv_own, kv_got = [None] * CHUNKS, [None] * CHUNKS
    oq_got[-1], back[-1] = lax.optimization_barrier((oq_got[-1], back[-1]))
    for c in reversed(range(CHUNKS)):
        kv_own[c], far = join(where, *back[c])
        kv_got[c] = swap(far)
    attended, query_grad = unpack_columns(where, oq_own, oq_got, queries.shape)
    key_grad, value_grad = unpack_rows(where, kv_own, kv_got[1 - LATE_CHUNK], queries.shape)
    key_grad, value_grad = unpack_last(where, kv_got[LATE_CHUNK], key_grad, value_grad)
    return attended, query_grad, key_grad, value_grad


def solution(mesh):
    spec = P(("outer", "inner"), None)
    return jax.shard_map(
        on_device,
        mesh=mesh,
        in_specs=(spec,) * 4,
        out_specs=(spec,) * 4,
        check_vma=False,
    )
```

```python
import functools
import math

import jax
import jax.numpy as jnp
from jax import lax
from jax.experimental import pallas as pl
from jax.experimental.pallas import tpu as pltpu
from jax.sharding import PartitionSpec as P

HEAD = 128
BLOCK = 128
PARENT = 256
LEVELS = 3
CHUNKS = 2
LATE_CHUNK = 1
INV_ROOT = HEAD**-0.5
TO_LOG2 = INV_ROOT * math.log2(math.e)
MASKED = -1e30
BF = jnp.bfloat16
F32 = jnp.float32


def dot_nt(a, b):
    return lax.dot_general(a, b, (((1,), (1,)), ((), ())), preferred_element_type=F32)


def dot_nn(a, b):
    return jnp.dot(a, b, preferred_element_type=F32)


def order_matrix(inverse):
    row = lax.broadcasted_iota(jnp.int32, (PARENT, PARENT), 0)
    col = lax.broadcasted_iota(jnp.int32, (PARENT, PARENT), 1)
    place, token = (col, row) if inverse else (row, col)
    slab = place // 64
    source = 4 * (place % 64) + 2 * (slab % 2) + slab // 2
    return jnp.where(source == token, 1.0, 0.0).astype(BF)


def pool1(x):
    return ((x[:BLOCK].astype(F32) + x[BLOCK:].astype(F32)) * 0.5).astype(BF)


def pool2(x):
    half = x[:BLOCK].astype(F32) + x[BLOCK:].astype(F32)
    return ((half[:64] + half[64:]) * 0.25).astype(BF)


def pool12(x):
    return ((x[:64].astype(F32) + x[64:].astype(F32)) * 0.5).astype(BF)


def twice(x, axis=0):
    return jnp.concatenate([x, x], axis=axis)


def pack_kernel(own, where, *refs):
    count = 4 if own else 2
    arrays, outs, (held, sems) = refs[:count], refs[count:-2], refs[-2:]
    rows, columns = arrays[0].shape
    half = columns // 2
    width = half // CHUNKS
    side = where[0] if own else 1 - where[0]
    at = pl.ds(pl.multiple_of(side * half, half), half)
    copies = [
        pltpu.make_async_copy(ref.at[:, at], held.at[m], sems.at[m]) for m, ref in enumerate(arrays)
    ]
    for copy in copies:
        copy.start()
    order = order_matrix(False)
    for m in range(count):
        copies[m].wait()
        first = m % 2 * width
        for i in range(rows // PARENT):
            at = slice(i * PARENT, (i + 1) * PARENT)
            x = dot_nn(order, held[m, at, :]).astype(BF)
            for c in range(CHUNKS):
                out = outs[m // 2 * CHUNKS + c]
                out[at, first : first + width] = x[:, c * width : (c + 1) * width]


def pack(own, where, *arrays):
    rows, columns = arrays[0].shape
    count = len(arrays)
    return pl.pallas_call(
        functools.partial(pack_kernel, own),
        in_specs=[smem()] + [pl.BlockSpec(memory_space=pltpu.HBM)] * count,
        out_specs=[vmem()] * (count // 2 * CHUNKS),
        out_shape=[jax.ShapeDtypeStruct((rows, columns // CHUNKS), BF)] * (count // 2 * CHUNKS),
        scratch_shapes=[
            pltpu.VMEM((count, rows, columns // 2), BF),
            pltpu.SemaphoreType.DMA((count,)),
        ],
        compiler_params=small(),
        cost_estimate=light(),
    )(where, *arrays)


def smem():
    return pl.BlockSpec(memory_space=pltpu.SMEM)


def vmem():
    return pl.BlockSpec(memory_space=pltpu.VMEM)


def small():
    return pltpu.CompilerParams(vmem_limit_bytes=8 * 1024 * 1024)


def light():
    return pl.CostEstimate(flops=1000, bytes_accessed=1000, transcendentals=0)


def halo_kernel(where, own, got, near, wide):
    def fill(first, second, to_right, to_left):
        to_right[0:256, :] = second[256:512, :]
        to_right[256:384, :] = pool1(second[0:256, :])
        to_right[384:448, :] = pool2(first[0:256, :])
        to_right[448:512, :] = pool2(first[256:512, :])
        to_left[0:256, :] = first[0:256, :]
        to_left[256:384, :] = pool1(first[256:512, :])
        to_left[384:448, :] = pool2(second[0:256, :])
        to_left[448:512, :] = pool2(second[256:512, :])

    for side in range(2):
        for odd in range(2):

            @pl.when((where[0] == side) & (where[3] == odd))
            def _(side=side, odd=odd):
                halves = (own, got) if side == 0 else (got, own)
                fill(*halves, *((near, wide) if odd == 0 else (wide, near)))


def halo(where, own, got):
    shape = jax.ShapeDtypeStruct(own.shape, BF)
    return pl.pallas_call(
        halo_kernel,
        in_specs=[smem(), vmem(), vmem()],
        out_specs=[vmem(), vmem()],
        out_shape=[shape, shape],
        compiler_params=small(),
        cost_estimate=light(),
    )(where, own, got)


def swap64(x):
    return pltpu.roll(x, 64, 1)


def low_lanes(shape):
    return lax.broadcasted_iota(jnp.int32, shape, 1) < 64


def spread64(x, half):
    other = swap64(x)
    low = low_lanes(x.shape)
    return jnp.where(low, x, other) if half == 0 else jnp.where(low, other, x)


def far_forward(k, v_t, q, bias, p_ref):
    k0, k1, k2, k3 = k
    v0, v1, v2, v3 = v_t
    left, right = bias
    outer = dot_nt(jnp.concatenate([k0, k3], axis=0), q)
    first, last = outer[:BLOCK], outer[BLOCK:]
    mid_low = dot_nt(k2, q[:BLOCK])
    mid_high = dot_nt(k1, q[BLOCK:])
    if left is not None:
        first = first + left
        mid_high = mid_high + left
    if right is not None:
        last = last + right
        mid_low = mid_low + right
    mid = jnp.concatenate([mid_low, mid_high], axis=1)
    peak = jnp.max(jnp.maximum(jnp.maximum(first, last), mid), axis=0, keepdims=True)
    parts = [jnp.exp2((x - peak) * TO_LOG2) for x in (first, last, mid)]
    for n, x in enumerate(parts):
        p_ref[n * BLOCK : (n + 1) * BLOCK, :] = x
    total = jnp.sum(parts[0] + parts[1] + parts[2], axis=0, keepdims=True)
    pb = [x.astype(BF) for x in parts]
    mixed = dot_nn(
        jnp.concatenate([v0, v3], axis=1), jnp.concatenate(pb[:2], axis=0)
    ) + jnp.concatenate([dot_nn(v2, pb[2][:, :BLOCK]), dot_nn(v1, pb[2][:, BLOCK:])], axis=1)
    return peak, total, mixed


def far_backward(k_t, v, q, p_ref, factor, g, ec):
    k0, k1, k2, k3 = k_t
    v0, v1, v2, v3 = v
    e_out = p_ref[: 2 * BLOCK, :] * factor
    e_mid = p_ref[2 * BLOCK :, :] * factor
    eb_out, eb_mid = e_out.astype(BF), e_mid.astype(BF)
    p_out = dot_nt(jnp.concatenate([v0, v3], axis=0), g)
    p_mid = jnp.concatenate([dot_nt(v2, g[:BLOCK]), dot_nt(v1, g[BLOCK:])], axis=1)
    r_out = (e_out * (p_out - ec)).astype(BF)
    r_mid = (e_mid * (p_mid - ec)).astype(BF)
    dv03 = dot_nn(eb_out, g)
    dv2 = dot_nn(eb_mid[:, :BLOCK], g[:BLOCK])
    dv1 = dot_nn(eb_mid[:, BLOCK:], g[BLOCK:])
    dk03 = dot_nn(r_out, q)
    dk2 = dot_nn(r_mid[:, :BLOCK], q[:BLOCK])
    dk1 = dot_nn(r_mid[:, BLOCK:], q[BLOCK:])
    dq_t = dot_nn(jnp.concatenate([k0, k3], axis=1), r_out) + jnp.concatenate(
        [dot_nn(k2, r_mid[:, :BLOCK]), dot_nn(k1, r_mid[:, BLOCK:])], axis=1
    )
    return (dk03[:BLOCK], dk1, dk2, dk03[BLOCK:]), (dv03[:BLOCK], dv1, dv2, dv03[BLOCK:]), dq_t


def main_kernel(
    where, kv_own, kv_got, near_got, wide_got, qg_own, qg_got,
    oq_own, oq_far, grad, near_out, wide_out,
    raw, raw_t, one, one_t, two, two_t, qs, gs, p0, p1, p2, acc0, acc1, acc2, oq, halos,
):
    side = where[0]
    odd = where[3]
    halos[1 - odd] = near_got[...]
    halos[odd] = wide_got[...]
    from_left, from_right = halos.at[0], halos.at[1]
    to_left, to_right = halos.at[0], halos.at[1]
    width = kv_own.shape[1] // 2
    left_bias = (1 - where[1]).astype(F32) * MASKED
    right_bias = (1 - where[2]).astype(F32) * MASKED
    own_at = pl.multiple_of(side * 512, 512)
    got_at = pl.multiple_of((1 - side) * 512, 512)
    for h in range(width // HEAD):
        kc = slice(h * HEAD, (h + 1) * HEAD)
        vc = slice(width + h * HEAD, width + (h + 1) * HEAD)
        for n, cols in ((0, kc), (1, vc)):
            raw[n, 0:256, :] = from_left[0:256, cols]
            raw[n, pl.ds(256 + own_at, 512), :] = kv_own[:, cols]
            raw[n, pl.ds(256 + got_at, 512), :] = kv_got[:, cols]
            raw[n, 1280:1536, :] = from_right[0:256, cols]
            one[n, 0:128, :] = from_left[256:384, cols]
            for i in range(6):
                block = pool1(raw[n, i * PARENT : (i + 1) * PARENT, :])
                at = (i + 1) * BLOCK
                one[n, at : at + BLOCK, :] = block
            one[n, 896:1024, :] = from_right[256:384, cols]
            two[n, 0:128, :] = from_left[384:512, cols]
            two[n, 128:192, :] = pool12(one[n, 0:128, :])
            two[n, 192:256, :] = pool2(raw[n, 0:256, :])
            two[n, 256:320, :] = pool2(raw[n, 1280:1536, :])
            two[n, 320:384, :] = pool12(one[n, 896:1024, :])
            two[n, 384:512, :] = from_right[384:512, cols]
            for i in range(6):
                rows = slice(i * PARENT, (i + 1) * PARENT)
                raw_t[n, :, rows] = raw[n, rows, :].T
            for i in range(8):
                rows = slice(i * BLOCK, (i + 1) * BLOCK)
                one_t[n, :, rows] = one[n, rows, :].T
            for i in range(4):
                rows = slice(i * BLOCK, (i + 1) * BLOCK)
                two_t[n, :, rows] = two[n, rows, :].T
        qs[pl.ds(own_at, 512), :] = qg_own[:, kc]
        qs[pl.ds(got_at, 512), :] = qg_got[:, kc]
        gs[pl.ds(own_at, 512), :] = qg_own[:, vc]
        gs[pl.ds(got_at, 512), :] = qg_got[:, vc]

        def blocks(ref, n, which):
            return [ref[n, b * BLOCK : (b + 1) * BLOCK, :] for b in which]

        def blocks_t(ref, n, which):
            return [ref[n, :, b * BLOCK : (b + 1) * BLOCK] for b in which]

        q_parents = [qs[i * PARENT : (i + 1) * PARENT, :] for i in range(4)]
        q1 = [
            jnp.concatenate([pool1(q_parents[2 * j]), pool1(q_parents[2 * j + 1])], axis=0)
            for j in range(2)
        ]
        q2 = jnp.concatenate([pool2(x) for x in q_parents], axis=0)
        which1 = [(0, 1, 4, 5), (2, 3, 6, 7)]
        bias1 = [(left_bias, None), (None, right_bias)]
        which2 = (0, 1, 2, 3)
        far1 = [
            far_forward(
                blocks(one, 0, which1[j]), blocks_t(one_t, 1, which1[j]), q1[j], bias1[j], p1.at[j]
            )
            for j in range(2)
        ]
        far2 = far_forward(
            blocks(two, 0, which2), blocks_t(two_t, 1, which2), q2, (left_bias, right_bias), p2
        )
        acc0[...] = jnp.zeros_like(acc0)
        g1_t, ec1, f1 = [], [], []
        g2_t, ec2, low2 = [], [], []
        dq0 = []
        for i in range(4):
            rows = slice(i * PARENT, i * PARENT + 3 * PARENT)
            q = q_parents[i]
            g = gs[i * PARENT : (i + 1) * PARENT, :]
            s = dot_nt(raw[0, rows, :], q)
            pieces = [s[:PARENT], s[PARENT : 2 * PARENT], s[2 * PARENT :]]
            if i == 0:
                pieces[0] = pieces[0] + left_bias
            if i == 3:
                pieces[2] = pieces[2] + right_bias
            m0 = jnp.max(
                jnp.maximum(jnp.maximum(pieces[0], pieces[1]), pieces[2]), axis=0, keepdims=True
            )
            e = [jnp.exp2((x - m0) * TO_LOG2) for x in pieces]
            for n in range(3):
                p0[n * PARENT : (n + 1) * PARENT, :] = e[n]
            z0 = jnp.sum(e[0] + e[1] + e[2], axis=0, keepdims=True)
            u0 = dot_nn(raw_t[1, :, rows], jnp.concatenate([x.astype(BF) for x in e], axis=0))
            j, half = i // 2, i % 2
            lanes = slice(half * BLOCK, (half + 1) * BLOCK)
            m1, z1, u1 = (x[:, lanes] for x in far1[j])
            lanes2 = slice(j * BLOCK, (j + 1) * BLOCK)
            m2, z2, u2 = (spread64(x[:, lanes2], half) for x in far2)
            m1w, m2w = twice(m1, 1), twice(m2, 1)
            m = jnp.maximum(jnp.maximum(m0, m1w), m2w)
            a0 = jnp.exp2((m0 - m) * TO_LOG2)
            a1 = 2.0 * jnp.exp2((m1w - m) * TO_LOG2)
            a2 = 4.0 * jnp.exp2((m2w - m) * TO_LOG2)
            z = a0 * z0 + a1 * twice(z1, 1) + a2 * twice(z2, 1)
            inv = 1.0 / z
            o = ((a0 * inv) * u0 + (a1 * inv) * twice(u1, 1) + (a2 * inv) * twice(u2, 1)).astype(BF)
            oq[i, 0, h * HEAD : (h + 1) * HEAD, :] = o
            lg = m * TO_LOG2 + jnp.log2(z)
            g_t = g.astype(F32).T
            dr = jnp.sum(o.astype(F32) * g_t, axis=0, keepdims=True)
            lg_a, lg_b = lg[:, :BLOCK], lg[:, BLOCK:]
            g_a, g_b = g_t[:, :BLOCK], g_t[:, BLOCK:]
            dr_a, dr_b = dr[:, :BLOCK], dr[:, BLOCK:]
            low = jnp.minimum(lg_a, lg_b)
            w_a, w_b = jnp.exp2(low - lg_a), jnp.exp2(low - lg_b)
            g1_t.append((w_a * g_a + w_b * g_b).astype(BF))
            ec1.append(w_a * dr_a + w_b * dr_b)
            f1.append(2.0 * jnp.exp2(m1 * TO_LOG2 - low))
            lower = jnp.minimum(low, swap64(low))
            w_a, w_b = jnp.exp2(lower - lg_a), jnp.exp2(lower - lg_b)
            part = w_a * g_a + w_b * g_b
            g2_t.append(part + swap64(part))
            part = w_a * dr_a + w_b * dr_b
            ec2.append(part + swap64(part))
            low2.append(lower)
            f0 = jnp.exp2(m0 * TO_LOG2 - lg)
            products = dot_nt(raw[1, rows, :], g)
            weights = p0[...] * f0
            eb = weights.astype(BF)
            r = (weights * (products - dr)).astype(BF)
            acc0[1, rows, :] += dot_nn(eb, g)
            acc0[0, rows, :] += dot_nn(r, q)
            dq0.append(dot_nn(raw_t[0, :, rows], r))
        acc1[...] = jnp.zeros_like(acc1)
        dq1 = []
        for j in range(2):
            pair = slice(2 * j, 2 * j + 2)
            g1 = jnp.concatenate([x.astype(F32).T.astype(BF) for x in g1_t[pair]], axis=0)
            dk, dv, dq = far_backward(
                blocks_t(one_t, 0, which1[j]), blocks(one, 1, which1[j]), q1[j], p1.at[j],
                jnp.concatenate(f1[pair], axis=1), g1, jnp.concatenate(ec1[pair], axis=1),
            )
            for n, b in enumerate(which1[j]):
                acc1[0, b * BLOCK : (b + 1) * BLOCK, :] += dk[n]
                acc1[1, b * BLOCK : (b + 1) * BLOCK, :] += dv[n]
            dq1.append(dq)

        def joined(parts):
            return jnp.concatenate(
                [
                    jnp.where(low_lanes(parts[0].shape), parts[2 * j], parts[2 * j + 1])
                    for j in range(2)
                ],
                axis=1,
            )

        g2 = joined(g2_t).T.astype(BF)
        f2 = 4.0 * jnp.exp2(far2[0] * TO_LOG2 - joined(low2))
        dk, dv, dq2 = far_backward(
            blocks_t(two_t, 0, which2), blocks(two, 1, which2), q2, p2, f2, g2, joined(ec2)
        )
        for n in range(4):
            acc2[0, n * BLOCK : (n + 1) * BLOCK, :] = dk[n]
            acc2[1, n * BLOCK : (n + 1) * BLOCK, :] = dv[n]
        for i in range(4):
            j, half = i // 2, i % 2
            d1 = dq1[j][:, half * BLOCK : (half + 1) * BLOCK]
            d2 = spread64(dq2[:, j * BLOCK : (j + 1) * BLOCK], half)
            coarse = 0.5 * d1 + 0.25 * d2
            oq[i, 1, h * HEAD : (h + 1) * HEAD, :] = ((dq0[i] + twice(coarse, 1)) * INV_ROOT).astype(BF)
        for n, cols, scale in ((0, kc, INV_ROOT), (1, vc, 1.0)):
            for i in range(4):
                rows = slice((i + 1) * PARENT, (i + 2) * PARENT)
                coarse = acc1[n, (i + 2) * BLOCK : (i + 3) * BLOCK, :] * (0.5 * scale)
                grad[i * PARENT : (i + 1) * PARENT, cols] = acc0[n, rows, :] * scale + twice(coarse)
            far = acc2[n, 128:256, :] * (0.25 * scale)
            mid = acc1[n, 0:256, :] * (0.5 * scale)
            near = acc0[n, 0:256, :] * scale
            to_left[0:256, cols] = (near + twice(mid[128:] + twice(far[64:]))).astype(BF)
            to_left[256:384, cols] = (mid[:128] + twice(far[:64])).astype(BF)
            to_left[384:512, cols] = (acc2[n, 0:128, :] * (0.25 * scale)).astype(BF)
            far = acc2[n, 256:384, :] * (0.25 * scale)
            mid = acc1[n, 768:1024, :] * (0.5 * scale)
            near = acc0[n, 1280:1536, :] * scale
            to_right[0:256, cols] = (near + twice(mid[:128] + twice(far[:64]))).astype(BF)
            to_right[256:384, cols] = (mid[128:] + twice(far[64:])).astype(BF)
            to_right[384:512, cols] = (acc2[n, 384:512, :] * (0.25 * scale)).astype(BF)
    oq_own[...] = oq[pl.ds(side * 2, 2)]
    oq_far[...] = oq[pl.ds((1 - side) * 2, 2)]
    near_out[...] = halos[1 - odd]
    wide_out[...] = halos[odd]


def main(where, kv_own, kv_got, near_got, wide_got, qg_own, qg_got):
    rows, both = kv_own.shape
    width = both // 2
    oq_shape = jax.ShapeDtypeStruct((2, 2, width, PARENT), BF)
    halo_shape = jax.ShapeDtypeStruct((512, both), BF)
    return pl.pallas_call(
        main_kernel,
        in_specs=[smem()] + [vmem()] * 6,
        out_specs=[vmem()] * 5,
        out_shape=[
            oq_shape,
            oq_shape,
            jax.ShapeDtypeStruct((2 * rows, both), F32),
            halo_shape,
            halo_shape,
        ],
        scratch_shapes=[
            pltpu.VMEM((2, 1536, HEAD), BF),
            pltpu.VMEM((2, HEAD, 1536), BF),
            pltpu.VMEM((2, 1024, HEAD), BF),
            pltpu.VMEM((2, HEAD, 1024), BF),
            pltpu.VMEM((2, 512, HEAD), BF),
            pltpu.VMEM((2, HEAD, 512), BF),
            pltpu.VMEM((1024, HEAD), BF),
            pltpu.VMEM((1024, HEAD), BF),
            pltpu.VMEM((768, PARENT), F32),
            pltpu.VMEM((2, 384, PARENT), F32),
            pltpu.VMEM((384, PARENT), F32),
            pltpu.VMEM((2, 1536, HEAD), F32),
            pltpu.VMEM((2, 1024, HEAD), F32),
            pltpu.VMEM((2, 512, HEAD), F32),
            pltpu.VMEM((4, 2, width, PARENT), BF),
            pltpu.VMEM((2, 512, both), BF),
        ],
        compiler_params=pltpu.CompilerParams(vmem_limit_bytes=24 * 1024 * 1024),
        cost_estimate=light(),
    )(where, kv_own, kv_got, near_got, wide_got, qg_own, qg_got)


def join_kernel(where, grad, near_got, wide_got, own, far):
    def fill(first, second, from_left, from_right):
        def parent(i):
            return grad[i * PARENT : (i + 1) * PARENT, :]

        def part(ref, start, stop):
            return ref[start:stop, :].astype(F32)

        first[0:256, :] = (
            parent(0) + part(from_left, 0, 256) + twice(twice(part(from_right, 384, 448)))
        ).astype(BF)
        first[256:512, :] = (
            parent(1) + twice(part(from_left, 256, 384) + twice(part(from_right, 448, 512)))
        ).astype(BF)
        second[0:256, :] = (
            parent(2) + twice(part(from_right, 256, 384) + twice(part(from_left, 384, 448)))
        ).astype(BF)
        second[256:512, :] = (
            parent(3) + part(from_right, 0, 256) + twice(twice(part(from_left, 448, 512)))
        ).astype(BF)

    for side in range(2):
        for odd in range(2):

            @pl.when((where[0] == side) & (where[3] == odd))
            def _(side=side, odd=odd):
                halves = (own, far) if side == 0 else (far, own)
                fill(*halves, *((wide_got, near_got) if odd == 0 else (near_got, wide_got)))


def join(where, grad, near_got, wide_got):
    shape = jax.ShapeDtypeStruct(near_got.shape, BF)
    return pl.pallas_call(
        join_kernel,
        in_specs=[smem(), vmem(), vmem(), vmem()],
        out_specs=[vmem(), vmem()],
        out_shape=[shape, shape],
        compiler_params=small(),
        cost_estimate=light(),
    )(where, grad, near_got, wide_got)


def unpack_rows_kernel(where, *refs):
    ins, (first, second) = refs[:-2], refs[-2:]
    order = order_matrix(True)
    width = ins[0].shape[1] // 2
    side = where[0]
    blocks = [(side * CHUNKS + c, ins[c]) for c in range(CHUNKS)]
    blocks += [((1 - side) * CHUNKS + 1 - LATE_CHUNK, ins[CHUNKS])]
    for block, ref in blocks:
        at = pl.ds(pl.multiple_of(block * width, width), width)
        for i in range(2):
            rows = slice(i * PARENT, (i + 1) * PARENT)
            first[rows, at] = dot_nn(order, ref[rows, :width]).astype(BF)
            second[rows, at] = dot_nn(order, ref[rows, width:]).astype(BF)


def unpack_rows(where, own, got, shape):
    out = jax.ShapeDtypeStruct(shape, BF)
    return pl.pallas_call(
        unpack_rows_kernel,
        in_specs=[smem()] + [vmem()] * (CHUNKS + 1),
        out_specs=[vmem(), vmem()],
        out_shape=[out, out],
        compiler_params=small(),
        cost_estimate=light(),
    )(where, *own, got)


def unpack_last_kernel(where, got, first_in, second_in, first, second, held, sems):
    del first_in, second_in
    order = order_matrix(True)
    width = got.shape[1] // 2
    block = (1 - where[0]) * CHUNKS + LATE_CHUNK
    at = pl.ds(pl.multiple_of(block * width, width), width)
    copies = []
    for m, ref in enumerate((first, second)):
        for i in range(2):
            rows = slice(i * PARENT, (i + 1) * PARENT)
            held[m, rows, :] = dot_nn(order, got[rows, m * width : (m + 1) * width]).astype(BF)
        copies.append(pltpu.make_async_copy(held.at[m], ref.at[:, at], sems.at[m]))
        copies[-1].start()
    for copy in copies:
        copy.wait()


def unpack_last(where, got, first, second):
    out = jax.ShapeDtypeStruct(first.shape, BF)
    hbm = pl.BlockSpec(memory_space=pltpu.HBM)
    return pl.pallas_call(
        unpack_last_kernel,
        in_specs=[smem(), vmem(), hbm, hbm],
        out_specs=[hbm, hbm],
        out_shape=[out, out],
        input_output_aliases={2: 0, 3: 1},
        scratch_shapes=[
            pltpu.VMEM((2, got.shape[0], got.shape[1] // 2), BF),
            pltpu.SemaphoreType.DMA((2,)),
        ],
        compiler_params=small(),
        cost_estimate=light(),
    )(where, got, first, second)


def unpack_columns_kernel(where, *refs):
    ins, (first, second) = refs[:-2], refs[-2:]
    order = order_matrix(True)
    width = ins[0].shape[2]
    for c in range(CHUNKS):
        for ref, side in ((ins[c], where[0]), (ins[CHUNKS + c], 1 - where[0])):
            at = pl.ds(pl.multiple_of((side * CHUNKS + c) * width, width), width)
            for i in range(2):
                rows = slice(i * PARENT, (i + 1) * PARENT)
                first[rows, at] = dot_nt(order, ref[i, 0]).astype(BF)
                second[rows, at] = dot_nt(order, ref[i, 1]).astype(BF)


def unpack_columns(where, own, got, shape):
    out = jax.ShapeDtypeStruct(shape, BF)
    return pl.pallas_call(
        unpack_columns_kernel,
        in_specs=[smem()] + [vmem()] * (2 * CHUNKS),
        out_specs=[vmem(), vmem()],
        out_shape=[out, out],
        compiler_params=small(),
        cost_estimate=light(),
    )(where, *own, *got)


def on_device(queries, key_matrix, value_matrix, cotangent):
    axes = ("outer", "inner")
    count = lax.axis_size("outer") * lax.axis_size("inner")
    device = lax.axis_index("outer") * lax.axis_size("inner") + lax.axis_index("inner")
    pair = device // 2
    where = jnp.stack([device % 2, pair > 0, pair < count // 2 - 1, pair % 2]).astype(jnp.int32)
    across = [(i, i ^ 1) for i in range(count)]
    near_edges = [(i, i ^ 2) for i in range(count) if i ^ 2 < count]
    wide_edges = [(i, i + 2 if i // 2 % 2 else i - 2) for i in range(count)]
    wide_edges = [(i, j) for i, j in wide_edges if 0 <= j < count]

    def swap(x):
        return lax.ppermute(x, axes, across)

    def beside(near, wide):
        near = lax.ppermute(near, axes, near_edges)
        return near, lax.ppermute(wide, axes, wide_edges)

    kv_far = pack(False, where, key_matrix, value_matrix)
    qg_far = pack(False, where, queries, cotangent)
    packed = pack(True, where, key_matrix, value_matrix, queries, cotangent)
    kv, qg = packed[:CHUNKS], packed[CHUNKS:]
    oq_own, oq_got, back = [], [], []
    for c in range(CHUNKS):
        got_kv = swap(kv_far[c])
        near, wide = halo(where, kv[c], got_kv)
        far = qg_far[c]
        if c > 0:
            near, wide, far = lax.optimization_barrier((near, wide, far))
        near, wide = beside(near, wide)
        own, far, grad, near, wide = main(where, kv[c], got_kv, near, wide, qg[c], swap(far))
        oq_own.append(own)
        oq_got.append(swap(far))
        if c > 0:
            oq_got[c - 1], near, wide = lax.optimization_barrier((oq_got[c - 1], near, wide))
        back.append([grad, *beside(near, wide)])
    oq_got[-1], back[-1] = lax.optimization_barrier((oq_got[-1], back[-1]))
    kv_own, kv_got = [], []
    for c in range(CHUNKS):
        own, far = join(where, *back[c])
        kv_own.append(own)
        kv_got.append(swap(far))
    attended, query_grad = unpack_columns(where, oq_own, oq_got, queries.shape)
    key_grad, value_grad = unpack_rows(where, kv_own, kv_got[1 - LATE_CHUNK], queries.shape)
    key_grad, value_grad = unpack_last(where, kv_got[LATE_CHUNK], key_grad, value_grad)
    return attended, query_grad, key_grad, value_grad


def solution(mesh):
    spec = P(("outer", "inner"), None)
    return jax.shard_map(
        on_device,
        mesh=mesh,
        in_specs=(spec,) * 4,
        out_specs=(spec,) * 4,
        check_vma=False,
    )
```

```python
import functools
import math

import jax
import jax.numpy as jnp
from jax import lax
from jax.experimental import pallas as pl
from jax.experimental.pallas import tpu as pltpu
from jax.sharding import PartitionSpec as P

HEAD = 128
BLOCK = 128
PARENT = 256
LEVELS = 3
CHUNKS = 2
LATE_CHUNK = 1
INV_ROOT = HEAD**-0.5
TO_LOG2 = INV_ROOT * math.log2(math.e)
MASKED = -1e30
BF = jnp.bfloat16
F32 = jnp.float32


def dot_nt(a, b):
    return lax.dot_general(a, b, (((1,), (1,)), ((), ())), preferred_element_type=F32)


def dot_nn(a, b):
    return jnp.dot(a, b, preferred_element_type=F32)


def order_matrix(inverse):
    row = lax.broadcasted_iota(jnp.int32, (PARENT, PARENT), 0)
    col = lax.broadcasted_iota(jnp.int32, (PARENT, PARENT), 1)
    place, token = (col, row) if inverse else (row, col)
    slab = place // 64
    source = 4 * (place % 64) + 2 * (slab % 2) + slab // 2
    return jnp.where(source == token, 1.0, 0.0).astype(BF)


def pool1(x):
    return ((x[:BLOCK].astype(F32) + x[BLOCK:].astype(F32)) * 0.5).astype(BF)


def pool2(x):
    half = x[:BLOCK].astype(F32) + x[BLOCK:].astype(F32)
    return ((half[:64] + half[64:]) * 0.25).astype(BF)


def pool12(x):
    return ((x[:64].astype(F32) + x[64:].astype(F32)) * 0.5).astype(BF)


def twice(x, axis=0):
    return jnp.concatenate([x, x], axis=axis)


def pack_kernel(own, where, *refs):
    count = 4 if own else 2
    arrays, outs, (held, sems) = refs[:count], refs[count:-2], refs[-2:]
    rows, columns = arrays[0].shape
    half = columns // 2
    width = half // CHUNKS
    side = where[0] if own else 1 - where[0]
    at = pl.ds(pl.multiple_of(side * half, half), half)
    copies = [
        pltpu.make_async_copy(ref.at[:, at], held.at[m], sems.at[m]) for m, ref in enumerate(arrays)
    ]
    for copy in copies:
        copy.start()
    order = order_matrix(False)
    for m in range(count):
        copies[m].wait()
        first = m % 2 * width
        for i in range(rows // PARENT):
            at = slice(i * PARENT, (i + 1) * PARENT)
            x = dot_nn(order, held[m, at, :]).astype(BF)
            for c in range(CHUNKS):
                out = outs[m // 2 * CHUNKS + c]
                out[at, first : first + width] = x[:, c * width : (c + 1) * width]


def pack(own, where, *arrays, limit=8):
    rows, columns = arrays[0].shape
    count = len(arrays)
    return pl.pallas_call(
        functools.partial(pack_kernel, own),
        in_specs=[smem()] + [pl.BlockSpec(memory_space=pltpu.HBM)] * count,
        out_specs=[vmem()] * (count // 2 * CHUNKS),
        out_shape=[jax.ShapeDtypeStruct((rows, columns // CHUNKS), BF)] * (count // 2 * CHUNKS),
        scratch_shapes=[
            pltpu.VMEM((count, rows, columns // 2), BF),
            pltpu.SemaphoreType.DMA((count,)),
        ],
        compiler_params=pltpu.CompilerParams(vmem_limit_bytes=limit * 1024 * 1024),
        cost_estimate=light(),
    )(where, *arrays)


def smem():
    return pl.BlockSpec(memory_space=pltpu.SMEM)


def vmem():
    return pl.BlockSpec(memory_space=pltpu.VMEM)


def small():
    return pltpu.CompilerParams(vmem_limit_bytes=8 * 1024 * 1024)


def light():
    return pl.CostEstimate(flops=1000, bytes_accessed=1000, transcendentals=0)


def halo_kernel(where, own, got, near, wide):
    def fill(first, second, to_right, to_left):
        to_right[0:256, :] = second[256:512, :]
        to_right[256:384, :] = pool1(second[0:256, :])
        to_right[384:448, :] = pool2(first[0:256, :])
        to_right[448:512, :] = pool2(first[256:512, :])
        to_left[0:256, :] = first[0:256, :]
        to_left[256:384, :] = pool1(first[256:512, :])
        to_left[384:448, :] = pool2(second[0:256, :])
        to_left[448:512, :] = pool2(second[256:512, :])

    for side in range(2):
        for odd in range(2):

            @pl.when((where[0] == side) & (where[3] == odd))
            def _(side=side, odd=odd):
                halves = (own, got) if side == 0 else (got, own)
                fill(*halves, *((near, wide) if odd == 0 else (wide, near)))


def halo(where, own, got):
    shape = jax.ShapeDtypeStruct(own.shape, BF)
    return pl.pallas_call(
        halo_kernel,
        in_specs=[smem(), vmem(), vmem()],
        out_specs=[vmem(), vmem()],
        out_shape=[shape, shape],
        compiler_params=small(),
        cost_estimate=light(),
    )(where, own, got)


def swap64(x):
    return pltpu.roll(x, 64, 1)


def low_lanes(shape):
    return lax.broadcasted_iota(jnp.int32, shape, 1) < 64


def spread64(x, half):
    other = swap64(x)
    low = low_lanes(x.shape)
    return jnp.where(low, x, other) if half == 0 else jnp.where(low, other, x)


def far_forward(k, v_t, q, bias, p_ref):
    left, right = bias
    s = dot_nt(k, q)
    masked = jnp.full((BLOCK, BLOCK), MASKED, F32)
    parts = [
        s[:BLOCK],
        jnp.concatenate([masked, s[BLOCK : 2 * BLOCK, BLOCK:]], axis=1),
        jnp.concatenate([s[2 * BLOCK : 3 * BLOCK, :BLOCK], masked], axis=1),
        s[3 * BLOCK :],
    ]
    if left is not None:
        parts[:2] = [x + left for x in parts[:2]]
    if right is not None:
        parts[2:] = [x + right for x in parts[2:]]
    peak = jnp.max(
        jnp.maximum(jnp.maximum(parts[0], parts[1]), jnp.maximum(parts[2], parts[3])),
        axis=0,
        keepdims=True,
    )
    parts = [jnp.exp2((x - peak) * TO_LOG2) for x in parts]
    for n, x in enumerate(parts):
        p_ref[n * BLOCK : (n + 1) * BLOCK, :] = x
    total = jnp.sum((parts[0] + parts[1]) + (parts[2] + parts[3]), axis=0, keepdims=True)
    mixed = dot_nn(v_t, jnp.concatenate([x.astype(BF) for x in parts], axis=0))
    return peak, total, mixed


def far_backward(k_t, v, q, p_ref, factor, g, ec):
    e = p_ref[...] * factor
    r = (e * (dot_nt(v, g) - ec)).astype(BF)
    return dot_nn(r, q), dot_nn(e.astype(BF), g), dot_nn(k_t, r)


def main_kernel(
    where, kv_own, kv_got, near_got, wide_got, qg_own, qg_got,
    oq_own, oq_far, grad, near_out, wide_out,
    raw, raw_t, one, one_t, two, two_t, qs, gs, p0, p1, p2, acc0, acc1, acc2, oq, halos,
):
    side = where[0]
    odd = where[3]
    halos[1 - odd] = near_got[...]
    halos[odd] = wide_got[...]
    from_left, from_right = halos.at[0], halos.at[1]
    to_left, to_right = halos.at[0], halos.at[1]
    width = kv_own.shape[1] // 2
    left_bias = (1 - where[1]).astype(F32) * MASKED
    right_bias = (1 - where[2]).astype(F32) * MASKED
    own_at = pl.multiple_of(side * 512, 512)
    got_at = pl.multiple_of((1 - side) * 512, 512)
    for h in range(width // HEAD):
        kc = slice(h * HEAD, (h + 1) * HEAD)
        vc = slice(width + h * HEAD, width + (h + 1) * HEAD)
        for n, cols in ((0, kc), (1, vc)):
            raw[n, 0:256, :] = from_left[0:256, cols]
            raw[n, pl.ds(256 + own_at, 512), :] = kv_own[:, cols]
            raw[n, pl.ds(256 + got_at, 512), :] = kv_got[:, cols]
            raw[n, 1280:1536, :] = from_right[0:256, cols]
            one[n, 0:128, :] = from_left[256:384, cols]
            for i in range(6):
                block = pool1(raw[n, i * PARENT : (i + 1) * PARENT, :])
                at = (i + 1) * BLOCK
                one[n, at : at + BLOCK, :] = block
            one[n, 896:1024, :] = from_right[256:384, cols]
            two[n, 0:128, :] = from_left[384:512, cols]
            two[n, 128:192, :] = pool12(one[n, 0:128, :])
            two[n, 192:256, :] = pool2(raw[n, 0:256, :])
            two[n, 256:320, :] = pool2(raw[n, 1280:1536, :])
            two[n, 320:384, :] = pool12(one[n, 896:1024, :])
            two[n, 384:512, :] = from_right[384:512, cols]
            for i in range(6):
                rows = slice(i * PARENT, (i + 1) * PARENT)
                raw_t[n, :, rows] = raw[n, rows, :].T
            for i in range(8):
                rows = slice(i * BLOCK, (i + 1) * BLOCK)
                one_t[n, :, rows] = one[n, rows, :].T
            for i in range(4):
                rows = slice(i * BLOCK, (i + 1) * BLOCK)
                two_t[n, :, rows] = two[n, rows, :].T
        qs[pl.ds(own_at, 512), :] = qg_own[:, kc]
        qs[pl.ds(got_at, 512), :] = qg_got[:, kc]
        gs[pl.ds(own_at, 512), :] = qg_own[:, vc]
        gs[pl.ds(got_at, 512), :] = qg_got[:, vc]

        def sides(ref, n, j):
            before, after = slice(2 * j * BLOCK, 2 * j * BLOCK + 256), slice(
                (2 * j + 4) * BLOCK, (2 * j + 4) * BLOCK + 256
            )
            if ref is one:
                return jnp.concatenate([ref[n, before, :], ref[n, after, :]], axis=0)
            return jnp.concatenate([ref[n, :, before], ref[n, :, after]], axis=1)

        q_parents = [qs[i * PARENT : (i + 1) * PARENT, :] for i in range(4)]
        q1 = [
            jnp.concatenate([pool1(q_parents[2 * j]), pool1(q_parents[2 * j + 1])], axis=0)
            for j in range(2)
        ]
        q2 = jnp.concatenate([pool2(x) for x in q_parents], axis=0)
        bias1 = [(left_bias, None), (None, right_bias)]
        far1 = [
            far_forward(sides(one, 0, j), sides(one_t, 1, j), q1[j], bias1[j], p1.at[j])
            for j in range(2)
        ]
        far2 = far_forward(two[0], two_t[1], q2, (left_bias, right_bias), p2)
        acc0[...] = jnp.zeros_like(acc0)
        g1_t, ec1, f1 = [], [], []
        g2_t, ec2, low2 = [], [], []
        dq0 = []
        for i in range(4):
            rows = slice(i * PARENT, i * PARENT + 3 * PARENT)
            q = q_parents[i]
            g = gs[i * PARENT : (i + 1) * PARENT, :]
            s = dot_nt(raw[0, rows, :], q)
            pieces = [s[:PARENT], s[PARENT : 2 * PARENT], s[2 * PARENT :]]
            if i == 0:
                pieces[0] = pieces[0] + left_bias
            if i == 3:
                pieces[2] = pieces[2] + right_bias
            m0 = jnp.max(
                jnp.maximum(jnp.maximum(pieces[0], pieces[1]), pieces[2]), axis=0, keepdims=True
            )
            e = [jnp.exp2((x - m0) * TO_LOG2) for x in pieces]
            for n in range(3):
                p0[n * PARENT : (n + 1) * PARENT, :] = e[n]
            z0 = jnp.sum(e[0] + e[1] + e[2], axis=0, keepdims=True)
            u0 = dot_nn(raw_t[1, :, rows], jnp.concatenate([x.astype(BF) for x in e], axis=0))
            j, half = i // 2, i % 2
            lanes = slice(half * BLOCK, (half + 1) * BLOCK)
            m1, z1, u1 = (x[:, lanes] for x in far1[j])
            lanes2 = slice(j * BLOCK, (j + 1) * BLOCK)
            m2, z2, u2 = (spread64(x[:, lanes2], half) for x in far2)
            m1w, m2w = twice(m1, 1), twice(m2, 1)
            m = jnp.maximum(jnp.maximum(m0, m1w), m2w)
            a0 = jnp.exp2((m0 - m) * TO_LOG2)
            a1 = 2.0 * jnp.exp2((m1w - m) * TO_LOG2)
            a2 = 4.0 * jnp.exp2((m2w - m) * TO_LOG2)
            z = a0 * z0 + a1 * twice(z1, 1) + a2 * twice(z2, 1)
            inv = 1.0 / z
            o = ((a0 * inv) * u0 + (a1 * inv) * twice(u1, 1) + (a2 * inv) * twice(u2, 1)).astype(BF)
            oq[i, 0, h * HEAD : (h + 1) * HEAD, :] = o
            lg = m * TO_LOG2 + jnp.log2(z)
            g_t = g.astype(F32).T
            dr = jnp.sum(o.astype(F32) * g_t, axis=0, keepdims=True)
            lg_a, lg_b = lg[:, :BLOCK], lg[:, BLOCK:]
            g_a, g_b = g_t[:, :BLOCK], g_t[:, BLOCK:]
            dr_a, dr_b = dr[:, :BLOCK], dr[:, BLOCK:]
            low = jnp.minimum(lg_a, lg_b)
            w_a, w_b = jnp.exp2(low - lg_a), jnp.exp2(low - lg_b)
            g1_t.append((w_a * g_a + w_b * g_b).astype(BF))
            ec1.append(w_a * dr_a + w_b * dr_b)
            f1.append(2.0 * jnp.exp2(m1 * TO_LOG2 - low))
            lower = jnp.minimum(low, swap64(low))
            w_a, w_b = jnp.exp2(lower - lg_a), jnp.exp2(lower - lg_b)
            part = w_a * g_a + w_b * g_b
            g2_t.append(part + swap64(part))
            part = w_a * dr_a + w_b * dr_b
            ec2.append(part + swap64(part))
            low2.append(lower)
            f0 = jnp.exp2(m0 * TO_LOG2 - lg)
            products = dot_nt(raw[1, rows, :], g)
            weights = p0[...] * f0
            eb = weights.astype(BF)
            r = (weights * (products - dr)).astype(BF)
            acc0[1, rows, :] += dot_nn(eb, g)
            acc0[0, rows, :] += dot_nn(r, q)
            dq0.append(dot_nn(raw_t[0, :, rows], r))
        acc1[...] = jnp.zeros_like(acc1)
        dq1 = []
        for j in range(2):
            pair = slice(2 * j, 2 * j + 2)
            g1 = jnp.concatenate([x.astype(F32).T.astype(BF) for x in g1_t[pair]], axis=0)
            dk, dv, dq = far_backward(
                sides(one_t, 0, j), sides(one, 1, j), q1[j], p1.at[j],
                jnp.concatenate(f1[pair], axis=1), g1, jnp.concatenate(ec1[pair], axis=1),
            )
            for n, x in ((0, dk), (1, dv)):
                acc1[n, 2 * j * BLOCK : 2 * j * BLOCK + 256, :] += x[:256]
                acc1[n, (2 * j + 4) * BLOCK : (2 * j + 4) * BLOCK + 256, :] += x[256:]
            dq1.append(dq)

        def joined(parts):
            return jnp.concatenate(
                [
                    jnp.where(low_lanes(parts[0].shape), parts[2 * j], parts[2 * j + 1])
                    for j in range(2)
                ],
                axis=1,
            )

        g2 = joined(g2_t).T.astype(BF)
        f2 = 4.0 * jnp.exp2(far2[0] * TO_LOG2 - joined(low2))
        acc2[0], acc2[1], dq2 = far_backward(two_t[0], two[1], q2, p2, f2, g2, joined(ec2))
        for i in range(4):
            j, half = i // 2, i % 2
            d1 = dq1[j][:, half * BLOCK : (half + 1) * BLOCK]
            d2 = spread64(dq2[:, j * BLOCK : (j + 1) * BLOCK], half)
            coarse = 0.5 * d1 + 0.25 * d2
            oq[i, 1, h * HEAD : (h + 1) * HEAD, :] = ((dq0[i] + twice(coarse, 1)) * INV_ROOT).astype(BF)
        for n, cols, scale in ((0, kc, INV_ROOT), (1, vc, 1.0)):
            for i in range(4):
                rows = slice((i + 1) * PARENT, (i + 2) * PARENT)
                coarse = acc1[n, (i + 2) * BLOCK : (i + 3) * BLOCK, :] * (0.5 * scale)
                grad[i * PARENT : (i + 1) * PARENT, cols] = acc0[n, rows, :] * scale + twice(coarse)
            far = acc2[n, 128:256, :] * (0.25 * scale)
            mid = acc1[n, 0:256, :] * (0.5 * scale)
            near = acc0[n, 0:256, :] * scale
            to_left[0:256, cols] = (near + twice(mid[128:] + twice(far[64:]))).astype(BF)
            to_left[256:384, cols] = (mid[:128] + twice(far[:64])).astype(BF)
            to_left[384:512, cols] = (acc2[n, 0:128, :] * (0.25 * scale)).astype(BF)
            far = acc2[n, 256:384, :] * (0.25 * scale)
            mid = acc1[n, 768:1024, :] * (0.5 * scale)
            near = acc0[n, 1280:1536, :] * scale
            to_right[0:256, cols] = (near + twice(mid[:128] + twice(far[:64]))).astype(BF)
            to_right[256:384, cols] = (mid[128:] + twice(far[64:])).astype(BF)
            to_right[384:512, cols] = (acc2[n, 384:512, :] * (0.25 * scale)).astype(BF)
    oq_own[...] = oq[pl.ds(side * 2, 2)]
    oq_far[...] = oq[pl.ds((1 - side) * 2, 2)]
    near_out[...] = halos[1 - odd]
    wide_out[...] = halos[odd]


def main(where, kv_own, kv_got, near_got, wide_got, qg_own, qg_got):
    rows, both = kv_own.shape
    width = both // 2
    oq_shape = jax.ShapeDtypeStruct((2, 2, width, PARENT), BF)
    halo_shape = jax.ShapeDtypeStruct((512, both), BF)
    return pl.pallas_call(
        main_kernel,
        in_specs=[smem()] + [vmem()] * 6,
        out_specs=[vmem()] * 5,
        out_shape=[
            oq_shape,
            oq_shape,
            jax.ShapeDtypeStruct((2 * rows, both), F32),
            halo_shape,
            halo_shape,
        ],
        scratch_shapes=[
            pltpu.VMEM((2, 1536, HEAD), BF),
            pltpu.VMEM((2, HEAD, 1536), BF),
            pltpu.VMEM((2, 1024, HEAD), BF),
            pltpu.VMEM((2, HEAD, 1024), BF),
            pltpu.VMEM((2, 512, HEAD), BF),
            pltpu.VMEM((2, HEAD, 512), BF),
            pltpu.VMEM((1024, HEAD), BF),
            pltpu.VMEM((1024, HEAD), BF),
            pltpu.VMEM((768, PARENT), F32),
            pltpu.VMEM((2, 512, PARENT), F32),
            pltpu.VMEM((512, PARENT), F32),
            pltpu.VMEM((2, 1536, HEAD), F32),
            pltpu.VMEM((2, 1024, HEAD), F32),
            pltpu.VMEM((2, 512, HEAD), F32),
            pltpu.VMEM((4, 2, width, PARENT), BF),
            pltpu.VMEM((2, 512, both), BF),
        ],
        compiler_params=pltpu.CompilerParams(vmem_limit_bytes=24 * 1024 * 1024),
        cost_estimate=light(),
    )(where, kv_own, kv_got, near_got, wide_got, qg_own, qg_got)


def join_kernel(where, grad, near_got, wide_got, own, far):
    def fill(first, second, from_left, from_right):
        def parent(i):
            return grad[i * PARENT : (i + 1) * PARENT, :]

        def part(ref, start, stop):
            return ref[start:stop, :].astype(F32)

        first[0:256, :] = (
            parent(0) + part(from_left, 0, 256) + twice(twice(part(from_right, 384, 448)))
        ).astype(BF)
        first[256:512, :] = (
            parent(1) + twice(part(from_left, 256, 384) + twice(part(from_right, 448, 512)))
        ).astype(BF)
        second[0:256, :] = (
            parent(2) + twice(part(from_right, 256, 384) + twice(part(from_left, 384, 448)))
        ).astype(BF)
        second[256:512, :] = (
            parent(3) + part(from_right, 0, 256) + twice(twice(part(from_left, 448, 512)))
        ).astype(BF)

    for side in range(2):
        for odd in range(2):

            @pl.when((where[0] == side) & (where[3] == odd))
            def _(side=side, odd=odd):
                halves = (own, far) if side == 0 else (far, own)
                fill(*halves, *((wide_got, near_got) if odd == 0 else (near_got, wide_got)))


def join(where, grad, near_got, wide_got):
    shape = jax.ShapeDtypeStruct(near_got.shape, BF)
    return pl.pallas_call(
        join_kernel,
        in_specs=[smem(), vmem(), vmem(), vmem()],
        out_specs=[vmem(), vmem()],
        out_shape=[shape, shape],
        compiler_params=small(),
        cost_estimate=light(),
    )(where, grad, near_got, wide_got)


def unpack_rows_kernel(where, *refs):
    ins, (first, second) = refs[:-2], refs[-2:]
    order = order_matrix(True)
    width = ins[0].shape[1] // 2
    side = where[0]
    blocks = [(side * CHUNKS + c, ins[c]) for c in range(CHUNKS)]
    blocks += [((1 - side) * CHUNKS + 1 - LATE_CHUNK, ins[CHUNKS])]
    for block, ref in blocks:
        at = pl.ds(pl.multiple_of(block * width, width), width)
        for i in range(2):
            rows = slice(i * PARENT, (i + 1) * PARENT)
            first[rows, at] = dot_nn(order, ref[rows, :width]).astype(BF)
            second[rows, at] = dot_nn(order, ref[rows, width:]).astype(BF)


def unpack_rows(where, own, got, shape):
    out = jax.ShapeDtypeStruct(shape, BF)
    return pl.pallas_call(
        unpack_rows_kernel,
        in_specs=[smem()] + [vmem()] * (CHUNKS + 1),
        out_specs=[vmem(), vmem()],
        out_shape=[out, out],
        compiler_params=small(),
        cost_estimate=light(),
    )(where, *own, got)


def unpack_last_kernel(where, got, first_in, second_in, first, second, held, sems):
    del first_in, second_in
    order = order_matrix(True)
    width = got.shape[1] // 2
    block = (1 - where[0]) * CHUNKS + LATE_CHUNK
    at = pl.ds(pl.multiple_of(block * width, width), width)
    copies = []
    for m, ref in enumerate((first, second)):
        for i in range(2):
            rows = slice(i * PARENT, (i + 1) * PARENT)
            held[m, rows, :] = dot_nn(order, got[rows, m * width : (m + 1) * width]).astype(BF)
        copies.append(pltpu.make_async_copy(held.at[m], ref.at[:, at], sems.at[m]))
        copies[-1].start()
    for copy in copies:
        copy.wait()


def unpack_last(where, got, first, second):
    out = jax.ShapeDtypeStruct(first.shape, BF)
    hbm = pl.BlockSpec(memory_space=pltpu.HBM)
    return pl.pallas_call(
        unpack_last_kernel,
        in_specs=[smem(), vmem(), hbm, hbm],
        out_specs=[hbm, hbm],
        out_shape=[out, out],
        input_output_aliases={2: 0, 3: 1},
        scratch_shapes=[
            pltpu.VMEM((2, got.shape[0], got.shape[1] // 2), BF),
            pltpu.SemaphoreType.DMA((2,)),
        ],
        compiler_params=small(),
        cost_estimate=light(),
    )(where, got, first, second)


def unpack_columns_kernel(where, *refs):
    ins, (first, second) = refs[:-2], refs[-2:]
    order = order_matrix(True)
    width = ins[0].shape[2]
    for c in range(CHUNKS):
        for ref, side in ((ins[c], where[0]), (ins[CHUNKS + c], 1 - where[0])):
            at = pl.ds(pl.multiple_of((side * CHUNKS + c) * width, width), width)
            for i in range(2):
                rows = slice(i * PARENT, (i + 1) * PARENT)
                first[rows, at] = dot_nt(order, ref[i, 0]).astype(BF)
                second[rows, at] = dot_nt(order, ref[i, 1]).astype(BF)


def unpack_columns(where, own, got, shape):
    out = jax.ShapeDtypeStruct(shape, BF)
    return pl.pallas_call(
        unpack_columns_kernel,
        in_specs=[smem()] + [vmem()] * (2 * CHUNKS),
        out_specs=[vmem(), vmem()],
        out_shape=[out, out],
        compiler_params=small(),
        cost_estimate=light(),
    )(where, *own, *got)


def on_device(queries, key_matrix, value_matrix, cotangent):
    axes = ("outer", "inner")
    count = lax.axis_size("outer") * lax.axis_size("inner")
    device = lax.axis_index("outer") * lax.axis_size("inner") + lax.axis_index("inner")
    pair = device // 2
    where = jnp.stack([device % 2, pair > 0, pair < count // 2 - 1, pair % 2]).astype(jnp.int32)
    across = [(i, i ^ 1) for i in range(count)]
    near_edges = [(i, i ^ 2) for i in range(count) if i ^ 2 < count]
    wide_edges = [(i, i + 2 if i // 2 % 2 else i - 2) for i in range(count)]
    wide_edges = [(i, j) for i, j in wide_edges if 0 <= j < count]

    def swap(x):
        return lax.ppermute(x, axes, across)

    def beside(near, wide):
        near = lax.ppermute(near, axes, near_edges)
        return near, lax.ppermute(wide, axes, wide_edges)

    kv_far = pack(False, where, key_matrix, value_matrix, limit=60)
    qg_far = pack(False, where, queries, cotangent)
    packed = pack(True, where, key_matrix, value_matrix, queries, cotangent)
    kv, qg = packed[:CHUNKS], packed[CHUNKS:]
    oq_own, oq_got, back = [], [], []
    for c in range(CHUNKS):
        got_kv = swap(kv_far[c])
        near, wide = halo(where, kv[c], got_kv)
        far = qg_far[c]
        if c > 0:
            near, wide, far = lax.optimization_barrier((near, wide, far))
        near, wide = beside(near, wide)
        own, far, grad, near, wide = main(where, kv[c], got_kv, near, wide, qg[c], swap(far))
        oq_own.append(own)
        oq_got.append(swap(far))
        if c > 0:
            oq_got[c - 1], near, wide = lax.optimization_barrier((oq_got[c - 1], near, wide))
        back.append([grad, *beside(near, wide)])
    oq_got[-1], back[-1] = lax.optimization_barrier((oq_got[-1], back[-1]))
    kv_own, kv_got = [], []
    for c in range(CHUNKS):
        own, far = join(where, *back[c])
        kv_own.append(own)
        kv_got.append(swap(far))
    attended, query_grad = unpack_columns(where, oq_own, oq_got, queries.shape)
    key_grad, value_grad = unpack_rows(where, kv_own, kv_got[1 - LATE_CHUNK], queries.shape)
    key_grad, value_grad = unpack_last(where, kv_got[LATE_CHUNK], key_grad, value_grad)
    return attended, query_grad, key_grad, value_grad


def solution(mesh):
    spec = P(("outer", "inner"), None)
    return jax.shard_map(
        on_device,
        mesh=mesh,
        in_specs=(spec,) * 4,
        out_specs=(spec,) * 4,
        check_vma=False,
    )
```

```python
import functools
import math

import jax
import jax.numpy as jnp
from jax import lax
from jax.experimental import pallas as pl
from jax.experimental.pallas import tpu as pltpu
from jax.sharding import PartitionSpec as P

HEAD = 128
BLOCK = 128
PARENT = 256
LEVELS = 3
CHUNKS = 2
LATE_CHUNK = 1
INV_ROOT = HEAD**-0.5
TO_LOG2 = INV_ROOT * math.log2(math.e)
MASKED = -1e30
BF = jnp.bfloat16
F32 = jnp.float32


def dot_nt(a, b):
    return lax.dot_general(a, b, (((1,), (1,)), ((), ())), preferred_element_type=F32)


def dot_nn(a, b):
    return jnp.dot(a, b, preferred_element_type=F32)


def order_matrix(inverse):
    row = lax.broadcasted_iota(jnp.int32, (PARENT, PARENT), 0)
    col = lax.broadcasted_iota(jnp.int32, (PARENT, PARENT), 1)
    place, token = (col, row) if inverse else (row, col)
    slab = place // 64
    source = 4 * (place % 64) + 2 * (slab % 2) + slab // 2
    return jnp.where(source == token, 1.0, 0.0).astype(BF)


def pool1(x):
    return ((x[:BLOCK].astype(F32) + x[BLOCK:].astype(F32)) * 0.5).astype(BF)


def pool2(x):
    half = x[:BLOCK].astype(F32) + x[BLOCK:].astype(F32)
    return ((half[:64] + half[64:]) * 0.25).astype(BF)


def pool12(x):
    return ((x[:64].astype(F32) + x[64:].astype(F32)) * 0.5).astype(BF)


def twice(x, axis=0):
    return jnp.concatenate([x, x], axis=axis)


def pack_kernel(own, where, *refs):
    count = 4 if own else 2
    arrays, outs, (held, sems) = refs[:count], refs[count:-2], refs[-2:]
    rows, columns = arrays[0].shape
    half = columns // 2
    width = half // CHUNKS
    side = where[0] if own else 1 - where[0]
    at = pl.ds(pl.multiple_of(side * half, half), half)
    copies = [
        pltpu.make_async_copy(ref.at[:, at], held.at[m], sems.at[m]) for m, ref in enumerate(arrays)
    ]
    for copy in copies:
        copy.start()
    order = order_matrix(False)
    for m in range(count):
        copies[m].wait()
        first = m % 2 * width
        for i in range(rows // PARENT):
            at = slice(i * PARENT, (i + 1) * PARENT)
            x = dot_nn(order, held[m, at, :]).astype(BF)
            for c in range(CHUNKS):
                out = outs[m // 2 * CHUNKS + c]
                out[at, first : first + width] = x[:, c * width : (c + 1) * width]


def pack(own, where, *arrays):
    rows, columns = arrays[0].shape
    count = len(arrays)
    return pl.pallas_call(
        functools.partial(pack_kernel, own),
        in_specs=[smem()] + [pl.BlockSpec(memory_space=pltpu.HBM)] * count,
        out_specs=[vmem()] * (count // 2 * CHUNKS),
        out_shape=[jax.ShapeDtypeStruct((rows, columns // CHUNKS), BF)] * (count // 2 * CHUNKS),
        scratch_shapes=[
            pltpu.VMEM((count, rows, columns // 2), BF),
            pltpu.SemaphoreType.DMA((count,)),
        ],
        compiler_params=small(),
        cost_estimate=light(),
    )(where, *arrays)


def smem():
    return pl.BlockSpec(memory_space=pltpu.SMEM)


def vmem():
    return pl.BlockSpec(memory_space=pltpu.VMEM)


def small():
    return pltpu.CompilerParams(vmem_limit_bytes=8 * 1024 * 1024)


def light():
    return pl.CostEstimate(flops=1000, bytes_accessed=1000, transcendentals=0)


def halo_kernel(where, own, got, near, wide):
    def fill(first, second, to_right, to_left):
        to_right[0:256, :] = second[256:512, :]
        to_right[256:384, :] = pool1(second[0:256, :])
        to_right[384:448, :] = pool2(first[0:256, :])
        to_right[448:512, :] = pool2(first[256:512, :])
        to_left[0:256, :] = first[0:256, :]
        to_left[256:384, :] = pool1(first[256:512, :])
        to_left[384:448, :] = pool2(second[0:256, :])
        to_left[448:512, :] = pool2(second[256:512, :])

    for side in range(2):
        for odd in range(2):

            @pl.when((where[0] == side) & (where[3] == odd))
            def _(side=side, odd=odd):
                halves = (own, got) if side == 0 else (got, own)
                fill(*halves, *((near, wide) if odd == 0 else (wide, near)))


def halo(where, own, got):
    shape = jax.ShapeDtypeStruct(own.shape, BF)
    return pl.pallas_call(
        halo_kernel,
        in_specs=[smem(), vmem(), vmem()],
        out_specs=[vmem(), vmem()],
        out_shape=[shape, shape],
        compiler_params=small(),
        cost_estimate=light(),
    )(where, own, got)


def swap64(x):
    return pltpu.roll(x, 64, 1)


def low_lanes(shape):
    return lax.broadcasted_iota(jnp.int32, shape, 1) < 64


def spread64(x, half):
    other = swap64(x)
    low = low_lanes(x.shape)
    return jnp.where(low, x, other) if half == 0 else jnp.where(low, other, x)


def split2(x):
    high = x.astype(BF)
    return high, (x - high.astype(F32)).astype(BF)


def scaled_queries(q):
    return jnp.concatenate(split2(q.astype(F32) * TO_LOG2), axis=1)


def with_offset(g_t, offset):
    high, low = split2(-offset)
    count = offset.shape[1]
    row = lax.broadcasted_iota(jnp.int32, (16, count), 0)
    tail = jnp.where(row == 0, high.astype(F32), jnp.where(row == 1, low.astype(F32), 0.0))
    zeros = jnp.zeros((HEAD - 16, count), BF)
    return jnp.concatenate([g_t.astype(BF), tail.astype(BF), zeros], axis=0)


def to_rows(factor):
    return jnp.broadcast_to(factor, (HEAD, factor.shape[1])).T


def times(x, rows):
    return (x.astype(F32) * rows).astype(BF)


def far_forward(k, v_t, q, bias, p_ref, pb_ref):
    k0, k1, k2, k3 = k
    v0, v1, v2, v3 = v_t
    left, right = bias
    outer = dot_nt(jnp.concatenate([k0, k3], axis=0), q)
    first, last = outer[:BLOCK], outer[BLOCK:]
    mid_low = dot_nt(k2, q[:BLOCK])
    mid_high = dot_nt(k1, q[BLOCK:])
    if left is not None:
        first = first + left
        mid_high = mid_high + left
    if right is not None:
        last = last + right
        mid_low = mid_low + right
    mid = jnp.concatenate([mid_low, mid_high], axis=1)
    peak = jnp.max(jnp.maximum(jnp.maximum(first, last), mid), axis=0, keepdims=True)
    for n, x in enumerate((first, last, mid)):
        x = jnp.exp2(x - peak)
        p_ref[n * BLOCK : (n + 1) * BLOCK, :] = x
        pb_ref[n * BLOCK : (n + 1) * BLOCK, :] = x.astype(BF)
    mixed = dot_nn(jnp.concatenate([v0, v3], axis=1), pb_ref[: 2 * BLOCK, :]) + jnp.concatenate(
        [dot_nn(v2, pb_ref[2 * BLOCK :, :BLOCK]), dot_nn(v1, pb_ref[2 * BLOCK :, BLOCK:])], axis=1
    )
    return peak, mixed[HEAD : HEAD + 1], mixed[:HEAD]


def far_backward(k_t, v, q, p_ref, pb_ref, g, g_t):
    k0, k1, k2, k3 = k_t
    v0, v1, v2, v3 = v
    p_out = dot_nn(jnp.concatenate([v0, v3], axis=0), g_t)
    p_mid = jnp.concatenate([dot_nn(v2, g_t[:, :BLOCK]), dot_nn(v1, g_t[:, BLOCK:])], axis=1)
    r_out = (p_ref[: 2 * BLOCK, :] * p_out).astype(BF)
    r_mid = (p_ref[2 * BLOCK :, :] * p_mid).astype(BF)
    dv03 = dot_nn(pb_ref[: 2 * BLOCK, :], g)
    dv2 = dot_nn(pb_ref[2 * BLOCK :, :BLOCK], g[:BLOCK])
    dv1 = dot_nn(pb_ref[2 * BLOCK :, BLOCK:], g[BLOCK:])
    dk03 = dot_nn(r_out, q)
    dk2 = dot_nn(r_mid[:, :BLOCK], q[:BLOCK])
    dk1 = dot_nn(r_mid[:, BLOCK:], q[BLOCK:])
    dq_t = dot_nn(jnp.concatenate([k0, k3], axis=1), r_out) + jnp.concatenate(
        [dot_nn(k2, r_mid[:, :BLOCK]), dot_nn(k1, r_mid[:, BLOCK:])], axis=1
    )
    return (dk03[:BLOCK], dk1, dk2, dk03[BLOCK:]), (dv03[:BLOCK], dv1, dv2, dv03[BLOCK:]), dq_t


def blocks(ref, which):
    return [ref[b * BLOCK : (b + 1) * BLOCK, :] for b in which]


def blocks_t(ref, which):
    return [ref[:, b * BLOCK : (b + 1) * BLOCK] for b in which]


def main_kernel(
    where, kv_own, kv_got, near_got, wide_got, qg_own, qg_got,
    oq_own, oq_far, grad, near_out, wide_out,
    k0, k0t, v0, v0t, k1, k1t, v1, v1t, k2, k2t, v2, v2t,
    qs, gs, p0, p1, p2, p0b, p1b, p2b, acc0, acc1, acc2, oq, halos,
):
    side = where[0]
    odd = where[3]
    halos[1 - odd] = near_got[...]
    halos[odd] = wide_got[...]
    from_left, from_right = halos.at[0], halos.at[1]
    to_left, to_right = halos.at[0], halos.at[1]
    width = kv_own.shape[1] // 2
    left_bias = (1 - where[1]).astype(F32) * MASKED
    right_bias = (1 - where[2]).astype(F32) * MASKED
    own_at = pl.multiple_of(side * 512, 512)
    got_at = pl.multiple_of((1 - side) * 512, 512)
    for ref in (v0, v1, v2):
        shape = (ref.shape[0], HEAD)
        lane = lax.broadcasted_iota(jnp.int32, shape, 1)
        ref[:, HEAD:] = jnp.where(lane < 2, 1.0, 0.0).astype(BF)
    for ref in (v0t, v1t, v2t):
        row = lax.broadcasted_iota(jnp.int32, (16, ref.shape[1]), 0)
        ref[HEAD:, :] = jnp.where(row == 0, 1.0, 0.0).astype(BF)
    for h in range(width // HEAD):
        kc = slice(h * HEAD, (h + 1) * HEAD)
        vc = slice(width + h * HEAD, width + (h + 1) * HEAD)
        for raw, raw_t, one, one_t, two, two_t, cols in (
            (k0, k0t, k1, k1t, k2, k2t, kc),
            (v0, v0t, v1, v1t, v2, v2t, vc),
        ):
            half = slice(0, HEAD)
            raw[0:256, half] = from_left[0:256, cols]
            raw[pl.ds(256 + own_at, 512), half] = kv_own[:, cols]
            raw[pl.ds(256 + got_at, 512), half] = kv_got[:, cols]
            raw[1280:1536, half] = from_right[0:256, cols]
            one[0:128, half] = from_left[256:384, cols]
            for i in range(6):
                one[(i + 1) * BLOCK : (i + 2) * BLOCK, half] = pool1(
                    raw[i * PARENT : (i + 1) * PARENT, half]
                )
            one[896:1024, half] = from_right[256:384, cols]
            two[0:128, half] = from_left[384:512, cols]
            two[128:192, half] = pool12(one[0:128, half])
            two[192:256, half] = pool2(raw[0:256, half])
            two[256:320, half] = pool2(raw[1280:1536, half])
            two[320:384, half] = pool12(one[896:1024, half])
            two[384:512, half] = from_right[384:512, cols]
            for ref, ref_t, size in ((raw, raw_t, PARENT), (one, one_t, BLOCK), (two, two_t, BLOCK)):
                for i in range(ref.shape[0] // size):
                    rows = slice(i * size, (i + 1) * size)
                    ref_t[:HEAD, rows] = ref[rows, half].T
        for ref in (k0, k1, k2):
            ref[:, HEAD:] = ref[:, :HEAD]
        qs[pl.ds(own_at, 512), :] = qg_own[:, kc]
        qs[pl.ds(got_at, 512), :] = qg_got[:, kc]
        gs[pl.ds(own_at, 512), :] = qg_own[:, vc]
        gs[pl.ds(got_at, 512), :] = qg_got[:, vc]

        q_parents = [qs[i * PARENT : (i + 1) * PARENT, :] for i in range(4)]
        q1 = [
            jnp.concatenate([pool1(q_parents[2 * j]), pool1(q_parents[2 * j + 1])], axis=0)
            for j in range(2)
        ]
        q2 = jnp.concatenate([pool2(x) for x in q_parents], axis=0)
        which1 = [(0, 1, 4, 5), (2, 3, 6, 7)]
        bias1 = [(left_bias, None), (None, right_bias)]
        which2 = (0, 1, 2, 3)
        far1 = [
            far_forward(
                blocks(k1, which1[j]), blocks_t(v1t, which1[j]), scaled_queries(q1[j]), bias1[j],
                p1.at[j], p1b.at[j],
            )
            for j in range(2)
        ]
        far2 = far_forward(
            blocks(k2, which2), blocks_t(v2t, which2), scaled_queries(q2), (left_bias, right_bias),
            p2, p2b,
        )
        acc0[...] = jnp.zeros_like(acc0)
        g1_t, ec1, f1 = [], [], []
        g2_t, ec2, low2 = [], [], []
        dq0 = []
        for i in range(4):
            rows = slice(i * PARENT, i * PARENT + 3 * PARENT)
            q = q_parents[i]
            g = gs[i * PARENT : (i + 1) * PARENT, :]
            s = dot_nt(k0[rows, :], scaled_queries(q))
            pieces = [s[:PARENT], s[PARENT : 2 * PARENT], s[2 * PARENT :]]
            if i == 0:
                pieces[0] = pieces[0] + left_bias
            if i == 3:
                pieces[2] = pieces[2] + right_bias
            m0 = jnp.max(
                jnp.maximum(jnp.maximum(pieces[0], pieces[1]), pieces[2]), axis=0, keepdims=True
            )
            for n, x in enumerate(pieces):
                x = jnp.exp2(x - m0)
                p0[n * PARENT : (n + 1) * PARENT, :] = x
                p0b[n * PARENT : (n + 1) * PARENT, :] = x.astype(BF)
            u0 = dot_nn(v0t[:, rows], p0b[...])
            z0, u0 = u0[HEAD : HEAD + 1], u0[:HEAD]
            j, half = i // 2, i % 2
            lanes = slice(half * BLOCK, (half + 1) * BLOCK)
            m1, z1, u1 = (x[:, lanes] for x in far1[j])
            lanes2 = slice(j * BLOCK, (j + 1) * BLOCK)
            m2, z2, u2 = (spread64(x[:, lanes2], half) for x in far2)
            m1w, m2w = twice(m1, 1), twice(m2, 1)
            m = jnp.maximum(jnp.maximum(m0, m1w), m2w)
            a0 = jnp.exp2(m0 - m)
            a1 = 2.0 * jnp.exp2(m1w - m)
            a2 = 4.0 * jnp.exp2(m2w - m)
            z = a0 * z0 + a1 * twice(z1, 1) + a2 * twice(z2, 1)
            inv = 1.0 / z
            o = ((a0 * inv) * u0 + (a1 * inv) * twice(u1, 1) + (a2 * inv) * twice(u2, 1)).astype(BF)
            oq[i, 0, h * HEAD : (h + 1) * HEAD, :] = o
            lg = m + jnp.log2(z)
            g_t = g.astype(F32).T
            dr = jnp.sum(o.astype(F32) * g_t, axis=0, keepdims=True)
            lg_a, lg_b = lg[:, :BLOCK], lg[:, BLOCK:]
            g_a, g_b = g_t[:, :BLOCK], g_t[:, BLOCK:]
            dr_a, dr_b = dr[:, :BLOCK], dr[:, BLOCK:]
            low = jnp.minimum(lg_a, lg_b)
            w_a, w_b = jnp.exp2(low - lg_a), jnp.exp2(low - lg_b)
            g1_t.append(w_a * g_a + w_b * g_b)
            ec1.append(w_a * dr_a + w_b * dr_b)
            f1.append(2.0 * jnp.exp2(m1 - low))
            lower = jnp.minimum(low, swap64(low))
            w_a, w_b = jnp.exp2(lower - lg_a), jnp.exp2(lower - lg_b)
            part = w_a * g_a + w_b * g_b
            g2_t.append(part + swap64(part))
            part = w_a * dr_a + w_b * dr_b
            ec2.append(part + swap64(part))
            low2.append(lower)
            f0 = jnp.exp2(m0 - lg)
            f_rows = to_rows(f0)
            products = dot_nn(v0[rows, :], with_offset(g_t, dr))
            r = (p0[...] * products).astype(BF)
            acc0[1, rows, :] += dot_nn(p0b[...], times(g, f_rows))
            acc0[0, rows, :] += dot_nn(r, times(q, f_rows))
            dq0.append(f0 * dot_nn(k0t[:, rows], r))
        acc1[...] = jnp.zeros_like(acc1)
        dq1 = []
        for j in range(2):
            pair = slice(2 * j, 2 * j + 2)
            g_t, ec, f = (jnp.concatenate(x[pair], axis=1) for x in (g1_t, ec1, f1))
            dk, dv, dq = far_backward(
                blocks_t(k1t, which1[j]), blocks(v1, which1[j]), times(q1[j], to_rows(f)),
                p1.at[j], p1b.at[j], (g_t * f).T.astype(BF), with_offset(g_t, ec),
            )
            for n, b in enumerate(which1[j]):
                acc1[0, b * BLOCK : (b + 1) * BLOCK, :] += dk[n]
                acc1[1, b * BLOCK : (b + 1) * BLOCK, :] += dv[n]
            dq1.append(f * dq)

        def joined(parts):
            return jnp.concatenate(
                [
                    jnp.where(low_lanes(parts[0].shape), parts[2 * j], parts[2 * j + 1])
                    for j in range(2)
                ],
                axis=1,
            )

        g_t, ec = joined(g2_t), joined(ec2)
        f = 4.0 * jnp.exp2(far2[0] - joined(low2))
        dk, dv, dq2 = far_backward(
            blocks_t(k2t, which2), blocks(v2, which2), times(q2, to_rows(f)), p2, p2b,
            (g_t * f).T.astype(BF), with_offset(g_t, ec),
        )
        dq2 = f * dq2
        for n in range(4):
            acc2[0, n * BLOCK : (n + 1) * BLOCK, :] = dk[n]
            acc2[1, n * BLOCK : (n + 1) * BLOCK, :] = dv[n]
        for i in range(4):
            j, half = i // 2, i % 2
            d1 = dq1[j][:, half * BLOCK : (half + 1) * BLOCK]
            d2 = spread64(dq2[:, j * BLOCK : (j + 1) * BLOCK], half)
            coarse = 0.5 * d1 + 0.25 * d2
            oq[i, 1, h * HEAD : (h + 1) * HEAD, :] = ((dq0[i] + twice(coarse, 1)) * INV_ROOT).astype(BF)
        for n, cols, scale in ((0, kc, INV_ROOT), (1, vc, 1.0)):
            for i in range(4):
                rows = slice((i + 1) * PARENT, (i + 2) * PARENT)
                coarse = acc1[n, (i + 2) * BLOCK : (i + 3) * BLOCK, :] * (0.5 * scale)
                grad[i * PARENT : (i + 1) * PARENT, cols] = acc0[n, rows, :] * scale + twice(coarse)
            far = acc2[n, 128:256, :] * (0.25 * scale)
            mid = acc1[n, 0:256, :] * (0.5 * scale)
            near = acc0[n, 0:256, :] * scale
            to_left[0:256, cols] = (near + twice(mid[128:] + twice(far[64:]))).astype(BF)
            to_left[256:384, cols] = (mid[:128] + twice(far[:64])).astype(BF)
            to_left[384:512, cols] = (acc2[n, 0:128, :] * (0.25 * scale)).astype(BF)
            far = acc2[n, 256:384, :] * (0.25 * scale)
            mid = acc1[n, 768:1024, :] * (0.5 * scale)
            near = acc0[n, 1280:1536, :] * scale
            to_right[0:256, cols] = (near + twice(mid[:128] + twice(far[:64]))).astype(BF)
            to_right[256:384, cols] = (mid[128:] + twice(far[64:])).astype(BF)
            to_right[384:512, cols] = (acc2[n, 384:512, :] * (0.25 * scale)).astype(BF)
    oq_own[...] = oq[pl.ds(side * 2, 2)]
    oq_far[...] = oq[pl.ds((1 - side) * 2, 2)]
    near_out[...] = halos[1 - odd]
    wide_out[...] = halos[odd]


def main(where, kv_own, kv_got, near_got, wide_got, qg_own, qg_got):
    rows, both = kv_own.shape
    width = both // 2
    oq_shape = jax.ShapeDtypeStruct((2, 2, width, PARENT), BF)
    halo_shape = jax.ShapeDtypeStruct((512, both), BF)
    return pl.pallas_call(
        main_kernel,
        in_specs=[smem()] + [vmem()] * 6,
        out_specs=[vmem()] * 5,
        out_shape=[
            oq_shape,
            oq_shape,
            jax.ShapeDtypeStruct((2 * rows, both), F32),
            halo_shape,
            halo_shape,
        ],
        scratch_shapes=[
            *(
                pltpu.VMEM(shape, BF)
                for rows in (1536, 1024, 512)
                for shape in ((rows, 2 * HEAD), (HEAD, rows), (rows, 2 * HEAD), (HEAD + 16, rows))
            ),
            pltpu.VMEM((1024, HEAD), BF),
            pltpu.VMEM((1024, HEAD), BF),
            *(
                pltpu.VMEM(shape, kind)
                for kind in (F32, BF)
                for shape in ((768, PARENT), (2, 384, PARENT), (384, PARENT))
            ),
            pltpu.VMEM((2, 1536, HEAD), F32),
            pltpu.VMEM((2, 1024, HEAD), F32),
            pltpu.VMEM((2, 512, HEAD), F32),
            pltpu.VMEM((4, 2, width, PARENT), BF),
            pltpu.VMEM((2, 512, both), BF),
        ],
        compiler_params=pltpu.CompilerParams(vmem_limit_bytes=24 * 1024 * 1024),
        cost_estimate=light(),
    )(where, kv_own, kv_got, near_got, wide_got, qg_own, qg_got)


def join_kernel(where, grad, near_got, wide_got, own, far):
    def fill(first, second, from_left, from_right):
        def parent(i):
            return grad[i * PARENT : (i + 1) * PARENT, :]

        def part(ref, start, stop):
            return ref[start:stop, :].astype(F32)

        first[0:256, :] = (
            parent(0) + part(from_left, 0, 256) + twice(twice(part(from_right, 384, 448)))
        ).astype(BF)
        first[256:512, :] = (
            parent(1) + twice(part(from_left, 256, 384) + twice(part(from_right, 448, 512)))
        ).astype(BF)
        second[0:256, :] = (
            parent(2) + twice(part(from_right, 256, 384) + twice(part(from_left, 384, 448)))
        ).astype(BF)
        second[256:512, :] = (
            parent(3) + part(from_right, 0, 256) + twice(twice(part(from_left, 448, 512)))
        ).astype(BF)

    for side in range(2):
        for odd in range(2):

            @pl.when((where[0] == side) & (where[3] == odd))
            def _(side=side, odd=odd):
                halves = (own, far) if side == 0 else (far, own)
                fill(*halves, *((wide_got, near_got) if odd == 0 else (near_got, wide_got)))


def join(where, grad, near_got, wide_got):
    shape = jax.ShapeDtypeStruct(near_got.shape, BF)
    return pl.pallas_call(
        join_kernel,
        in_specs=[smem(), vmem(), vmem(), vmem()],
        out_specs=[vmem(), vmem()],
        out_shape=[shape, shape],
        compiler_params=small(),
        cost_estimate=light(),
    )(where, grad, near_got, wide_got)


def unpack_rows_kernel(where, *refs):
    ins, (first, second) = refs[:-2], refs[-2:]
    order = order_matrix(True)
    width = ins[0].shape[1] // 2
    side = where[0]
    blocks = [(side * CHUNKS + c, ins[c]) for c in range(CHUNKS)]
    blocks += [((1 - side) * CHUNKS + 1 - LATE_CHUNK, ins[CHUNKS])]
    for block, ref in blocks:
        at = pl.ds(pl.multiple_of(block * width, width), width)
        for i in range(2):
            rows = slice(i * PARENT, (i + 1) * PARENT)
            first[rows, at] = dot_nn(order, ref[rows, :width]).astype(BF)
            second[rows, at] = dot_nn(order, ref[rows, width:]).astype(BF)


def unpack_rows(where, own, got, shape):
    out = jax.ShapeDtypeStruct(shape, BF)
    return pl.pallas_call(
        unpack_rows_kernel,
        in_specs=[smem()] + [vmem()] * (CHUNKS + 1),
        out_specs=[vmem(), vmem()],
        out_shape=[out, out],
        compiler_params=small(),
        cost_estimate=light(),
    )(where, *own, got)


def unpack_last_kernel(where, got, first_in, second_in, first, second, held, sems):
    del first_in, second_in
    order = order_matrix(True)
    width = got.shape[1] // 2
    block = (1 - where[0]) * CHUNKS + LATE_CHUNK
    at = pl.ds(pl.multiple_of(block * width, width), width)
    copies = []
    for m, ref in enumerate((first, second)):
        for i in range(2):
            rows = slice(i * PARENT, (i + 1) * PARENT)
            held[m, rows, :] = dot_nn(order, got[rows, m * width : (m + 1) * width]).astype(BF)
        copies.append(pltpu.make_async_copy(held.at[m], ref.at[:, at], sems.at[m]))
        copies[-1].start()
    for copy in copies:
        copy.wait()


def unpack_last(where, got, first, second):
    out = jax.ShapeDtypeStruct(first.shape, BF)
    hbm = pl.BlockSpec(memory_space=pltpu.HBM)
    return pl.pallas_call(
        unpack_last_kernel,
        in_specs=[smem(), vmem(), hbm, hbm],
        out_specs=[hbm, hbm],
        out_shape=[out, out],
        input_output_aliases={2: 0, 3: 1},
        scratch_shapes=[
            pltpu.VMEM((2, got.shape[0], got.shape[1] // 2), BF),
            pltpu.SemaphoreType.DMA((2,)),
        ],
        compiler_params=small(),
        cost_estimate=light(),
    )(where, got, first, second)


def unpack_columns_kernel(where, *refs):
    ins, (first, second) = refs[:-2], refs[-2:]
    order = order_matrix(True)
    width = ins[0].shape[2]
    for c in range(CHUNKS):
        for ref, side in ((ins[c], where[0]), (ins[CHUNKS + c], 1 - where[0])):
            at = pl.ds(pl.multiple_of((side * CHUNKS + c) * width, width), width)
            for i in range(2):
                rows = slice(i * PARENT, (i + 1) * PARENT)
                first[rows, at] = dot_nt(order, ref[i, 0]).astype(BF)
                second[rows, at] = dot_nt(order, ref[i, 1]).astype(BF)


def unpack_columns(where, own, got, shape):
    out = jax.ShapeDtypeStruct(shape, BF)
    return pl.pallas_call(
        unpack_columns_kernel,
        in_specs=[smem()] + [vmem()] * (2 * CHUNKS),
        out_specs=[vmem(), vmem()],
        out_shape=[out, out],
        compiler_params=small(),
        cost_estimate=light(),
    )(where, *own, *got)


def on_device(queries, key_matrix, value_matrix, cotangent):
    axes = ("outer", "inner")
    count = lax.axis_size("outer") * lax.axis_size("inner")
    device = lax.axis_index("outer") * lax.axis_size("inner") + lax.axis_index("inner")
    pair = device // 2
    where = jnp.stack([device % 2, pair > 0, pair < count // 2 - 1, pair % 2]).astype(jnp.int32)
    across = [(i, i ^ 1) for i in range(count)]
    near_edges = [(i, i ^ 2) for i in range(count) if i ^ 2 < count]
    wide_edges = [(i, i + 2 if i // 2 % 2 else i - 2) for i in range(count)]
    wide_edges = [(i, j) for i, j in wide_edges if 0 <= j < count]

    def swap(x):
        return lax.ppermute(x, axes, across)

    def beside(near, wide):
        near = lax.ppermute(near, axes, near_edges)
        return near, lax.ppermute(wide, axes, wide_edges)

    kv_far = pack(False, where, key_matrix, value_matrix)
    qg_far = pack(False, where, queries, cotangent)
    packed = pack(True, where, key_matrix, value_matrix, queries, cotangent)
    kv, qg = packed[:CHUNKS], packed[CHUNKS:]
    oq_own, oq_got, back = [], [], []
    for c in range(CHUNKS):
        got_kv = swap(kv_far[c])
        near, wide = halo(where, kv[c], got_kv)
        far = qg_far[c]
        if c > 0:
            near, wide, far = lax.optimization_barrier((near, wide, far))
        near, wide = beside(near, wide)
        own, far, grad, near, wide = main(where, kv[c], got_kv, near, wide, qg[c], swap(far))
        oq_own.append(own)
        oq_got.append(swap(far))
        if c > 0:
            oq_got[c - 1], near, wide = lax.optimization_barrier((oq_got[c - 1], near, wide))
        back.append([grad, *beside(near, wide)])
    oq_got[-1], back[-1] = lax.optimization_barrier((oq_got[-1], back[-1]))
    kv_own, kv_got = [], []
    for c in range(CHUNKS):
        own, far = join(where, *back[c])
        kv_own.append(own)
        kv_got.append(swap(far))
    attended, query_grad = unpack_columns(where, oq_own, oq_got, queries.shape)
    key_grad, value_grad = unpack_rows(where, kv_own, kv_got[1 - LATE_CHUNK], queries.shape)
    key_grad, value_grad = unpack_last(where, kv_got[LATE_CHUNK], key_grad, value_grad)
    return attended, query_grad, key_grad, value_grad


def solution(mesh):
    spec = P(("outer", "inner"), None)
    return jax.shard_map(
        on_device,
        mesh=mesh,
        in_specs=(spec,) * 4,
        out_specs=(spec,) * 4,
        check_vma=False,
    )
```

```python
import functools
import math

import jax
import jax.numpy as jnp
from jax import lax
from jax.experimental import pallas as pl
from jax.experimental.pallas import tpu as pltpu
from jax.sharding import PartitionSpec as P

HEAD = 128
BLOCK = 128
PARENT = 256
LEVELS = 3
CHUNKS = 2
LATE_CHUNK = 1
INV_ROOT = HEAD**-0.5
TO_LOG2 = INV_ROOT * math.log2(math.e)
MASKED = -1e30
BF = jnp.bfloat16
F32 = jnp.float32


def dot_nt(a, b):
    return lax.dot_general(a, b, (((1,), (1,)), ((), ())), preferred_element_type=F32)


def dot_nn(a, b):
    return jnp.dot(a, b, preferred_element_type=F32)


def order_matrix(inverse):
    row = lax.broadcasted_iota(jnp.int32, (PARENT, PARENT), 0)
    col = lax.broadcasted_iota(jnp.int32, (PARENT, PARENT), 1)
    place, token = (col, row) if inverse else (row, col)
    slab = place // 64
    source = 4 * (place % 64) + 2 * (slab % 2) + slab // 2
    return jnp.where(source == token, 1.0, 0.0).astype(BF)


def pool1(x):
    return ((x[:BLOCK].astype(F32) + x[BLOCK:].astype(F32)) * 0.5).astype(BF)


def pool2(x):
    half = x[:BLOCK].astype(F32) + x[BLOCK:].astype(F32)
    return ((half[:64] + half[64:]) * 0.25).astype(BF)


def pool12(x):
    return ((x[:64].astype(F32) + x[64:].astype(F32)) * 0.5).astype(BF)


def twice(x, axis=0):
    return jnp.concatenate([x, x], axis=axis)


def pack_kernel(own, where, *refs):
    count = 4 if own else 2
    arrays, outs, (held, sems) = refs[:count], refs[count:-2], refs[-2:]
    rows, columns = arrays[0].shape
    half = columns // 2
    width = half // CHUNKS
    side = where[0] if own else 1 - where[0]
    at = pl.ds(pl.multiple_of(side * half, half), half)
    copies = [
        pltpu.make_async_copy(ref.at[:, at], held.at[m], sems.at[m]) for m, ref in enumerate(arrays)
    ]
    for copy in copies:
        copy.start()
    order = order_matrix(False)
    for m in range(count):
        copies[m].wait()
        first = m % 2 * width
        for i in range(rows // PARENT):
            at = slice(i * PARENT, (i + 1) * PARENT)
            x = dot_nn(order, held[m, at, :]).astype(BF)
            for c in range(CHUNKS):
                out = outs[m // 2 * CHUNKS + c]
                out[at, first : first + width] = x[:, c * width : (c + 1) * width]


def pack(own, where, *arrays):
    rows, columns = arrays[0].shape
    count = len(arrays)
    return pl.pallas_call(
        functools.partial(pack_kernel, own),
        in_specs=[smem()] + [pl.BlockSpec(memory_space=pltpu.HBM)] * count,
        out_specs=[vmem()] * (count // 2 * CHUNKS),
        out_shape=[jax.ShapeDtypeStruct((rows, columns // CHUNKS), BF)] * (count // 2 * CHUNKS),
        scratch_shapes=[
            pltpu.VMEM((count, rows, columns // 2), BF),
            pltpu.SemaphoreType.DMA((count,)),
        ],
        compiler_params=small(),
        cost_estimate=light(),
    )(where, *arrays)


def pack_cut_kernel(a, b, *outs):
    order = order_matrix(False)
    width = a.shape[1] // CHUNKS
    for m, ref in enumerate((a, b)):
        for i in range(a.shape[0] // PARENT):
            rows = slice(i * PARENT, (i + 1) * PARENT)
            x = dot_nn(order, ref[rows, :]).astype(BF)
            for c in range(CHUNKS):
                outs[c][rows, m * width : (m + 1) * width] = x[:, c * width : (c + 1) * width]


def pack_cut(side, a, b):
    rows, columns = a.shape
    half = columns // 2
    cut = [lax.dynamic_slice_in_dim(x, side * half, half, 1) for x in (a, b)]
    return pl.pallas_call(
        pack_cut_kernel,
        in_specs=[vmem(), vmem()],
        out_specs=[vmem()] * CHUNKS,
        out_shape=[jax.ShapeDtypeStruct((rows, columns // CHUNKS), BF)] * CHUNKS,
        compiler_params=small(),
        cost_estimate=light(),
    )(*cut)


def smem():
    return pl.BlockSpec(memory_space=pltpu.SMEM)


def vmem():
    return pl.BlockSpec(memory_space=pltpu.VMEM)


def small():
    return pltpu.CompilerParams(vmem_limit_bytes=8 * 1024 * 1024)


def light():
    return pl.CostEstimate(flops=1000, bytes_accessed=1000, transcendentals=0)


def halo_kernel(where, own, got, wide, near):
    def fill(first, second, to_right, to_left):
        to_right[0:256, :] = second[256:512, :]
        to_right[256:384, :] = pool1(second[0:256, :])
        to_right[384:448, :] = pool2(first[0:256, :])
        to_right[448:512, :] = pool2(first[256:512, :])
        to_left[0:256, :] = first[0:256, :]
        to_left[256:384, :] = pool1(first[256:512, :])
        to_left[384:448, :] = pool2(second[0:256, :])
        to_left[448:512, :] = pool2(second[256:512, :])

    for side in range(2):
        for odd in range(2):

            @pl.when((where[0] == side) & (where[3] == odd))
            def _(side=side, odd=odd):
                halves = (own, got) if side == 0 else (got, own)
                fill(*halves, *((near, wide) if odd == 0 else (wide, near)))


def halo(where, own, got):
    shape = jax.ShapeDtypeStruct(own.shape, BF)
    return pl.pallas_call(
        halo_kernel,
        in_specs=[smem(), vmem(), vmem()],
        out_specs=[vmem(), vmem()],
        out_shape=[shape, shape],
        compiler_params=small(),
        cost_estimate=light(),
    )(where, own, got)


def swap64(x):
    return pltpu.roll(x, 64, 1)


def low_lanes(shape):
    return lax.broadcasted_iota(jnp.int32, shape, 1) < 64


def spread64(x, half):
    other = swap64(x)
    low = low_lanes(x.shape)
    return jnp.where(low, x, other) if half == 0 else jnp.where(low, other, x)


def far_forward(k, v_t, q, bias, p_ref):
    k0, k1, k2, k3 = k
    v0, v1, v2, v3 = v_t
    left, right = bias
    outer = dot_nt(jnp.concatenate([k0, k3], axis=0), q)
    first, last = outer[:BLOCK], outer[BLOCK:]
    mid_low = dot_nt(k2, q[:BLOCK])
    mid_high = dot_nt(k1, q[BLOCK:])
    if left is not None:
        first = first + left
        mid_high = mid_high + left
    if right is not None:
        last = last + right
        mid_low = mid_low + right
    mid = jnp.concatenate([mid_low, mid_high], axis=1)
    peak = jnp.max(jnp.maximum(jnp.maximum(first, last), mid), axis=0, keepdims=True)
    parts = [jnp.exp2((x - peak) * TO_LOG2) for x in (first, last, mid)]
    for n, x in enumerate(parts):
        p_ref[n * BLOCK : (n + 1) * BLOCK, :] = x
    total = jnp.sum(parts[0] + parts[1] + parts[2], axis=0, keepdims=True)
    pb = [x.astype(BF) for x in parts]
    mixed = dot_nn(
        jnp.concatenate([v0, v3], axis=1), jnp.concatenate(pb[:2], axis=0)
    ) + jnp.concatenate([dot_nn(v2, pb[2][:, :BLOCK]), dot_nn(v1, pb[2][:, BLOCK:])], axis=1)
    return peak, total, mixed


def far_backward(k_t, v, q, p_ref, factor, g, ec):
    k0, k1, k2, k3 = k_t
    v0, v1, v2, v3 = v
    e_out = p_ref[: 2 * BLOCK, :] * factor
    e_mid = p_ref[2 * BLOCK :, :] * factor
    eb_out, eb_mid = e_out.astype(BF), e_mid.astype(BF)
    p_out = dot_nt(jnp.concatenate([v0, v3], axis=0), g)
    p_mid = jnp.concatenate([dot_nt(v2, g[:BLOCK]), dot_nt(v1, g[BLOCK:])], axis=1)
    r_out = (e_out * (p_out - ec)).astype(BF)
    r_mid = (e_mid * (p_mid - ec)).astype(BF)
    dv03 = dot_nn(eb_out, g)
    dv2 = dot_nn(eb_mid[:, :BLOCK], g[:BLOCK])
    dv1 = dot_nn(eb_mid[:, BLOCK:], g[BLOCK:])
    dk03 = dot_nn(r_out, q)
    dk2 = dot_nn(r_mid[:, :BLOCK], q[:BLOCK])
    dk1 = dot_nn(r_mid[:, BLOCK:], q[BLOCK:])
    dq_t = dot_nn(jnp.concatenate([k0, k3], axis=1), r_out) + jnp.concatenate(
        [dot_nn(k2, r_mid[:, :BLOCK]), dot_nn(k1, r_mid[:, BLOCK:])], axis=1
    )
    return (dk03[:BLOCK], dk1, dk2, dk03[BLOCK:]), (dv03[:BLOCK], dv1, dv2, dv03[BLOCK:]), dq_t


def main_kernel(
    where, kv_own, kv_got, wide_got, near_got, qg_own, qg_got,
    oq_own, oq_far, grad, near_out, wide_out,
    raw, raw_t, one, one_t, two, two_t, qs, gs, p0, p1, p2, acc0, acc1, acc2, oq, halos,
):
    side = where[0]
    odd = where[3]
    halos[1 - odd] = near_got[...]
    halos[odd] = wide_got[...]
    from_left, from_right = halos.at[0], halos.at[1]
    to_left, to_right = halos.at[0], halos.at[1]
    width = kv_own.shape[1] // 2
    left_bias = (1 - where[1]).astype(F32) * MASKED
    right_bias = (1 - where[2]).astype(F32) * MASKED
    own_at = pl.multiple_of(side * 512, 512)
    got_at = pl.multiple_of((1 - side) * 512, 512)
    for h in range(width // HEAD):
        kc = slice(h * HEAD, (h + 1) * HEAD)
        vc = slice(width + h * HEAD, width + (h + 1) * HEAD)
        for n, cols in ((0, kc), (1, vc)):
            raw[n, 0:256, :] = from_left[0:256, cols]
            raw[n, pl.ds(256 + own_at, 512), :] = kv_own[:, cols]
            raw[n, pl.ds(256 + got_at, 512), :] = kv_got[:, cols]
            raw[n, 1280:1536, :] = from_right[0:256, cols]
            one[n, 0:128, :] = from_left[256:384, cols]
            for i in range(6):
                block = pool1(raw[n, i * PARENT : (i + 1) * PARENT, :])
                at = (i + 1) * BLOCK
                one[n, at : at + BLOCK, :] = block
            one[n, 896:1024, :] = from_right[256:384, cols]
            two[n, 0:128, :] = from_left[384:512, cols]
            two[n, 128:192, :] = pool12(one[n, 0:128, :])
            two[n, 192:256, :] = pool2(raw[n, 0:256, :])
            two[n, 256:320, :] = pool2(raw[n, 1280:1536, :])
            two[n, 320:384, :] = pool12(one[n, 896:1024, :])
            two[n, 384:512, :] = from_right[384:512, cols]
            for i in range(6):
                rows = slice(i * PARENT, (i + 1) * PARENT)
                raw_t[n, :, rows] = raw[n, rows, :].T
            for i in range(8):
                rows = slice(i * BLOCK, (i + 1) * BLOCK)
                one_t[n, :, rows] = one[n, rows, :].T
            for i in range(4):
                rows = slice(i * BLOCK, (i + 1) * BLOCK)
                two_t[n, :, rows] = two[n, rows, :].T
        qs[pl.ds(own_at, 512), :] = qg_own[:, kc]
        qs[pl.ds(got_at, 512), :] = qg_got[:, kc]
        gs[pl.ds(own_at, 512), :] = qg_own[:, vc]
        gs[pl.ds(got_at, 512), :] = qg_got[:, vc]

        def blocks(ref, n, which):
            return [ref[n, b * BLOCK : (b + 1) * BLOCK, :] for b in which]

        def blocks_t(ref, n, which):
            return [ref[n, :, b * BLOCK : (b + 1) * BLOCK] for b in which]

        q_parents = [qs[i * PARENT : (i + 1) * PARENT, :] for i in range(4)]
        q1 = [
            jnp.concatenate([pool1(q_parents[2 * j]), pool1(q_parents[2 * j + 1])], axis=0)
            for j in range(2)
        ]
        q2 = jnp.concatenate([pool2(x) for x in q_parents], axis=0)
        which1 = [(0, 1, 4, 5), (2, 3, 6, 7)]
        bias1 = [(left_bias, None), (None, right_bias)]
        which2 = (0, 1, 2, 3)
        far1 = [
            far_forward(
                blocks(one, 0, which1[j]), blocks_t(one_t, 1, which1[j]), q1[j], bias1[j], p1.at[j]
            )
            for j in range(2)
        ]
        far2 = far_forward(
            blocks(two, 0, which2), blocks_t(two_t, 1, which2), q2, (left_bias, right_bias), p2
        )
        acc0[...] = jnp.zeros_like(acc0)
        g1_t, ec1, f1 = [], [], []
        g2_t, ec2, low2 = [], [], []
        dq0 = []
        for i in range(4):
            rows = slice(i * PARENT, i * PARENT + 3 * PARENT)
            q = q_parents[i]
            g = gs[i * PARENT : (i + 1) * PARENT, :]
            s = dot_nt(raw[0, rows, :], q)
            pieces = [s[:PARENT], s[PARENT : 2 * PARENT], s[2 * PARENT :]]
            if i == 0:
                pieces[0] = pieces[0] + left_bias
            if i == 3:
                pieces[2] = pieces[2] + right_bias
            m0 = jnp.max(
                jnp.maximum(jnp.maximum(pieces[0], pieces[1]), pieces[2]), axis=0, keepdims=True
            )
            e = [jnp.exp2((x - m0) * TO_LOG2) for x in pieces]
            for n in range(3):
                p0[n * PARENT : (n + 1) * PARENT, :] = e[n]
            z0 = jnp.sum(e[0] + e[1] + e[2], axis=0, keepdims=True)
            u0 = dot_nn(raw_t[1, :, rows], jnp.concatenate([x.astype(BF) for x in e], axis=0))
            j, half = i // 2, i % 2
            lanes = slice(half * BLOCK, (half + 1) * BLOCK)
            m1, z1, u1 = (x[:, lanes] for x in far1[j])
            lanes2 = slice(j * BLOCK, (j + 1) * BLOCK)
            m2, z2, u2 = (spread64(x[:, lanes2], half) for x in far2)
            m1w, m2w = twice(m1, 1), twice(m2, 1)
            m = jnp.maximum(jnp.maximum(m0, m1w), m2w)
            a0 = jnp.exp2((m0 - m) * TO_LOG2)
            a1 = 2.0 * jnp.exp2((m1w - m) * TO_LOG2)
            a2 = 4.0 * jnp.exp2((m2w - m) * TO_LOG2)
            z = a0 * z0 + a1 * twice(z1, 1) + a2 * twice(z2, 1)
            inv = 1.0 / z
            o = ((a0 * inv) * u0 + (a1 * inv) * twice(u1, 1) + (a2 * inv) * twice(u2, 1)).astype(BF)
            oq[i, 0, h * HEAD : (h + 1) * HEAD, :] = o
            lg = m * TO_LOG2 + jnp.log2(z)
            g_t = g.astype(F32).T
            dr = jnp.sum(o.astype(F32) * g_t, axis=0, keepdims=True)
            lg_a, lg_b = lg[:, :BLOCK], lg[:, BLOCK:]
            g_a, g_b = g_t[:, :BLOCK], g_t[:, BLOCK:]
            dr_a, dr_b = dr[:, :BLOCK], dr[:, BLOCK:]
            low = jnp.minimum(lg_a, lg_b)
            w_a, w_b = jnp.exp2(low - lg_a), jnp.exp2(low - lg_b)
            g1_t.append((w_a * g_a + w_b * g_b).astype(BF))
            ec1.append(w_a * dr_a + w_b * dr_b)
            f1.append(2.0 * jnp.exp2(m1 * TO_LOG2 - low))
            lower = jnp.minimum(low, swap64(low))
            w_a, w_b = jnp.exp2(lower - lg_a), jnp.exp2(lower - lg_b)
            part = w_a * g_a + w_b * g_b
            g2_t.append(part + swap64(part))
            part = w_a * dr_a + w_b * dr_b
            ec2.append(part + swap64(part))
            low2.append(lower)
            f0 = jnp.exp2(m0 * TO_LOG2 - lg)
            products = dot_nt(raw[1, rows, :], g)
            weights = p0[...] * f0
            eb = weights.astype(BF)
            r = (weights * (products - dr)).astype(BF)
            acc0[1, rows, :] += dot_nn(eb, g)
            acc0[0, rows, :] += dot_nn(r, q)
            dq0.append(dot_nn(raw_t[0, :, rows], r))
        acc1[...] = jnp.zeros_like(acc1)
        dq1 = []
        for j in range(2):
            pair = slice(2 * j, 2 * j + 2)
            g1 = jnp.concatenate([x.astype(F32).T.astype(BF) for x in g1_t[pair]], axis=0)
            dk, dv, dq = far_backward(
                blocks_t(one_t, 0, which1[j]), blocks(one, 1, which1[j]), q1[j], p1.at[j],
                jnp.concatenate(f1[pair], axis=1), g1, jnp.concatenate(ec1[pair], axis=1),
            )
            for n, b in enumerate(which1[j]):
                acc1[0, b * BLOCK : (b + 1) * BLOCK, :] += dk[n]
                acc1[1, b * BLOCK : (b + 1) * BLOCK, :] += dv[n]
            dq1.append(dq)

        def joined(parts):
            return jnp.concatenate(
                [
                    jnp.where(low_lanes(parts[0].shape), parts[2 * j], parts[2 * j + 1])
                    for j in range(2)
                ],
                axis=1,
            )

        g2 = joined(g2_t).T.astype(BF)
        f2 = 4.0 * jnp.exp2(far2[0] * TO_LOG2 - joined(low2))
        dk, dv, dq2 = far_backward(
            blocks_t(two_t, 0, which2), blocks(two, 1, which2), q2, p2, f2, g2, joined(ec2)
        )
        for n in range(4):
            acc2[0, n * BLOCK : (n + 1) * BLOCK, :] = dk[n]
            acc2[1, n * BLOCK : (n + 1) * BLOCK, :] = dv[n]
        for i in range(4):
            j, half = i // 2, i % 2
            d1 = dq1[j][:, half * BLOCK : (half + 1) * BLOCK]
            d2 = spread64(dq2[:, j * BLOCK : (j + 1) * BLOCK], half)
            coarse = 0.5 * d1 + 0.25 * d2
            oq[i, 1, h * HEAD : (h + 1) * HEAD, :] = ((dq0[i] + twice(coarse, 1)) * INV_ROOT).astype(BF)
        for n, cols, scale in ((0, kc, INV_ROOT), (1, vc, 1.0)):
            for i in range(4):
                rows = slice((i + 1) * PARENT, (i + 2) * PARENT)
                coarse = acc1[n, (i + 2) * BLOCK : (i + 3) * BLOCK, :] * (0.5 * scale)
                grad[i * PARENT : (i + 1) * PARENT, cols] = acc0[n, rows, :] * scale + twice(coarse)
            far = acc2[n, 128:256, :] * (0.25 * scale)
            mid = acc1[n, 0:256, :] * (0.5 * scale)
            near = acc0[n, 0:256, :] * scale
            to_left[0:256, cols] = (near + twice(mid[128:] + twice(far[64:]))).astype(BF)
            to_left[256:384, cols] = (mid[:128] + twice(far[:64])).astype(BF)
            to_left[384:512, cols] = (acc2[n, 0:128, :] * (0.25 * scale)).astype(BF)
            far = acc2[n, 256:384, :] * (0.25 * scale)
            mid = acc1[n, 768:1024, :] * (0.5 * scale)
            near = acc0[n, 1280:1536, :] * scale
            to_right[0:256, cols] = (near + twice(mid[:128] + twice(far[:64]))).astype(BF)
            to_right[256:384, cols] = (mid[128:] + twice(far[64:])).astype(BF)
            to_right[384:512, cols] = (acc2[n, 384:512, :] * (0.25 * scale)).astype(BF)
    oq_own[...] = oq[pl.ds(side * 2, 2)]
    oq_far[...] = oq[pl.ds((1 - side) * 2, 2)]
    near_out[...] = halos[1 - odd]
    wide_out[...] = halos[odd]


def main(where, kv_own, kv_got, wide_got, near_got, qg_own, qg_got):
    rows, both = kv_own.shape
    width = both // 2
    oq_shape = jax.ShapeDtypeStruct((2, 2, width, PARENT), BF)
    halo_shape = jax.ShapeDtypeStruct((512, both), BF)
    return pl.pallas_call(
        main_kernel,
        in_specs=[smem()] + [vmem()] * 6,
        out_specs=[vmem()] * 5,
        out_shape=[
            oq_shape,
            oq_shape,
            jax.ShapeDtypeStruct((2 * rows, both), F32),
            halo_shape,
            halo_shape,
        ],
        scratch_shapes=[
            pltpu.VMEM((2, 1536, HEAD), BF),
            pltpu.VMEM((2, HEAD, 1536), BF),
            pltpu.VMEM((2, 1024, HEAD), BF),
            pltpu.VMEM((2, HEAD, 1024), BF),
            pltpu.VMEM((2, 512, HEAD), BF),
            pltpu.VMEM((2, HEAD, 512), BF),
            pltpu.VMEM((1024, HEAD), BF),
            pltpu.VMEM((1024, HEAD), BF),
            pltpu.VMEM((768, PARENT), F32),
            pltpu.VMEM((2, 384, PARENT), F32),
            pltpu.VMEM((384, PARENT), F32),
            pltpu.VMEM((2, 1536, HEAD), F32),
            pltpu.VMEM((2, 1024, HEAD), F32),
            pltpu.VMEM((2, 512, HEAD), F32),
            pltpu.VMEM((4, 2, width, PARENT), BF),
            pltpu.VMEM((2, 512, both), BF),
        ],
        compiler_params=pltpu.CompilerParams(vmem_limit_bytes=24 * 1024 * 1024),
        cost_estimate=light(),
    )(where, kv_own, kv_got, wide_got, near_got, qg_own, qg_got)


def join_kernel(where, grad, wide_got, near_got, own, far):
    def fill(first, second, from_left, from_right):
        def parent(i):
            return grad[i * PARENT : (i + 1) * PARENT, :]

        def part(ref, start, stop):
            return ref[start:stop, :].astype(F32)

        first[0:256, :] = (
            parent(0) + part(from_left, 0, 256) + twice(twice(part(from_right, 384, 448)))
        ).astype(BF)
        first[256:512, :] = (
            parent(1) + twice(part(from_left, 256, 384) + twice(part(from_right, 448, 512)))
        ).astype(BF)
        second[0:256, :] = (
            parent(2) + twice(part(from_right, 256, 384) + twice(part(from_left, 384, 448)))
        ).astype(BF)
        second[256:512, :] = (
            parent(3) + part(from_right, 0, 256) + twice(twice(part(from_left, 448, 512)))
        ).astype(BF)

    for side in range(2):
        for odd in range(2):

            @pl.when((where[0] == side) & (where[3] == odd))
            def _(side=side, odd=odd):
                halves = (own, far) if side == 0 else (far, own)
                fill(*halves, *((wide_got, near_got) if odd == 0 else (near_got, wide_got)))


def join(where, grad, wide_got, near_got):
    shape = jax.ShapeDtypeStruct(near_got.shape, BF)
    return pl.pallas_call(
        join_kernel,
        in_specs=[smem(), vmem(), vmem(), vmem()],
        out_specs=[vmem(), vmem()],
        out_shape=[shape, shape],
        compiler_params=small(),
        cost_estimate=light(),
    )(where, grad, wide_got, near_got)


def unpack_rows_kernel(where, *refs):
    ins, (first, second) = refs[:-2], refs[-2:]
    order = order_matrix(True)
    width = ins[0].shape[1] // 2
    side = where[0]
    blocks = [(side * CHUNKS + c, ins[c]) for c in range(CHUNKS)]
    blocks += [((1 - side) * CHUNKS + 1 - LATE_CHUNK, ins[CHUNKS])]
    for block, ref in blocks:
        at = pl.ds(pl.multiple_of(block * width, width), width)
        for i in range(2):
            rows = slice(i * PARENT, (i + 1) * PARENT)
            first[rows, at] = dot_nn(order, ref[rows, :width]).astype(BF)
            second[rows, at] = dot_nn(order, ref[rows, width:]).astype(BF)


def unpack_rows(where, own, got, shape):
    out = jax.ShapeDtypeStruct(shape, BF)
    return pl.pallas_call(
        unpack_rows_kernel,
        in_specs=[smem()] + [vmem()] * (CHUNKS + 1),
        out_specs=[vmem(), vmem()],
        out_shape=[out, out],
        compiler_params=small(),
        cost_estimate=light(),
    )(where, *own, got)


def unpack_last_kernel(where, got, first_in, second_in, first, second, held, sems):
    del first_in, second_in
    order = order_matrix(True)
    width = got.shape[1] // 2
    block = (1 - where[0]) * CHUNKS + LATE_CHUNK
    at = pl.ds(pl.multiple_of(block * width, width), width)
    copies = []
    for m, ref in enumerate((first, second)):
        for i in range(2):
            rows = slice(i * PARENT, (i + 1) * PARENT)
            held[m, rows, :] = dot_nn(order, got[rows, m * width : (m + 1) * width]).astype(BF)
        copies.append(pltpu.make_async_copy(held.at[m], ref.at[:, at], sems.at[m]))
        copies[-1].start()
    for copy in copies:
        copy.wait()


def unpack_last(where, got, first, second):
    out = jax.ShapeDtypeStruct(first.shape, BF)
    hbm = pl.BlockSpec(memory_space=pltpu.HBM)
    return pl.pallas_call(
        unpack_last_kernel,
        in_specs=[smem(), vmem(), hbm, hbm],
        out_specs=[hbm, hbm],
        out_shape=[out, out],
        input_output_aliases={2: 0, 3: 1},
        scratch_shapes=[
            pltpu.VMEM((2, got.shape[0], got.shape[1] // 2), BF),
            pltpu.SemaphoreType.DMA((2,)),
        ],
        compiler_params=small(),
        cost_estimate=light(),
    )(where, got, first, second)


def unpack_columns_kernel(where, *refs):
    ins, (first, second) = refs[:-2], refs[-2:]
    order = order_matrix(True)
    width = ins[0].shape[2]
    for c in range(CHUNKS):
        for ref, side in ((ins[c], where[0]), (ins[CHUNKS + c], 1 - where[0])):
            at = pl.ds(pl.multiple_of((side * CHUNKS + c) * width, width), width)
            for i in range(2):
                rows = slice(i * PARENT, (i + 1) * PARENT)
                first[rows, at] = dot_nt(order, ref[i, 0]).astype(BF)
                second[rows, at] = dot_nt(order, ref[i, 1]).astype(BF)


def unpack_columns(where, own, got, shape):
    out = jax.ShapeDtypeStruct(shape, BF)
    return pl.pallas_call(
        unpack_columns_kernel,
        in_specs=[smem()] + [vmem()] * (2 * CHUNKS),
        out_specs=[vmem(), vmem()],
        out_shape=[out, out],
        compiler_params=small(),
        cost_estimate=light(),
    )(where, *own, *got)


def on_device(queries, key_matrix, value_matrix, cotangent):
    axes = ("outer", "inner")
    count = lax.axis_size("outer") * lax.axis_size("inner")
    device = lax.axis_index("outer") * lax.axis_size("inner") + lax.axis_index("inner")
    pair = device // 2
    where = jnp.stack([device % 2, pair > 0, pair < count // 2 - 1, pair % 2]).astype(jnp.int32)
    across = [(i, i ^ 1) for i in range(count)]
    near_edges = [(i, i ^ 2) for i in range(count) if i ^ 2 < count]
    wide_edges = [(i, i + 2 if i // 2 % 2 else i - 2) for i in range(count)]
    wide_edges = [(i, j) for i, j in wide_edges if 0 <= j < count]

    def swap(x):
        return lax.ppermute(x, axes, across)

    def beside(near, wide):
        wide = lax.ppermute(wide, axes, wide_edges)
        return wide, lax.ppermute(near, axes, near_edges)

    kv_far = pack_cut(1 - device % 2, key_matrix, value_matrix)
    qg_far = pack(False, where, queries, cotangent)
    packed = pack(True, where, key_matrix, value_matrix, queries, cotangent)
    kv, qg = packed[:CHUNKS], packed[CHUNKS:]
    oq_own, oq_got, back = [], [], []
    for c in range(CHUNKS):
        got_kv = swap(kv_far[c])
        wide, near = halo(where, kv[c], got_kv)
        far = qg_far[c]
        if c > 0:
            wide, near, far = lax.optimization_barrier((wide, near, far))
        wide, near = beside(near, wide)
        own, far, grad, near, wide = main(where, kv[c], got_kv, wide, near, qg[c], swap(far))
        oq_own.append(own)
        oq_got.append(swap(far))
        if c > 0:
            oq_got[c - 1], wide, near = lax.optimization_barrier((oq_got[c - 1], wide, near))
        back.append([grad, *beside(near, wide)])
    oq_got[-1], back[-1] = lax.optimization_barrier((oq_got[-1], back[-1]))
    kv_own, kv_got = [], []
    for c in range(CHUNKS):
        own, far = join(where, *back[c])
        kv_own.append(own)
        kv_got.append(swap(far))
    attended, query_grad = unpack_columns(where, oq_own, oq_got, queries.shape)
    key_grad, value_grad = unpack_rows(where, kv_own, kv_got[1 - LATE_CHUNK], queries.shape)
    key_grad, value_grad = unpack_last(where, kv_got[LATE_CHUNK], key_grad, value_grad)
    return attended, query_grad, key_grad, value_grad


def solution(mesh):
    spec = P(("outer", "inner"), None)
    return jax.shard_map(
        on_device,
        mesh=mesh,
        in_specs=(spec,) * 4,
        out_specs=(spec,) * 4,
        check_vma=False,
    )
```

```python
import functools
import math

import jax
import jax.numpy as jnp
from jax import lax
from jax.experimental import pallas as pl
from jax.experimental.pallas import tpu as pltpu
from jax.sharding import PartitionSpec as P

HEAD = 128
BLOCK = 128
PARENT = 256
LEVELS = 3
CHUNKS = 2
LATE_CHUNK = 1
INV_ROOT = HEAD**-0.5
TO_LOG2 = INV_ROOT * math.log2(math.e)
MASKED = -1e30
BF = jnp.bfloat16
F32 = jnp.float32


def dot_nt(a, b):
    return lax.dot_general(a, b, (((1,), (1,)), ((), ())), preferred_element_type=F32)


def dot_nn(a, b):
    return jnp.dot(a, b, preferred_element_type=F32)


def order_matrix(inverse):
    row = lax.broadcasted_iota(jnp.int32, (PARENT, PARENT), 0)
    col = lax.broadcasted_iota(jnp.int32, (PARENT, PARENT), 1)
    place, token = (col, row) if inverse else (row, col)
    slab = place // 64
    source = 4 * (place % 64) + 2 * (slab % 2) + slab // 2
    return jnp.where(source == token, 1.0, 0.0).astype(BF)


def pool1(x):
    return ((x[:BLOCK].astype(F32) + x[BLOCK:].astype(F32)) * 0.5).astype(BF)


def pool2(x):
    half = x[:BLOCK].astype(F32) + x[BLOCK:].astype(F32)
    return ((half[:64] + half[64:]) * 0.25).astype(BF)


def pool12(x):
    return ((x[:64].astype(F32) + x[64:].astype(F32)) * 0.5).astype(BF)


def twice(x, axis=0):
    return jnp.concatenate([x, x], axis=axis)


def pack_kernel(own, where, *refs):
    count = 4 if own else 2
    arrays, outs, (held, sems) = refs[:count], refs[count:-2], refs[-2:]
    rows, columns = arrays[0].shape
    half = columns // 2
    width = half // CHUNKS
    side = where[0] if own else 1 - where[0]
    at = pl.ds(pl.multiple_of(side * half, half), half)
    copies = [
        pltpu.make_async_copy(ref.at[:, at], held.at[m], sems.at[m]) for m, ref in enumerate(arrays)
    ]
    for copy in copies:
        copy.start()
    order = order_matrix(False)
    for m in range(count):
        copies[m].wait()
        first = m % 2 * width
        for i in range(rows // PARENT):
            at = slice(i * PARENT, (i + 1) * PARENT)
            x = dot_nn(order, held[m, at, :]).astype(BF)
            for c in range(CHUNKS):
                out = outs[m // 2 * CHUNKS + c]
                out[at, first : first + width] = x[:, c * width : (c + 1) * width]


def pack(own, where, *arrays):
    rows, columns = arrays[0].shape
    count = len(arrays)
    return pl.pallas_call(
        functools.partial(pack_kernel, own),
        in_specs=[smem()] + [pl.BlockSpec(memory_space=pltpu.HBM)] * count,
        out_specs=[vmem()] * (count // 2 * CHUNKS),
        out_shape=[jax.ShapeDtypeStruct((rows, columns // CHUNKS), BF)] * (count // 2 * CHUNKS),
        scratch_shapes=[
            pltpu.VMEM((count, rows, columns // 2), BF),
            pltpu.SemaphoreType.DMA((count,)),
        ],
        compiler_params=small(),
        cost_estimate=light(),
    )(where, *arrays)


def pack_cut_kernel(a, b, out):
    order = order_matrix(False)
    width = a.shape[1]
    for m, ref in enumerate((a, b)):
        for i in range(a.shape[0] // PARENT):
            rows = slice(i * PARENT, (i + 1) * PARENT)
            out[rows, m * width : (m + 1) * width] = dot_nn(order, ref[rows, :]).astype(BF)


def pack_cut(side, chunk, a, b):
    rows, columns = a.shape
    width = columns // 2 // CHUNKS
    cut = [lax.dynamic_slice_in_dim(x, (side * CHUNKS + chunk) * width, width, 1) for x in (a, b)]
    return pl.pallas_call(
        pack_cut_kernel,
        in_specs=[vmem(), vmem()],
        out_specs=vmem(),
        out_shape=jax.ShapeDtypeStruct((rows, 2 * width), BF),
        compiler_params=small(),
        cost_estimate=light(),
    )(*cut)


def smem():
    return pl.BlockSpec(memory_space=pltpu.SMEM)


def vmem():
    return pl.BlockSpec(memory_space=pltpu.VMEM)


def small():
    return pltpu.CompilerParams(vmem_limit_bytes=8 * 1024 * 1024)


def light():
    return pl.CostEstimate(flops=1000, bytes_accessed=1000, transcendentals=0)


def halo_kernel(where, own, got, near, wide):
    def fill(first, second, to_right, to_left):
        to_right[0:256, :] = second[256:512, :]
        to_right[256:384, :] = pool1(second[0:256, :])
        to_right[384:448, :] = pool2(first[0:256, :])
        to_right[448:512, :] = pool2(first[256:512, :])
        to_left[0:256, :] = first[0:256, :]
        to_left[256:384, :] = pool1(first[256:512, :])
        to_left[384:448, :] = pool2(second[0:256, :])
        to_left[448:512, :] = pool2(second[256:512, :])

    for side in range(2):
        for odd in range(2):

            @pl.when((where[0] == side) & (where[3] == odd))
            def _(side=side, odd=odd):
                halves = (own, got) if side == 0 else (got, own)
                fill(*halves, *((near, wide) if odd == 0 else (wide, near)))


def halo(where, own, got):
    shape = jax.ShapeDtypeStruct(own.shape, BF)
    return pl.pallas_call(
        halo_kernel,
        in_specs=[smem(), vmem(), vmem()],
        out_specs=[vmem(), vmem()],
        out_shape=[shape, shape],
        compiler_params=small(),
        cost_estimate=light(),
    )(where, own, got)


def swap64(x):
    return pltpu.roll(x, 64, 1)


def low_lanes(shape):
    return lax.broadcasted_iota(jnp.int32, shape, 1) < 64


def spread64(x, half):
    other = swap64(x)
    low = low_lanes(x.shape)
    return jnp.where(low, x, other) if half == 0 else jnp.where(low, other, x)


def far_forward(k, v_t, q, bias, p_ref):
    k0, k1, k2, k3 = k
    v0, v1, v2, v3 = v_t
    left, right = bias
    outer = dot_nt(jnp.concatenate([k0, k3], axis=0), q)
    first, last = outer[:BLOCK], outer[BLOCK:]
    mid_low = dot_nt(k2, q[:BLOCK])
    mid_high = dot_nt(k1, q[BLOCK:])
    if left is not None:
        first = first + left
        mid_high = mid_high + left
    if right is not None:
        last = last + right
        mid_low = mid_low + right
    mid = jnp.concatenate([mid_low, mid_high], axis=1)
    peak = jnp.max(jnp.maximum(jnp.maximum(first, last), mid), axis=0, keepdims=True)
    parts = [jnp.exp2((x - peak) * TO_LOG2) for x in (first, last, mid)]
    for n, x in enumerate(parts):
        p_ref[n * BLOCK : (n + 1) * BLOCK, :] = x
    total = jnp.sum(parts[0] + parts[1] + parts[2], axis=0, keepdims=True)
    pb = [x.astype(BF) for x in parts]
    mixed = dot_nn(
        jnp.concatenate([v0, v3], axis=1), jnp.concatenate(pb[:2], axis=0)
    ) + jnp.concatenate([dot_nn(v2, pb[2][:, :BLOCK]), dot_nn(v1, pb[2][:, BLOCK:])], axis=1)
    return peak, total, mixed


def far_backward(k_t, v, q, p_ref, factor, g, ec):
    k0, k1, k2, k3 = k_t
    v0, v1, v2, v3 = v
    e_out = p_ref[: 2 * BLOCK, :] * factor
    e_mid = p_ref[2 * BLOCK :, :] * factor
    eb_out, eb_mid = e_out.astype(BF), e_mid.astype(BF)
    p_out = dot_nt(jnp.concatenate([v0, v3], axis=0), g)
    p_mid = jnp.concatenate([dot_nt(v2, g[:BLOCK]), dot_nt(v1, g[BLOCK:])], axis=1)
    r_out = (e_out * (p_out - ec)).astype(BF)
    r_mid = (e_mid * (p_mid - ec)).astype(BF)
    dv03 = dot_nn(eb_out, g)
    dv2 = dot_nn(eb_mid[:, :BLOCK], g[:BLOCK])
    dv1 = dot_nn(eb_mid[:, BLOCK:], g[BLOCK:])
    dk03 = dot_nn(r_out, q)
    dk2 = dot_nn(r_mid[:, :BLOCK], q[:BLOCK])
    dk1 = dot_nn(r_mid[:, BLOCK:], q[BLOCK:])
    dq_t = dot_nn(jnp.concatenate([k0, k3], axis=1), r_out) + jnp.concatenate(
        [dot_nn(k2, r_mid[:, :BLOCK]), dot_nn(k1, r_mid[:, BLOCK:])], axis=1
    )
    return (dk03[:BLOCK], dk1, dk2, dk03[BLOCK:]), (dv03[:BLOCK], dv1, dv2, dv03[BLOCK:]), dq_t


def main_kernel(qg_first, where, kv_own, kv_got, *refs):
    if qg_first:
        refs = (*refs[2:4], *refs[:2], *refs[4:])
    one_chunk(where, kv_own, kv_got, *refs)


def one_chunk(
    where, kv_own, kv_got, near_got, wide_got, qg_own, qg_got,
    oq_own, oq_far, grad, near_out, wide_out,
    raw, raw_t, one, one_t, two, two_t, qs, gs, p0, p1, p2, acc0, acc1, acc2, oq, halos,
):
    side = where[0]
    odd = where[3]
    halos[1 - odd] = near_got[...]
    halos[odd] = wide_got[...]
    from_left, from_right = halos.at[0], halos.at[1]
    to_left, to_right = halos.at[0], halos.at[1]
    width = kv_own.shape[1] // 2
    left_bias = (1 - where[1]).astype(F32) * MASKED
    right_bias = (1 - where[2]).astype(F32) * MASKED
    own_at = pl.multiple_of(side * 512, 512)
    got_at = pl.multiple_of((1 - side) * 512, 512)
    for h in range(width // HEAD):
        kc = slice(h * HEAD, (h + 1) * HEAD)
        vc = slice(width + h * HEAD, width + (h + 1) * HEAD)
        for n, cols in ((0, kc), (1, vc)):
            raw[n, 0:256, :] = from_left[0:256, cols]
            raw[n, pl.ds(256 + own_at, 512), :] = kv_own[:, cols]
            raw[n, pl.ds(256 + got_at, 512), :] = kv_got[:, cols]
            raw[n, 1280:1536, :] = from_right[0:256, cols]
            one[n, 0:128, :] = from_left[256:384, cols]
            for i in range(6):
                block = pool1(raw[n, i * PARENT : (i + 1) * PARENT, :])
                at = (i + 1) * BLOCK
                one[n, at : at + BLOCK, :] = block
            one[n, 896:1024, :] = from_right[256:384, cols]
            two[n, 0:128, :] = from_left[384:512, cols]
            two[n, 128:192, :] = pool12(one[n, 0:128, :])
            two[n, 192:256, :] = pool2(raw[n, 0:256, :])
            two[n, 256:320, :] = pool2(raw[n, 1280:1536, :])
            two[n, 320:384, :] = pool12(one[n, 896:1024, :])
            two[n, 384:512, :] = from_right[384:512, cols]
            for i in range(6):
                rows = slice(i * PARENT, (i + 1) * PARENT)
                raw_t[n, :, rows] = raw[n, rows, :].T
            for i in range(8):
                rows = slice(i * BLOCK, (i + 1) * BLOCK)
                one_t[n, :, rows] = one[n, rows, :].T
            for i in range(4):
                rows = slice(i * BLOCK, (i + 1) * BLOCK)
                two_t[n, :, rows] = two[n, rows, :].T
        qs[pl.ds(own_at, 512), :] = qg_own[:, kc]
        qs[pl.ds(got_at, 512), :] = qg_got[:, kc]
        gs[pl.ds(own_at, 512), :] = qg_own[:, vc]
        gs[pl.ds(got_at, 512), :] = qg_got[:, vc]

        def blocks(ref, n, which):
            return [ref[n, b * BLOCK : (b + 1) * BLOCK, :] for b in which]

        def blocks_t(ref, n, which):
            return [ref[n, :, b * BLOCK : (b + 1) * BLOCK] for b in which]

        q_parents = [qs[i * PARENT : (i + 1) * PARENT, :] for i in range(4)]
        q1 = [
            jnp.concatenate([pool1(q_parents[2 * j]), pool1(q_parents[2 * j + 1])], axis=0)
            for j in range(2)
        ]
        q2 = jnp.concatenate([pool2(x) for x in q_parents], axis=0)
        which1 = [(0, 1, 4, 5), (2, 3, 6, 7)]
        bias1 = [(left_bias, None), (None, right_bias)]
        which2 = (0, 1, 2, 3)
        far1 = [
            far_forward(
                blocks(one, 0, which1[j]), blocks_t(one_t, 1, which1[j]), q1[j], bias1[j], p1.at[j]
            )
            for j in range(2)
        ]
        far2 = far_forward(
            blocks(two, 0, which2), blocks_t(two_t, 1, which2), q2, (left_bias, right_bias), p2
        )
        acc0[...] = jnp.zeros_like(acc0)
        g1_t, ec1, f1 = [], [], []
        g2_t, ec2, low2 = [], [], []
        dq0 = []
        for i in range(4):
            rows = slice(i * PARENT, i * PARENT + 3 * PARENT)
            q = q_parents[i]
            g = gs[i * PARENT : (i + 1) * PARENT, :]
            s = dot_nt(raw[0, rows, :], q)
            pieces = [s[:PARENT], s[PARENT : 2 * PARENT], s[2 * PARENT :]]
            if i == 0:
                pieces[0] = pieces[0] + left_bias
            if i == 3:
                pieces[2] = pieces[2] + right_bias
            m0 = jnp.max(
                jnp.maximum(jnp.maximum(pieces[0], pieces[1]), pieces[2]), axis=0, keepdims=True
            )
            e = [jnp.exp2((x - m0) * TO_LOG2) for x in pieces]
            for n in range(3):
                p0[n * PARENT : (n + 1) * PARENT, :] = e[n]
            z0 = jnp.sum(e[0] + e[1] + e[2], axis=0, keepdims=True)
            u0 = dot_nn(raw_t[1, :, rows], jnp.concatenate([x.astype(BF) for x in e], axis=0))
            j, half = i // 2, i % 2
            lanes = slice(half * BLOCK, (half + 1) * BLOCK)
            m1, z1, u1 = (x[:, lanes] for x in far1[j])
            lanes2 = slice(j * BLOCK, (j + 1) * BLOCK)
            m2, z2, u2 = (spread64(x[:, lanes2], half) for x in far2)
            m1w, m2w = twice(m1, 1), twice(m2, 1)
            m = jnp.maximum(jnp.maximum(m0, m1w), m2w)
            a0 = jnp.exp2((m0 - m) * TO_LOG2)
            a1 = 2.0 * jnp.exp2((m1w - m) * TO_LOG2)
            a2 = 4.0 * jnp.exp2((m2w - m) * TO_LOG2)
            z = a0 * z0 + a1 * twice(z1, 1) + a2 * twice(z2, 1)
            inv = 1.0 / z
            o = ((a0 * inv) * u0 + (a1 * inv) * twice(u1, 1) + (a2 * inv) * twice(u2, 1)).astype(BF)
            oq[i, 0, h * HEAD : (h + 1) * HEAD, :] = o
            lg = m * TO_LOG2 + jnp.log2(z)
            g_t = g.astype(F32).T
            dr = jnp.sum(o.astype(F32) * g_t, axis=0, keepdims=True)
            lg_a, lg_b = lg[:, :BLOCK], lg[:, BLOCK:]
            g_a, g_b = g_t[:, :BLOCK], g_t[:, BLOCK:]
            dr_a, dr_b = dr[:, :BLOCK], dr[:, BLOCK:]
            low = jnp.minimum(lg_a, lg_b)
            w_a, w_b = jnp.exp2(low - lg_a), jnp.exp2(low - lg_b)
            g1_t.append((w_a * g_a + w_b * g_b).astype(BF))
            ec1.append(w_a * dr_a + w_b * dr_b)
            f1.append(2.0 * jnp.exp2(m1 * TO_LOG2 - low))
            lower = jnp.minimum(low, swap64(low))
            w_a, w_b = jnp.exp2(lower - lg_a), jnp.exp2(lower - lg_b)
            part = w_a * g_a + w_b * g_b
            g2_t.append(part + swap64(part))
            part = w_a * dr_a + w_b * dr_b
            ec2.append(part + swap64(part))
            low2.append(lower)
            f0 = jnp.exp2(m0 * TO_LOG2 - lg)
            products = dot_nt(raw[1, rows, :], g)
            weights = p0[...] * f0
            eb = weights.astype(BF)
            r = (weights * (products - dr)).astype(BF)
            acc0[1, rows, :] += dot_nn(eb, g)
            acc0[0, rows, :] += dot_nn(r, q)
            dq0.append(dot_nn(raw_t[0, :, rows], r))
        acc1[...] = jnp.zeros_like(acc1)
        dq1 = []
        for j in range(2):
            pair = slice(2 * j, 2 * j + 2)
            g1 = jnp.concatenate([x.astype(F32).T.astype(BF) for x in g1_t[pair]], axis=0)
            dk, dv, dq = far_backward(
                blocks_t(one_t, 0, which1[j]), blocks(one, 1, which1[j]), q1[j], p1.at[j],
                jnp.concatenate(f1[pair], axis=1), g1, jnp.concatenate(ec1[pair], axis=1),
            )
            for n, b in enumerate(which1[j]):
                acc1[0, b * BLOCK : (b + 1) * BLOCK, :] += dk[n]
                acc1[1, b * BLOCK : (b + 1) * BLOCK, :] += dv[n]
            dq1.append(dq)

        def joined(parts):
            return jnp.concatenate(
                [
                    jnp.where(low_lanes(parts[0].shape), parts[2 * j], parts[2 * j + 1])
                    for j in range(2)
                ],
                axis=1,
            )

        g2 = joined(g2_t).T.astype(BF)
        f2 = 4.0 * jnp.exp2(far2[0] * TO_LOG2 - joined(low2))
        dk, dv, dq2 = far_backward(
            blocks_t(two_t, 0, which2), blocks(two, 1, which2), q2, p2, f2, g2, joined(ec2)
        )
        for n in range(4):
            acc2[0, n * BLOCK : (n + 1) * BLOCK, :] = dk[n]
            acc2[1, n * BLOCK : (n + 1) * BLOCK, :] = dv[n]
        for i in range(4):
            j, half = i // 2, i % 2
            d1 = dq1[j][:, half * BLOCK : (half + 1) * BLOCK]
            d2 = spread64(dq2[:, j * BLOCK : (j + 1) * BLOCK], half)
            coarse = 0.5 * d1 + 0.25 * d2
            oq[i, 1, h * HEAD : (h + 1) * HEAD, :] = ((dq0[i] + twice(coarse, 1)) * INV_ROOT).astype(BF)
        for n, cols, scale in ((0, kc, INV_ROOT), (1, vc, 1.0)):
            for i in range(4):
                rows = slice((i + 1) * PARENT, (i + 2) * PARENT)
                coarse = acc1[n, (i + 2) * BLOCK : (i + 3) * BLOCK, :] * (0.5 * scale)
                grad[i * PARENT : (i + 1) * PARENT, cols] = acc0[n, rows, :] * scale + twice(coarse)
            far = acc2[n, 128:256, :] * (0.25 * scale)
            mid = acc1[n, 0:256, :] * (0.5 * scale)
            near = acc0[n, 0:256, :] * scale
            to_left[0:256, cols] = (near + twice(mid[128:] + twice(far[64:]))).astype(BF)
            to_left[256:384, cols] = (mid[:128] + twice(far[:64])).astype(BF)
            to_left[384:512, cols] = (acc2[n, 0:128, :] * (0.25 * scale)).astype(BF)
            far = acc2[n, 256:384, :] * (0.25 * scale)
            mid = acc1[n, 768:1024, :] * (0.5 * scale)
            near = acc0[n, 1280:1536, :] * scale
            to_right[0:256, cols] = (near + twice(mid[:128] + twice(far[:64]))).astype(BF)
            to_right[256:384, cols] = (mid[128:] + twice(far[64:])).astype(BF)
            to_right[384:512, cols] = (acc2[n, 384:512, :] * (0.25 * scale)).astype(BF)
    oq_own[...] = oq[pl.ds(side * 2, 2)]
    oq_far[...] = oq[pl.ds((1 - side) * 2, 2)]
    near_out[...] = halos[1 - odd]
    wide_out[...] = halos[odd]


def main(where, kv_own, kv_got, near_got, wide_got, qg_own, qg_got, qg_first):
    rows, both = kv_own.shape
    width = both // 2
    oq_shape = jax.ShapeDtypeStruct((2, 2, width, PARENT), BF)
    halo_shape = jax.ShapeDtypeStruct((512, both), BF)
    operands = [kv_own, kv_got, near_got, wide_got, qg_own, qg_got]
    if qg_first:
        operands = operands[:2] + operands[4:] + operands[2:4]
    return pl.pallas_call(
        functools.partial(main_kernel, qg_first),
        in_specs=[smem()] + [vmem()] * 6,
        out_specs=[vmem()] * 5,
        out_shape=[
            oq_shape,
            oq_shape,
            jax.ShapeDtypeStruct((2 * rows, both), F32),
            halo_shape,
            halo_shape,
        ],
        scratch_shapes=[
            pltpu.VMEM((2, 1536, HEAD), BF),
            pltpu.VMEM((2, HEAD, 1536), BF),
            pltpu.VMEM((2, 1024, HEAD), BF),
            pltpu.VMEM((2, HEAD, 1024), BF),
            pltpu.VMEM((2, 512, HEAD), BF),
            pltpu.VMEM((2, HEAD, 512), BF),
            pltpu.VMEM((1024, HEAD), BF),
            pltpu.VMEM((1024, HEAD), BF),
            pltpu.VMEM((768, PARENT), F32),
            pltpu.VMEM((2, 384, PARENT), F32),
            pltpu.VMEM((384, PARENT), F32),
            pltpu.VMEM((2, 1536, HEAD), F32),
            pltpu.VMEM((2, 1024, HEAD), F32),
            pltpu.VMEM((2, 512, HEAD), F32),
            pltpu.VMEM((4, 2, width, PARENT), BF),
            pltpu.VMEM((2, 512, both), BF),
        ],
        compiler_params=pltpu.CompilerParams(vmem_limit_bytes=24 * 1024 * 1024),
        cost_estimate=light(),
    )(where, *operands)


def join_kernel(where, grad, near_got, wide_got, own, far):
    def fill(first, second, from_left, from_right):
        def parent(i):
            return grad[i * PARENT : (i + 1) * PARENT, :]

        def part(ref, start, stop):
            return ref[start:stop, :].astype(F32)

        first[0:256, :] = (
            parent(0) + part(from_left, 0, 256) + twice(twice(part(from_right, 384, 448)))
        ).astype(BF)
        first[256:512, :] = (
            parent(1) + twice(part(from_left, 256, 384) + twice(part(from_right, 448, 512)))
        ).astype(BF)
        second[0:256, :] = (
            parent(2) + twice(part(from_right, 256, 384) + twice(part(from_left, 384, 448)))
        ).astype(BF)
        second[256:512, :] = (
            parent(3) + part(from_right, 0, 256) + twice(twice(part(from_left, 448, 512)))
        ).astype(BF)

    for side in range(2):
        for odd in range(2):

            @pl.when((where[0] == side) & (where[3] == odd))
            def _(side=side, odd=odd):
                halves = (own, far) if side == 0 else (far, own)
                fill(*halves, *((wide_got, near_got) if odd == 0 else (near_got, wide_got)))


def join(where, grad, near_got, wide_got):
    shape = jax.ShapeDtypeStruct(near_got.shape, BF)
    return pl.pallas_call(
        join_kernel,
        in_specs=[smem(), vmem(), vmem(), vmem()],
        out_specs=[vmem(), vmem()],
        out_shape=[shape, shape],
        compiler_params=small(),
        cost_estimate=light(),
    )(where, grad, near_got, wide_got)


def unpack_rows_kernel(where, *refs):
    ins, (first, second) = refs[:-2], refs[-2:]
    order = order_matrix(True)
    width = ins[0].shape[1] // 2
    side = where[0]
    blocks = [(side * CHUNKS + c, ins[c]) for c in range(CHUNKS)]
    blocks += [((1 - side) * CHUNKS + 1 - LATE_CHUNK, ins[CHUNKS])]
    for block, ref in blocks:
        at = pl.ds(pl.multiple_of(block * width, width), width)
        for i in range(2):
            rows = slice(i * PARENT, (i + 1) * PARENT)
            first[rows, at] = dot_nn(order, ref[rows, :width]).astype(BF)
            second[rows, at] = dot_nn(order, ref[rows, width:]).astype(BF)


def unpack_rows(where, own, got, shape):
    out = jax.ShapeDtypeStruct(shape, BF)
    return pl.pallas_call(
        unpack_rows_kernel,
        in_specs=[smem()] + [vmem()] * (CHUNKS + 1),
        out_specs=[vmem(), vmem()],
        out_shape=[out, out],
        compiler_params=small(),
        cost_estimate=light(),
    )(where, *own, got)


def unpack_last_kernel(where, got, first_in, second_in, first, second, held, sems):
    del first_in, second_in
    order = order_matrix(True)
    width = got.shape[1] // 2
    block = (1 - where[0]) * CHUNKS + LATE_CHUNK
    at = pl.ds(pl.multiple_of(block * width, width), width)
    copies = []
    for m, ref in enumerate((first, second)):
        for i in range(2):
            rows = slice(i * PARENT, (i + 1) * PARENT)
            held[m, rows, :] = dot_nn(order, got[rows, m * width : (m + 1) * width]).astype(BF)
        copies.append(pltpu.make_async_copy(held.at[m], ref.at[:, at], sems.at[m]))
        copies[-1].start()
    for copy in copies:
        copy.wait()


def unpack_last(where, got, first, second):
    out = jax.ShapeDtypeStruct(first.shape, BF)
    hbm = pl.BlockSpec(memory_space=pltpu.HBM)
    return pl.pallas_call(
        unpack_last_kernel,
        in_specs=[smem(), vmem(), hbm, hbm],
        out_specs=[hbm, hbm],
        out_shape=[out, out],
        input_output_aliases={2: 0, 3: 1},
        scratch_shapes=[
            pltpu.VMEM((2, got.shape[0], got.shape[1] // 2), BF),
            pltpu.SemaphoreType.DMA((2,)),
        ],
        compiler_params=small(),
        cost_estimate=light(),
    )(where, got, first, second)


def unpack_columns_kernel(where, *refs):
    ins, (first, second) = refs[:-2], refs[-2:]
    order = order_matrix(True)
    width = ins[0].shape[2]
    for c in range(CHUNKS):
        for ref, side in ((ins[c], where[0]), (ins[CHUNKS + c], 1 - where[0])):
            at = pl.ds(pl.multiple_of((side * CHUNKS + c) * width, width), width)
            for i in range(2):
                rows = slice(i * PARENT, (i + 1) * PARENT)
                first[rows, at] = dot_nt(order, ref[i, 0]).astype(BF)
                second[rows, at] = dot_nt(order, ref[i, 1]).astype(BF)


def unpack_columns(where, own, got, shape):
    out = jax.ShapeDtypeStruct(shape, BF)
    return pl.pallas_call(
        unpack_columns_kernel,
        in_specs=[smem()] + [vmem()] * (2 * CHUNKS),
        out_specs=[vmem(), vmem()],
        out_shape=[out, out],
        compiler_params=small(),
        cost_estimate=light(),
    )(where, *own, *got)


def on_device(queries, key_matrix, value_matrix, cotangent):
    axes = ("outer", "inner")
    count = lax.axis_size("outer") * lax.axis_size("inner")
    device = lax.axis_index("outer") * lax.axis_size("inner") + lax.axis_index("inner")
    pair = device // 2
    where = jnp.stack([device % 2, pair > 0, pair < count // 2 - 1, pair % 2]).astype(jnp.int32)
    across = [(i, i ^ 1) for i in range(count)]
    near_edges = [(i, i ^ 2) for i in range(count) if i ^ 2 < count]
    wide_edges = [(i, i + 2 if i // 2 % 2 else i - 2) for i in range(count)]
    wide_edges = [(i, j) for i, j in wide_edges if 0 <= j < count]

    def swap(x):
        return lax.ppermute(x, axes, across)

    def beside(near, wide):
        near = lax.ppermute(near, axes, near_edges)
        return near, lax.ppermute(wide, axes, wide_edges)

    kv_far = [pack_cut(1 - device % 2, 0, key_matrix, value_matrix)]
    for c in range(1, CHUNKS):
        later, kv_far[0] = lax.optimization_barrier(((key_matrix, value_matrix), kv_far[0]))
        kv_far.append(pack_cut(1 - device % 2, c, *later))
    qg_far = pack(False, where, queries, cotangent)
    packed = pack(True, where, key_matrix, value_matrix, queries, cotangent)
    kv, qg = packed[:CHUNKS], packed[CHUNKS:]
    oq_own, oq_got, back = [], [], []
    for c in range(CHUNKS):
        got_kv = swap(kv_far[c])
        near, wide = halo(where, kv[c], got_kv)
        far = qg_far[c]
        if c > 0:
            near, wide, far = lax.optimization_barrier((near, wide, far))
        near, wide = beside(near, wide)
        own, far, grad, near, wide = main(where, kv[c], got_kv, near, wide, qg[c], swap(far), c == 0)
        oq_own.append(own)
        oq_got.append(swap(far))
        if c > 0:
            oq_got[c - 1], near, wide = lax.optimization_barrier((oq_got[c - 1], near, wide))
        back.append([grad, *beside(near, wide)])
    oq_got[-1], back[-1] = lax.optimization_barrier((oq_got[-1], back[-1]))
    kv_own, kv_got = [], []
    for c in range(CHUNKS):
        own, far = join(where, *back[c])
        kv_own.append(own)
        kv_got.append(swap(far))
    attended, query_grad = unpack_columns(where, oq_own, oq_got, queries.shape)
    key_grad, value_grad = unpack_rows(where, kv_own, kv_got[1 - LATE_CHUNK], queries.shape)
    key_grad, value_grad = unpack_last(where, kv_got[LATE_CHUNK], key_grad, value_grad)
    return attended, query_grad, key_grad, value_grad


def solution(mesh):
    spec = P(("outer", "inner"), None)
    return jax.shard_map(
        on_device,
        mesh=mesh,
        in_specs=(spec,) * 4,
        out_specs=(spec,) * 4,
        check_vma=False,
    )
```

```python
import functools
import math

import jax
import jax.numpy as jnp
from jax import lax
from jax.experimental import pallas as pl
from jax.experimental.pallas import tpu as pltpu
from jax.sharding import PartitionSpec as P

HEAD = 128
BLOCK = 128
PARENT = 256
LEVELS = 3
CHUNKS = 2
LATE_CHUNK = 1
INV_ROOT = HEAD**-0.5
TO_LOG2 = INV_ROOT * math.log2(math.e)
MASKED = -1e30
BF = jnp.bfloat16
F32 = jnp.float32


def dot_nt(a, b):
    return lax.dot_general(a, b, (((1,), (1,)), ((), ())), preferred_element_type=F32)


def dot_nn(a, b):
    return jnp.dot(a, b, preferred_element_type=F32)


def order_matrix(inverse):
    row = lax.broadcasted_iota(jnp.int32, (PARENT, PARENT), 0)
    col = lax.broadcasted_iota(jnp.int32, (PARENT, PARENT), 1)
    place, token = (col, row) if inverse else (row, col)
    slab = place // 64
    source = 4 * (place % 64) + 2 * (slab % 2) + slab // 2
    return jnp.where(source == token, 1.0, 0.0).astype(BF)


def pool1(x):
    return ((x[:BLOCK].astype(F32) + x[BLOCK:].astype(F32)) * 0.5).astype(BF)


def pool2(x):
    half = x[:BLOCK].astype(F32) + x[BLOCK:].astype(F32)
    return ((half[:64] + half[64:]) * 0.25).astype(BF)


def pool12(x):
    return ((x[:64].astype(F32) + x[64:].astype(F32)) * 0.5).astype(BF)


def twice(x, axis=0):
    return jnp.concatenate([x, x], axis=axis)


def pack_kernel(own, where, *refs):
    count = 4 if own else 2
    arrays, outs, (held, sems) = refs[:count], refs[count:-2], refs[-2:]
    rows, columns = arrays[0].shape
    half = columns // 2
    width = half // CHUNKS
    side = where[0] if own else 1 - where[0]
    at = pl.ds(pl.multiple_of(side * half, half), half)
    copies = [
        pltpu.make_async_copy(ref.at[:, at], held.at[m], sems.at[m]) for m, ref in enumerate(arrays)
    ]
    for copy in copies:
        copy.start()
    order = order_matrix(False)
    for m in range(count):
        copies[m].wait()
        first = m % 2 * width
        for i in range(rows // PARENT):
            at = slice(i * PARENT, (i + 1) * PARENT)
            x = dot_nn(order, held[m, at, :]).astype(BF)
            for c in range(CHUNKS):
                out = outs[m // 2 * CHUNKS + c]
                out[at, first : first + width] = x[:, c * width : (c + 1) * width]


def pack(own, where, *arrays):
    rows, columns = arrays[0].shape
    count = len(arrays)
    return pl.pallas_call(
        functools.partial(pack_kernel, own),
        in_specs=[smem()] + [pl.BlockSpec(memory_space=pltpu.HBM)] * count,
        out_specs=[vmem()] * (count // 2 * CHUNKS),
        out_shape=[jax.ShapeDtypeStruct((rows, columns // CHUNKS), BF)] * (count // 2 * CHUNKS),
        scratch_shapes=[
            pltpu.VMEM((count, rows, columns // 2), BF),
            pltpu.SemaphoreType.DMA((count,)),
        ],
        compiler_params=small(),
        cost_estimate=light(),
    )(where, *arrays)


def pack_cut_kernel(a, b, out):
    order = order_matrix(False)
    width = a.shape[1]
    for m, ref in enumerate((a, b)):
        for i in range(a.shape[0] // PARENT):
            rows = slice(i * PARENT, (i + 1) * PARENT)
            out[rows, m * width : (m + 1) * width] = dot_nn(order, ref[rows, :]).astype(BF)


def pack_cut(side, chunk, a, b):
    rows, columns = a.shape
    width = columns // 2 // CHUNKS
    cut = [lax.dynamic_slice_in_dim(x, (side * CHUNKS + chunk) * width, width, 1) for x in (a, b)]
    return pl.pallas_call(
        pack_cut_kernel,
        in_specs=[vmem(), vmem()],
        out_specs=vmem(),
        out_shape=jax.ShapeDtypeStruct((rows, 2 * width), BF),
        compiler_params=small(),
        cost_estimate=light(),
    )(*cut)


def smem():
    return pl.BlockSpec(memory_space=pltpu.SMEM)


def vmem():
    return pl.BlockSpec(memory_space=pltpu.VMEM)


def small():
    return pltpu.CompilerParams(vmem_limit_bytes=8 * 1024 * 1024)


def light():
    return pl.CostEstimate(flops=1000, bytes_accessed=1000, transcendentals=0)


def halo_kernel(where, own, got, near, wide):
    def fill(first, second, to_right, to_left):
        to_right[0:256, :] = second[256:512, :]
        to_right[256:384, :] = pool1(second[0:256, :])
        to_right[384:448, :] = pool2(first[0:256, :])
        to_right[448:512, :] = pool2(first[256:512, :])
        to_left[0:256, :] = first[0:256, :]
        to_left[256:384, :] = pool1(first[256:512, :])
        to_left[384:448, :] = pool2(second[0:256, :])
        to_left[448:512, :] = pool2(second[256:512, :])

    for side in range(2):
        for odd in range(2):

            @pl.when((where[0] == side) & (where[3] == odd))
            def _(side=side, odd=odd):
                halves = (own, got) if side == 0 else (got, own)
                fill(*halves, *((near, wide) if odd == 0 else (wide, near)))


def halo(where, own, got):
    shape = jax.ShapeDtypeStruct(own.shape, BF)
    return pl.pallas_call(
        halo_kernel,
        in_specs=[smem(), vmem(), vmem()],
        out_specs=[vmem(), vmem()],
        out_shape=[shape, shape],
        compiler_params=small(),
        cost_estimate=light(),
    )(where, own, got)


def swap64(x):
    return pltpu.roll(x, 64, 1)


def low_lanes(shape):
    return lax.broadcasted_iota(jnp.int32, shape, 1) < 64


def spread64(x, half):
    other = swap64(x)
    low = low_lanes(x.shape)
    return jnp.where(low, x, other) if half == 0 else jnp.where(low, other, x)


def far_forward(k, v_t, q, bias, p_ref):
    k0, k1, k2, k3 = k
    v0, v1, v2, v3 = v_t
    left, right = bias
    outer = dot_nt(jnp.concatenate([k0, k3], axis=0), q)
    first, last = outer[:BLOCK], outer[BLOCK:]
    mid_low = dot_nt(k2, q[:BLOCK])
    mid_high = dot_nt(k1, q[BLOCK:])
    if left is not None:
        first = first + left
        mid_high = mid_high + left
    if right is not None:
        last = last + right
        mid_low = mid_low + right
    mid = jnp.concatenate([mid_low, mid_high], axis=1)
    peak = jnp.max(jnp.maximum(jnp.maximum(first, last), mid), axis=0, keepdims=True)
    parts = [jnp.exp2((x - peak) * TO_LOG2) for x in (first, last, mid)]
    for n, x in enumerate(parts):
        p_ref[n * BLOCK : (n + 1) * BLOCK, :] = x
    total = jnp.sum(parts[0] + parts[1] + parts[2], axis=0, keepdims=True)
    pb = [x.astype(BF) for x in parts]
    mixed = dot_nn(
        jnp.concatenate([v0, v3], axis=1), jnp.concatenate(pb[:2], axis=0)
    ) + jnp.concatenate([dot_nn(v2, pb[2][:, :BLOCK]), dot_nn(v1, pb[2][:, BLOCK:])], axis=1)
    return peak, total, mixed


def far_backward(k_t, v, q, p_ref, factor, g, ec):
    k0, k1, k2, k3 = k_t
    v0, v1, v2, v3 = v
    e_out = p_ref[: 2 * BLOCK, :] * factor
    e_mid = p_ref[2 * BLOCK :, :] * factor
    eb_out, eb_mid = e_out.astype(BF), e_mid.astype(BF)
    p_out = dot_nt(jnp.concatenate([v0, v3], axis=0), g)
    p_mid = jnp.concatenate([dot_nt(v2, g[:BLOCK]), dot_nt(v1, g[BLOCK:])], axis=1)
    r_out = (e_out * (p_out - ec)).astype(BF)
    r_mid = (e_mid * (p_mid - ec)).astype(BF)
    dv03 = dot_nn(eb_out, g)
    dv2 = dot_nn(eb_mid[:, :BLOCK], g[:BLOCK])
    dv1 = dot_nn(eb_mid[:, BLOCK:], g[BLOCK:])
    dk03 = dot_nn(r_out, q)
    dk2 = dot_nn(r_mid[:, :BLOCK], q[:BLOCK])
    dk1 = dot_nn(r_mid[:, BLOCK:], q[BLOCK:])
    dq_t = dot_nn(jnp.concatenate([k0, k3], axis=1), r_out) + jnp.concatenate(
        [dot_nn(k2, r_mid[:, :BLOCK]), dot_nn(k1, r_mid[:, BLOCK:])], axis=1
    )
    return (dk03[:BLOCK], dk1, dk2, dk03[BLOCK:]), (dv03[:BLOCK], dv1, dv2, dv03[BLOCK:]), dq_t


def main_kernel(qg_first, where, kv_own, kv_got, *refs):
    if qg_first:
        refs = (*refs[2:4], *refs[:2], *refs[4:])
    one_chunk(where, kv_own, kv_got, *refs)


def one_chunk(
    where, kv_own, kv_got, near_got, wide_got, qg_own, qg_got,
    oq_own, oq_far, grad, near_out, wide_out,
    raw, raw_t, one, one_t, two, two_t, qs, gs, p0, p1, p2, acc0_t, acc0, acc1, acc2, oq, halos,
):
    side = where[0]
    odd = where[3]
    halos[1 - odd] = near_got[...]
    halos[odd] = wide_got[...]
    from_left, from_right = halos.at[0], halos.at[1]
    to_left, to_right = halos.at[0], halos.at[1]
    width = kv_own.shape[1] // 2
    left_bias = (1 - where[1]).astype(F32) * MASKED
    right_bias = (1 - where[2]).astype(F32) * MASKED
    own_at = pl.multiple_of(side * 512, 512)
    got_at = pl.multiple_of((1 - side) * 512, 512)
    for h in range(width // HEAD):
        kc = slice(h * HEAD, (h + 1) * HEAD)
        vc = slice(width + h * HEAD, width + (h + 1) * HEAD)
        for n, cols in ((0, kc), (1, vc)):
            raw[n, 0:256, :] = from_left[0:256, cols]
            raw[n, pl.ds(256 + own_at, 512), :] = kv_own[:, cols]
            raw[n, pl.ds(256 + got_at, 512), :] = kv_got[:, cols]
            raw[n, 1280:1536, :] = from_right[0:256, cols]
            one[n, 0:128, :] = from_left[256:384, cols]
            for i in range(6):
                block = pool1(raw[n, i * PARENT : (i + 1) * PARENT, :])
                at = (i + 1) * BLOCK
                one[n, at : at + BLOCK, :] = block
            one[n, 896:1024, :] = from_right[256:384, cols]
            two[n, 0:128, :] = from_left[384:512, cols]
            two[n, 128:192, :] = pool12(one[n, 0:128, :])
            two[n, 192:256, :] = pool2(raw[n, 0:256, :])
            two[n, 256:320, :] = pool2(raw[n, 1280:1536, :])
            two[n, 320:384, :] = pool12(one[n, 896:1024, :])
            two[n, 384:512, :] = from_right[384:512, cols]
            for i in range(6):
                rows = slice(i * PARENT, (i + 1) * PARENT)
                raw_t[n, :, rows] = raw[n, rows, :].T
            for i in range(8):
                rows = slice(i * BLOCK, (i + 1) * BLOCK)
                one_t[n, :, rows] = one[n, rows, :].T
            for i in range(4):
                rows = slice(i * BLOCK, (i + 1) * BLOCK)
                two_t[n, :, rows] = two[n, rows, :].T
        qs[pl.ds(own_at, 512), :] = qg_own[:, kc]
        qs[pl.ds(got_at, 512), :] = qg_got[:, kc]
        gs[pl.ds(own_at, 512), :] = qg_own[:, vc]
        gs[pl.ds(got_at, 512), :] = qg_got[:, vc]

        def blocks(ref, n, which):
            return [ref[n, b * BLOCK : (b + 1) * BLOCK, :] for b in which]

        def blocks_t(ref, n, which):
            return [ref[n, :, b * BLOCK : (b + 1) * BLOCK] for b in which]

        q_parents = [qs[i * PARENT : (i + 1) * PARENT, :] for i in range(4)]
        q1 = [
            jnp.concatenate([pool1(q_parents[2 * j]), pool1(q_parents[2 * j + 1])], axis=0)
            for j in range(2)
        ]
        q2 = jnp.concatenate([pool2(x) for x in q_parents], axis=0)
        which1 = [(0, 1, 4, 5), (2, 3, 6, 7)]
        bias1 = [(left_bias, None), (None, right_bias)]
        which2 = (0, 1, 2, 3)
        far1 = [
            far_forward(
                blocks(one, 0, which1[j]), blocks_t(one_t, 1, which1[j]), q1[j], bias1[j], p1.at[j]
            )
            for j in range(2)
        ]
        far2 = far_forward(
            blocks(two, 0, which2), blocks_t(two_t, 1, which2), q2, (left_bias, right_bias), p2
        )
        acc0_t[...] = jnp.zeros_like(acc0_t)
        g1_t, ec1, f1 = [], [], []
        g2_t, ec2, low2 = [], [], []
        dq0 = []
        for i in range(4):
            rows = slice(i * PARENT, i * PARENT + 3 * PARENT)
            q = q_parents[i]
            g = gs[i * PARENT : (i + 1) * PARENT, :]
            s = dot_nt(raw[0, rows, :], q)
            pieces = [s[:PARENT], s[PARENT : 2 * PARENT], s[2 * PARENT :]]
            if i == 0:
                pieces[0] = pieces[0] + left_bias
            if i == 3:
                pieces[2] = pieces[2] + right_bias
            m0 = jnp.max(
                jnp.maximum(jnp.maximum(pieces[0], pieces[1]), pieces[2]), axis=0, keepdims=True
            )
            e = [jnp.exp2((x - m0) * TO_LOG2) for x in pieces]
            for n in range(3):
                p0[n * PARENT : (n + 1) * PARENT, :] = e[n]
            z0 = jnp.sum(e[0] + e[1] + e[2], axis=0, keepdims=True)
            u0 = dot_nn(raw_t[1, :, rows], jnp.concatenate([x.astype(BF) for x in e], axis=0))
            j, half = i // 2, i % 2
            lanes = slice(half * BLOCK, (half + 1) * BLOCK)
            m1, z1, u1 = (x[:, lanes] for x in far1[j])
            lanes2 = slice(j * BLOCK, (j + 1) * BLOCK)
            m2, z2, u2 = (spread64(x[:, lanes2], half) for x in far2)
            m1w, m2w = twice(m1, 1), twice(m2, 1)
            m = jnp.maximum(jnp.maximum(m0, m1w), m2w)
            a0 = jnp.exp2((m0 - m) * TO_LOG2)
            a1 = 2.0 * jnp.exp2((m1w - m) * TO_LOG2)
            a2 = 4.0 * jnp.exp2((m2w - m) * TO_LOG2)
            z = a0 * z0 + a1 * twice(z1, 1) + a2 * twice(z2, 1)
            inv = 1.0 / z
            o = ((a0 * inv) * u0 + (a1 * inv) * twice(u1, 1) + (a2 * inv) * twice(u2, 1)).astype(BF)
            oq[i, 0, h * HEAD : (h + 1) * HEAD, :] = o
            lg = m * TO_LOG2 + jnp.log2(z)
            g_t = g.astype(F32).T
            dr = jnp.sum(o.astype(F32) * g_t, axis=0, keepdims=True)
            lg_a, lg_b = lg[:, :BLOCK], lg[:, BLOCK:]
            g_a, g_b = g_t[:, :BLOCK], g_t[:, BLOCK:]
            dr_a, dr_b = dr[:, :BLOCK], dr[:, BLOCK:]
            low = jnp.minimum(lg_a, lg_b)
            w_a, w_b = jnp.exp2(low - lg_a), jnp.exp2(low - lg_b)
            g1_t.append((w_a * g_a + w_b * g_b).astype(BF))
            ec1.append(w_a * dr_a + w_b * dr_b)
            f1.append(2.0 * jnp.exp2(m1 * TO_LOG2 - low))
            lower = jnp.minimum(low, swap64(low))
            w_a, w_b = jnp.exp2(lower - lg_a), jnp.exp2(lower - lg_b)
            part = w_a * g_a + w_b * g_b
            g2_t.append(part + swap64(part))
            part = w_a * dr_a + w_b * dr_b
            ec2.append(part + swap64(part))
            low2.append(lower)
            f0 = jnp.exp2(m0 * TO_LOG2 - lg)
            products = dot_nt(raw[1, rows, :], g)
            weights = p0[...] * f0
            eb = weights.astype(BF)
            r = (weights * (products - dr)).astype(BF)
            acc0_t[1, :, rows] += dot_nt(g_t.astype(BF), eb)
            acc0_t[0, :, rows] += dot_nt(q.T, r)
            dq0.append(dot_nn(raw_t[0, :, rows], r))
        for n in range(2):
            acc0[n] = acc0_t[n].T
        acc1[...] = jnp.zeros_like(acc1)
        dq1 = []
        for j in range(2):
            pair = slice(2 * j, 2 * j + 2)
            g1 = jnp.concatenate([x.astype(F32).T.astype(BF) for x in g1_t[pair]], axis=0)
            dk, dv, dq = far_backward(
                blocks_t(one_t, 0, which1[j]), blocks(one, 1, which1[j]), q1[j], p1.at[j],
                jnp.concatenate(f1[pair], axis=1), g1, jnp.concatenate(ec1[pair], axis=1),
            )
            for n, b in enumerate(which1[j]):
                acc1[0, b * BLOCK : (b + 1) * BLOCK, :] += dk[n]
                acc1[1, b * BLOCK : (b + 1) * BLOCK, :] += dv[n]
            dq1.append(dq)

        def joined(parts):
            return jnp.concatenate(
                [
                    jnp.where(low_lanes(parts[0].shape), parts[2 * j], parts[2 * j + 1])
                    for j in range(2)
                ],
                axis=1,
            )

        g2 = joined(g2_t).T.astype(BF)
        f2 = 4.0 * jnp.exp2(far2[0] * TO_LOG2 - joined(low2))
        dk, dv, dq2 = far_backward(
            blocks_t(two_t, 0, which2), blocks(two, 1, which2), q2, p2, f2, g2, joined(ec2)
        )
        for n in range(4):
            acc2[0, n * BLOCK : (n + 1) * BLOCK, :] = dk[n]
            acc2[1, n * BLOCK : (n + 1) * BLOCK, :] = dv[n]
        for i in range(4):
            j, half = i // 2, i % 2
            d1 = dq1[j][:, half * BLOCK : (half + 1) * BLOCK]
            d2 = spread64(dq2[:, j * BLOCK : (j + 1) * BLOCK], half)
            coarse = 0.5 * d1 + 0.25 * d2
            oq[i, 1, h * HEAD : (h + 1) * HEAD, :] = ((dq0[i] + twice(coarse, 1)) * INV_ROOT).astype(BF)
        for n, cols, scale in ((0, kc, INV_ROOT), (1, vc, 1.0)):
            for i in range(4):
                rows = slice((i + 1) * PARENT, (i + 2) * PARENT)
                coarse = acc1[n, (i + 2) * BLOCK : (i + 3) * BLOCK, :] * (0.5 * scale)
                grad[i * PARENT : (i + 1) * PARENT, cols] = acc0[n, rows, :] * scale + twice(coarse)
            far = acc2[n, 128:256, :] * (0.25 * scale)
            mid = acc1[n, 0:256, :] * (0.5 * scale)
            near = acc0[n, 0:256, :] * scale
            to_left[0:256, cols] = (near + twice(mid[128:] + twice(far[64:]))).astype(BF)
            to_left[256:384, cols] = (mid[:128] + twice(far[:64])).astype(BF)
            to_left[384:512, cols] = (acc2[n, 0:128, :] * (0.25 * scale)).astype(BF)
            far = acc2[n, 256:384, :] * (0.25 * scale)
            mid = acc1[n, 768:1024, :] * (0.5 * scale)
            near = acc0[n, 1280:1536, :] * scale
            to_right[0:256, cols] = (near + twice(mid[:128] + twice(far[:64]))).astype(BF)
            to_right[256:384, cols] = (mid[128:] + twice(far[64:])).astype(BF)
            to_right[384:512, cols] = (acc2[n, 384:512, :] * (0.25 * scale)).astype(BF)
    oq_own[...] = oq[pl.ds(side * 2, 2)]
    oq_far[...] = oq[pl.ds((1 - side) * 2, 2)]
    near_out[...] = halos[1 - odd]
    wide_out[...] = halos[odd]


def main(where, kv_own, kv_got, near_got, wide_got, qg_own, qg_got, qg_first):
    rows, both = kv_own.shape
    width = both // 2
    oq_shape = jax.ShapeDtypeStruct((2, 2, width, PARENT), BF)
    halo_shape = jax.ShapeDtypeStruct((512, both), BF)
    operands = [kv_own, kv_got, near_got, wide_got, qg_own, qg_got]
    if qg_first:
        operands = operands[:2] + operands[4:] + operands[2:4]
    return pl.pallas_call(
        functools.partial(main_kernel, qg_first),
        in_specs=[smem()] + [vmem()] * 6,
        out_specs=[vmem()] * 5,
        out_shape=[
            oq_shape,
            oq_shape,
            jax.ShapeDtypeStruct((2 * rows, both), F32),
            halo_shape,
            halo_shape,
        ],
        scratch_shapes=[
            pltpu.VMEM((2, 1536, HEAD), BF),
            pltpu.VMEM((2, HEAD, 1536), BF),
            pltpu.VMEM((2, 1024, HEAD), BF),
            pltpu.VMEM((2, HEAD, 1024), BF),
            pltpu.VMEM((2, 512, HEAD), BF),
            pltpu.VMEM((2, HEAD, 512), BF),
            pltpu.VMEM((1024, HEAD), BF),
            pltpu.VMEM((1024, HEAD), BF),
            pltpu.VMEM((768, PARENT), F32),
            pltpu.VMEM((2, 384, PARENT), F32),
            pltpu.VMEM((384, PARENT), F32),
            pltpu.VMEM((2, HEAD, 1536), F32),
            pltpu.VMEM((2, 1536, HEAD), F32),
            pltpu.VMEM((2, 1024, HEAD), F32),
            pltpu.VMEM((2, 512, HEAD), F32),
            pltpu.VMEM((4, 2, width, PARENT), BF),
            pltpu.VMEM((2, 512, both), BF),
        ],
        compiler_params=pltpu.CompilerParams(vmem_limit_bytes=24 * 1024 * 1024),
        cost_estimate=light(),
    )(where, *operands)


def join_kernel(where, grad, near_got, wide_got, own, far):
    def fill(first, second, from_left, from_right):
        def parent(i):
            return grad[i * PARENT : (i + 1) * PARENT, :]

        def part(ref, start, stop):
            return ref[start:stop, :].astype(F32)

        first[0:256, :] = (
            parent(0) + part(from_left, 0, 256) + twice(twice(part(from_right, 384, 448)))
        ).astype(BF)
        first[256:512, :] = (
            parent(1) + twice(part(from_left, 256, 384) + twice(part(from_right, 448, 512)))
        ).astype(BF)
        second[0:256, :] = (
            parent(2) + twice(part(from_right, 256, 384) + twice(part(from_left, 384, 448)))
        ).astype(BF)
        second[256:512, :] = (
            parent(3) + part(from_right, 0, 256) + twice(twice(part(from_left, 448, 512)))
        ).astype(BF)

    for side in range(2):
        for odd in range(2):

            @pl.when((where[0] == side) & (where[3] == odd))
            def _(side=side, odd=odd):
                halves = (own, far) if side == 0 else (far, own)
                fill(*halves, *((wide_got, near_got) if odd == 0 else (near_got, wide_got)))


def join(where, grad, near_got, wide_got):
    shape = jax.ShapeDtypeStruct(near_got.shape, BF)
    return pl.pallas_call(
        join_kernel,
        in_specs=[smem(), vmem(), vmem(), vmem()],
        out_specs=[vmem(), vmem()],
        out_shape=[shape, shape],
        compiler_params=small(),
        cost_estimate=light(),
    )(where, grad, near_got, wide_got)


def unpack_rows_kernel(where, *refs):
    ins, (first, second) = refs[:-2], refs[-2:]
    order = order_matrix(True)
    width = ins[0].shape[1] // 2
    side = where[0]
    blocks = [(side * CHUNKS + c, ins[c]) for c in range(CHUNKS)]
    blocks += [((1 - side) * CHUNKS + 1 - LATE_CHUNK, ins[CHUNKS])]
    for block, ref in blocks:
        at = pl.ds(pl.multiple_of(block * width, width), width)
        for i in range(2):
            rows = slice(i * PARENT, (i + 1) * PARENT)
            first[rows, at] = dot_nn(order, ref[rows, :width]).astype(BF)
            second[rows, at] = dot_nn(order, ref[rows, width:]).astype(BF)


def unpack_rows(where, own, got, shape):
    out = jax.ShapeDtypeStruct(shape, BF)
    return pl.pallas_call(
        unpack_rows_kernel,
        in_specs=[smem()] + [vmem()] * (CHUNKS + 1),
        out_specs=[vmem(), vmem()],
        out_shape=[out, out],
        compiler_params=small(),
        cost_estimate=light(),
    )(where, *own, got)


def unpack_last_kernel(where, got, first_in, second_in, first, second, held, sems):
    del first_in, second_in
    order = order_matrix(True)
    width = got.shape[1] // 2
    block = (1 - where[0]) * CHUNKS + LATE_CHUNK
    at = pl.ds(pl.multiple_of(block * width, width), width)
    copies = []
    for m, ref in enumerate((first, second)):
        for i in range(2):
            rows = slice(i * PARENT, (i + 1) * PARENT)
            held[m, rows, :] = dot_nn(order, got[rows, m * width : (m + 1) * width]).astype(BF)
        copies.append(pltpu.make_async_copy(held.at[m], ref.at[:, at], sems.at[m]))
        copies[-1].start()
    for copy in copies:
        copy.wait()


def unpack_last(where, got, first, second):
    out = jax.ShapeDtypeStruct(first.shape, BF)
    hbm = pl.BlockSpec(memory_space=pltpu.HBM)
    return pl.pallas_call(
        unpack_last_kernel,
        in_specs=[smem(), vmem(), hbm, hbm],
        out_specs=[hbm, hbm],
        out_shape=[out, out],
        input_output_aliases={2: 0, 3: 1},
        scratch_shapes=[
            pltpu.VMEM((2, got.shape[0], got.shape[1] // 2), BF),
            pltpu.SemaphoreType.DMA((2,)),
        ],
        compiler_params=small(),
        cost_estimate=light(),
    )(where, got, first, second)


def unpack_columns_kernel(where, *refs):
    ins, (first, second) = refs[:-2], refs[-2:]
    order = order_matrix(True)
    width = ins[0].shape[2]
    for c in range(CHUNKS):
        for ref, side in ((ins[c], where[0]), (ins[CHUNKS + c], 1 - where[0])):
            at = pl.ds(pl.multiple_of((side * CHUNKS + c) * width, width), width)
            for i in range(2):
                rows = slice(i * PARENT, (i + 1) * PARENT)
                first[rows, at] = dot_nt(order, ref[i, 0]).astype(BF)
                second[rows, at] = dot_nt(order, ref[i, 1]).astype(BF)


def unpack_columns(where, own, got, shape):
    out = jax.ShapeDtypeStruct(shape, BF)
    return pl.pallas_call(
        unpack_columns_kernel,
        in_specs=[smem()] + [vmem()] * (2 * CHUNKS),
        out_specs=[vmem(), vmem()],
        out_shape=[out, out],
        compiler_params=small(),
        cost_estimate=light(),
    )(where, *own, *got)


def on_device(queries, key_matrix, value_matrix, cotangent):
    axes = ("outer", "inner")
    count = lax.axis_size("outer") * lax.axis_size("inner")
    device = lax.axis_index("outer") * lax.axis_size("inner") + lax.axis_index("inner")
    pair = device // 2
    where = jnp.stack([device % 2, pair > 0, pair < count // 2 - 1, pair % 2]).astype(jnp.int32)
    across = [(i, i ^ 1) for i in range(count)]
    near_edges = [(i, i ^ 2) for i in range(count) if i ^ 2 < count]
    wide_edges = [(i, i + 2 if i // 2 % 2 else i - 2) for i in range(count)]
    wide_edges = [(i, j) for i, j in wide_edges if 0 <= j < count]

    def swap(x):
        return lax.ppermute(x, axes, across)

    def beside(near, wide):
        near = lax.ppermute(near, axes, near_edges)
        return near, lax.ppermute(wide, axes, wide_edges)

    kv_far = [pack_cut(1 - device % 2, 0, key_matrix, value_matrix)]
    for c in range(1, CHUNKS):
        later, kv_far[0] = lax.optimization_barrier(((key_matrix, value_matrix), kv_far[0]))
        kv_far.append(pack_cut(1 - device % 2, c, *later))
    qg_far = pack(False, where, queries, cotangent)
    packed = pack(True, where, key_matrix, value_matrix, queries, cotangent)
    kv, qg = packed[:CHUNKS], packed[CHUNKS:]
    oq_own, oq_got, back = [], [], []
    for c in range(CHUNKS):
        got_kv = swap(kv_far[c])
        near, wide = halo(where, kv[c], got_kv)
        far = qg_far[c]
        if c > 0:
            near, wide, far = lax.optimization_barrier((near, wide, far))
        near, wide = beside(near, wide)
        own, far, grad, near, wide = main(where, kv[c], got_kv, near, wide, qg[c], swap(far), c == 0)
        oq_own.append(own)
        oq_got.append(swap(far))
        if c > 0:
            oq_got[c - 1], near, wide = lax.optimization_barrier((oq_got[c - 1], near, wide))
        back.append([grad, *beside(near, wide)])
    oq_got[-1], back[-1] = lax.optimization_barrier((oq_got[-1], back[-1]))
    kv_own, kv_got = [], []
    for c in range(CHUNKS):
        own, far = join(where, *back[c])
        kv_own.append(own)
        kv_got.append(swap(far))
    attended, query_grad = unpack_columns(where, oq_own, oq_got, queries.shape)
    key_grad, value_grad = unpack_rows(where, kv_own, kv_got[1 - LATE_CHUNK], queries.shape)
    key_grad, value_grad = unpack_last(where, kv_got[LATE_CHUNK], key_grad, value_grad)
    return attended, query_grad, key_grad, value_grad


def solution(mesh):
    spec = P(("outer", "inner"), None)
    return jax.shard_map(
        on_device,
        mesh=mesh,
        in_specs=(spec,) * 4,
        out_specs=(spec,) * 4,
        check_vma=False,
    )
```

```python
import functools
import math

import jax
import jax.numpy as jnp
from jax import lax
from jax.experimental import pallas as pl
from jax.experimental.pallas import tpu as pltpu
from jax.sharding import PartitionSpec as P

HEAD = 128
BLOCK = 128
PARENT = 256
LEVELS = 3
CHUNKS = 2
LATE_CHUNK = 1
INV_ROOT = HEAD**-0.5
TO_LOG2 = INV_ROOT * math.log2(math.e)
MASKED = -1e30
BF = jnp.bfloat16
F32 = jnp.float32


def dot_nt(a, b):
    return lax.dot_general(a, b, (((1,), (1,)), ((), ())), preferred_element_type=F32)


def dot_nn(a, b):
    return jnp.dot(a, b, preferred_element_type=F32)


def order_matrix(inverse):
    row = lax.broadcasted_iota(jnp.int32, (PARENT, PARENT), 0)
    col = lax.broadcasted_iota(jnp.int32, (PARENT, PARENT), 1)
    place, token = (col, row) if inverse else (row, col)
    slab = place // 64
    source = 4 * (place % 64) + 2 * (slab % 2) + slab // 2
    return jnp.where(source == token, 1.0, 0.0).astype(BF)


def pool1(x):
    return ((x[:BLOCK].astype(F32) + x[BLOCK:].astype(F32)) * 0.5).astype(BF)


def pool2(x):
    half = x[:BLOCK].astype(F32) + x[BLOCK:].astype(F32)
    return ((half[:64] + half[64:]) * 0.25).astype(BF)


def pool12(x):
    return ((x[:64].astype(F32) + x[64:].astype(F32)) * 0.5).astype(BF)


def twice(x, axis=0):
    return jnp.concatenate([x, x], axis=axis)


def pack_kernel(own, where, *refs):
    count = 4 if own else 2
    arrays, outs, (held, sems) = refs[:count], refs[count:-2], refs[-2:]
    rows, columns = arrays[0].shape
    half = columns // 2
    width = half // CHUNKS
    side = where[0] if own else 1 - where[0]
    at = pl.ds(pl.multiple_of(side * half, half), half)
    copies = [
        pltpu.make_async_copy(ref.at[:, at], held.at[m], sems.at[m]) for m, ref in enumerate(arrays)
    ]
    for copy in copies:
        copy.start()
    order = order_matrix(False)
    for m in range(count):
        copies[m].wait()
        first = m % 2 * width
        for i in range(rows // PARENT):
            at = slice(i * PARENT, (i + 1) * PARENT)
            x = dot_nn(order, held[m, at, :]).astype(BF)
            for c in range(CHUNKS):
                out = outs[m // 2 * CHUNKS + c]
                out[at, first : first + width] = x[:, c * width : (c + 1) * width]


def pack(own, where, *arrays):
    rows, columns = arrays[0].shape
    count = len(arrays)
    return pl.pallas_call(
        functools.partial(pack_kernel, own),
        in_specs=[smem()] + [pl.BlockSpec(memory_space=pltpu.HBM)] * count,
        out_specs=[vmem()] * (count // 2 * CHUNKS),
        out_shape=[jax.ShapeDtypeStruct((rows, columns // CHUNKS), BF)] * (count // 2 * CHUNKS),
        scratch_shapes=[
            pltpu.VMEM((count, rows, columns // 2), BF),
            pltpu.SemaphoreType.DMA((count,)),
        ],
        compiler_params=small(),
        cost_estimate=light(),
    )(where, *arrays)


def pack_cut_kernel(a, b, out):
    order = order_matrix(False)
    width = a.shape[1]
    for m, ref in enumerate((a, b)):
        for i in range(a.shape[0] // PARENT):
            rows = slice(i * PARENT, (i + 1) * PARENT)
            out[rows, m * width : (m + 1) * width] = dot_nn(order, ref[rows, :]).astype(BF)


def pack_cut(side, chunk, a, b):
    rows, columns = a.shape
    width = columns // 2 // CHUNKS
    cut = [lax.dynamic_slice_in_dim(x, (side * CHUNKS + chunk) * width, width, 1) for x in (a, b)]
    return pl.pallas_call(
        pack_cut_kernel,
        in_specs=[vmem(), vmem()],
        out_specs=vmem(),
        out_shape=jax.ShapeDtypeStruct((rows, 2 * width), BF),
        compiler_params=small(),
        cost_estimate=light(),
    )(*cut)


def smem():
    return pl.BlockSpec(memory_space=pltpu.SMEM)


def vmem():
    return pl.BlockSpec(memory_space=pltpu.VMEM)


def small():
    return pltpu.CompilerParams(vmem_limit_bytes=8 * 1024 * 1024)


def light():
    return pl.CostEstimate(flops=1000, bytes_accessed=1000, transcendentals=0)


def halo_kernel(where, own, got, near, wide):
    def fill(first, second, to_right, to_left):
        to_right[0:256, :] = second[256:512, :]
        to_right[256:384, :] = pool1(second[0:256, :])
        to_right[384:448, :] = pool2(first[0:256, :])
        to_right[448:512, :] = pool2(first[256:512, :])
        to_left[0:256, :] = first[0:256, :]
        to_left[256:384, :] = pool1(first[256:512, :])
        to_left[384:448, :] = pool2(second[0:256, :])
        to_left[448:512, :] = pool2(second[256:512, :])

    for side in range(2):
        for odd in range(2):

            @pl.when((where[0] == side) & (where[3] == odd))
            def _(side=side, odd=odd):
                halves = (own, got) if side == 0 else (got, own)
                fill(*halves, *((near, wide) if odd == 0 else (wide, near)))


def halo(where, own, got):
    shape = jax.ShapeDtypeStruct(own.shape, BF)
    return pl.pallas_call(
        halo_kernel,
        in_specs=[smem(), vmem(), vmem()],
        out_specs=[vmem(), vmem()],
        out_shape=[shape, shape],
        compiler_params=small(),
        cost_estimate=light(),
    )(where, own, got)


def swap64(x):
    return pltpu.roll(x, 64, 1)


def low_lanes(shape):
    return lax.broadcasted_iota(jnp.int32, shape, 1) < 64


def spread64(x, half):
    other = swap64(x)
    low = low_lanes(x.shape)
    return jnp.where(low, x, other) if half == 0 else jnp.where(low, other, x)


def far_forward(k, v_t, q, bias, p_ref):
    k0, k1, k2, k3 = k
    v0, v1, v2, v3 = v_t
    left, right = bias
    outer = dot_nt(jnp.concatenate([k0, k3], axis=0), q)
    first, last = outer[:BLOCK], outer[BLOCK:]
    mid_low = dot_nt(k2, q[:BLOCK])
    mid_high = dot_nt(k1, q[BLOCK:])
    if left is not None:
        first = first + left
        mid_high = mid_high + left
    if right is not None:
        last = last + right
        mid_low = mid_low + right
    mid = jnp.concatenate([mid_low, mid_high], axis=1)
    peak = jnp.max(jnp.maximum(jnp.maximum(first, last), mid), axis=0, keepdims=True)
    parts = [jnp.exp2((x - peak) * TO_LOG2) for x in (first, last, mid)]
    for n, x in enumerate(parts):
        p_ref[n * BLOCK : (n + 1) * BLOCK, :] = x
    total = jnp.sum(parts[0] + parts[1] + parts[2], axis=0, keepdims=True)
    pb = [x.astype(BF) for x in parts]
    mixed = dot_nn(
        jnp.concatenate([v0, v3], axis=1), jnp.concatenate(pb[:2], axis=0)
    ) + jnp.concatenate([dot_nn(v2, pb[2][:, :BLOCK]), dot_nn(v1, pb[2][:, BLOCK:])], axis=1)
    return peak, total, mixed


def far_backward(k_t, v, q, p_ref, factor, g, ec):
    k0, k1, k2, k3 = k_t
    v0, v1, v2, v3 = v
    e_out = p_ref[: 2 * BLOCK, :] * factor
    e_mid = p_ref[2 * BLOCK :, :] * factor
    eb_out, eb_mid = e_out.astype(BF), e_mid.astype(BF)
    p_out = dot_nt(jnp.concatenate([v0, v3], axis=0), g)
    p_mid = jnp.concatenate([dot_nt(v2, g[:BLOCK]), dot_nt(v1, g[BLOCK:])], axis=1)
    r_out = (e_out * (p_out - ec)).astype(BF)
    r_mid = (e_mid * (p_mid - ec)).astype(BF)
    dv03 = dot_nn(eb_out, g)
    dv2 = dot_nn(eb_mid[:, :BLOCK], g[:BLOCK])
    dv1 = dot_nn(eb_mid[:, BLOCK:], g[BLOCK:])
    dk03 = dot_nn(r_out, q)
    dk2 = dot_nn(r_mid[:, :BLOCK], q[:BLOCK])
    dk1 = dot_nn(r_mid[:, BLOCK:], q[BLOCK:])
    dq_t = dot_nn(jnp.concatenate([k0, k3], axis=1), r_out) + jnp.concatenate(
        [dot_nn(k2, r_mid[:, :BLOCK]), dot_nn(k1, r_mid[:, BLOCK:])], axis=1
    )
    return (dk03[:BLOCK], dk1, dk2, dk03[BLOCK:]), (dv03[:BLOCK], dv1, dv2, dv03[BLOCK:]), dq_t


def main_kernel(qg_first, where, kv_own, kv_got, *refs):
    if qg_first:
        refs = (*refs[2:4], *refs[:2], *refs[4:])
    one_chunk(where, kv_own, kv_got, *refs)


def one_chunk(
    where, kv_own, kv_got, near_got, wide_got, qg_own, qg_got,
    oq_own, oq_far, grad, near_out, wide_out,
    raw, raw_t, one, one_t, two, two_t, qs, gs, p0, p1, p2, acc0, acc1, acc2, oq, halos,
):
    side = where[0]
    odd = where[3]
    halos[1 - odd] = near_got[...]
    halos[odd] = wide_got[...]
    from_left, from_right = halos.at[0], halos.at[1]
    to_left, to_right = halos.at[0], halos.at[1]
    width = kv_own.shape[1] // 2
    left_bias = (1 - where[1]).astype(F32) * MASKED
    right_bias = (1 - where[2]).astype(F32) * MASKED
    own_at = pl.multiple_of(side * 512, 512)
    got_at = pl.multiple_of((1 - side) * 512, 512)
    for h in range(width // HEAD):
        kc = slice(h * HEAD, (h + 1) * HEAD)
        vc = slice(width + h * HEAD, width + (h + 1) * HEAD)
        for n, cols in ((0, kc), (1, vc)):
            raw[n, 0:256, :] = from_left[0:256, cols]
            raw[n, pl.ds(256 + own_at, 512), :] = kv_own[:, cols]
            raw[n, pl.ds(256 + got_at, 512), :] = kv_got[:, cols]
            raw[n, 1280:1536, :] = from_right[0:256, cols]
            one[n, 0:128, :] = from_left[256:384, cols]
            for i in range(6):
                block = pool1(raw[n, i * PARENT : (i + 1) * PARENT, :])
                at = (i + 1) * BLOCK
                one[n, at : at + BLOCK, :] = block
            one[n, 896:1024, :] = from_right[256:384, cols]
            two[n, 0:128, :] = from_left[384:512, cols]
            two[n, 128:192, :] = pool12(one[n, 0:128, :])
            two[n, 192:256, :] = pool2(raw[n, 0:256, :])
            two[n, 256:320, :] = pool2(raw[n, 1280:1536, :])
            two[n, 320:384, :] = pool12(one[n, 896:1024, :])
            two[n, 384:512, :] = from_right[384:512, cols]
            for i in range(6):
                rows = slice(i * PARENT, (i + 1) * PARENT)
                raw_t[n, :, rows] = raw[n, rows, :].T
            for i in range(8):
                rows = slice(i * BLOCK, (i + 1) * BLOCK)
                one_t[n, :, rows] = one[n, rows, :].T
            for i in range(4):
                rows = slice(i * BLOCK, (i + 1) * BLOCK)
                two_t[n, :, rows] = two[n, rows, :].T
        qs[pl.ds(own_at, 512), :] = qg_own[:, kc]
        qs[pl.ds(got_at, 512), :] = qg_got[:, kc]
        gs[pl.ds(own_at, 512), :] = qg_own[:, vc]
        gs[pl.ds(got_at, 512), :] = qg_got[:, vc]

        def blocks(ref, n, which):
            return [ref[n, b * BLOCK : (b + 1) * BLOCK, :] for b in which]

        def blocks_t(ref, n, which):
            return [ref[n, :, b * BLOCK : (b + 1) * BLOCK] for b in which]

        q_parents = [qs[i * PARENT : (i + 1) * PARENT, :] for i in range(4)]
        q1 = [
            jnp.concatenate([pool1(q_parents[2 * j]), pool1(q_parents[2 * j + 1])], axis=0)
            for j in range(2)
        ]
        q2 = jnp.concatenate([pool2(x) for x in q_parents], axis=0)
        which1 = [(0, 1, 4, 5), (2, 3, 6, 7)]
        bias1 = [(left_bias, None), (None, right_bias)]
        which2 = (0, 1, 2, 3)
        far1 = [
            far_forward(
                blocks(one, 0, which1[j]), blocks_t(one_t, 1, which1[j]), q1[j], bias1[j], p1.at[j]
            )
            for j in range(2)
        ]
        far2 = far_forward(
            blocks(two, 0, which2), blocks_t(two_t, 1, which2), q2, (left_bias, right_bias), p2
        )
        acc0[...] = jnp.zeros_like(acc0)
        g1_t, ec1, f1 = [], [], []
        g2_t, ec2, low2 = [], [], []
        dq0 = []
        for i in range(4):
            rows = slice(i * PARENT, i * PARENT + 3 * PARENT)
            q = q_parents[i]
            g = gs[i * PARENT : (i + 1) * PARENT, :]
            s = dot_nt(raw[0, rows, :], q)
            pieces = [s[:PARENT], s[PARENT : 2 * PARENT], s[2 * PARENT :]]
            if i == 0:
                pieces[0] = pieces[0] + left_bias
            if i == 3:
                pieces[2] = pieces[2] + right_bias
            m0 = jnp.max(
                jnp.maximum(jnp.maximum(pieces[0], pieces[1]), pieces[2]), axis=0, keepdims=True
            )
            e = [jnp.exp2((x - m0) * TO_LOG2) for x in pieces]
            for n in range(3):
                p0[n * PARENT : (n + 1) * PARENT, :] = e[n]
            z0 = jnp.sum(e[0] + e[1] + e[2], axis=0, keepdims=True)
            u0 = dot_nn(raw_t[1, :, rows], jnp.concatenate([x.astype(BF) for x in e], axis=0))
            j, half = i // 2, i % 2
            lanes = slice(half * BLOCK, (half + 1) * BLOCK)
            m1, z1, u1 = (x[:, lanes] for x in far1[j])
            lanes2 = slice(j * BLOCK, (j + 1) * BLOCK)
            m2, z2, u2 = (spread64(x[:, lanes2], half) for x in far2)
            m1w, m2w = twice(m1, 1), twice(m2, 1)
            m = jnp.maximum(jnp.maximum(m0, m1w), m2w)
            a0 = jnp.exp2((m0 - m) * TO_LOG2)
            a1 = 2.0 * jnp.exp2((m1w - m) * TO_LOG2)
            a2 = 4.0 * jnp.exp2((m2w - m) * TO_LOG2)
            z = a0 * z0 + a1 * twice(z1, 1) + a2 * twice(z2, 1)
            inv = 1.0 / z
            o = ((a0 * inv) * u0 + (a1 * inv) * twice(u1, 1) + (a2 * inv) * twice(u2, 1)).astype(BF)
            oq[i, 0, h * HEAD : (h + 1) * HEAD, :] = o
            lg = m * TO_LOG2 + jnp.log2(z)
            g_t = g.astype(F32).T
            dr = jnp.sum(o.astype(F32) * g_t, axis=0, keepdims=True)
            lg_a, lg_b = lg[:, :BLOCK], lg[:, BLOCK:]
            g_a, g_b = g_t[:, :BLOCK], g_t[:, BLOCK:]
            dr_a, dr_b = dr[:, :BLOCK], dr[:, BLOCK:]
            low = jnp.minimum(lg_a, lg_b)
            w_a, w_b = jnp.exp2(low - lg_a), jnp.exp2(low - lg_b)
            g1_t.append((w_a * g_a + w_b * g_b).astype(BF))
            ec1.append(w_a * dr_a + w_b * dr_b)
            f1.append(2.0 * jnp.exp2(m1 * TO_LOG2 - low))
            lower = jnp.minimum(low, swap64(low))
            w_a, w_b = jnp.exp2(lower - lg_a), jnp.exp2(lower - lg_b)
            part = w_a * g_a + w_b * g_b
            g2_t.append(part + swap64(part))
            part = w_a * dr_a + w_b * dr_b
            ec2.append(part + swap64(part))
            low2.append(lower)
            f0 = jnp.exp2(m0 * TO_LOG2 - lg)
            products = dot_nt(raw[1, rows, :], g)
            weights = p0[...] * f0
            eb = weights.astype(BF)
            r = (weights * (products - dr)).astype(BF)
            acc0[1, rows, :] += dot_nn(eb, g)
            acc0[0, rows, :] += dot_nn(r, q)
            dq0.append(dot_nn(raw_t[0, :, rows], r))
        acc1[...] = jnp.zeros_like(acc1)
        dq1 = []
        for j in range(2):
            pair = slice(2 * j, 2 * j + 2)
            g1 = jnp.concatenate([x.astype(F32).T.astype(BF) for x in g1_t[pair]], axis=0)
            dk, dv, dq = far_backward(
                blocks_t(one_t, 0, which1[j]), blocks(one, 1, which1[j]), q1[j], p1.at[j],
                jnp.concatenate(f1[pair], axis=1), g1, jnp.concatenate(ec1[pair], axis=1),
            )
            for n, b in enumerate(which1[j]):
                acc1[0, b * BLOCK : (b + 1) * BLOCK, :] += dk[n]
                acc1[1, b * BLOCK : (b + 1) * BLOCK, :] += dv[n]
            dq1.append(dq)

        def joined(parts):
            return jnp.concatenate(
                [
                    jnp.where(low_lanes(parts[0].shape), parts[2 * j], parts[2 * j + 1])
                    for j in range(2)
                ],
                axis=1,
            )

        g2 = joined(g2_t).T.astype(BF)
        f2 = 4.0 * jnp.exp2(far2[0] * TO_LOG2 - joined(low2))
        dk, dv, dq2 = far_backward(
            blocks_t(two_t, 0, which2), blocks(two, 1, which2), q2, p2, f2, g2, joined(ec2)
        )
        for n in range(4):
            acc2[0, n * BLOCK : (n + 1) * BLOCK, :] = dk[n]
            acc2[1, n * BLOCK : (n + 1) * BLOCK, :] = dv[n]
        for i in range(4):
            j, half = i // 2, i % 2
            d1 = dq1[j][:, half * BLOCK : (half + 1) * BLOCK]
            d2 = spread64(dq2[:, j * BLOCK : (j + 1) * BLOCK], half)
            coarse = 0.5 * d1 + 0.25 * d2
            oq[i, 1, h * HEAD : (h + 1) * HEAD, :] = ((dq0[i] + twice(coarse, 1)) * INV_ROOT).astype(BF)
        for n, cols, scale in ((0, kc, INV_ROOT), (1, vc, 1.0)):
            for i in range(4):
                rows = slice((i + 1) * PARENT, (i + 2) * PARENT)
                coarse = acc1[n, (i + 2) * BLOCK : (i + 3) * BLOCK, :] * (0.5 * scale)
                grad[i * PARENT : (i + 1) * PARENT, cols] = acc0[n, rows, :] * scale + twice(coarse)
            far = acc2[n, 128:256, :] * (0.25 * scale)
            mid = acc1[n, 0:256, :] * (0.5 * scale)
            near = acc0[n, 0:256, :] * scale
            to_left[0:256, cols] = (near + twice(mid[128:] + twice(far[64:]))).astype(BF)
            to_left[256:384, cols] = (mid[:128] + twice(far[:64])).astype(BF)
            to_left[384:512, cols] = (acc2[n, 0:128, :] * (0.25 * scale)).astype(BF)
            far = acc2[n, 256:384, :] * (0.25 * scale)
            mid = acc1[n, 768:1024, :] * (0.5 * scale)
            near = acc0[n, 1280:1536, :] * scale
            to_right[0:256, cols] = (near + twice(mid[:128] + twice(far[:64]))).astype(BF)
            to_right[256:384, cols] = (mid[128:] + twice(far[64:])).astype(BF)
            to_right[384:512, cols] = (acc2[n, 384:512, :] * (0.25 * scale)).astype(BF)
    oq_own[...] = oq[pl.ds(side * 2, 2)]
    oq_far[...] = oq[pl.ds((1 - side) * 2, 2)]
    near_out[...] = halos[1 - odd]
    wide_out[...] = halos[odd]


def main(where, kv_own, kv_got, near_got, wide_got, qg_own, qg_got, qg_first):
    rows, both = kv_own.shape
    width = both // 2
    oq_shape = jax.ShapeDtypeStruct((2, 2, width, PARENT), BF)
    halo_shape = jax.ShapeDtypeStruct((512, both), BF)
    operands = [kv_own, kv_got, near_got, wide_got, qg_own, qg_got]
    if qg_first:
        operands = operands[:2] + operands[4:] + operands[2:4]
    return pl.pallas_call(
        functools.partial(main_kernel, qg_first),
        in_specs=[smem()] + [vmem()] * 6,
        out_specs=[vmem()] * 5,
        out_shape=[
            oq_shape,
            oq_shape,
            jax.ShapeDtypeStruct((2 * rows, both), F32),
            halo_shape,
            halo_shape,
        ],
        scratch_shapes=[
            pltpu.VMEM((2, 1536, HEAD), BF),
            pltpu.VMEM((2, HEAD, 1536), BF),
            pltpu.VMEM((2, 1024, HEAD), BF),
            pltpu.VMEM((2, HEAD, 1024), BF),
            pltpu.VMEM((2, 512, HEAD), BF),
            pltpu.VMEM((2, HEAD, 512), BF),
            pltpu.VMEM((1024, HEAD), BF),
            pltpu.VMEM((1024, HEAD), BF),
            pltpu.VMEM((768, PARENT), F32),
            pltpu.VMEM((2, 384, PARENT), F32),
            pltpu.VMEM((384, PARENT), F32),
            pltpu.VMEM((2, 1536, HEAD), F32),
            pltpu.VMEM((2, 1024, HEAD), F32),
            pltpu.VMEM((2, 512, HEAD), F32),
            pltpu.VMEM((4, 2, width, PARENT), BF),
            pltpu.VMEM((2, 512, both), BF),
        ],
        compiler_params=pltpu.CompilerParams(vmem_limit_bytes=24 * 1024 * 1024),
        cost_estimate=light(),
    )(where, *operands)


def join_kernel(where, grad, near_got, wide_got, own, far):
    def fill(first, second, from_left, from_right):
        def parent(i):
            return grad[i * PARENT : (i + 1) * PARENT, :]

        def part(ref, start, stop):
            return ref[start:stop, :].astype(F32)

        first[0:256, :] = (
            parent(0) + part(from_left, 0, 256) + twice(twice(part(from_right, 384, 448)))
        ).astype(BF)
        first[256:512, :] = (
            parent(1) + twice(part(from_left, 256, 384) + twice(part(from_right, 448, 512)))
        ).astype(BF)
        second[0:256, :] = (
            parent(2) + twice(part(from_right, 256, 384) + twice(part(from_left, 384, 448)))
        ).astype(BF)
        second[256:512, :] = (
            parent(3) + part(from_right, 0, 256) + twice(twice(part(from_left, 448, 512)))
        ).astype(BF)

    for side in range(2):
        for odd in range(2):

            @pl.when((where[0] == side) & (where[3] == odd))
            def _(side=side, odd=odd):
                halves = (own, far) if side == 0 else (far, own)
                fill(*halves, *((wide_got, near_got) if odd == 0 else (near_got, wide_got)))


def join(where, grad, near_got, wide_got):
    shape = jax.ShapeDtypeStruct(near_got.shape, BF)
    return pl.pallas_call(
        join_kernel,
        in_specs=[smem(), vmem(), vmem(), vmem()],
        out_specs=[vmem(), vmem()],
        out_shape=[shape, shape],
        compiler_params=small(),
        cost_estimate=light(),
    )(where, grad, near_got, wide_got)


def unpack_rows_kernel(where, *refs):
    ins, (first, second) = refs[:-2], refs[-2:]
    order = order_matrix(True)
    width = ins[0].shape[1] // 2
    side = where[0]
    blocks = [(side * CHUNKS + c, ins[c]) for c in range(CHUNKS)]
    blocks += [((1 - side) * CHUNKS + 1 - LATE_CHUNK, ins[CHUNKS])]
    for block, ref in blocks:
        at = pl.ds(pl.multiple_of(block * width, width), width)
        for i in range(2):
            rows = slice(i * PARENT, (i + 1) * PARENT)
            first[rows, at] = dot_nn(order, ref[rows, :width]).astype(BF)
            second[rows, at] = dot_nn(order, ref[rows, width:]).astype(BF)


def unpack_rows(where, own, got, shape):
    out = jax.ShapeDtypeStruct(shape, BF)
    return pl.pallas_call(
        unpack_rows_kernel,
        in_specs=[smem()] + [vmem()] * (CHUNKS + 1),
        out_specs=[vmem(), vmem()],
        out_shape=[out, out],
        compiler_params=small(),
        cost_estimate=light(),
    )(where, *own, got)


def unpack_last_kernel(where, got, first_in, second_in, first, second, held, sems):
    del first_in, second_in
    order = order_matrix(True)
    width = got.shape[1] // 2
    block = (1 - where[0]) * CHUNKS + LATE_CHUNK
    at = pl.ds(pl.multiple_of(block * width, width), width)
    copies = []
    for m, ref in enumerate((first, second)):
        for i in range(2):
            rows = slice(i * PARENT, (i + 1) * PARENT)
            held[m, rows, :] = dot_nn(order, got[rows, m * width : (m + 1) * width]).astype(BF)
        copies.append(pltpu.make_async_copy(held.at[m], ref.at[:, at], sems.at[m]))
        copies[-1].start()
    for copy in copies:
        copy.wait()


def unpack_last(where, got, first, second):
    out = jax.ShapeDtypeStruct(first.shape, BF)
    hbm = pl.BlockSpec(memory_space=pltpu.HBM)
    return pl.pallas_call(
        unpack_last_kernel,
        in_specs=[smem(), vmem(), hbm, hbm],
        out_specs=[hbm, hbm],
        out_shape=[out, out],
        input_output_aliases={2: 0, 3: 1},
        scratch_shapes=[
            pltpu.VMEM((2, got.shape[0], got.shape[1] // 2), BF),
            pltpu.SemaphoreType.DMA((2,)),
        ],
        compiler_params=small(),
        cost_estimate=light(),
    )(where, got, first, second)


def unpack_columns_kernel(where, *refs):
    ins, (first, second) = refs[:-2], refs[-2:]
    order = order_matrix(True)
    width = ins[0].shape[2]
    for c in range(CHUNKS):
        for ref, side in ((ins[c], where[0]), (ins[CHUNKS + c], 1 - where[0])):
            at = pl.ds(pl.multiple_of((side * CHUNKS + c) * width, width), width)
            for i in range(2):
                rows = slice(i * PARENT, (i + 1) * PARENT)
                first[rows, at] = dot_nt(order, ref[i, 0]).astype(BF)
                second[rows, at] = dot_nt(order, ref[i, 1]).astype(BF)


def unpack_columns(where, own, got, shape):
    out = jax.ShapeDtypeStruct(shape, BF)
    return pl.pallas_call(
        unpack_columns_kernel,
        in_specs=[smem()] + [vmem()] * (2 * CHUNKS),
        out_specs=[vmem(), vmem()],
        out_shape=[out, out],
        compiler_params=small(),
        cost_estimate=light(),
    )(where, *own, *got)


def on_device(queries, key_matrix, value_matrix, cotangent):
    axes = ("outer", "inner")
    count = lax.axis_size("outer") * lax.axis_size("inner")
    device = lax.axis_index("outer") * lax.axis_size("inner") + lax.axis_index("inner")
    pair = device // 2
    where = jnp.stack([device % 2, pair > 0, pair < count // 2 - 1, pair % 2]).astype(jnp.int32)
    across = [(i, i ^ 1) for i in range(count)]
    near_edges = [(i, i ^ 2) for i in range(count) if i ^ 2 < count]
    wide_edges = [(i, i + 2 if i // 2 % 2 else i - 2) for i in range(count)]
    wide_edges = [(i, j) for i, j in wide_edges if 0 <= j < count]

    def swap(x):
        return lax.ppermute(x, axes, across)

    def to_near(x):
        return lax.ppermute(x, axes, near_edges)

    def to_wide(x):
        return lax.ppermute(x, axes, wide_edges)

    kv_far = [pack_cut(1 - device % 2, 0, key_matrix, value_matrix)]
    for c in range(1, CHUNKS):
        later, kv_far[0] = lax.optimization_barrier(((key_matrix, value_matrix), kv_far[0]))
        kv_far.append(pack_cut(1 - device % 2, c, *later))
    qg_far = pack(False, where, queries, cotangent)
    packed = pack(True, where, key_matrix, value_matrix, queries, cotangent)
    kv, qg = packed[:CHUNKS], packed[CHUNKS:]
    oq_own, oq_got, back = [], [], []
    for c in range(CHUNKS):
        got_kv = swap(kv_far[c])
        near, wide = halo(where, kv[c], got_kv)
        far = qg_far[c]
        if c > 0:
            near, wide, far = lax.optimization_barrier((near, wide, far))
        near, wide = to_near(near), to_wide(wide)
        own, far, grad, near, wide = main(where, kv[c], got_kv, near, wide, qg[c], swap(far), c == 0)
        oq_own.append(own)
        oq_got.append(swap(far))
        if c > 0:
            oq_got[c - 1], back[c - 1][1], near, wide = lax.optimization_barrier(
                (oq_got[c - 1], back[c - 1][1], near, wide)
            )
        back.append([grad, near, to_wide(wide)])
    for parts in back:
        parts[1] = to_near(parts[1])
    oq_got[-1], back[-1] = lax.optimization_barrier((oq_got[-1], back[-1]))
    kv_own, kv_got = [], []
    for c in range(CHUNKS):
        own, far = join(where, *back[c])
        kv_own.append(own)
        kv_got.append(swap(far))
    attended, query_grad = unpack_columns(where, oq_own, oq_got, queries.shape)
    key_grad, value_grad = unpack_rows(where, kv_own, kv_got[1 - LATE_CHUNK], queries.shape)
    key_grad, value_grad = unpack_last(where, kv_got[LATE_CHUNK], key_grad, value_grad)
    return attended, query_grad, key_grad, value_grad


def solution(mesh):
    spec = P(("outer", "inner"), None)
    return jax.shard_map(
        on_device,
        mesh=mesh,
        in_specs=(spec,) * 4,
        out_specs=(spec,) * 4,
        check_vma=False,
    )
```

```python
import functools
import math

import jax
import jax.numpy as jnp
from jax import lax
from jax.experimental import pallas as pl
from jax.experimental.pallas import tpu as pltpu
from jax.sharding import PartitionSpec as P

HEAD = 128
BLOCK = 128
PARENT = 256
LEVELS = 3
CHUNKS = 2
LATE_CHUNK = 1
INV_ROOT = HEAD**-0.5
TO_LOG2 = INV_ROOT * math.log2(math.e)
MASKED = -1e30
BF = jnp.bfloat16
F32 = jnp.float32


def dot_nt(a, b):
    return lax.dot_general(a, b, (((1,), (1,)), ((), ())), preferred_element_type=F32)


def dot_nn(a, b):
    return jnp.dot(a, b, preferred_element_type=F32)


def order_matrix(inverse):
    row = lax.broadcasted_iota(jnp.int32, (PARENT, PARENT), 0)
    col = lax.broadcasted_iota(jnp.int32, (PARENT, PARENT), 1)
    place, token = (col, row) if inverse else (row, col)
    slab = place // 64
    source = 4 * (place % 64) + 2 * (slab % 2) + slab // 2
    return jnp.where(source == token, 1.0, 0.0).astype(BF)


def pool1(x):
    return ((x[:BLOCK].astype(F32) + x[BLOCK:].astype(F32)) * 0.5).astype(BF)


def pool2(x):
    half = x[:BLOCK].astype(F32) + x[BLOCK:].astype(F32)
    return ((half[:64] + half[64:]) * 0.25).astype(BF)


def pool12(x):
    return ((x[:64].astype(F32) + x[64:].astype(F32)) * 0.5).astype(BF)


def twice(x, axis=0):
    return jnp.concatenate([x, x], axis=axis)


def pack_kernel(own, where, *refs):
    count = 4 if own else 2
    arrays, outs, (held, sems) = refs[:count], refs[count:-2], refs[-2:]
    rows, columns = arrays[0].shape
    half = columns // 2
    width = half // CHUNKS
    side = where[0] if own else 1 - where[0]
    at = pl.ds(pl.multiple_of(side * half, half), half)
    copies = [
        pltpu.make_async_copy(ref.at[:, at], held.at[m], sems.at[m]) for m, ref in enumerate(arrays)
    ]
    for copy in copies:
        copy.start()
    order = order_matrix(False)
    for m in range(count):
        copies[m].wait()
        first = m % 2 * width
        for i in range(rows // PARENT):
            at = slice(i * PARENT, (i + 1) * PARENT)
            x = dot_nn(order, held[m, at, :]).astype(BF)
            for c in range(CHUNKS):
                out = outs[m // 2 * CHUNKS + c]
                out[at, first : first + width] = x[:, c * width : (c + 1) * width]


def pack(own, where, *arrays):
    rows, columns = arrays[0].shape
    count = len(arrays)
    return pl.pallas_call(
        functools.partial(pack_kernel, own),
        in_specs=[smem()] + [pl.BlockSpec(memory_space=pltpu.HBM)] * count,
        out_specs=[vmem()] * (count // 2 * CHUNKS),
        out_shape=[jax.ShapeDtypeStruct((rows, columns // CHUNKS), BF)] * (count // 2 * CHUNKS),
        scratch_shapes=[
            pltpu.VMEM((count, rows, columns // 2), BF),
            pltpu.SemaphoreType.DMA((count,)),
        ],
        compiler_params=small(),
        cost_estimate=light(),
    )(where, *arrays)


def pack_cut_kernel(a, b, out):
    order = order_matrix(False)
    width = a.shape[1]
    for m, ref in enumerate((a, b)):
        for i in range(a.shape[0] // PARENT):
            rows = slice(i * PARENT, (i + 1) * PARENT)
            out[rows, m * width : (m + 1) * width] = dot_nn(order, ref[rows, :]).astype(BF)


def pack_cut(side, chunk, a, b):
    rows, columns = a.shape
    width = columns // 2 // CHUNKS
    cut = [lax.dynamic_slice_in_dim(x, (side * CHUNKS + chunk) * width, width, 1) for x in (a, b)]
    return pl.pallas_call(
        pack_cut_kernel,
        in_specs=[vmem(), vmem()],
        out_specs=vmem(),
        out_shape=jax.ShapeDtypeStruct((rows, 2 * width), BF),
        compiler_params=small(),
        cost_estimate=light(),
    )(*cut)


def smem():
    return pl.BlockSpec(memory_space=pltpu.SMEM)


def vmem():
    return pl.BlockSpec(memory_space=pltpu.VMEM)


def small():
    return pltpu.CompilerParams(vmem_limit_bytes=8 * 1024 * 1024)


def light():
    return pl.CostEstimate(flops=1000, bytes_accessed=1000, transcendentals=0)


def halo_kernel(where, own, got, near, wide):
    def fill(first, second, to_right, to_left):
        to_right[0:256, :] = second[256:512, :]
        to_right[256:384, :] = pool1(second[0:256, :])
        to_right[384:448, :] = pool2(first[0:256, :])
        to_right[448:512, :] = pool2(first[256:512, :])
        to_left[0:256, :] = first[0:256, :]
        to_left[256:384, :] = pool1(first[256:512, :])
        to_left[384:448, :] = pool2(second[0:256, :])
        to_left[448:512, :] = pool2(second[256:512, :])

    for side in range(2):
        for odd in range(2):

            @pl.when((where[0] == side) & (where[3] == odd))
            def _(side=side, odd=odd):
                halves = (own, got) if side == 0 else (got, own)
                fill(*halves, *((near, wide) if odd == 0 else (wide, near)))


def halo(where, own, got):
    shape = jax.ShapeDtypeStruct(own.shape, BF)
    return pl.pallas_call(
        halo_kernel,
        in_specs=[smem(), vmem(), vmem()],
        out_specs=[vmem(), vmem()],
        out_shape=[shape, shape],
        compiler_params=small(),
        cost_estimate=light(),
    )(where, own, got)


def swap64(x):
    return pltpu.roll(x, 64, 1)


def low_lanes(shape):
    return lax.broadcasted_iota(jnp.int32, shape, 1) < 64


def spread64(x, half):
    other = swap64(x)
    low = low_lanes(x.shape)
    return jnp.where(low, x, other) if half == 0 else jnp.where(low, other, x)


def far_forward(k, v_t, q, bias, p_ref):
    k0, k1, k2, k3 = k
    v0, v1, v2, v3 = v_t
    left, right = bias
    outer = dot_nt(jnp.concatenate([k0, k3], axis=0), q)
    first, last = outer[:BLOCK], outer[BLOCK:]
    mid_low = dot_nt(k2, q[:BLOCK])
    mid_high = dot_nt(k1, q[BLOCK:])
    if left is not None:
        first = first + left
        mid_high = mid_high + left
    if right is not None:
        last = last + right
        mid_low = mid_low + right
    mid = jnp.concatenate([mid_low, mid_high], axis=1)
    peak = jnp.max(jnp.maximum(jnp.maximum(first, last), mid), axis=0, keepdims=True)
    parts = [jnp.exp2((x - peak) * TO_LOG2) for x in (first, last, mid)]
    for n, x in enumerate(parts):
        p_ref[n * BLOCK : (n + 1) * BLOCK, :] = x
    total = jnp.sum(parts[0] + parts[1] + parts[2], axis=0, keepdims=True)
    pb = [x.astype(BF) for x in parts]
    mixed = dot_nn(
        jnp.concatenate([v0, v3], axis=1), jnp.concatenate(pb[:2], axis=0)
    ) + jnp.concatenate([dot_nn(v2, pb[2][:, :BLOCK]), dot_nn(v1, pb[2][:, BLOCK:])], axis=1)
    return peak, total, mixed


def far_backward(k_t, v, q, p_ref, factor, g, ec):
    k0, k1, k2, k3 = k_t
    v0, v1, v2, v3 = v
    e_out = p_ref[: 2 * BLOCK, :] * factor
    e_mid = p_ref[2 * BLOCK :, :] * factor
    eb_out, eb_mid = e_out.astype(BF), e_mid.astype(BF)
    p_out = dot_nt(jnp.concatenate([v0, v3], axis=0), g)
    p_mid = jnp.concatenate([dot_nt(v2, g[:BLOCK]), dot_nt(v1, g[BLOCK:])], axis=1)
    r_out = (e_out * (p_out - ec)).astype(BF)
    r_mid = (e_mid * (p_mid - ec)).astype(BF)
    dv03 = dot_nn(eb_out, g)
    dv2 = dot_nn(eb_mid[:, :BLOCK], g[:BLOCK])
    dv1 = dot_nn(eb_mid[:, BLOCK:], g[BLOCK:])
    dk03 = dot_nn(r_out, q)
    dk2 = dot_nn(r_mid[:, :BLOCK], q[:BLOCK])
    dk1 = dot_nn(r_mid[:, BLOCK:], q[BLOCK:])
    dq_t = dot_nn(jnp.concatenate([k0, k3], axis=1), r_out) + jnp.concatenate(
        [dot_nn(k2, r_mid[:, :BLOCK]), dot_nn(k1, r_mid[:, BLOCK:])], axis=1
    )
    return (dk03[:BLOCK], dk1, dk2, dk03[BLOCK:]), (dv03[:BLOCK], dv1, dv2, dv03[BLOCK:]), dq_t


def main_kernel(qg_first, where, kv_own, kv_got, *refs):
    if qg_first:
        refs = (*refs[2:4], *refs[:2], *refs[4:])
    one_chunk(where, kv_own, kv_got, *refs)


def one_chunk(
    where, kv_own, kv_got, near_got, wide_got, qg_own, qg_got,
    oq_own, oq_far, grad, near_out, wide_out,
    raw, raw_t, one, one_t, two, two_t, qs, gs, p0, p1, p2, f0_rows, dr_rows, dq0, acc0, acc1, acc2, oq, halos,
):
    side = where[0]
    odd = where[3]
    halos[1 - odd] = near_got[...]
    halos[odd] = wide_got[...]
    from_left, from_right = halos.at[0], halos.at[1]
    to_left, to_right = halos.at[0], halos.at[1]
    width = kv_own.shape[1] // 2
    left_bias = (1 - where[1]).astype(F32) * MASKED
    right_bias = (1 - where[2]).astype(F32) * MASKED
    own_at = pl.multiple_of(side * 512, 512)
    got_at = pl.multiple_of((1 - side) * 512, 512)
    for h in range(width // HEAD):
        kc = slice(h * HEAD, (h + 1) * HEAD)
        vc = slice(width + h * HEAD, width + (h + 1) * HEAD)
        for n, cols in ((0, kc), (1, vc)):
            raw[n, 0:256, :] = from_left[0:256, cols]
            raw[n, pl.ds(256 + own_at, 512), :] = kv_own[:, cols]
            raw[n, pl.ds(256 + got_at, 512), :] = kv_got[:, cols]
            raw[n, 1280:1536, :] = from_right[0:256, cols]
            one[n, 0:128, :] = from_left[256:384, cols]
            for i in range(6):
                block = pool1(raw[n, i * PARENT : (i + 1) * PARENT, :])
                at = (i + 1) * BLOCK
                one[n, at : at + BLOCK, :] = block
            one[n, 896:1024, :] = from_right[256:384, cols]
            two[n, 0:128, :] = from_left[384:512, cols]
            two[n, 128:192, :] = pool12(one[n, 0:128, :])
            two[n, 192:256, :] = pool2(raw[n, 0:256, :])
            two[n, 256:320, :] = pool2(raw[n, 1280:1536, :])
            two[n, 320:384, :] = pool12(one[n, 896:1024, :])
            two[n, 384:512, :] = from_right[384:512, cols]
            for i in range(6):
                rows = slice(i * PARENT, (i + 1) * PARENT)
                raw_t[n, :, rows] = raw[n, rows, :].T
            for i in range(8):
                rows = slice(i * BLOCK, (i + 1) * BLOCK)
                one_t[n, :, rows] = one[n, rows, :].T
            for i in range(4):
                rows = slice(i * BLOCK, (i + 1) * BLOCK)
                two_t[n, :, rows] = two[n, rows, :].T
        qs[pl.ds(own_at, 512), :] = qg_own[:, kc]
        qs[pl.ds(got_at, 512), :] = qg_got[:, kc]
        gs[pl.ds(own_at, 512), :] = qg_own[:, vc]
        gs[pl.ds(got_at, 512), :] = qg_got[:, vc]

        def blocks(ref, n, which):
            return [ref[n, b * BLOCK : (b + 1) * BLOCK, :] for b in which]

        def blocks_t(ref, n, which):
            return [ref[n, :, b * BLOCK : (b + 1) * BLOCK] for b in which]

        q_parents = [qs[i * PARENT : (i + 1) * PARENT, :] for i in range(4)]
        q1 = [
            jnp.concatenate([pool1(q_parents[2 * j]), pool1(q_parents[2 * j + 1])], axis=0)
            for j in range(2)
        ]
        q2 = jnp.concatenate([pool2(x) for x in q_parents], axis=0)
        which1 = [(0, 1, 4, 5), (2, 3, 6, 7)]
        bias1 = [(left_bias, None), (None, right_bias)]
        which2 = (0, 1, 2, 3)
        far1 = [
            far_forward(
                blocks(one, 0, which1[j]), blocks_t(one_t, 1, which1[j]), q1[j], bias1[j], p1.at[j]
            )
            for j in range(2)
        ]
        far2 = far_forward(
            blocks(two, 0, which2), blocks_t(two_t, 1, which2), q2, (left_bias, right_bias), p2
        )
        acc0[...] = jnp.zeros_like(acc0)
        g1_t, ec1, f1 = [], [], []
        g2_t, ec2, low2 = [], [], []
        for i in range(4):
            rows = slice(i * PARENT, i * PARENT + 3 * PARENT)
            q = q_parents[i]
            g = gs[i * PARENT : (i + 1) * PARENT, :]
            s = dot_nt(raw[0, rows, :], q)
            pieces = [s[:PARENT], s[PARENT : 2 * PARENT], s[2 * PARENT :]]
            if i == 0:
                pieces[0] = pieces[0] + left_bias
            if i == 3:
                pieces[2] = pieces[2] + right_bias
            m0 = jnp.max(
                jnp.maximum(jnp.maximum(pieces[0], pieces[1]), pieces[2]), axis=0, keepdims=True
            )
            e = [jnp.exp2((x - m0) * TO_LOG2) for x in pieces]
            for n in range(3):
                p0[i, n * PARENT : (n + 1) * PARENT, :] = e[n]
            z0 = jnp.sum(e[0] + e[1] + e[2], axis=0, keepdims=True)
            u0 = dot_nn(raw_t[1, :, rows], jnp.concatenate([x.astype(BF) for x in e], axis=0))
            j, half = i // 2, i % 2
            lanes = slice(half * BLOCK, (half + 1) * BLOCK)
            m1, z1, u1 = (x[:, lanes] for x in far1[j])
            lanes2 = slice(j * BLOCK, (j + 1) * BLOCK)
            m2, z2, u2 = (spread64(x[:, lanes2], half) for x in far2)
            m1w, m2w = twice(m1, 1), twice(m2, 1)
            m = jnp.maximum(jnp.maximum(m0, m1w), m2w)
            a0 = jnp.exp2((m0 - m) * TO_LOG2)
            a1 = 2.0 * jnp.exp2((m1w - m) * TO_LOG2)
            a2 = 4.0 * jnp.exp2((m2w - m) * TO_LOG2)
            z = a0 * z0 + a1 * twice(z1, 1) + a2 * twice(z2, 1)
            inv = 1.0 / z
            o = ((a0 * inv) * u0 + (a1 * inv) * twice(u1, 1) + (a2 * inv) * twice(u2, 1)).astype(BF)
            oq[i, 0, h * HEAD : (h + 1) * HEAD, :] = o
            lg = m * TO_LOG2 + jnp.log2(z)
            g_t = g.astype(F32).T
            dr = jnp.sum(o.astype(F32) * g_t, axis=0, keepdims=True)
            lg_a, lg_b = lg[:, :BLOCK], lg[:, BLOCK:]
            g_a, g_b = g_t[:, :BLOCK], g_t[:, BLOCK:]
            dr_a, dr_b = dr[:, :BLOCK], dr[:, BLOCK:]
            low = jnp.minimum(lg_a, lg_b)
            w_a, w_b = jnp.exp2(low - lg_a), jnp.exp2(low - lg_b)
            g1_t.append((w_a * g_a + w_b * g_b).astype(BF))
            ec1.append(w_a * dr_a + w_b * dr_b)
            f1.append(2.0 * jnp.exp2(m1 * TO_LOG2 - low))
            lower = jnp.minimum(low, swap64(low))
            w_a, w_b = jnp.exp2(lower - lg_a), jnp.exp2(lower - lg_b)
            part = w_a * g_a + w_b * g_b
            g2_t.append(part + swap64(part))
            part = w_a * dr_a + w_b * dr_b
            ec2.append(part + swap64(part))
            low2.append(lower)
            f0_rows[i] = jnp.exp2(m0 * TO_LOG2 - lg)
            dr_rows[i] = dr

        @pl.loop(0, 4)
        def _(i):
            at = pl.multiple_of(i * PARENT, PARENT)
            rows = pl.ds(at, 3 * PARENT)
            q = qs[pl.ds(at, PARENT), :]
            g = gs[pl.ds(at, PARENT), :]
            products = dot_nt(raw[1, rows, :], g)
            weights = p0[i] * f0_rows[i]
            eb = weights.astype(BF)
            r = (weights * (products - dr_rows[i])).astype(BF)
            acc0[1, rows, :] += dot_nn(eb, g)
            acc0[0, rows, :] += dot_nn(r, q)
            dq0[i] = dot_nn(raw_t[0, :, rows], r)

        acc1[...] = jnp.zeros_like(acc1)
        dq1 = []
        for j in range(2):
            pair = slice(2 * j, 2 * j + 2)
            g1 = jnp.concatenate([x.astype(F32).T.astype(BF) for x in g1_t[pair]], axis=0)
            dk, dv, dq = far_backward(
                blocks_t(one_t, 0, which1[j]), blocks(one, 1, which1[j]), q1[j], p1.at[j],
                jnp.concatenate(f1[pair], axis=1), g1, jnp.concatenate(ec1[pair], axis=1),
            )
            for n, b in enumerate(which1[j]):
                acc1[0, b * BLOCK : (b + 1) * BLOCK, :] += dk[n]
                acc1[1, b * BLOCK : (b + 1) * BLOCK, :] += dv[n]
            dq1.append(dq)

        def joined(parts):
            return jnp.concatenate(
                [
                    jnp.where(low_lanes(parts[0].shape), parts[2 * j], parts[2 * j + 1])
                    for j in range(2)
                ],
                axis=1,
            )

        g2 = joined(g2_t).T.astype(BF)
        f2 = 4.0 * jnp.exp2(far2[0] * TO_LOG2 - joined(low2))
        dk, dv, dq2 = far_backward(
            blocks_t(two_t, 0, which2), blocks(two, 1, which2), q2, p2, f2, g2, joined(ec2)
        )
        for n in range(4):
            acc2[0, n * BLOCK : (n + 1) * BLOCK, :] = dk[n]
            acc2[1, n * BLOCK : (n + 1) * BLOCK, :] = dv[n]
        for i in range(4):
            j, half = i // 2, i % 2
            d1 = dq1[j][:, half * BLOCK : (half + 1) * BLOCK]
            d2 = spread64(dq2[:, j * BLOCK : (j + 1) * BLOCK], half)
            coarse = 0.5 * d1 + 0.25 * d2
            oq[i, 1, h * HEAD : (h + 1) * HEAD, :] = ((dq0[i] + twice(coarse, 1)) * INV_ROOT).astype(BF)
        for n, cols, scale in ((0, kc, INV_ROOT), (1, vc, 1.0)):
            for i in range(4):
                rows = slice((i + 1) * PARENT, (i + 2) * PARENT)
                coarse = acc1[n, (i + 2) * BLOCK : (i + 3) * BLOCK, :] * (0.5 * scale)
                grad[i * PARENT : (i + 1) * PARENT, cols] = acc0[n, rows, :] * scale + twice(coarse)
            far = acc2[n, 128:256, :] * (0.25 * scale)
            mid = acc1[n, 0:256, :] * (0.5 * scale)
            near = acc0[n, 0:256, :] * scale
            to_left[0:256, cols] = (near + twice(mid[128:] + twice(far[64:]))).astype(BF)
            to_left[256:384, cols] = (mid[:128] + twice(far[:64])).astype(BF)
            to_left[384:512, cols] = (acc2[n, 0:128, :] * (0.25 * scale)).astype(BF)
            far = acc2[n, 256:384, :] * (0.25 * scale)
            mid = acc1[n, 768:1024, :] * (0.5 * scale)
            near = acc0[n, 1280:1536, :] * scale
            to_right[0:256, cols] = (near + twice(mid[:128] + twice(far[:64]))).astype(BF)
            to_right[256:384, cols] = (mid[128:] + twice(far[64:])).astype(BF)
            to_right[384:512, cols] = (acc2[n, 384:512, :] * (0.25 * scale)).astype(BF)
    oq_own[...] = oq[pl.ds(side * 2, 2)]
    oq_far[...] = oq[pl.ds((1 - side) * 2, 2)]
    near_out[...] = halos[1 - odd]
    wide_out[...] = halos[odd]


def main(where, kv_own, kv_got, near_got, wide_got, qg_own, qg_got, qg_first):
    rows, both = kv_own.shape
    width = both // 2
    oq_shape = jax.ShapeDtypeStruct((2, 2, width, PARENT), BF)
    halo_shape = jax.ShapeDtypeStruct((512, both), BF)
    operands = [kv_own, kv_got, near_got, wide_got, qg_own, qg_got]
    if qg_first:
        operands = operands[:2] + operands[4:] + operands[2:4]
    return pl.pallas_call(
        functools.partial(main_kernel, qg_first),
        in_specs=[smem()] + [vmem()] * 6,
        out_specs=[vmem()] * 5,
        out_shape=[
            oq_shape,
            oq_shape,
            jax.ShapeDtypeStruct((2 * rows, both), F32),
            halo_shape,
            halo_shape,
        ],
        scratch_shapes=[
            pltpu.VMEM((2, 1536, HEAD), BF),
            pltpu.VMEM((2, HEAD, 1536), BF),
            pltpu.VMEM((2, 1024, HEAD), BF),
            pltpu.VMEM((2, HEAD, 1024), BF),
            pltpu.VMEM((2, 512, HEAD), BF),
            pltpu.VMEM((2, HEAD, 512), BF),
            pltpu.VMEM((1024, HEAD), BF),
            pltpu.VMEM((1024, HEAD), BF),
            pltpu.VMEM((4, 768, PARENT), F32),
            pltpu.VMEM((2, 384, PARENT), F32),
            pltpu.VMEM((384, PARENT), F32),
            pltpu.VMEM((4, 1, PARENT), F32),
            pltpu.VMEM((4, 1, PARENT), F32),
            pltpu.VMEM((4, HEAD, PARENT), F32),
            pltpu.VMEM((2, 1536, HEAD), F32),
            pltpu.VMEM((2, 1024, HEAD), F32),
            pltpu.VMEM((2, 512, HEAD), F32),
            pltpu.VMEM((4, 2, width, PARENT), BF),
            pltpu.VMEM((2, 512, both), BF),
        ],
        compiler_params=pltpu.CompilerParams(vmem_limit_bytes=24 * 1024 * 1024),
        cost_estimate=light(),
    )(where, *operands)


def join_kernel(where, grad, near_got, wide_got, own, far):
    def fill(first, second, from_left, from_right):
        def parent(i):
            return grad[i * PARENT : (i + 1) * PARENT, :]

        def part(ref, start, stop):
            return ref[start:stop, :].astype(F32)

        first[0:256, :] = (
            parent(0) + part(from_left, 0, 256) + twice(twice(part(from_right, 384, 448)))
        ).astype(BF)
        first[256:512, :] = (
            parent(1) + twice(part(from_left, 256, 384) + twice(part(from_right, 448, 512)))
        ).astype(BF)
        second[0:256, :] = (
            parent(2) + twice(part(from_right, 256, 384) + twice(part(from_left, 384, 448)))
        ).astype(BF)
        second[256:512, :] = (
            parent(3) + part(from_right, 0, 256) + twice(twice(part(from_left, 448, 512)))
        ).astype(BF)

    for side in range(2):
        for odd in range(2):

            @pl.when((where[0] == side) & (where[3] == odd))
            def _(side=side, odd=odd):
                halves = (own, far) if side == 0 else (far, own)
                fill(*halves, *((wide_got, near_got) if odd == 0 else (near_got, wide_got)))


def join(where, grad, near_got, wide_got):
    shape = jax.ShapeDtypeStruct(near_got.shape, BF)
    return pl.pallas_call(
        join_kernel,
        in_specs=[smem(), vmem(), vmem(), vmem()],
        out_specs=[vmem(), vmem()],
        out_shape=[shape, shape],
        compiler_params=small(),
        cost_estimate=light(),
    )(where, grad, near_got, wide_got)


def unpack_rows_kernel(where, *refs):
    ins, (first, second) = refs[:-2], refs[-2:]
    order = order_matrix(True)
    width = ins[0].shape[1] // 2
    side = where[0]
    blocks = [(side * CHUNKS + c, ins[c]) for c in range(CHUNKS)]
    blocks += [((1 - side) * CHUNKS + 1 - LATE_CHUNK, ins[CHUNKS])]
    for block, ref in blocks:
        at = pl.ds(pl.multiple_of(block * width, width), width)
        for i in range(2):
            rows = slice(i * PARENT, (i + 1) * PARENT)
            first[rows, at] = dot_nn(order, ref[rows, :width]).astype(BF)
            second[rows, at] = dot_nn(order, ref[rows, width:]).astype(BF)


def unpack_rows(where, own, got, shape):
    out = jax.ShapeDtypeStruct(shape, BF)
    return pl.pallas_call(
        unpack_rows_kernel,
        in_specs=[smem()] + [vmem()] * (CHUNKS + 1),
        out_specs=[vmem(), vmem()],
        out_shape=[out, out],
        compiler_params=small(),
        cost_estimate=light(),
    )(where, *own, got)


def unpack_last_kernel(where, got, first_in, second_in, first, second, held, sems):
    del first_in, second_in
    order = order_matrix(True)
    width = got.shape[1] // 2
    block = (1 - where[0]) * CHUNKS + LATE_CHUNK
    at = pl.ds(pl.multiple_of(block * width, width), width)
    copies = []
    for m, ref in enumerate((first, second)):
        for i in range(2):
            rows = slice(i * PARENT, (i + 1) * PARENT)
            held[m, rows, :] = dot_nn(order, got[rows, m * width : (m + 1) * width]).astype(BF)
        copies.append(pltpu.make_async_copy(held.at[m], ref.at[:, at], sems.at[m]))
        copies[-1].start()
    for copy in copies:
        copy.wait()


def unpack_last(where, got, first, second):
    out = jax.ShapeDtypeStruct(first.shape, BF)
    hbm = pl.BlockSpec(memory_space=pltpu.HBM)
    return pl.pallas_call(
        unpack_last_kernel,
        in_specs=[smem(), vmem(), hbm, hbm],
        out_specs=[hbm, hbm],
        out_shape=[out, out],
        input_output_aliases={2: 0, 3: 1},
        scratch_shapes=[
            pltpu.VMEM((2, got.shape[0], got.shape[1] // 2), BF),
            pltpu.SemaphoreType.DMA((2,)),
        ],
        compiler_params=small(),
        cost_estimate=light(),
    )(where, got, first, second)


def unpack_columns_kernel(where, *refs):
    ins, (first, second) = refs[:-2], refs[-2:]
    order = order_matrix(True)
    width = ins[0].shape[2]
    for c in range(CHUNKS):
        for ref, side in ((ins[c], where[0]), (ins[CHUNKS + c], 1 - where[0])):
            at = pl.ds(pl.multiple_of((side * CHUNKS + c) * width, width), width)
            for i in range(2):
                rows = slice(i * PARENT, (i + 1) * PARENT)
                first[rows, at] = dot_nt(order, ref[i, 0]).astype(BF)
                second[rows, at] = dot_nt(order, ref[i, 1]).astype(BF)


def unpack_columns(where, own, got, shape):
    out = jax.ShapeDtypeStruct(shape, BF)
    return pl.pallas_call(
        unpack_columns_kernel,
        in_specs=[smem()] + [vmem()] * (2 * CHUNKS),
        out_specs=[vmem(), vmem()],
        out_shape=[out, out],
        compiler_params=small(),
        cost_estimate=light(),
    )(where, *own, *got)


def on_device(queries, key_matrix, value_matrix, cotangent):
    axes = ("outer", "inner")
    count = lax.axis_size("outer") * lax.axis_size("inner")
    device = lax.axis_index("outer") * lax.axis_size("inner") + lax.axis_index("inner")
    pair = device // 2
    where = jnp.stack([device % 2, pair > 0, pair < count // 2 - 1, pair % 2]).astype(jnp.int32)
    across = [(i, i ^ 1) for i in range(count)]
    near_edges = [(i, i ^ 2) for i in range(count) if i ^ 2 < count]
    wide_edges = [(i, i + 2 if i // 2 % 2 else i - 2) for i in range(count)]
    wide_edges = [(i, j) for i, j in wide_edges if 0 <= j < count]

    def swap(x):
        return lax.ppermute(x, axes, across)

    def beside(near, wide):
        near = lax.ppermute(near, axes, near_edges)
        return near, lax.ppermute(wide, axes, wide_edges)

    kv_far = [pack_cut(1 - device % 2, 0, key_matrix, value_matrix)]
    for c in range(1, CHUNKS):
        later, kv_far[0] = lax.optimization_barrier(((key_matrix, value_matrix), kv_far[0]))
        kv_far.append(pack_cut(1 - device % 2, c, *later))
    qg_far = pack(False, where, queries, cotangent)
    packed = pack(True, where, key_matrix, value_matrix, queries, cotangent)
    kv, qg = packed[:CHUNKS], packed[CHUNKS:]
    oq_own, oq_got, back = [], [], []
    for c in range(CHUNKS):
        got_kv = swap(kv_far[c])
        near, wide = halo(where, kv[c], got_kv)
        far = qg_far[c]
        if c > 0:
            near, wide, far = lax.optimization_barrier((near, wide, far))
        near, wide = beside(near, wide)
        own, far, grad, near, wide = main(where, kv[c], got_kv, near, wide, qg[c], swap(far), c == 0)
        oq_own.append(own)
        oq_got.append(swap(far))
        if c > 0:
            oq_got[c - 1], near, wide = lax.optimization_barrier((oq_got[c - 1], near, wide))
        back.append([grad, *beside(near, wide)])
    oq_got[-1], back[-1] = lax.optimization_barrier((oq_got[-1], back[-1]))
    kv_own, kv_got = [], []
    for c in range(CHUNKS):
        own, far = join(where, *back[c])
        kv_own.append(own)
        kv_got.append(swap(far))
    attended, query_grad = unpack_columns(where, oq_own, oq_got, queries.shape)
    key_grad, value_grad = unpack_rows(where, kv_own, kv_got[1 - LATE_CHUNK], queries.shape)
    key_grad, value_grad = unpack_last(where, kv_got[LATE_CHUNK], key_grad, value_grad)
    return attended, query_grad, key_grad, value_grad


def solution(mesh):
    spec = P(("outer", "inner"), None)
    return jax.shard_map(
        on_device,
        mesh=mesh,
        in_specs=(spec,) * 4,
        out_specs=(spec,) * 4,
        check_vma=False,
    )
```

```python
import functools
import math

import jax
import jax.numpy as jnp
from jax import lax
from jax.experimental import pallas as pl
from jax.experimental.pallas import tpu as pltpu
from jax.sharding import PartitionSpec as P

HEAD = 128
BLOCK = 128
PARENT = 256
LEVELS = 3
CHUNKS = 2
LATE_CHUNK = 1
INV_ROOT = HEAD**-0.5
TO_LOG2 = INV_ROOT * math.log2(math.e)
MASKED = -1e30
BF = jnp.bfloat16
F32 = jnp.float32


def dot_nt(a, b):
    return lax.dot_general(a, b, (((1,), (1,)), ((), ())), preferred_element_type=F32)


def dot_nn(a, b):
    return jnp.dot(a, b, preferred_element_type=F32)


def order_matrix(inverse):
    row = lax.broadcasted_iota(jnp.int32, (PARENT, PARENT), 0)
    col = lax.broadcasted_iota(jnp.int32, (PARENT, PARENT), 1)
    place, token = (col, row) if inverse else (row, col)
    slab = place // 64
    source = 4 * (place % 64) + 2 * (slab % 2) + slab // 2
    return jnp.where(source == token, 1.0, 0.0).astype(BF)


def pool1(x):
    return ((x[:BLOCK].astype(F32) + x[BLOCK:].astype(F32)) * 0.5).astype(BF)


def pool2(x):
    half = x[:BLOCK].astype(F32) + x[BLOCK:].astype(F32)
    return ((half[:64] + half[64:]) * 0.25).astype(BF)


def pool12(x):
    return ((x[:64].astype(F32) + x[64:].astype(F32)) * 0.5).astype(BF)


def twice(x, axis=0):
    return jnp.concatenate([x, x], axis=axis)


def pack_kernel(own, where, *refs):
    count = 4 if own else 2
    arrays, outs, (held, sems) = refs[:count], refs[count:-2], refs[-2:]
    rows, columns = arrays[0].shape
    half = columns // 2
    width = half // CHUNKS
    side = where[0] if own else 1 - where[0]
    at = pl.ds(pl.multiple_of(side * half, half), half)
    copies = [
        pltpu.make_async_copy(ref.at[:, at], held.at[m], sems.at[m]) for m, ref in enumerate(arrays)
    ]
    for copy in copies:
        copy.start()
    order = order_matrix(False)
    for m in range(count):
        copies[m].wait()
        first = m % 2 * width
        for i in range(rows // PARENT):
            at = slice(i * PARENT, (i + 1) * PARENT)
            x = dot_nn(order, held[m, at, :]).astype(BF)
            for c in range(CHUNKS):
                out = outs[m // 2 * CHUNKS + c]
                out[at, first : first + width] = x[:, c * width : (c + 1) * width]


def pack(own, where, *arrays):
    rows, columns = arrays[0].shape
    count = len(arrays)
    return pl.pallas_call(
        functools.partial(pack_kernel, own),
        in_specs=[smem()] + [pl.BlockSpec(memory_space=pltpu.HBM)] * count,
        out_specs=[vmem()] * (count // 2 * CHUNKS),
        out_shape=[jax.ShapeDtypeStruct((rows, columns // CHUNKS), BF)] * (count // 2 * CHUNKS),
        scratch_shapes=[
            pltpu.VMEM((count, rows, columns // 2), BF),
            pltpu.SemaphoreType.DMA((count,)),
        ],
        compiler_params=small(),
        cost_estimate=light(),
    )(where, *arrays)


def pack_cut_kernel(a, b, out):
    order = order_matrix(False)
    width = a.shape[1]
    for m, ref in enumerate((a, b)):
        for i in range(a.shape[0] // PARENT):
            rows = slice(i * PARENT, (i + 1) * PARENT)
            out[rows, m * width : (m + 1) * width] = dot_nn(order, ref[rows, :]).astype(BF)


def pack_cut(side, chunk, a, b):
    rows, columns = a.shape
    width = columns // 2 // CHUNKS
    cut = [lax.dynamic_slice_in_dim(x, (side * CHUNKS + chunk) * width, width, 1) for x in (a, b)]
    return pl.pallas_call(
        pack_cut_kernel,
        in_specs=[vmem(), vmem()],
        out_specs=vmem(),
        out_shape=jax.ShapeDtypeStruct((rows, 2 * width), BF),
        compiler_params=small(),
        cost_estimate=light(),
    )(*cut)


def smem():
    return pl.BlockSpec(memory_space=pltpu.SMEM)


def vmem():
    return pl.BlockSpec(memory_space=pltpu.VMEM)


def small():
    return pltpu.CompilerParams(vmem_limit_bytes=8 * 1024 * 1024)


def light():
    return pl.CostEstimate(flops=1000, bytes_accessed=1000, transcendentals=0)


def halo_kernel(where, own, got, near, wide):
    def fill(first, second, to_right, to_left):
        to_right[0:256, :] = second[256:512, :]
        to_right[256:384, :] = pool1(second[0:256, :])
        to_right[384:448, :] = pool2(first[0:256, :])
        to_right[448:512, :] = pool2(first[256:512, :])
        to_left[0:256, :] = first[0:256, :]
        to_left[256:384, :] = pool1(first[256:512, :])
        to_left[384:448, :] = pool2(second[0:256, :])
        to_left[448:512, :] = pool2(second[256:512, :])

    for side in range(2):
        for odd in range(2):

            @pl.when((where[0] == side) & (where[3] == odd))
            def _(side=side, odd=odd):
                halves = (own, got) if side == 0 else (got, own)
                fill(*halves, *((near, wide) if odd == 0 else (wide, near)))


def halo(where, own, got):
    shape = jax.ShapeDtypeStruct(own.shape, BF)
    return pl.pallas_call(
        halo_kernel,
        in_specs=[smem(), vmem(), vmem()],
        out_specs=[vmem(), vmem()],
        out_shape=[shape, shape],
        compiler_params=small(),
        cost_estimate=light(),
    )(where, own, got)


def swap64(x):
    return pltpu.roll(x, 64, 1)


def low_lanes(shape):
    return lax.broadcasted_iota(jnp.int32, shape, 1) < 64


def spread64(x, half):
    other = swap64(x)
    low = low_lanes(x.shape)
    return jnp.where(low, x, other) if half == 0 else jnp.where(low, other, x)


def far_forward(k, v_t, q, bias, p_ref):
    k0, k1, k2, k3 = k
    v0, v1, v2, v3 = v_t
    left, right = bias
    outer = dot_nt(jnp.concatenate([k0, k3], axis=0), q)
    first, last = outer[:BLOCK], outer[BLOCK:]
    mid_low = dot_nt(k2, q[:BLOCK])
    mid_high = dot_nt(k1, q[BLOCK:])
    if left is not None:
        first = first + left
        mid_high = mid_high + left
    if right is not None:
        last = last + right
        mid_low = mid_low + right
    mid = jnp.concatenate([mid_low, mid_high], axis=1)
    peak = jnp.max(jnp.maximum(jnp.maximum(first, last), mid), axis=0, keepdims=True)
    parts = [jnp.exp2((x - peak) * TO_LOG2) for x in (first, last, mid)]
    for n, x in enumerate(parts):
        p_ref[n * BLOCK : (n + 1) * BLOCK, :] = x
    total = jnp.sum(parts[0] + parts[1] + parts[2], axis=0, keepdims=True)
    pb = [x.astype(BF) for x in parts]
    mixed = dot_nn(
        jnp.concatenate([v0, v3], axis=1), jnp.concatenate(pb[:2], axis=0)
    ) + jnp.concatenate([dot_nn(v2, pb[2][:, :BLOCK]), dot_nn(v1, pb[2][:, BLOCK:])], axis=1)
    return peak, total, mixed


def far_backward(k_t, v, q, p_ref, factor, g, ec):
    k0, k1, k2, k3 = k_t
    v0, v1, v2, v3 = v
    e_out = p_ref[: 2 * BLOCK, :] * factor
    e_mid = p_ref[2 * BLOCK :, :] * factor
    eb_out, eb_mid = e_out.astype(BF), e_mid.astype(BF)
    p_out = dot_nt(jnp.concatenate([v0, v3], axis=0), g)
    p_mid = jnp.concatenate([dot_nt(v2, g[:BLOCK]), dot_nt(v1, g[BLOCK:])], axis=1)
    r_out = (e_out * (p_out - ec)).astype(BF)
    r_mid = (e_mid * (p_mid - ec)).astype(BF)
    dv03 = dot_nn(eb_out, g)
    dv2 = dot_nn(eb_mid[:, :BLOCK], g[:BLOCK])
    dv1 = dot_nn(eb_mid[:, BLOCK:], g[BLOCK:])
    dk03 = dot_nn(r_out, q)
    dk2 = dot_nn(r_mid[:, :BLOCK], q[:BLOCK])
    dk1 = dot_nn(r_mid[:, BLOCK:], q[BLOCK:])
    dq_t = dot_nn(jnp.concatenate([k0, k3], axis=1), r_out) + jnp.concatenate(
        [dot_nn(k2, r_mid[:, :BLOCK]), dot_nn(k1, r_mid[:, BLOCK:])], axis=1
    )
    return (dk03[:BLOCK], dk1, dk2, dk03[BLOCK:]), (dv03[:BLOCK], dv1, dv2, dv03[BLOCK:]), dq_t


def main_kernel(qg_first, where, kv_own, kv_got, *refs):
    if qg_first:
        refs = (*refs[2:4], *refs[:2], *refs[4:])
    one_chunk(where, kv_own, kv_got, *refs)


def one_chunk(
    where, kv_own, kv_got, near_got, wide_got, qg_own, qg_got,
    oq_own, oq_far, grad, near_out, wide_out,
    raw, raw_t, one, one_t, two, two_t, qs, gs, p0, p1, p2, acc0, acc1, acc2, oq, halos,
):
    side = where[0]
    odd = where[3]
    halos[1 - odd] = near_got[...]
    halos[odd] = wide_got[...]
    from_left, from_right = halos.at[0], halos.at[1]
    to_left, to_right = halos.at[0], halos.at[1]
    width = kv_own.shape[1] // 2
    left_bias = (1 - where[1]).astype(F32) * MASKED
    right_bias = (1 - where[2]).astype(F32) * MASKED
    own_at = pl.multiple_of(side * 512, 512)
    got_at = pl.multiple_of((1 - side) * 512, 512)
    for h in range(width // HEAD):
        kc = slice(h * HEAD, (h + 1) * HEAD)
        vc = slice(width + h * HEAD, width + (h + 1) * HEAD)
        for n, cols in ((0, kc), (1, vc)):
            raw[n, 0:256, :] = from_left[0:256, cols]
            raw[n, pl.ds(256 + own_at, 512), :] = kv_own[:, cols]
            raw[n, pl.ds(256 + got_at, 512), :] = kv_got[:, cols]
            raw[n, 1280:1536, :] = from_right[0:256, cols]
            one[n, 0:128, :] = from_left[256:384, cols]
            for i in range(6):
                block = pool1(raw[n, i * PARENT : (i + 1) * PARENT, :])
                at = (i + 1) * BLOCK
                one[n, at : at + BLOCK, :] = block
            one[n, 896:1024, :] = from_right[256:384, cols]
            two[n, 0:128, :] = from_left[384:512, cols]
            two[n, 128:192, :] = pool12(one[n, 0:128, :])
            two[n, 192:256, :] = pool2(raw[n, 0:256, :])
            two[n, 256:320, :] = pool2(raw[n, 1280:1536, :])
            two[n, 320:384, :] = pool12(one[n, 896:1024, :])
            two[n, 384:512, :] = from_right[384:512, cols]
            for i in range(6):
                rows = slice(i * PARENT, (i + 1) * PARENT)
                raw_t[n, :, rows] = raw[n, rows, :].T
            for i in range(8):
                rows = slice(i * BLOCK, (i + 1) * BLOCK)
                one_t[n, :, rows] = one[n, rows, :].T
            for i in range(4):
                rows = slice(i * BLOCK, (i + 1) * BLOCK)
                two_t[n, :, rows] = two[n, rows, :].T
        qs[pl.ds(own_at, 512), :] = qg_own[:, kc]
        qs[pl.ds(got_at, 512), :] = qg_got[:, kc]
        gs[pl.ds(own_at, 512), :] = qg_own[:, vc]
        gs[pl.ds(got_at, 512), :] = qg_got[:, vc]

        def blocks(ref, n, which):
            return [ref[n, b * BLOCK : (b + 1) * BLOCK, :] for b in which]

        def blocks_t(ref, n, which):
            return [ref[n, :, b * BLOCK : (b + 1) * BLOCK] for b in which]

        q_parents = [qs[i * PARENT : (i + 1) * PARENT, :] for i in range(4)]
        q1 = [
            jnp.concatenate([pool1(q_parents[2 * j]), pool1(q_parents[2 * j + 1])], axis=0)
            for j in range(2)
        ]
        q2 = jnp.concatenate([pool2(x) for x in q_parents], axis=0)
        which1 = [(0, 1, 4, 5), (2, 3, 6, 7)]
        bias1 = [(left_bias, None), (None, right_bias)]
        which2 = (0, 1, 2, 3)
        far1 = [
            far_forward(
                blocks(one, 0, which1[j]), blocks_t(one_t, 1, which1[j]), q1[j], bias1[j], p1.at[j]
            )
            for j in range(2)
        ]
        far2 = far_forward(
            blocks(two, 0, which2), blocks_t(two_t, 1, which2), q2, (left_bias, right_bias), p2
        )
        g1_t, ec1, f1 = [], [], []
        g2_t, ec2, low2 = [], [], []
        dq0 = []
        for i in range(4):
            rows = slice(i * PARENT, i * PARENT + 3 * PARENT)
            q = q_parents[i]
            g = gs[i * PARENT : (i + 1) * PARENT, :]
            s = dot_nt(raw[0, rows, :], q)
            pieces = [s[:PARENT], s[PARENT : 2 * PARENT], s[2 * PARENT :]]
            if i == 0:
                pieces[0] = pieces[0] + left_bias
            if i == 3:
                pieces[2] = pieces[2] + right_bias
            m0 = jnp.max(
                jnp.maximum(jnp.maximum(pieces[0], pieces[1]), pieces[2]), axis=0, keepdims=True
            )
            e = [jnp.exp2((x - m0) * TO_LOG2) for x in pieces]
            for n in range(3):
                p0[i % 2, n * PARENT : (n + 1) * PARENT, :] = e[n]
            z0 = jnp.sum(e[0] + e[1] + e[2], axis=0, keepdims=True)
            u0 = dot_nn(raw_t[1, :, rows], jnp.concatenate([x.astype(BF) for x in e], axis=0))
            j, half = i // 2, i % 2
            lanes = slice(half * BLOCK, (half + 1) * BLOCK)
            m1, z1, u1 = (x[:, lanes] for x in far1[j])
            lanes2 = slice(j * BLOCK, (j + 1) * BLOCK)
            m2, z2, u2 = (spread64(x[:, lanes2], half) for x in far2)
            m1w, m2w = twice(m1, 1), twice(m2, 1)
            m = jnp.maximum(jnp.maximum(m0, m1w), m2w)
            a0 = jnp.exp2((m0 - m) * TO_LOG2)
            a1 = 2.0 * jnp.exp2((m1w - m) * TO_LOG2)
            a2 = 4.0 * jnp.exp2((m2w - m) * TO_LOG2)
            z = a0 * z0 + a1 * twice(z1, 1) + a2 * twice(z2, 1)
            inv = 1.0 / z
            o = ((a0 * inv) * u0 + (a1 * inv) * twice(u1, 1) + (a2 * inv) * twice(u2, 1)).astype(BF)
            oq[i, 0, h * HEAD : (h + 1) * HEAD, :] = o
            lg = m * TO_LOG2 + jnp.log2(z)
            g_t = g.astype(F32).T
            dr = jnp.sum(o.astype(F32) * g_t, axis=0, keepdims=True)
            lg_a, lg_b = lg[:, :BLOCK], lg[:, BLOCK:]
            g_a, g_b = g_t[:, :BLOCK], g_t[:, BLOCK:]
            dr_a, dr_b = dr[:, :BLOCK], dr[:, BLOCK:]
            low = jnp.minimum(lg_a, lg_b)
            w_a, w_b = jnp.exp2(low - lg_a), jnp.exp2(low - lg_b)
            g1_t.append((w_a * g_a + w_b * g_b).astype(BF))
            ec1.append(w_a * dr_a + w_b * dr_b)
            f1.append(2.0 * jnp.exp2(m1 * TO_LOG2 - low))
            lower = jnp.minimum(low, swap64(low))
            w_a, w_b = jnp.exp2(lower - lg_a), jnp.exp2(lower - lg_b)
            part = w_a * g_a + w_b * g_b
            g2_t.append(part + swap64(part))
            part = w_a * dr_a + w_b * dr_b
            ec2.append(part + swap64(part))
            low2.append(lower)
            f0 = jnp.exp2(m0 * TO_LOG2 - lg)
            products = dot_nt(raw[1, rows, :], g)
            weights = p0[i % 2] * f0
            eb = weights.astype(BF)
            r = (weights * (products - dr)).astype(BF)
            for n, x in ((1, dot_nn(eb, g)), (0, dot_nn(r, q))):
                if i == 0:
                    acc0[n, rows, :] = x
                else:
                    old = slice(i * PARENT, (i + 2) * PARENT)
                    acc0[n, old, :] += x[: 2 * PARENT]
                    acc0[n, (i + 2) * PARENT : (i + 3) * PARENT, :] = x[2 * PARENT :]
            dq0.append(dot_nn(raw_t[0, :, rows], r))
        dq1 = []
        for j in range(2):
            pair = slice(2 * j, 2 * j + 2)
            g1 = jnp.concatenate([x.astype(F32).T.astype(BF) for x in g1_t[pair]], axis=0)
            dk, dv, dq = far_backward(
                blocks_t(one_t, 0, which1[j]), blocks(one, 1, which1[j]), q1[j], p1.at[j],
                jnp.concatenate(f1[pair], axis=1), g1, jnp.concatenate(ec1[pair], axis=1),
            )
            for n, b in enumerate(which1[j]):
                acc1[0, b * BLOCK : (b + 1) * BLOCK, :] = dk[n]
                acc1[1, b * BLOCK : (b + 1) * BLOCK, :] = dv[n]
            dq1.append(dq)

        def joined(parts):
            return jnp.concatenate(
                [
                    jnp.where(low_lanes(parts[0].shape), parts[2 * j], parts[2 * j + 1])
                    for j in range(2)
                ],
                axis=1,
            )

        g2 = joined(g2_t).T.astype(BF)
        f2 = 4.0 * jnp.exp2(far2[0] * TO_LOG2 - joined(low2))
        dk, dv, dq2 = far_backward(
            blocks_t(two_t, 0, which2), blocks(two, 1, which2), q2, p2, f2, g2, joined(ec2)
        )
        for n in range(4):
            acc2[0, n * BLOCK : (n + 1) * BLOCK, :] = dk[n]
            acc2[1, n * BLOCK : (n + 1) * BLOCK, :] = dv[n]
        for i in range(4):
            j, half = i // 2, i % 2
            d1 = dq1[j][:, half * BLOCK : (half + 1) * BLOCK]
            d2 = spread64(dq2[:, j * BLOCK : (j + 1) * BLOCK], half)
            coarse = 0.5 * d1 + 0.25 * d2
            oq[i, 1, h * HEAD : (h + 1) * HEAD, :] = ((dq0[i] + twice(coarse, 1)) * INV_ROOT).astype(BF)
        for n, cols, scale in ((0, kc, INV_ROOT), (1, vc, 1.0)):
            for i in range(4):
                rows = slice((i + 1) * PARENT, (i + 2) * PARENT)
                coarse = acc1[n, (i + 2) * BLOCK : (i + 3) * BLOCK, :] * (0.5 * scale)
                grad[i * PARENT : (i + 1) * PARENT, cols] = acc0[n, rows, :] * scale + twice(coarse)
            far = acc2[n, 128:256, :] * (0.25 * scale)
            mid = acc1[n, 0:256, :] * (0.5 * scale)
            near = acc0[n, 0:256, :] * scale
            to_left[0:256, cols] = (near + twice(mid[128:] + twice(far[64:]))).astype(BF)
            to_left[256:384, cols] = (mid[:128] + twice(far[:64])).astype(BF)
            to_left[384:512, cols] = (acc2[n, 0:128, :] * (0.25 * scale)).astype(BF)
            far = acc2[n, 256:384, :] * (0.25 * scale)
            mid = acc1[n, 768:1024, :] * (0.5 * scale)
            near = acc0[n, 1280:1536, :] * scale
            to_right[0:256, cols] = (near + twice(mid[:128] + twice(far[:64]))).astype(BF)
            to_right[256:384, cols] = (mid[128:] + twice(far[64:])).astype(BF)
            to_right[384:512, cols] = (acc2[n, 384:512, :] * (0.25 * scale)).astype(BF)
    oq_own[...] = oq[pl.ds(side * 2, 2)]
    oq_far[...] = oq[pl.ds((1 - side) * 2, 2)]
    near_out[...] = halos[1 - odd]
    wide_out[...] = halos[odd]


def main(where, kv_own, kv_got, near_got, wide_got, qg_own, qg_got, qg_first):
    rows, both = kv_own.shape
    width = both // 2
    oq_shape = jax.ShapeDtypeStruct((2, 2, width, PARENT), BF)
    halo_shape = jax.ShapeDtypeStruct((512, both), BF)
    operands = [kv_own, kv_got, near_got, wide_got, qg_own, qg_got]
    if qg_first:
        operands = operands[:2] + operands[4:] + operands[2:4]
    return pl.pallas_call(
        functools.partial(main_kernel, qg_first),
        in_specs=[smem()] + [vmem()] * 6,
        out_specs=[vmem()] * 5,
        out_shape=[
            oq_shape,
            oq_shape,
            jax.ShapeDtypeStruct((2 * rows, both), F32),
            halo_shape,
            halo_shape,
        ],
        scratch_shapes=[
            pltpu.VMEM((2, 1536, HEAD), BF),
            pltpu.VMEM((2, HEAD, 1536), BF),
            pltpu.VMEM((2, 1024, HEAD), BF),
            pltpu.VMEM((2, HEAD, 1024), BF),
            pltpu.VMEM((2, 512, HEAD), BF),
            pltpu.VMEM((2, HEAD, 512), BF),
            pltpu.VMEM((1024, HEAD), BF),
            pltpu.VMEM((1024, HEAD), BF),
            pltpu.VMEM((2, 768, PARENT), F32),
            pltpu.VMEM((2, 384, PARENT), F32),
            pltpu.VMEM((384, PARENT), F32),
            pltpu.VMEM((2, 1536, HEAD), F32),
            pltpu.VMEM((2, 1024, HEAD), F32),
            pltpu.VMEM((2, 512, HEAD), F32),
            pltpu.VMEM((4, 2, width, PARENT), BF),
            pltpu.VMEM((2, 512, both), BF),
        ],
        compiler_params=pltpu.CompilerParams(vmem_limit_bytes=24 * 1024 * 1024),
        cost_estimate=light(),
    )(where, *operands)


def join_kernel(where, grad, near_got, wide_got, own, far):
    def fill(first, second, from_left, from_right):
        def parent(i):
            return grad[i * PARENT : (i + 1) * PARENT, :]

        def part(ref, start, stop):
            return ref[start:stop, :].astype(F32)

        first[0:256, :] = (
            parent(0) + part(from_left, 0, 256) + twice(twice(part(from_right, 384, 448)))
        ).astype(BF)
        first[256:512, :] = (
            parent(1) + twice(part(from_left, 256, 384) + twice(part(from_right, 448, 512)))
        ).astype(BF)
        second[0:256, :] = (
            parent(2) + twice(part(from_right, 256, 384) + twice(part(from_left, 384, 448)))
        ).astype(BF)
        second[256:512, :] = (
            parent(3) + part(from_right, 0, 256) + twice(twice(part(from_left, 448, 512)))
        ).astype(BF)

    for side in range(2):
        for odd in range(2):

            @pl.when((where[0] == side) & (where[3] == odd))
            def _(side=side, odd=odd):
                halves = (own, far) if side == 0 else (far, own)
                fill(*halves, *((wide_got, near_got) if odd == 0 else (near_got, wide_got)))


def join(where, grad, near_got, wide_got):
    shape = jax.ShapeDtypeStruct(near_got.shape, BF)
    return pl.pallas_call(
        join_kernel,
        in_specs=[smem(), vmem(), vmem(), vmem()],
        out_specs=[vmem(), vmem()],
        out_shape=[shape, shape],
        compiler_params=small(),
        cost_estimate=light(),
    )(where, grad, near_got, wide_got)


def unpack_rows_kernel(where, *refs):
    ins, (first, second) = refs[:-2], refs[-2:]
    order = order_matrix(True)
    width = ins[0].shape[1] // 2
    side = where[0]
    blocks = [(side * CHUNKS + c, ins[c]) for c in range(CHUNKS)]
    blocks += [((1 - side) * CHUNKS + 1 - LATE_CHUNK, ins[CHUNKS])]
    for block, ref in blocks:
        at = pl.ds(pl.multiple_of(block * width, width), width)
        for i in range(2):
            rows = slice(i * PARENT, (i + 1) * PARENT)
            first[rows, at] = dot_nn(order, ref[rows, :width]).astype(BF)
            second[rows, at] = dot_nn(order, ref[rows, width:]).astype(BF)


def unpack_rows(where, own, got, shape):
    out = jax.ShapeDtypeStruct(shape, BF)
    return pl.pallas_call(
        unpack_rows_kernel,
        in_specs=[smem()] + [vmem()] * (CHUNKS + 1),
        out_specs=[vmem(), vmem()],
        out_shape=[out, out],
        compiler_params=small(),
        cost_estimate=light(),
    )(where, *own, got)


def unpack_last_kernel(where, got, first_in, second_in, first, second, held, sems):
    del first_in, second_in
    order = order_matrix(True)
    width = got.shape[1] // 2
    block = (1 - where[0]) * CHUNKS + LATE_CHUNK
    at = pl.ds(pl.multiple_of(block * width, width), width)
    copies = []
    for i in range(2):
        rows = slice(i * PARENT, (i + 1) * PARENT)
        x = dot_nn(order, got[rows, :]).astype(BF)
        for m, ref in enumerate((first, second)):
            held[m, rows, :] = x[:, m * width : (m + 1) * width]
            copies.append(
                pltpu.make_async_copy(held.at[m, rows, :], ref.at[rows, at], sems.at[2 * i + m])
            )
            copies[-1].start()
    for copy in copies:
        copy.wait()


def unpack_last(where, got, first, second):
    out = jax.ShapeDtypeStruct(first.shape, BF)
    hbm = pl.BlockSpec(memory_space=pltpu.HBM)
    return pl.pallas_call(
        unpack_last_kernel,
        in_specs=[smem(), vmem(), hbm, hbm],
        out_specs=[hbm, hbm],
        out_shape=[out, out],
        input_output_aliases={2: 0, 3: 1},
        scratch_shapes=[
            pltpu.VMEM((2, got.shape[0], got.shape[1] // 2), BF),
            pltpu.SemaphoreType.DMA((4,)),
        ],
        compiler_params=small(),
        cost_estimate=light(),
    )(where, got, first, second)


def unpack_columns_kernel(where, *refs):
    ins, (first, second) = refs[:-2], refs[-2:]
    order = order_matrix(True)
    width = ins[0].shape[2]
    for c in range(CHUNKS):
        for ref, side in ((ins[c], where[0]), (ins[CHUNKS + c], 1 - where[0])):
            at = pl.ds(pl.multiple_of((side * CHUNKS + c) * width, width), width)
            for i in range(2):
                rows = slice(i * PARENT, (i + 1) * PARENT)
                first[rows, at] = dot_nt(order, ref[i, 0]).astype(BF)
                second[rows, at] = dot_nt(order, ref[i, 1]).astype(BF)


def unpack_columns(where, own, got, shape):
    out = jax.ShapeDtypeStruct(shape, BF)
    return pl.pallas_call(
        unpack_columns_kernel,
        in_specs=[smem()] + [vmem()] * (2 * CHUNKS),
        out_specs=[vmem(), vmem()],
        out_shape=[out, out],
        compiler_params=small(),
        cost_estimate=light(),
    )(where, *own, *got)


def on_device(queries, key_matrix, value_matrix, cotangent):
    axes = ("outer", "inner")
    count = lax.axis_size("outer") * lax.axis_size("inner")
    device = lax.axis_index("outer") * lax.axis_size("inner") + lax.axis_index("inner")
    pair = device // 2
    where = jnp.stack([device % 2, pair > 0, pair < count // 2 - 1, pair % 2]).astype(jnp.int32)
    across = [(i, i ^ 1) for i in range(count)]
    near_edges = [(i, i ^ 2) for i in range(count) if i ^ 2 < count]
    wide_edges = [(i, i + 2 if i // 2 % 2 else i - 2) for i in range(count)]
    wide_edges = [(i, j) for i, j in wide_edges if 0 <= j < count]

    def swap(x):
        return lax.ppermute(x, axes, across)

    def beside(near, wide):
        near = lax.ppermute(near, axes, near_edges)
        return near, lax.ppermute(wide, axes, wide_edges)

    kv_far = [pack_cut(1 - device % 2, 0, key_matrix, value_matrix)]
    for c in range(1, CHUNKS):
        later, kv_far[0] = lax.optimization_barrier(((key_matrix, value_matrix), kv_far[0]))
        kv_far.append(pack_cut(1 - device % 2, c, *later))
    qg_far = pack(False, where, queries, cotangent)
    packed = pack(True, where, key_matrix, value_matrix, queries, cotangent)
    kv, qg = packed[:CHUNKS], packed[CHUNKS:]
    oq_own, oq_got, back = [], [], []
    for c in range(CHUNKS):
        got_kv = swap(kv_far[c])
        near, wide = halo(where, kv[c], got_kv)
        far = qg_far[c]
        if c > 0:
            near, wide, far = lax.optimization_barrier((near, wide, far))
        near, wide = beside(near, wide)
        own, far, grad, near, wide = main(where, kv[c], got_kv, near, wide, qg[c], swap(far), c == 0)
        oq_own.append(own)
        oq_got.append(swap(far))
        if c > 0:
            oq_got[c - 1], near, wide = lax.optimization_barrier((oq_got[c - 1], near, wide))
        back.append([grad, *beside(near, wide)])
    oq_got[-1], back[-1] = lax.optimization_barrier((oq_got[-1], back[-1]))
    kv_own, kv_got = [], []
    for c in range(CHUNKS):
        own, far = join(where, *back[c])
        kv_own.append(own)
        kv_got.append(swap(far))
    attended, query_grad = unpack_columns(where, oq_own, oq_got, queries.shape)
    key_grad, value_grad = unpack_rows(where, kv_own, kv_got[1 - LATE_CHUNK], queries.shape)
    key_grad, value_grad = unpack_last(where, kv_got[LATE_CHUNK], key_grad, value_grad)
    return attended, query_grad, key_grad, value_grad


def solution(mesh):
    spec = P(("outer", "inner"), None)
    return jax.shard_map(
        on_device,
        mesh=mesh,
        in_specs=(spec,) * 4,
        out_specs=(spec,) * 4,
        check_vma=False,
    )
```

```python
import functools
import math

import jax
import jax.numpy as jnp
from jax import lax
from jax.experimental import pallas as pl
from jax.experimental.pallas import tpu as pltpu
from jax.sharding import PartitionSpec as P

HEAD = 128
BLOCK = 128
PARENT = 256
LEVELS = 3
CHUNKS = 2
LATE_CHUNK = 1
INV_ROOT = HEAD**-0.5
TO_LOG2 = INV_ROOT * math.log2(math.e)
MASKED = -1e30
BF = jnp.bfloat16
F32 = jnp.float32


def dot_nt(a, b):
    return lax.dot_general(a, b, (((1,), (1,)), ((), ())), preferred_element_type=F32)


def dot_nn(a, b):
    return jnp.dot(a, b, preferred_element_type=F32)


def order_matrix(inverse):
    row = lax.broadcasted_iota(jnp.int32, (PARENT, PARENT), 0)
    col = lax.broadcasted_iota(jnp.int32, (PARENT, PARENT), 1)
    place, token = (col, row) if inverse else (row, col)
    slab = place // 64
    source = 4 * (place % 64) + 2 * (slab % 2) + slab // 2
    return jnp.where(source == token, 1.0, 0.0).astype(BF)


def pool1(x):
    return ((x[:BLOCK].astype(F32) + x[BLOCK:].astype(F32)) * 0.5).astype(BF)


def pool2(x):
    half = x[:BLOCK].astype(F32) + x[BLOCK:].astype(F32)
    return ((half[:64] + half[64:]) * 0.25).astype(BF)


def pool12(x):
    return ((x[:64].astype(F32) + x[64:].astype(F32)) * 0.5).astype(BF)


def twice(x, axis=0):
    return jnp.concatenate([x, x], axis=axis)


def pack_kernel(own, where, *refs):
    count = 4 if own else 2
    arrays, outs, (held, sems) = refs[:count], refs[count:-2], refs[-2:]
    rows, columns = arrays[0].shape
    half = columns // 2
    width = half // CHUNKS
    side = where[0] if own else 1 - where[0]
    at = pl.ds(pl.multiple_of(side * half, half), half)
    copies = [
        pltpu.make_async_copy(ref.at[:, at], held.at[m], sems.at[m]) for m, ref in enumerate(arrays)
    ]
    for copy in copies:
        copy.start()
    order = order_matrix(False)
    for m in range(count):
        copies[m].wait()
        first = m % 2 * width
        for i in range(rows // PARENT):
            at = slice(i * PARENT, (i + 1) * PARENT)
            x = dot_nn(order, held[m, at, :]).astype(BF)
            for c in range(CHUNKS):
                out = outs[m // 2 * CHUNKS + c]
                out[at, first : first + width] = x[:, c * width : (c + 1) * width]


def pack(own, where, *arrays):
    rows, columns = arrays[0].shape
    count = len(arrays)
    return pl.pallas_call(
        functools.partial(pack_kernel, own),
        in_specs=[smem()] + [pl.BlockSpec(memory_space=pltpu.HBM)] * count,
        out_specs=[vmem()] * (count // 2 * CHUNKS),
        out_shape=[jax.ShapeDtypeStruct((rows, columns // CHUNKS), BF)] * (count // 2 * CHUNKS),
        scratch_shapes=[
            pltpu.VMEM((count, rows, columns // 2), BF),
            pltpu.SemaphoreType.DMA((count,)),
        ],
        compiler_params=small(),
        cost_estimate=light(),
    )(where, *arrays)


def pack_cut_kernel(a, b, out):
    order = order_matrix(False)
    width = a.shape[1]
    for m, ref in enumerate((a, b)):
        for i in range(a.shape[0] // PARENT):
            rows = slice(i * PARENT, (i + 1) * PARENT)
            out[rows, m * width : (m + 1) * width] = dot_nn(order, ref[rows, :]).astype(BF)


def pack_cut(side, chunk, a, b):
    rows, columns = a.shape
    width = columns // 2 // CHUNKS
    cut = [lax.dynamic_slice_in_dim(x, (side * CHUNKS + chunk) * width, width, 1) for x in (a, b)]
    return pl.pallas_call(
        pack_cut_kernel,
        in_specs=[vmem(), vmem()],
        out_specs=vmem(),
        out_shape=jax.ShapeDtypeStruct((rows, 2 * width), BF),
        compiler_params=small(),
        cost_estimate=light(),
    )(*cut)


def smem():
    return pl.BlockSpec(memory_space=pltpu.SMEM)


def vmem():
    return pl.BlockSpec(memory_space=pltpu.VMEM)


def small():
    return pltpu.CompilerParams(vmem_limit_bytes=8 * 1024 * 1024)


def light():
    return pl.CostEstimate(flops=1000, bytes_accessed=1000, transcendentals=0)


def halo_kernel(where, own, got, near, wide):
    def fill(first, second, to_right, to_left):
        to_right[0:256, :] = second[256:512, :]
        to_right[256:384, :] = pool1(second[0:256, :])
        to_right[384:448, :] = pool2(first[0:256, :])
        to_right[448:512, :] = pool2(first[256:512, :])
        to_left[0:256, :] = first[0:256, :]
        to_left[256:384, :] = pool1(first[256:512, :])
        to_left[384:448, :] = pool2(second[0:256, :])
        to_left[448:512, :] = pool2(second[256:512, :])

    for side in range(2):
        for odd in range(2):

            @pl.when((where[0] == side) & (where[3] == odd))
            def _(side=side, odd=odd):
                halves = (own, got) if side == 0 else (got, own)
                fill(*halves, *((near, wide) if odd == 0 else (wide, near)))


def halo(where, own, got):
    shape = jax.ShapeDtypeStruct(own.shape, BF)
    return pl.pallas_call(
        halo_kernel,
        in_specs=[smem(), vmem(), vmem()],
        out_specs=[vmem(), vmem()],
        out_shape=[shape, shape],
        compiler_params=small(),
        cost_estimate=light(),
    )(where, own, got)


def swap64(x):
    return pltpu.roll(x, 64, 1)


def low_lanes(shape):
    return lax.broadcasted_iota(jnp.int32, shape, 1) < 64


def spread64(x, half):
    other = swap64(x)
    low = low_lanes(x.shape)
    return jnp.where(low, x, other) if half == 0 else jnp.where(low, other, x)


def far_forward(k, v_t, q, bias, p_ref):
    k0, k1, k2, k3 = k
    v0, v1, v2, v3 = v_t
    left, right = bias
    outer = dot_nt(jnp.concatenate([k0, k3], axis=0), q)
    first, last = outer[:BLOCK], outer[BLOCK:]
    mid_low = dot_nt(k2, q[:BLOCK])
    mid_high = dot_nt(k1, q[BLOCK:])
    if left is not None:
        first = first + left
        mid_high = mid_high + left
    if right is not None:
        last = last + right
        mid_low = mid_low + right
    mid = jnp.concatenate([mid_low, mid_high], axis=1)
    peak = jnp.max(jnp.maximum(jnp.maximum(first, last), mid), axis=0, keepdims=True)
    parts = [jnp.exp2((x - peak) * TO_LOG2) for x in (first, last, mid)]
    for n, x in enumerate(parts):
        p_ref[n * BLOCK : (n + 1) * BLOCK, :] = x
    total = jnp.sum(parts[0] + parts[1] + parts[2], axis=0, keepdims=True)
    pb = [x.astype(BF) for x in parts]
    mixed = dot_nn(
        jnp.concatenate([v0, v3], axis=1), jnp.concatenate(pb[:2], axis=0)
    ) + jnp.concatenate([dot_nn(v2, pb[2][:, :BLOCK]), dot_nn(v1, pb[2][:, BLOCK:])], axis=1)
    return peak, total, mixed


def far_backward(k_t, v, q, p_ref, factor, g, ec):
    k0, k1, k2, k3 = k_t
    v0, v1, v2, v3 = v
    e_out = p_ref[: 2 * BLOCK, :] * factor
    e_mid = p_ref[2 * BLOCK :, :] * factor
    eb_out, eb_mid = e_out.astype(BF), e_mid.astype(BF)
    p_out = dot_nt(jnp.concatenate([v0, v3], axis=0), g)
    p_mid = jnp.concatenate([dot_nt(v2, g[:BLOCK]), dot_nt(v1, g[BLOCK:])], axis=1)
    r_out = (e_out * (p_out - ec)).astype(BF)
    r_mid = (e_mid * (p_mid - ec)).astype(BF)
    dv03 = dot_nn(eb_out, g)
    dv2 = dot_nn(eb_mid[:, :BLOCK], g[:BLOCK])
    dv1 = dot_nn(eb_mid[:, BLOCK:], g[BLOCK:])
    dk03 = dot_nn(r_out, q)
    dk2 = dot_nn(r_mid[:, :BLOCK], q[:BLOCK])
    dk1 = dot_nn(r_mid[:, BLOCK:], q[BLOCK:])
    dq_t = dot_nn(jnp.concatenate([k0, k3], axis=1), r_out) + jnp.concatenate(
        [dot_nn(k2, r_mid[:, :BLOCK]), dot_nn(k1, r_mid[:, BLOCK:])], axis=1
    )
    return (dk03[:BLOCK], dk1, dk2, dk03[BLOCK:]), (dv03[:BLOCK], dv1, dv2, dv03[BLOCK:]), dq_t


def main_kernel(qg_first, where, kv_own, kv_got, *refs):
    if qg_first:
        refs = (*refs[2:4], *refs[:2], *refs[4:])
    one_chunk(where, kv_own, kv_got, *refs)


def one_chunk(
    where, kv_own, kv_got, near_got, wide_got, qg_own, qg_got,
    oq_own, oq_far, grad, near_out, wide_out,
    raw, raw_t, one, one_t, two, two_t, qs, gs, p0, p1, p2, acc0, acc1, acc2, oq, halos,
):
    side = where[0]
    odd = where[3]
    halos[1 - odd] = near_got[...]
    halos[odd] = wide_got[...]
    from_left, from_right = halos.at[0], halos.at[1]
    to_left, to_right = halos.at[0], halos.at[1]
    width = kv_own.shape[1] // 2
    left_bias = (1 - where[1]).astype(F32) * MASKED
    right_bias = (1 - where[2]).astype(F32) * MASKED
    own_at = pl.multiple_of(side * 512, 512)
    got_at = pl.multiple_of((1 - side) * 512, 512)
    for h in range(width // HEAD):
        kc = slice(h * HEAD, (h + 1) * HEAD)
        vc = slice(width + h * HEAD, width + (h + 1) * HEAD)
        for n, cols in ((0, kc), (1, vc)):
            raw[n, 0:256, :] = from_left[0:256, cols]
            raw[n, pl.ds(256 + own_at, 512), :] = kv_own[:, cols]
            raw[n, pl.ds(256 + got_at, 512), :] = kv_got[:, cols]
            raw[n, 1280:1536, :] = from_right[0:256, cols]
            one[n, 0:128, :] = from_left[256:384, cols]
            for i in range(6):
                block = pool1(raw[n, i * PARENT : (i + 1) * PARENT, :])
                at = (i + 1) * BLOCK
                one[n, at : at + BLOCK, :] = block
            one[n, 896:1024, :] = from_right[256:384, cols]
            two[n, 0:128, :] = from_left[384:512, cols]
            two[n, 128:192, :] = pool12(one[n, 0:128, :])
            two[n, 192:256, :] = pool2(raw[n, 0:256, :])
            two[n, 256:320, :] = pool2(raw[n, 1280:1536, :])
            two[n, 320:384, :] = pool12(one[n, 896:1024, :])
            two[n, 384:512, :] = from_right[384:512, cols]
            for i in range(6):
                rows = slice(i * PARENT, (i + 1) * PARENT)
                raw_t[n, :, rows] = raw[n, rows, :].T
            for i in range(8):
                rows = slice(i * BLOCK, (i + 1) * BLOCK)
                one_t[n, :, rows] = one[n, rows, :].T
            for i in range(4):
                rows = slice(i * BLOCK, (i + 1) * BLOCK)
                two_t[n, :, rows] = two[n, rows, :].T
        qs[pl.ds(own_at, 512), :] = qg_own[:, kc]
        qs[pl.ds(got_at, 512), :] = qg_got[:, kc]
        gs[pl.ds(own_at, 512), :] = qg_own[:, vc]
        gs[pl.ds(got_at, 512), :] = qg_got[:, vc]

        def blocks(ref, n, which):
            return [ref[n, b * BLOCK : (b + 1) * BLOCK, :] for b in which]

        def blocks_t(ref, n, which):
            return [ref[n, :, b * BLOCK : (b + 1) * BLOCK] for b in which]

        q_parents = [qs[i * PARENT : (i + 1) * PARENT, :] for i in range(4)]
        q1 = [
            jnp.concatenate([pool1(q_parents[2 * j]), pool1(q_parents[2 * j + 1])], axis=0)
            for j in range(2)
        ]
        q2 = jnp.concatenate([pool2(x) for x in q_parents], axis=0)
        which1 = [(0, 1, 4, 5), (2, 3, 6, 7)]
        bias1 = [(left_bias, None), (None, right_bias)]
        which2 = (0, 1, 2, 3)
        far1 = [
            far_forward(
                blocks(one, 0, which1[j]), blocks_t(one_t, 1, which1[j]), q1[j], bias1[j], p1.at[j]
            )
            for j in range(2)
        ]
        far2 = far_forward(
            blocks(two, 0, which2), blocks_t(two_t, 1, which2), q2, (left_bias, right_bias), p2
        )
        g1_t, ec1, f1 = [], [], []
        g2_t, ec2, low2 = [], [], []
        dq0 = []
        for i in range(4):
            rows = slice(i * PARENT, i * PARENT + 3 * PARENT)
            q = q_parents[i]
            g = gs[i * PARENT : (i + 1) * PARENT, :]
            s = dot_nt(raw[0, rows, :], q)
            pieces = [s[:PARENT], s[PARENT : 2 * PARENT], s[2 * PARENT :]]
            if i == 0:
                pieces[0] = pieces[0] + left_bias
            if i == 3:
                pieces[2] = pieces[2] + right_bias
            m0 = jnp.max(
                jnp.maximum(jnp.maximum(pieces[0], pieces[1]), pieces[2]), axis=0, keepdims=True
            )
            e = [jnp.exp2((x - m0) * TO_LOG2) for x in pieces]
            for n in range(3):
                p0[i % 2, n * PARENT : (n + 1) * PARENT, :] = e[n]
            z0 = jnp.sum(e[0] + e[1] + e[2], axis=0, keepdims=True)
            u0 = dot_nn(raw_t[1, :, rows], jnp.concatenate([x.astype(BF) for x in e], axis=0))
            j, half = i // 2, i % 2
            lanes = slice(half * BLOCK, (half + 1) * BLOCK)
            m1, z1, u1 = (x[:, lanes] for x in far1[j])
            lanes2 = slice(j * BLOCK, (j + 1) * BLOCK)
            m2, z2, u2 = (spread64(x[:, lanes2], half) for x in far2)
            m1w, m2w = twice(m1, 1), twice(m2, 1)
            m = jnp.maximum(jnp.maximum(m0, m1w), m2w)
            a0 = jnp.exp2((m0 - m) * TO_LOG2)
            a1 = 2.0 * jnp.exp2((m1w - m) * TO_LOG2)
            a2 = 4.0 * jnp.exp2((m2w - m) * TO_LOG2)
            z = a0 * z0 + a1 * twice(z1, 1) + a2 * twice(z2, 1)
            inv = 1.0 / z
            o = ((a0 * inv) * u0 + (a1 * inv) * twice(u1, 1) + (a2 * inv) * twice(u2, 1)).astype(BF)
            oq[i, 0, h * HEAD : (h + 1) * HEAD, :] = o
            lg = m * TO_LOG2 + jnp.log2(z)
            g_t = g.astype(F32).T
            dr = jnp.sum(o.astype(F32) * g_t, axis=0, keepdims=True)
            lg_a, lg_b = lg[:, :BLOCK], lg[:, BLOCK:]
            g_a, g_b = g_t[:, :BLOCK], g_t[:, BLOCK:]
            dr_a, dr_b = dr[:, :BLOCK], dr[:, BLOCK:]
            low = jnp.minimum(lg_a, lg_b)
            w_a, w_b = jnp.exp2(low - lg_a), jnp.exp2(low - lg_b)
            g1_t.append((w_a * g_a + w_b * g_b).astype(BF))
            ec1.append(w_a * dr_a + w_b * dr_b)
            f1.append(2.0 * jnp.exp2(m1 * TO_LOG2 - low))
            lower = jnp.minimum(low, swap64(low))
            w_a, w_b = jnp.exp2(lower - lg_a), jnp.exp2(lower - lg_b)
            part = w_a * g_a + w_b * g_b
            g2_t.append(part + swap64(part))
            part = w_a * dr_a + w_b * dr_b
            ec2.append(part + swap64(part))
            low2.append(lower)
            f0 = jnp.exp2(m0 * TO_LOG2 - lg)
            products = dot_nt(raw[1, rows, :], g)
            weights = p0[i % 2] * f0
            eb = weights.astype(BF)
            r = (weights * (products - dr)).astype(BF)
            for n, x in ((1, dot_nn(eb, g)), (0, dot_nn(r, q))):
                if i == 0:
                    acc0[n, rows, :] = x
                else:
                    old = slice(i * PARENT, (i + 2) * PARENT)
                    acc0[n, old, :] += x[: 2 * PARENT]
                    acc0[n, (i + 2) * PARENT : (i + 3) * PARENT, :] = x[2 * PARENT :]
            dq0.append(dot_nn(raw_t[0, :, rows], r))
        dq1 = []
        for j in range(2):
            pair = slice(2 * j, 2 * j + 2)
            g1 = jnp.concatenate([x.astype(F32).T.astype(BF) for x in g1_t[pair]], axis=0)
            dk, dv, dq = far_backward(
                blocks_t(one_t, 0, which1[j]), blocks(one, 1, which1[j]), q1[j], p1.at[j],
                jnp.concatenate(f1[pair], axis=1), g1, jnp.concatenate(ec1[pair], axis=1),
            )
            for n, b in enumerate(which1[j]):
                acc1[0, b * BLOCK : (b + 1) * BLOCK, :] = dk[n]
                acc1[1, b * BLOCK : (b + 1) * BLOCK, :] = dv[n]
            dq1.append(dq)

        def joined(parts):
            return jnp.concatenate(
                [
                    jnp.where(low_lanes(parts[0].shape), parts[2 * j], parts[2 * j + 1])
                    for j in range(2)
                ],
                axis=1,
            )

        g2 = joined(g2_t).T.astype(BF)
        f2 = 4.0 * jnp.exp2(far2[0] * TO_LOG2 - joined(low2))
        dk, dv, dq2 = far_backward(
            blocks_t(two_t, 0, which2), blocks(two, 1, which2), q2, p2, f2, g2, joined(ec2)
        )
        for n in range(4):
            acc2[0, n * BLOCK : (n + 1) * BLOCK, :] = dk[n]
            acc2[1, n * BLOCK : (n + 1) * BLOCK, :] = dv[n]
        for i in range(4):
            j, half = i // 2, i % 2
            d1 = dq1[j][:, half * BLOCK : (half + 1) * BLOCK]
            d2 = spread64(dq2[:, j * BLOCK : (j + 1) * BLOCK], half)
            coarse = 0.5 * d1 + 0.25 * d2
            oq[i, 1, h * HEAD : (h + 1) * HEAD, :] = ((dq0[i] + twice(coarse, 1)) * INV_ROOT).astype(BF)
        for n, cols, scale in ((0, kc, INV_ROOT), (1, vc, 1.0)):
            for i in range(4):
                rows = slice((i + 1) * PARENT, (i + 2) * PARENT)
                coarse = acc1[n, (i + 2) * BLOCK : (i + 3) * BLOCK, :] * (0.5 * scale)
                grad[i * PARENT : (i + 1) * PARENT, cols] = acc0[n, rows, :] * scale + twice(coarse)
            far = acc2[n, 128:256, :] * (0.25 * scale)
            mid = acc1[n, 0:256, :] * (0.5 * scale)
            near = acc0[n, 0:256, :] * scale
            to_left[0:256, cols] = (near + twice(mid[128:] + twice(far[64:]))).astype(BF)
            to_left[256:384, cols] = (mid[:128] + twice(far[:64])).astype(BF)
            to_left[384:512, cols] = (acc2[n, 0:128, :] * (0.25 * scale)).astype(BF)
            far = acc2[n, 256:384, :] * (0.25 * scale)
            mid = acc1[n, 768:1024, :] * (0.5 * scale)
            near = acc0[n, 1280:1536, :] * scale
            to_right[0:256, cols] = (near + twice(mid[:128] + twice(far[:64]))).astype(BF)
            to_right[256:384, cols] = (mid[128:] + twice(far[64:])).astype(BF)
            to_right[384:512, cols] = (acc2[n, 384:512, :] * (0.25 * scale)).astype(BF)
    oq_own[...] = oq[pl.ds(side * 2, 2)]
    oq_far[...] = oq[pl.ds((1 - side) * 2, 2)]
    near_out[...] = halos[1 - odd]
    wide_out[...] = halos[odd]


def main(where, kv_own, kv_got, near_got, wide_got, qg_own, qg_got, qg_first):
    rows, both = kv_own.shape
    width = both // 2
    oq_shape = jax.ShapeDtypeStruct((2, 2, width, PARENT), BF)
    halo_shape = jax.ShapeDtypeStruct((512, both), BF)
    operands = [kv_own, kv_got, near_got, wide_got, qg_own, qg_got]
    if qg_first:
        operands = operands[:2] + operands[4:] + operands[2:4]
    return pl.pallas_call(
        functools.partial(main_kernel, qg_first),
        in_specs=[smem()] + [vmem()] * 6,
        out_specs=[vmem()] * 5,
        out_shape=[
            oq_shape,
            oq_shape,
            jax.ShapeDtypeStruct((2 * rows, both), F32),
            halo_shape,
            halo_shape,
        ],
        scratch_shapes=[
            pltpu.VMEM((2, 1536, HEAD), BF),
            pltpu.VMEM((2, HEAD, 1536), BF),
            pltpu.VMEM((2, 1024, HEAD), BF),
            pltpu.VMEM((2, HEAD, 1024), BF),
            pltpu.VMEM((2, 512, HEAD), BF),
            pltpu.VMEM((2, HEAD, 512), BF),
            pltpu.VMEM((1024, HEAD), BF),
            pltpu.VMEM((1024, HEAD), BF),
            pltpu.VMEM((2, 768, PARENT), F32),
            pltpu.VMEM((2, 384, PARENT), F32),
            pltpu.VMEM((384, PARENT), F32),
            pltpu.VMEM((2, 1536, HEAD), F32),
            pltpu.VMEM((2, 1024, HEAD), F32),
            pltpu.VMEM((2, 512, HEAD), F32),
            pltpu.VMEM((4, 2, width, PARENT), BF),
            pltpu.VMEM((2, 512, both), BF),
        ],
        compiler_params=pltpu.CompilerParams(vmem_limit_bytes=24 * 1024 * 1024),
        cost_estimate=light(),
    )(where, *operands)


def join_kernel(where, grad, near_got, wide_got, own, far):
    def fill(first, second, from_left, from_right):
        def parent(i):
            return grad[i * PARENT : (i + 1) * PARENT, :]

        def part(ref, start, stop):
            return ref[start:stop, :].astype(F32)

        first[0:256, :] = (
            parent(0) + part(from_left, 0, 256) + twice(twice(part(from_right, 384, 448)))
        ).astype(BF)
        first[256:512, :] = (
            parent(1) + twice(part(from_left, 256, 384) + twice(part(from_right, 448, 512)))
        ).astype(BF)
        second[0:256, :] = (
            parent(2) + twice(part(from_right, 256, 384) + twice(part(from_left, 384, 448)))
        ).astype(BF)
        second[256:512, :] = (
            parent(3) + part(from_right, 0, 256) + twice(twice(part(from_left, 448, 512)))
        ).astype(BF)

    for side in range(2):
        for odd in range(2):

            @pl.when((where[0] == side) & (where[3] == odd))
            def _(side=side, odd=odd):
                halves = (own, far) if side == 0 else (far, own)
                fill(*halves, *((wide_got, near_got) if odd == 0 else (near_got, wide_got)))


def join(where, grad, near_got, wide_got):
    shape = jax.ShapeDtypeStruct(near_got.shape, BF)
    return pl.pallas_call(
        join_kernel,
        in_specs=[smem(), vmem(), vmem(), vmem()],
        out_specs=[vmem(), vmem()],
        out_shape=[shape, shape],
        compiler_params=small(),
        cost_estimate=light(),
    )(where, grad, near_got, wide_got)


def unpack_rows_kernel(where, *refs):
    ins, (first, second) = refs[:-2], refs[-2:]
    order = order_matrix(True)
    width = ins[0].shape[1] // 2
    side = where[0]
    blocks = [(side * CHUNKS + c, ins[c]) for c in range(CHUNKS)]
    blocks += [((1 - side) * CHUNKS + 1 - LATE_CHUNK, ins[CHUNKS])]
    for block, ref in blocks:
        at = pl.ds(pl.multiple_of(block * width, width), width)
        for i in range(2):
            rows = slice(i * PARENT, (i + 1) * PARENT)
            first[rows, at] = dot_nn(order, ref[rows, :width]).astype(BF)
            second[rows, at] = dot_nn(order, ref[rows, width:]).astype(BF)


def unpack_rows(where, own, got, shape):
    out = jax.ShapeDtypeStruct(shape, BF)
    return pl.pallas_call(
        unpack_rows_kernel,
        in_specs=[smem()] + [vmem()] * (CHUNKS + 1),
        out_specs=[vmem(), vmem()],
        out_shape=[out, out],
        compiler_params=small(),
        cost_estimate=light(),
    )(where, *own, got)


def unpack_last_kernel(where, got, first_in, second_in, first, second, held, sems):
    del first_in, second_in
    order = order_matrix(True)
    width = got.shape[1] // 2
    block = (1 - where[0]) * CHUNKS + LATE_CHUNK
    at = pl.ds(pl.multiple_of(block * width, width), width)
    copies = []
    for i in range(2):
        rows = slice(i * PARENT, (i + 1) * PARENT)
        x = dot_nn(order, got[rows, :]).astype(BF)
        for m, ref in enumerate((first, second)):
            held[m, rows, :] = x[:, m * width : (m + 1) * width]
            copies.append(
                pltpu.make_async_copy(held.at[m, rows, :], ref.at[rows, at], sems.at[2 * i + m])
            )
            copies[-1].start()
    for copy in copies:
        copy.wait()


def unpack_last(where, got, first, second):
    out = jax.ShapeDtypeStruct(first.shape, BF)
    hbm = pl.BlockSpec(memory_space=pltpu.HBM)
    return pl.pallas_call(
        unpack_last_kernel,
        in_specs=[smem(), vmem(), hbm, hbm],
        out_specs=[hbm, hbm],
        out_shape=[out, out],
        input_output_aliases={2: 0, 3: 1},
        scratch_shapes=[
            pltpu.VMEM((2, got.shape[0], got.shape[1] // 2), BF),
            pltpu.SemaphoreType.DMA((4,)),
        ],
        compiler_params=small(),
        cost_estimate=light(),
    )(where, got, first, second)


def unpack_columns_kernel(where, *refs):
    ins, (first, second) = refs[:-2], refs[-2:]
    order = order_matrix(True)
    width = ins[0].shape[2]
    for c in range(CHUNKS):
        for ref, side in ((ins[c], where[0]), (ins[CHUNKS + c], 1 - where[0])):
            at = pl.ds(pl.multiple_of((side * CHUNKS + c) * width, width), width)
            for i in range(2):
                rows = slice(i * PARENT, (i + 1) * PARENT)
                first[rows, at] = dot_nt(order, ref[i, 0]).astype(BF)
                second[rows, at] = dot_nt(order, ref[i, 1]).astype(BF)


def unpack_columns(where, own, got, shape):
    out = jax.ShapeDtypeStruct(shape, BF)
    return pl.pallas_call(
        unpack_columns_kernel,
        in_specs=[smem()] + [vmem()] * (2 * CHUNKS),
        out_specs=[vmem(), vmem()],
        out_shape=[out, out],
        compiler_params=small(),
        cost_estimate=light(),
    )(where, *own, *got)


def on_device(queries, key_matrix, value_matrix, cotangent):
    axes = ("outer", "inner")
    count = lax.axis_size("outer") * lax.axis_size("inner")
    device = lax.axis_index("outer") * lax.axis_size("inner") + lax.axis_index("inner")
    pair = device // 2
    where = jnp.stack([device % 2, pair > 0, pair < count // 2 - 1, pair % 2]).astype(jnp.int32)
    across = [(i, i ^ 1) for i in range(count)]
    near_edges = [(i, i ^ 2) for i in range(count) if i ^ 2 < count]
    wide_edges = [(i, i + 2 if i // 2 % 2 else i - 2) for i in range(count)]
    wide_edges = [(i, j) for i, j in wide_edges if 0 <= j < count]

    def swap(x):
        return lax.ppermute(x, axes, across)

    def beside(near, wide):
        near = lax.ppermute(near, axes, near_edges)
        return near, lax.ppermute(wide, axes, wide_edges)

    kv_far = [pack_cut(1 - device % 2, 0, key_matrix, value_matrix)]
    for c in range(1, CHUNKS):
        later, kv_far[0] = lax.optimization_barrier(((key_matrix, value_matrix), kv_far[0]))
        kv_far.append(pack_cut(1 - device % 2, c, *later))
    qg_far = pack(False, where, queries, cotangent)
    packed = pack(True, where, key_matrix, value_matrix, queries, cotangent)
    kv, qg = packed[:CHUNKS], packed[CHUNKS:]
    oq_own, oq_got, back = [], [], []
    for c in range(CHUNKS):
        got_kv = swap(kv_far[c])
        near, wide = halo(where, kv[c], got_kv)
        far = qg_far[c]
        if c > 0:
            near, wide, far = lax.optimization_barrier((near, wide, far))
        near, wide = beside(near, wide)
        own, far, grad, near, wide = main(where, kv[c], got_kv, near, wide, qg[c], swap(far), c == 0)
        oq_own.append(own)
        oq_got.append(swap(far))
        if c > 0:
            back[c - 1], near, wide = lax.optimization_barrier((back[c - 1], near, wide))
        back.append([grad, *beside(near, wide)])
    for c in range(CHUNKS):
        oq_got[c], back[c] = lax.optimization_barrier((oq_got[c], back[c]))
    kv_own, kv_got = [], []
    for c in range(CHUNKS):
        own, far = join(where, *back[c])
        kv_own.append(own)
        kv_got.append(swap(far))
    attended, query_grad = unpack_columns(where, oq_own, oq_got, queries.shape)
    key_grad, value_grad = unpack_rows(where, kv_own, kv_got[1 - LATE_CHUNK], queries.shape)
    key_grad, value_grad = unpack_last(where, kv_got[LATE_CHUNK], key_grad, value_grad)
    return attended, query_grad, key_grad, value_grad


def solution(mesh):
    spec = P(("outer", "inner"), None)
    return jax.shard_map(
        on_device,
        mesh=mesh,
        in_specs=(spec,) * 4,
        out_specs=(spec,) * 4,
        check_vma=False,
    )
```

```python
import functools
import math

import jax
import jax.numpy as jnp
from jax import lax
from jax.experimental import pallas as pl
from jax.experimental.pallas import tpu as pltpu
from jax.sharding import PartitionSpec as P

HEAD = 128
BLOCK = 128
PARENT = 256
LEVELS = 3
CHUNKS = 2
LATE_CHUNK = 1
INV_ROOT = HEAD**-0.5
TO_LOG2 = INV_ROOT * math.log2(math.e)
MASKED = -1e30
BF = jnp.bfloat16
F32 = jnp.float32


def dot_nt(a, b):
    return lax.dot_general(a, b, (((1,), (1,)), ((), ())), preferred_element_type=F32)


def dot_nn(a, b):
    return jnp.dot(a, b, preferred_element_type=F32)


def order_matrix(inverse):
    row = lax.broadcasted_iota(jnp.int32, (PARENT, PARENT), 0)
    col = lax.broadcasted_iota(jnp.int32, (PARENT, PARENT), 1)
    place, token = (col, row) if inverse else (row, col)
    slab = place // 64
    source = 4 * (place % 64) + 2 * (slab % 2) + slab // 2
    return jnp.where(source == token, 1.0, 0.0).astype(BF)


def pool1(x):
    return ((x[:BLOCK].astype(F32) + x[BLOCK:].astype(F32)) * 0.5).astype(BF)


def pool2(x):
    half = x[:BLOCK].astype(F32) + x[BLOCK:].astype(F32)
    return ((half[:64] + half[64:]) * 0.25).astype(BF)


def pool12(x):
    return ((x[:64].astype(F32) + x[64:].astype(F32)) * 0.5).astype(BF)


def twice(x, axis=0):
    return jnp.concatenate([x, x], axis=axis)


def pack_kernel(own, where, *refs):
    count = 4 if own else 2
    arrays, outs, (held, sems) = refs[:count], refs[count:-2], refs[-2:]
    rows, columns = arrays[0].shape
    half = columns // 2
    width = half // CHUNKS
    side = where[0] if own else 1 - where[0]
    at = pl.ds(pl.multiple_of(side * half, half), half)
    copies = [
        pltpu.make_async_copy(ref.at[:, at], held.at[m], sems.at[m]) for m, ref in enumerate(arrays)
    ]
    for copy in copies:
        copy.start()
    order = order_matrix(False)
    for m in range(count):
        copies[m].wait()
        first = m % 2 * width
        for i in range(rows // PARENT):
            at = slice(i * PARENT, (i + 1) * PARENT)
            x = dot_nn(order, held[m, at, :]).astype(BF)
            for c in range(CHUNKS):
                out = outs[m // 2 * CHUNKS + c]
                out[at, first : first + width] = x[:, c * width : (c + 1) * width]


def pack(own, where, *arrays):
    rows, columns = arrays[0].shape
    count = len(arrays)
    return pl.pallas_call(
        placed(functools.partial(pack_kernel, own), where),
        in_specs=[pl.BlockSpec(memory_space=pltpu.HBM)] * count,
        out_specs=[vmem()] * (count // 2 * CHUNKS),
        out_shape=[jax.ShapeDtypeStruct((rows, columns // CHUNKS), BF)] * (count // 2 * CHUNKS),
        scratch_shapes=[
            pltpu.VMEM((count, rows, columns // 2), BF),
            pltpu.SemaphoreType.DMA((count,)),
        ],
        compiler_params=small(),
        cost_estimate=light(),
    )(*arrays)


def pack_cut_kernel(a, b, out):
    order = order_matrix(False)
    width = a.shape[1]
    for m, ref in enumerate((a, b)):
        for i in range(a.shape[0] // PARENT):
            rows = slice(i * PARENT, (i + 1) * PARENT)
            out[rows, m * width : (m + 1) * width] = dot_nn(order, ref[rows, :]).astype(BF)


def pack_cut(side, chunk, a, b):
    rows, columns = a.shape
    width = columns // 2 // CHUNKS
    cut = [lax.dynamic_slice_in_dim(x, (side * CHUNKS + chunk) * width, width, 1) for x in (a, b)]
    return pl.pallas_call(
        pack_cut_kernel,
        in_specs=[vmem(), vmem()],
        out_specs=vmem(),
        out_shape=jax.ShapeDtypeStruct((rows, 2 * width), BF),
        compiler_params=small(),
        cost_estimate=light(),
    )(*cut)


def placed(kernel, grid):
    inner, count = grid

    def body(*refs):
        device = lax.axis_index("outer") * inner + lax.axis_index("inner")
        pair = device // 2
        left = jnp.where(pair > 0, 1, 0)
        right = jnp.where(pair < count // 2 - 1, 1, 0)
        kernel((device % 2, left, right, pair % 2), *refs)

    return body


def vmem():
    return pl.BlockSpec(memory_space=pltpu.VMEM)


def small():
    return pltpu.CompilerParams(vmem_limit_bytes=8 * 1024 * 1024)


def light():
    return pl.CostEstimate(flops=1000, bytes_accessed=1000, transcendentals=0)


def halo_kernel(where, own, got, near, wide):
    def fill(first, second, to_right, to_left):
        to_right[0:256, :] = second[256:512, :]
        to_right[256:384, :] = pool1(second[0:256, :])
        to_right[384:448, :] = pool2(first[0:256, :])
        to_right[448:512, :] = pool2(first[256:512, :])
        to_left[0:256, :] = first[0:256, :]
        to_left[256:384, :] = pool1(first[256:512, :])
        to_left[384:448, :] = pool2(second[0:256, :])
        to_left[448:512, :] = pool2(second[256:512, :])

    for side in range(2):
        for odd in range(2):

            @pl.when((where[0] == side) & (where[3] == odd))
            def _(side=side, odd=odd):
                halves = (own, got) if side == 0 else (got, own)
                fill(*halves, *((near, wide) if odd == 0 else (wide, near)))


def halo(where, own, got):
    shape = jax.ShapeDtypeStruct(own.shape, BF)
    return pl.pallas_call(
        placed(halo_kernel, where),
        in_specs=[vmem(), vmem()],
        out_specs=[vmem(), vmem()],
        out_shape=[shape, shape],
        compiler_params=small(),
        cost_estimate=light(),
    )(own, got)


def swap64(x):
    return pltpu.roll(x, 64, 1)


def low_lanes(shape):
    return lax.broadcasted_iota(jnp.int32, shape, 1) < 64


def spread64(x, half):
    other = swap64(x)
    low = low_lanes(x.shape)
    return jnp.where(low, x, other) if half == 0 else jnp.where(low, other, x)


def far_forward(k, v_t, q, bias, p_ref):
    k0, k1, k2, k3 = k
    v0, v1, v2, v3 = v_t
    left, right = bias
    outer = dot_nt(jnp.concatenate([k0, k3], axis=0), q)
    first, last = outer[:BLOCK], outer[BLOCK:]
    mid_low = dot_nt(k2, q[:BLOCK])
    mid_high = dot_nt(k1, q[BLOCK:])
    if left is not None:
        first = first + left
        mid_high = mid_high + left
    if right is not None:
        last = last + right
        mid_low = mid_low + right
    mid = jnp.concatenate([mid_low, mid_high], axis=1)
    peak = jnp.max(jnp.maximum(jnp.maximum(first, last), mid), axis=0, keepdims=True)
    parts = [jnp.exp2((x - peak) * TO_LOG2) for x in (first, last, mid)]
    for n, x in enumerate(parts):
        p_ref[n * BLOCK : (n + 1) * BLOCK, :] = x
    total = jnp.sum(parts[0] + parts[1] + parts[2], axis=0, keepdims=True)
    pb = [x.astype(BF) for x in parts]
    mixed = dot_nn(
        jnp.concatenate([v0, v3], axis=1), jnp.concatenate(pb[:2], axis=0)
    ) + jnp.concatenate([dot_nn(v2, pb[2][:, :BLOCK]), dot_nn(v1, pb[2][:, BLOCK:])], axis=1)
    return peak, total, mixed


def far_backward(k_t, v, q, p_ref, factor, g, ec):
    k0, k1, k2, k3 = k_t
    v0, v1, v2, v3 = v
    e_out = p_ref[: 2 * BLOCK, :] * factor
    e_mid = p_ref[2 * BLOCK :, :] * factor
    eb_out, eb_mid = e_out.astype(BF), e_mid.astype(BF)
    p_out = dot_nt(jnp.concatenate([v0, v3], axis=0), g)
    p_mid = jnp.concatenate([dot_nt(v2, g[:BLOCK]), dot_nt(v1, g[BLOCK:])], axis=1)
    r_out = (e_out * (p_out - ec)).astype(BF)
    r_mid = (e_mid * (p_mid - ec)).astype(BF)
    dv03 = dot_nn(eb_out, g)
    dv2 = dot_nn(eb_mid[:, :BLOCK], g[:BLOCK])
    dv1 = dot_nn(eb_mid[:, BLOCK:], g[BLOCK:])
    dk03 = dot_nn(r_out, q)
    dk2 = dot_nn(r_mid[:, :BLOCK], q[:BLOCK])
    dk1 = dot_nn(r_mid[:, BLOCK:], q[BLOCK:])
    dq_t = dot_nn(jnp.concatenate([k0, k3], axis=1), r_out) + jnp.concatenate(
        [dot_nn(k2, r_mid[:, :BLOCK]), dot_nn(k1, r_mid[:, BLOCK:])], axis=1
    )
    return (dk03[:BLOCK], dk1, dk2, dk03[BLOCK:]), (dv03[:BLOCK], dv1, dv2, dv03[BLOCK:]), dq_t


def main_kernel(qg_first, where, kv_own, kv_got, *refs):
    if qg_first:
        refs = (*refs[2:4], *refs[:2], *refs[4:])
    one_chunk(where, kv_own, kv_got, *refs)


def one_chunk(
    where, kv_own, kv_got, near_got, wide_got, qg_own, qg_got,
    oq_own, oq_far, grad, near_out, wide_out,
    raw, raw_t, one, one_t, two, two_t, qs, gs, p0, p1, p2, acc0, acc1, acc2, oq, halos,
):
    side = where[0]
    odd = where[3]
    halos[1 - odd] = near_got[...]
    halos[odd] = wide_got[...]
    from_left, from_right = halos.at[0], halos.at[1]
    to_left, to_right = halos.at[0], halos.at[1]
    width = kv_own.shape[1] // 2
    left_bias = (1 - where[1]).astype(F32) * MASKED
    right_bias = (1 - where[2]).astype(F32) * MASKED
    own_at = pl.multiple_of(side * 512, 512)
    got_at = pl.multiple_of((1 - side) * 512, 512)
    for h in range(width // HEAD):
        kc = slice(h * HEAD, (h + 1) * HEAD)
        vc = slice(width + h * HEAD, width + (h + 1) * HEAD)
        for n, cols in ((0, kc), (1, vc)):
            raw[n, 0:256, :] = from_left[0:256, cols]
            raw[n, pl.ds(256 + own_at, 512), :] = kv_own[:, cols]
            raw[n, pl.ds(256 + got_at, 512), :] = kv_got[:, cols]
            raw[n, 1280:1536, :] = from_right[0:256, cols]
            one[n, 0:128, :] = from_left[256:384, cols]
            for i in range(6):
                block = pool1(raw[n, i * PARENT : (i + 1) * PARENT, :])
                at = (i + 1) * BLOCK
                one[n, at : at + BLOCK, :] = block
            one[n, 896:1024, :] = from_right[256:384, cols]
            two[n, 0:128, :] = from_left[384:512, cols]
            two[n, 128:192, :] = pool12(one[n, 0:128, :])
            two[n, 192:256, :] = pool2(raw[n, 0:256, :])
            two[n, 256:320, :] = pool2(raw[n, 1280:1536, :])
            two[n, 320:384, :] = pool12(one[n, 896:1024, :])
            two[n, 384:512, :] = from_right[384:512, cols]
            for i in range(6):
                rows = slice(i * PARENT, (i + 1) * PARENT)
                raw_t[n, :, rows] = raw[n, rows, :].T
            for i in range(8):
                rows = slice(i * BLOCK, (i + 1) * BLOCK)
                one_t[n, :, rows] = one[n, rows, :].T
            for i in range(4):
                rows = slice(i * BLOCK, (i + 1) * BLOCK)
                two_t[n, :, rows] = two[n, rows, :].T
        qs[pl.ds(own_at, 512), :] = qg_own[:, kc]
        qs[pl.ds(got_at, 512), :] = qg_got[:, kc]
        gs[pl.ds(own_at, 512), :] = qg_own[:, vc]
        gs[pl.ds(got_at, 512), :] = qg_got[:, vc]

        def blocks(ref, n, which):
            return [ref[n, b * BLOCK : (b + 1) * BLOCK, :] for b in which]

        def blocks_t(ref, n, which):
            return [ref[n, :, b * BLOCK : (b + 1) * BLOCK] for b in which]

        q_parents = [qs[i * PARENT : (i + 1) * PARENT, :] for i in range(4)]
        q1 = [
            jnp.concatenate([pool1(q_parents[2 * j]), pool1(q_parents[2 * j + 1])], axis=0)
            for j in range(2)
        ]
        q2 = jnp.concatenate([pool2(x) for x in q_parents], axis=0)
        which1 = [(0, 1, 4, 5), (2, 3, 6, 7)]
        bias1 = [(left_bias, None), (None, right_bias)]
        which2 = (0, 1, 2, 3)
        far1 = [
            far_forward(
                blocks(one, 0, which1[j]), blocks_t(one_t, 1, which1[j]), q1[j], bias1[j], p1.at[j]
            )
            for j in range(2)
        ]
        far2 = far_forward(
            blocks(two, 0, which2), blocks_t(two_t, 1, which2), q2, (left_bias, right_bias), p2
        )
        g1_t, ec1, f1 = [], [], []
        g2_t, ec2, low2 = [], [], []
        dq0 = []
        for i in range(4):
            rows = slice(i * PARENT, i * PARENT + 3 * PARENT)
            q = q_parents[i]
            g = gs[i * PARENT : (i + 1) * PARENT, :]
            s = dot_nt(raw[0, rows, :], q)
            pieces = [s[:PARENT], s[PARENT : 2 * PARENT], s[2 * PARENT :]]
            if i == 0:
                pieces[0] = pieces[0] + left_bias
            if i == 3:
                pieces[2] = pieces[2] + right_bias
            m0 = jnp.max(
                jnp.maximum(jnp.maximum(pieces[0], pieces[1]), pieces[2]), axis=0, keepdims=True
            )
            e = [jnp.exp2((x - m0) * TO_LOG2) for x in pieces]
            for n in range(3):
                p0[i % 2, n * PARENT : (n + 1) * PARENT, :] = e[n]
            z0 = jnp.sum(e[0] + e[1] + e[2], axis=0, keepdims=True)
            u0 = dot_nn(raw_t[1, :, rows], jnp.concatenate([x.astype(BF) for x in e], axis=0))
            j, half = i // 2, i % 2
            lanes = slice(half * BLOCK, (half + 1) * BLOCK)
            m1, z1, u1 = (x[:, lanes] for x in far1[j])
            lanes2 = slice(j * BLOCK, (j + 1) * BLOCK)
            m2, z2, u2 = (spread64(x[:, lanes2], half) for x in far2)
            m1w, m2w = twice(m1, 1), twice(m2, 1)
            m = jnp.maximum(jnp.maximum(m0, m1w), m2w)
            a0 = jnp.exp2((m0 - m) * TO_LOG2)
            a1 = 2.0 * jnp.exp2((m1w - m) * TO_LOG2)
            a2 = 4.0 * jnp.exp2((m2w - m) * TO_LOG2)
            z = a0 * z0 + a1 * twice(z1, 1) + a2 * twice(z2, 1)
            inv = 1.0 / z
            o = ((a0 * inv) * u0 + (a1 * inv) * twice(u1, 1) + (a2 * inv) * twice(u2, 1)).astype(BF)
            oq[i, 0, h * HEAD : (h + 1) * HEAD, :] = o
            lg = m * TO_LOG2 + jnp.log2(z)
            g_t = g.astype(F32).T
            dr = jnp.sum(o.astype(F32) * g_t, axis=0, keepdims=True)
            lg_a, lg_b = lg[:, :BLOCK], lg[:, BLOCK:]
            g_a, g_b = g_t[:, :BLOCK], g_t[:, BLOCK:]
            dr_a, dr_b = dr[:, :BLOCK], dr[:, BLOCK:]
            low = jnp.minimum(lg_a, lg_b)
            w_a, w_b = jnp.exp2(low - lg_a), jnp.exp2(low - lg_b)
            g1_t.append((w_a * g_a + w_b * g_b).astype(BF))
            ec1.append(w_a * dr_a + w_b * dr_b)
            f1.append(2.0 * jnp.exp2(m1 * TO_LOG2 - low))
            lower = jnp.minimum(low, swap64(low))
            w_a, w_b = jnp.exp2(lower - lg_a), jnp.exp2(lower - lg_b)
            part = w_a * g_a + w_b * g_b
            g2_t.append(part + swap64(part))
            part = w_a * dr_a + w_b * dr_b
            ec2.append(part + swap64(part))
            low2.append(lower)
            f0 = jnp.exp2(m0 * TO_LOG2 - lg)
            products = dot_nt(raw[1, rows, :], g)
            weights = p0[i % 2] * f0
            eb = weights.astype(BF)
            r = (weights * (products - dr)).astype(BF)
            for n, x in ((1, dot_nn(eb, g)), (0, dot_nn(r, q))):
                if i == 0:
                    acc0[n, rows, :] = x
                else:
                    old = slice(i * PARENT, (i + 2) * PARENT)
                    acc0[n, old, :] += x[: 2 * PARENT]
                    acc0[n, (i + 2) * PARENT : (i + 3) * PARENT, :] = x[2 * PARENT :]
            dq0.append(dot_nn(raw_t[0, :, rows], r))
        dq1 = []
        for j in range(2):
            pair = slice(2 * j, 2 * j + 2)
            g1 = jnp.concatenate([x.astype(F32).T.astype(BF) for x in g1_t[pair]], axis=0)
            dk, dv, dq = far_backward(
                blocks_t(one_t, 0, which1[j]), blocks(one, 1, which1[j]), q1[j], p1.at[j],
                jnp.concatenate(f1[pair], axis=1), g1, jnp.concatenate(ec1[pair], axis=1),
            )
            for n, b in enumerate(which1[j]):
                acc1[0, b * BLOCK : (b + 1) * BLOCK, :] = dk[n]
                acc1[1, b * BLOCK : (b + 1) * BLOCK, :] = dv[n]
            dq1.append(dq)

        def joined(parts):
            return jnp.concatenate(
                [
                    jnp.where(low_lanes(parts[0].shape), parts[2 * j], parts[2 * j + 1])
                    for j in range(2)
                ],
                axis=1,
            )

        g2 = joined(g2_t).T.astype(BF)
        f2 = 4.0 * jnp.exp2(far2[0] * TO_LOG2 - joined(low2))
        dk, dv, dq2 = far_backward(
            blocks_t(two_t, 0, which2), blocks(two, 1, which2), q2, p2, f2, g2, joined(ec2)
        )
        for n in range(4):
            acc2[0, n * BLOCK : (n + 1) * BLOCK, :] = dk[n]
            acc2[1, n * BLOCK : (n + 1) * BLOCK, :] = dv[n]
        for i in range(4):
            j, half = i // 2, i % 2
            d1 = dq1[j][:, half * BLOCK : (half + 1) * BLOCK]
            d2 = spread64(dq2[:, j * BLOCK : (j + 1) * BLOCK], half)
            coarse = 0.5 * d1 + 0.25 * d2
            oq[i, 1, h * HEAD : (h + 1) * HEAD, :] = ((dq0[i] + twice(coarse, 1)) * INV_ROOT).astype(BF)
        for n, cols, scale in ((0, kc, INV_ROOT), (1, vc, 1.0)):
            for i in range(4):
                rows = slice((i + 1) * PARENT, (i + 2) * PARENT)
                coarse = acc1[n, (i + 2) * BLOCK : (i + 3) * BLOCK, :] * (0.5 * scale)
                grad[i * PARENT : (i + 1) * PARENT, cols] = acc0[n, rows, :] * scale + twice(coarse)
            far = acc2[n, 128:256, :] * (0.25 * scale)
            mid = acc1[n, 0:256, :] * (0.5 * scale)
            near = acc0[n, 0:256, :] * scale
            to_left[0:256, cols] = (near + twice(mid[128:] + twice(far[64:]))).astype(BF)
            to_left[256:384, cols] = (mid[:128] + twice(far[:64])).astype(BF)
            to_left[384:512, cols] = (acc2[n, 0:128, :] * (0.25 * scale)).astype(BF)
            far = acc2[n, 256:384, :] * (0.25 * scale)
            mid = acc1[n, 768:1024, :] * (0.5 * scale)
            near = acc0[n, 1280:1536, :] * scale
            to_right[0:256, cols] = (near + twice(mid[:128] + twice(far[:64]))).astype(BF)
            to_right[256:384, cols] = (mid[128:] + twice(far[64:])).astype(BF)
            to_right[384:512, cols] = (acc2[n, 384:512, :] * (0.25 * scale)).astype(BF)
    oq_own[...] = oq[pl.ds(side * 2, 2)]
    oq_far[...] = oq[pl.ds((1 - side) * 2, 2)]
    near_out[...] = halos[1 - odd]
    wide_out[...] = halos[odd]


def main(where, kv_own, kv_got, near_got, wide_got, qg_own, qg_got, qg_first):
    rows, both = kv_own.shape
    width = both // 2
    oq_shape = jax.ShapeDtypeStruct((2, 2, width, PARENT), BF)
    halo_shape = jax.ShapeDtypeStruct((512, both), BF)
    operands = [kv_own, kv_got, near_got, wide_got, qg_own, qg_got]
    if qg_first:
        operands = operands[:2] + operands[4:] + operands[2:4]
    return pl.pallas_call(
        placed(functools.partial(main_kernel, qg_first), where),
        in_specs=[vmem()] * 6,
        out_specs=[vmem()] * 5,
        out_shape=[
            oq_shape,
            oq_shape,
            jax.ShapeDtypeStruct((2 * rows, both), F32),
            halo_shape,
            halo_shape,
        ],
        scratch_shapes=[
            pltpu.VMEM((2, 1536, HEAD), BF),
            pltpu.VMEM((2, HEAD, 1536), BF),
            pltpu.VMEM((2, 1024, HEAD), BF),
            pltpu.VMEM((2, HEAD, 1024), BF),
            pltpu.VMEM((2, 512, HEAD), BF),
            pltpu.VMEM((2, HEAD, 512), BF),
            pltpu.VMEM((1024, HEAD), BF),
            pltpu.VMEM((1024, HEAD), BF),
            pltpu.VMEM((2, 768, PARENT), F32),
            pltpu.VMEM((2, 384, PARENT), F32),
            pltpu.VMEM((384, PARENT), F32),
            pltpu.VMEM((2, 1536, HEAD), F32),
            pltpu.VMEM((2, 1024, HEAD), F32),
            pltpu.VMEM((2, 512, HEAD), F32),
            pltpu.VMEM((4, 2, width, PARENT), BF),
            pltpu.VMEM((2, 512, both), BF),
        ],
        compiler_params=pltpu.CompilerParams(vmem_limit_bytes=24 * 1024 * 1024),
        cost_estimate=light(),
    )(*operands)


def join_kernel(where, grad, near_got, wide_got, own, far):
    def fill(first, second, from_left, from_right):
        def parent(i):
            return grad[i * PARENT : (i + 1) * PARENT, :]

        def part(ref, start, stop):
            return ref[start:stop, :].astype(F32)

        first[0:256, :] = (
            parent(0) + part(from_left, 0, 256) + twice(twice(part(from_right, 384, 448)))
        ).astype(BF)
        first[256:512, :] = (
            parent(1) + twice(part(from_left, 256, 384) + twice(part(from_right, 448, 512)))
        ).astype(BF)
        second[0:256, :] = (
            parent(2) + twice(part(from_right, 256, 384) + twice(part(from_left, 384, 448)))
        ).astype(BF)
        second[256:512, :] = (
            parent(3) + part(from_right, 0, 256) + twice(twice(part(from_left, 448, 512)))
        ).astype(BF)

    for side in range(2):
        for odd in range(2):

            @pl.when((where[0] == side) & (where[3] == odd))
            def _(side=side, odd=odd):
                halves = (own, far) if side == 0 else (far, own)
                fill(*halves, *((wide_got, near_got) if odd == 0 else (near_got, wide_got)))


def join(where, grad, near_got, wide_got):
    shape = jax.ShapeDtypeStruct(near_got.shape, BF)
    return pl.pallas_call(
        placed(join_kernel, where),
        in_specs=[vmem(), vmem(), vmem()],
        out_specs=[vmem(), vmem()],
        out_shape=[shape, shape],
        compiler_params=small(),
        cost_estimate=light(),
    )(grad, near_got, wide_got)


def unpack_rows_kernel(where, *refs):
    ins, (first, second) = refs[:-2], refs[-2:]
    order = order_matrix(True)
    width = ins[0].shape[1] // 2
    side = where[0]
    blocks = [(side * CHUNKS + c, ins[c]) for c in range(CHUNKS)]
    blocks += [((1 - side) * CHUNKS + 1 - LATE_CHUNK, ins[CHUNKS])]
    for block, ref in blocks:
        at = pl.ds(pl.multiple_of(block * width, width), width)
        for i in range(2):
            rows = slice(i * PARENT, (i + 1) * PARENT)
            first[rows, at] = dot_nn(order, ref[rows, :width]).astype(BF)
            second[rows, at] = dot_nn(order, ref[rows, width:]).astype(BF)


def unpack_rows(where, own, got, shape):
    out = jax.ShapeDtypeStruct(shape, BF)
    return pl.pallas_call(
        placed(unpack_rows_kernel, where),
        in_specs=[vmem()] * (CHUNKS + 1),
        out_specs=[vmem(), vmem()],
        out_shape=[out, out],
        compiler_params=small(),
        cost_estimate=light(),
    )(*own, got)


def unpack_last_kernel(where, got, first_in, second_in, first, second, held, sems):
    del first_in, second_in
    order = order_matrix(True)
    width = got.shape[1] // 2
    block = (1 - where[0]) * CHUNKS + LATE_CHUNK
    at = pl.ds(pl.multiple_of(block * width, width), width)
    copies = []
    for i in range(2):
        rows = slice(i * PARENT, (i + 1) * PARENT)
        x = dot_nn(order, got[rows, :]).astype(BF)
        for m, ref in enumerate((first, second)):
            held[m, rows, :] = x[:, m * width : (m + 1) * width]
            copies.append(
                pltpu.make_async_copy(held.at[m, rows, :], ref.at[rows, at], sems.at[2 * i + m])
            )
            copies[-1].start()
    for copy in copies:
        copy.wait()


def unpack_last(where, got, first, second):
    out = jax.ShapeDtypeStruct(first.shape, BF)
    hbm = pl.BlockSpec(memory_space=pltpu.HBM)
    return pl.pallas_call(
        placed(unpack_last_kernel, where),
        in_specs=[vmem(), hbm, hbm],
        out_specs=[hbm, hbm],
        out_shape=[out, out],
        input_output_aliases={1: 0, 2: 1},
        scratch_shapes=[
            pltpu.VMEM((2, got.shape[0], got.shape[1] // 2), BF),
            pltpu.SemaphoreType.DMA((4,)),
        ],
        compiler_params=small(),
        cost_estimate=light(),
    )(got, first, second)


def unpack_columns_kernel(where, *refs):
    ins, (first, second) = refs[:-2], refs[-2:]
    order = order_matrix(True)
    width = ins[0].shape[2]
    for c in range(CHUNKS):
        for ref, side in ((ins[c], where[0]), (ins[CHUNKS + c], 1 - where[0])):
            at = pl.ds(pl.multiple_of((side * CHUNKS + c) * width, width), width)
            for i in range(2):
                rows = slice(i * PARENT, (i + 1) * PARENT)
                first[rows, at] = dot_nt(order, ref[i, 0]).astype(BF)
                second[rows, at] = dot_nt(order, ref[i, 1]).astype(BF)


def unpack_columns(where, own, got, shape):
    out = jax.ShapeDtypeStruct(shape, BF)
    return pl.pallas_call(
        placed(unpack_columns_kernel, where),
        in_specs=[vmem()] * (2 * CHUNKS),
        out_specs=[vmem(), vmem()],
        out_shape=[out, out],
        compiler_params=small(),
        cost_estimate=light(),
    )(*own, *got)


def on_device(queries, key_matrix, value_matrix, cotangent):
    axes = ("outer", "inner")
    count = lax.axis_size("outer") * lax.axis_size("inner")
    device = lax.axis_index("outer") * lax.axis_size("inner") + lax.axis_index("inner")
    where = (lax.axis_size("inner"), count)
    across = [(i, i ^ 1) for i in range(count)]
    near_edges = [(i, i ^ 2) for i in range(count) if i ^ 2 < count]
    wide_edges = [(i, i + 2 if i // 2 % 2 else i - 2) for i in range(count)]
    wide_edges = [(i, j) for i, j in wide_edges if 0 <= j < count]

    def swap(x):
        return lax.ppermute(x, axes, across)

    def beside(near, wide):
        near = lax.ppermute(near, axes, near_edges)
        return near, lax.ppermute(wide, axes, wide_edges)

    kv_far = [pack_cut(1 - device % 2, 0, key_matrix, value_matrix)]
    for c in range(1, CHUNKS):
        later, kv_far[0] = lax.optimization_barrier(((key_matrix, value_matrix), kv_far[0]))
        kv_far.append(pack_cut(1 - device % 2, c, *later))
    qg_far = pack(False, where, queries, cotangent)
    packed = pack(True, where, key_matrix, value_matrix, queries, cotangent)
    kv, qg = packed[:CHUNKS], packed[CHUNKS:]
    oq_own, oq_got, back = [], [], []
    for c in range(CHUNKS):
        got_kv = swap(kv_far[c])
        near, wide = halo(where, kv[c], got_kv)
        far = qg_far[c]
        if c > 0:
            near, wide, far = lax.optimization_barrier((near, wide, far))
        near, wide = beside(near, wide)
        own, far, grad, near, wide = main(where, kv[c], got_kv, near, wide, qg[c], swap(far), c == 0)
        oq_own.append(own)
        oq_got.append(swap(far))
        if c > 0:
            back[c - 1], near, wide = lax.optimization_barrier((back[c - 1], near, wide))
        back.append([grad, *beside(near, wide)])
    for c in range(CHUNKS):
        oq_got[c], back[c] = lax.optimization_barrier((oq_got[c], back[c]))
    kv_own, kv_got = [], []
    for c in range(CHUNKS):
        own, far = join(where, *back[c])
        kv_own.append(own)
        kv_got.append(swap(far))
    attended, query_grad = unpack_columns(where, oq_own, oq_got, queries.shape)
    key_grad, value_grad = unpack_rows(where, kv_own, kv_got[1 - LATE_CHUNK], queries.shape)
    key_grad, value_grad = unpack_last(where, kv_got[LATE_CHUNK], key_grad, value_grad)
    return attended, query_grad, key_grad, value_grad


def solution(mesh):
    spec = P(("outer", "inner"), None)
    return jax.shard_map(
        on_device,
        mesh=mesh,
        in_specs=(spec,) * 4,
        out_specs=(spec,) * 4,
        check_vma=False,
    )
```

```python
import functools
import math

import jax
import jax.numpy as jnp
from jax import lax
from jax.experimental import pallas as pl
from jax.experimental.pallas import tpu as pltpu
from jax.sharding import PartitionSpec as P

HEAD = 128
BLOCK = 128
PARENT = 256
LEVELS = 3
CHUNKS = 2
LATE_CHUNK = 1
INV_ROOT = HEAD**-0.5
TO_LOG2 = INV_ROOT * math.log2(math.e)
MASKED = -1e30
BF = jnp.bfloat16
F32 = jnp.float32


def dot_nt(a, b):
    return lax.dot_general(a, b, (((1,), (1,)), ((), ())), preferred_element_type=F32)


def dot_nn(a, b):
    return jnp.dot(a, b, preferred_element_type=F32)


def order_matrix(inverse):
    row = lax.broadcasted_iota(jnp.int32, (PARENT, PARENT), 0)
    col = lax.broadcasted_iota(jnp.int32, (PARENT, PARENT), 1)
    place, token = (col, row) if inverse else (row, col)
    slab = place // 64
    source = 4 * (place % 64) + 2 * (slab % 2) + slab // 2
    return jnp.where(source == token, 1.0, 0.0).astype(BF)


def pool1(x):
    return ((x[:BLOCK].astype(F32) + x[BLOCK:].astype(F32)) * 0.5).astype(BF)


def pool2(x):
    half = x[:BLOCK].astype(F32) + x[BLOCK:].astype(F32)
    return ((half[:64] + half[64:]) * 0.25).astype(BF)


def pool12(x):
    return ((x[:64].astype(F32) + x[64:].astype(F32)) * 0.5).astype(BF)


def twice(x, axis=0):
    return jnp.concatenate([x, x], axis=axis)


def pack_kernel(own, where, *refs):
    count = 4 if own else 2
    arrays, outs, (held, sems) = refs[:count], refs[count:-2], refs[-2:]
    rows, columns = arrays[0].shape
    half = columns // 2
    width = half // CHUNKS
    side = where[0] if own else 1 - where[0]
    at = pl.ds(pl.multiple_of(side * half, half), half)
    copies = [
        pltpu.make_async_copy(ref.at[:, at], held.at[m], sems.at[m]) for m, ref in enumerate(arrays)
    ]
    for copy in copies:
        copy.start()
    order = order_matrix(False)
    for m in range(count):
        copies[m].wait()
        first = m % 2 * width
        for i in range(rows // PARENT):
            at = slice(i * PARENT, (i + 1) * PARENT)
            x = dot_nn(order, held[m, at, :]).astype(BF)
            for c in range(CHUNKS):
                out = outs[m // 2 * CHUNKS + c]
                out[at, first : first + width] = x[:, c * width : (c + 1) * width]


def pack(own, where, *arrays):
    rows, columns = arrays[0].shape
    count = len(arrays)
    return pl.pallas_call(
        placed(functools.partial(pack_kernel, own), where),
        in_specs=[pl.BlockSpec(memory_space=pltpu.HBM)] * count,
        out_specs=[vmem()] * (count // 2 * CHUNKS),
        out_shape=[jax.ShapeDtypeStruct((rows, columns // CHUNKS), BF)] * (count // 2 * CHUNKS),
        scratch_shapes=[
            pltpu.VMEM((count, rows, columns // 2), BF),
            pltpu.SemaphoreType.DMA((count,)),
        ],
        compiler_params=small(),
        cost_estimate=light(),
    )(*arrays)


def pack_cut_kernel(a, b, out):
    order = order_matrix(False)
    width = a.shape[1]
    for m, ref in enumerate((a, b)):
        for i in range(a.shape[0] // PARENT):
            rows = slice(i * PARENT, (i + 1) * PARENT)
            out[rows, m * width : (m + 1) * width] = dot_nn(order, ref[rows, :]).astype(BF)


def pack_cut(side, chunk, a, b):
    rows, columns = a.shape
    width = columns // 2 // CHUNKS
    cut = [lax.dynamic_slice_in_dim(x, (side * CHUNKS + chunk) * width, width, 1) for x in (a, b)]
    return pl.pallas_call(
        pack_cut_kernel,
        in_specs=[vmem(), vmem()],
        out_specs=vmem(),
        out_shape=jax.ShapeDtypeStruct((rows, 2 * width), BF),
        compiler_params=small(),
        cost_estimate=light(),
    )(*cut)


def placed(kernel, grid):
    inner, count = grid

    def body(*refs):
        device = lax.axis_index("outer") * inner + lax.axis_index("inner")
        pair = device // 2
        left = jnp.where(pair > 0, 1, 0)
        right = jnp.where(pair < count // 2 - 1, 1, 0)
        kernel((device % 2, left, right, pair % 2), *refs)

    return body


def vmem():
    return pl.BlockSpec(memory_space=pltpu.VMEM)


def small():
    return pltpu.CompilerParams(vmem_limit_bytes=8 * 1024 * 1024)


def light():
    return pl.CostEstimate(flops=1000, bytes_accessed=1000, transcendentals=0)


def halo_kernel(where, own, got, near, wide):
    def fill(first, second, to_right, to_left):
        to_right[0:256, :] = second[256:512, :]
        to_right[256:384, :] = pool1(second[0:256, :])
        to_right[384:448, :] = pool2(first[0:256, :])
        to_right[448:512, :] = pool2(first[256:512, :])
        to_left[0:256, :] = first[0:256, :]
        to_left[256:384, :] = pool1(first[256:512, :])
        to_left[384:448, :] = pool2(second[0:256, :])
        to_left[448:512, :] = pool2(second[256:512, :])

    for side in range(2):
        for odd in range(2):

            @pl.when((where[0] == side) & (where[3] == odd))
            def _(side=side, odd=odd):
                halves = (own, got) if side == 0 else (got, own)
                fill(*halves, *((near, wide) if odd == 0 else (wide, near)))


def halo(where, own, got):
    shape = jax.ShapeDtypeStruct(own.shape, BF)
    return pl.pallas_call(
        placed(halo_kernel, where),
        in_specs=[vmem(), vmem()],
        out_specs=[vmem(), vmem()],
        out_shape=[shape, shape],
        compiler_params=small(),
        cost_estimate=light(),
    )(own, got)


def swap64(x):
    return pltpu.roll(x, 64, 1)


def low_lanes(shape):
    return lax.broadcasted_iota(jnp.int32, shape, 1) < 64


def spread64(x, half):
    other = swap64(x)
    low = low_lanes(x.shape)
    return jnp.where(low, x, other) if half == 0 else jnp.where(low, other, x)


def far_forward(k, v_t, q, bias, p_ref):
    k0, k1, k2, k3 = k
    v0, v1, v2, v3 = v_t
    left, right = bias
    outer = dot_nt(jnp.concatenate([k0, k3], axis=0), q)
    first, last = outer[:BLOCK], outer[BLOCK:]
    mid_low = dot_nt(k2, q[:BLOCK])
    mid_high = dot_nt(k1, q[BLOCK:])
    if left is not None:
        first = first + left
        mid_high = mid_high + left
    if right is not None:
        last = last + right
        mid_low = mid_low + right
    mid = jnp.concatenate([mid_low, mid_high], axis=1)
    peak = jnp.max(jnp.maximum(jnp.maximum(first, last), mid), axis=0, keepdims=True)
    parts = [jnp.exp2((x - peak) * TO_LOG2) for x in (first, last, mid)]
    for n, x in enumerate(parts):
        p_ref[n * BLOCK : (n + 1) * BLOCK, :] = x
    total = jnp.sum(parts[0] + parts[1] + parts[2], axis=0, keepdims=True)
    pb = [x.astype(BF) for x in parts]
    mixed = dot_nn(
        jnp.concatenate([v0, v3], axis=1), jnp.concatenate(pb[:2], axis=0)
    ) + jnp.concatenate([dot_nn(v2, pb[2][:, :BLOCK]), dot_nn(v1, pb[2][:, BLOCK:])], axis=1)
    return peak, total, mixed


def far_backward(k_t, v, q, p_ref, factor, g, ec):
    k0, k1, k2, k3 = k_t
    v0, v1, v2, v3 = v
    e_out = p_ref[: 2 * BLOCK, :] * factor
    e_mid = p_ref[2 * BLOCK :, :] * factor
    eb_out, eb_mid = e_out.astype(BF), e_mid.astype(BF)
    p_out = dot_nt(jnp.concatenate([v0, v3], axis=0), g)
    p_mid = jnp.concatenate([dot_nt(v2, g[:BLOCK]), dot_nt(v1, g[BLOCK:])], axis=1)
    r_out = (e_out * (p_out - ec)).astype(BF)
    r_mid = (e_mid * (p_mid - ec)).astype(BF)
    dv03 = dot_nn(eb_out, g)
    dv2 = dot_nn(eb_mid[:, :BLOCK], g[:BLOCK])
    dv1 = dot_nn(eb_mid[:, BLOCK:], g[BLOCK:])
    dk03 = dot_nn(r_out, q)
    dk2 = dot_nn(r_mid[:, :BLOCK], q[:BLOCK])
    dk1 = dot_nn(r_mid[:, BLOCK:], q[BLOCK:])
    dq_t = dot_nn(jnp.concatenate([k0, k3], axis=1), r_out) + jnp.concatenate(
        [dot_nn(k2, r_mid[:, :BLOCK]), dot_nn(k1, r_mid[:, BLOCK:])], axis=1
    )
    return (dk03[:BLOCK], dk1, dk2, dk03[BLOCK:]), (dv03[:BLOCK], dv1, dv2, dv03[BLOCK:]), dq_t


def main_kernel(qg_first, where, kv_own, kv_got, *refs):
    if qg_first:
        refs = (*refs[2:4], *refs[:2], *refs[4:])
    one_chunk(where, kv_own, kv_got, *refs)


def one_chunk(
    where, kv_own, kv_got, near_got, wide_got, qg_own, qg_got,
    oq_own, oq_far, grad, near_out, wide_out,
    raw, raw_t, one, one_t, two, two_t, qs, gs, p0, p1, p2, acc0, acc1, acc2, oq, halos,
):
    side = where[0]
    odd = where[3]
    halos[1 - odd] = near_got[...]
    halos[odd] = wide_got[...]
    from_left, from_right = halos.at[0], halos.at[1]
    to_left, to_right = halos.at[0], halos.at[1]
    width = kv_own.shape[1] // 2
    left_bias = (1 - where[1]).astype(F32) * MASKED
    right_bias = (1 - where[2]).astype(F32) * MASKED
    own_at = pl.multiple_of(side * 512, 512)
    got_at = pl.multiple_of((1 - side) * 512, 512)
    for h in range(width // HEAD):
        kc = slice(h * HEAD, (h + 1) * HEAD)
        vc = slice(width + h * HEAD, width + (h + 1) * HEAD)
        for n, cols in ((0, kc), (1, vc)):
            raw[n, 0:256, :] = from_left[0:256, cols]
            raw[n, pl.ds(256 + own_at, 512), :] = kv_own[:, cols]
            raw[n, pl.ds(256 + got_at, 512), :] = kv_got[:, cols]
            raw[n, 1280:1536, :] = from_right[0:256, cols]
            one[n, 0:128, :] = from_left[256:384, cols]
            for i in range(6):
                block = pool1(raw[n, i * PARENT : (i + 1) * PARENT, :])
                at = (i + 1) * BLOCK
                one[n, at : at + BLOCK, :] = block
            one[n, 896:1024, :] = from_right[256:384, cols]
            two[n, 0:128, :] = from_left[384:512, cols]
            two[n, 128:192, :] = pool12(one[n, 0:128, :])
            two[n, 192:256, :] = pool2(raw[n, 0:256, :])
            two[n, 256:320, :] = pool2(raw[n, 1280:1536, :])
            two[n, 320:384, :] = pool12(one[n, 896:1024, :])
            two[n, 384:512, :] = from_right[384:512, cols]
            for i in range(6):
                rows = slice(i * PARENT, (i + 1) * PARENT)
                raw_t[n, :, rows] = raw[n, rows, :].T
            for i in range(8):
                rows = slice(i * BLOCK, (i + 1) * BLOCK)
                one_t[n, :, rows] = one[n, rows, :].T
            for i in range(4):
                rows = slice(i * BLOCK, (i + 1) * BLOCK)
                two_t[n, :, rows] = two[n, rows, :].T
        qs[pl.ds(own_at, 512), :] = qg_own[:, kc]
        qs[pl.ds(got_at, 512), :] = qg_got[:, kc]
        gs[pl.ds(own_at, 512), :] = qg_own[:, vc]
        gs[pl.ds(got_at, 512), :] = qg_got[:, vc]

        def blocks(ref, n, which):
            return [ref[n, b * BLOCK : (b + 1) * BLOCK, :] for b in which]

        def blocks_t(ref, n, which):
            return [ref[n, :, b * BLOCK : (b + 1) * BLOCK] for b in which]

        q_parents = [qs[i * PARENT : (i + 1) * PARENT, :] for i in range(4)]
        q1 = [
            jnp.concatenate([pool1(q_parents[2 * j]), pool1(q_parents[2 * j + 1])], axis=0)
            for j in range(2)
        ]
        q2 = jnp.concatenate([pool2(x) for x in q_parents], axis=0)
        which1 = [(0, 1, 4, 5), (2, 3, 6, 7)]
        bias1 = [(left_bias, None), (None, right_bias)]
        which2 = (0, 1, 2, 3)
        far1 = [
            far_forward(
                blocks(one, 0, which1[j]), blocks_t(one_t, 1, which1[j]), q1[j], bias1[j], p1.at[j]
            )
            for j in range(2)
        ]
        far2 = far_forward(
            blocks(two, 0, which2), blocks_t(two_t, 1, which2), q2, (left_bias, right_bias), p2
        )
        g1_t, ec1, f1 = [], [], []
        g2_t, ec2, low2 = [], [], []
        dq0 = []
        for i in range(4):
            rows = slice(i * PARENT, i * PARENT + 3 * PARENT)
            q = q_parents[i]
            g = gs[i * PARENT : (i + 1) * PARENT, :]
            s = dot_nt(raw[0, rows, :], q)
            pieces = [s[:PARENT], s[PARENT : 2 * PARENT], s[2 * PARENT :]]
            if i == 0:
                pieces[0] = pieces[0] + left_bias
            if i == 3:
                pieces[2] = pieces[2] + right_bias
            m0 = jnp.max(
                jnp.maximum(jnp.maximum(pieces[0], pieces[1]), pieces[2]), axis=0, keepdims=True
            )
            e = [jnp.exp2((x - m0) * TO_LOG2) for x in pieces]
            for n in range(3):
                p0[i % 2, n * PARENT : (n + 1) * PARENT, :] = e[n]
            z0 = jnp.sum(e[0] + e[1] + e[2], axis=0, keepdims=True)
            u0 = dot_nn(raw_t[1, :, rows], jnp.concatenate([x.astype(BF) for x in e], axis=0))
            j, half = i // 2, i % 2
            lanes = slice(half * BLOCK, (half + 1) * BLOCK)
            m1, z1, u1 = (x[:, lanes] for x in far1[j])
            lanes2 = slice(j * BLOCK, (j + 1) * BLOCK)
            m2, z2, u2 = (spread64(x[:, lanes2], half) for x in far2)
            m1w, m2w = twice(m1, 1), twice(m2, 1)
            m = jnp.maximum(jnp.maximum(m0, m1w), m2w)
            a0 = jnp.exp2((m0 - m) * TO_LOG2)
            a1 = 2.0 * jnp.exp2((m1w - m) * TO_LOG2)
            a2 = 4.0 * jnp.exp2((m2w - m) * TO_LOG2)
            z = a0 * z0 + a1 * twice(z1, 1) + a2 * twice(z2, 1)
            inv = 1.0 / z
            o = ((a0 * inv) * u0 + (a1 * inv) * twice(u1, 1) + (a2 * inv) * twice(u2, 1)).astype(BF)
            oq[i, 0, h * HEAD : (h + 1) * HEAD, :] = o
            lg = m * TO_LOG2 + jnp.log2(z)
            g_t = g.astype(F32).T
            dr = jnp.sum(o.astype(F32) * g_t, axis=0, keepdims=True)
            lg_a, lg_b = lg[:, :BLOCK], lg[:, BLOCK:]
            g_a, g_b = g_t[:, :BLOCK], g_t[:, BLOCK:]
            dr_a, dr_b = dr[:, :BLOCK], dr[:, BLOCK:]
            low = jnp.minimum(lg_a, lg_b)
            w_a, w_b = jnp.exp2(low - lg_a), jnp.exp2(low - lg_b)
            g1_t.append((w_a * g_a + w_b * g_b).astype(BF))
            ec1.append(w_a * dr_a + w_b * dr_b)
            f1.append(2.0 * jnp.exp2(m1 * TO_LOG2 - low))
            lower = jnp.minimum(low, swap64(low))
            w_a, w_b = jnp.exp2(lower - lg_a), jnp.exp2(lower - lg_b)
            part = w_a * g_a + w_b * g_b
            g2_t.append(part + swap64(part))
            part = w_a * dr_a + w_b * dr_b
            ec2.append(part + swap64(part))
            low2.append(lower)
            f0 = jnp.exp2(m0 * TO_LOG2 - lg)
            products = dot_nt(raw[1, rows, :], g)
            weights = p0[i % 2] * f0
            eb = weights.astype(BF)
            r = (weights * (products - dr)).astype(BF)
            for n, x in ((1, dot_nn(eb, g)), (0, dot_nn(r, q))):
                if i == 0:
                    acc0[n, rows, :] = x
                else:
                    old = slice(i * PARENT, (i + 2) * PARENT)
                    acc0[n, old, :] += x[: 2 * PARENT]
                    acc0[n, (i + 2) * PARENT : (i + 3) * PARENT, :] = x[2 * PARENT :]
            dq0.append(dot_nn(raw_t[0, :, rows], r))
        dq1 = []
        for j in range(2):
            pair = slice(2 * j, 2 * j + 2)
            g1 = jnp.concatenate([x.astype(F32).T.astype(BF) for x in g1_t[pair]], axis=0)
            dk, dv, dq = far_backward(
                blocks_t(one_t, 0, which1[j]), blocks(one, 1, which1[j]), q1[j], p1.at[j],
                jnp.concatenate(f1[pair], axis=1), g1, jnp.concatenate(ec1[pair], axis=1),
            )
            for n, b in enumerate(which1[j]):
                acc1[0, b * BLOCK : (b + 1) * BLOCK, :] = dk[n]
                acc1[1, b * BLOCK : (b + 1) * BLOCK, :] = dv[n]
            dq1.append(dq)

        def joined(parts):
            return jnp.concatenate(
                [
                    jnp.where(low_lanes(parts[0].shape), parts[2 * j], parts[2 * j + 1])
                    for j in range(2)
                ],
                axis=1,
            )

        g2 = joined(g2_t).T.astype(BF)
        f2 = 4.0 * jnp.exp2(far2[0] * TO_LOG2 - joined(low2))
        dk, dv, dq2 = far_backward(
            blocks_t(two_t, 0, which2), blocks(two, 1, which2), q2, p2, f2, g2, joined(ec2)
        )
        for n in range(4):
            acc2[0, n * BLOCK : (n + 1) * BLOCK, :] = dk[n]
            acc2[1, n * BLOCK : (n + 1) * BLOCK, :] = dv[n]
        for i in range(4):
            j, half = i // 2, i % 2
            d1 = dq1[j][:, half * BLOCK : (half + 1) * BLOCK]
            d2 = spread64(dq2[:, j * BLOCK : (j + 1) * BLOCK], half)
            coarse = 0.5 * d1 + 0.25 * d2
            oq[i, 1, h * HEAD : (h + 1) * HEAD, :] = ((dq0[i] + twice(coarse, 1)) * INV_ROOT).astype(BF)
        for n, cols, scale in ((0, kc, INV_ROOT), (1, vc, 1.0)):
            for i in range(4):
                rows = slice((i + 1) * PARENT, (i + 2) * PARENT)
                coarse = acc1[n, (i + 2) * BLOCK : (i + 3) * BLOCK, :] * (0.5 * scale)
                grad[i * PARENT : (i + 1) * PARENT, cols] = acc0[n, rows, :] * scale + twice(coarse)
            far = acc2[n, 128:256, :] * (0.25 * scale)
            mid = acc1[n, 0:256, :] * (0.5 * scale)
            near = acc0[n, 0:256, :] * scale
            to_left[0:256, cols] = (near + twice(mid[128:] + twice(far[64:]))).astype(BF)
            to_left[256:384, cols] = (mid[:128] + twice(far[:64])).astype(BF)
            to_left[384:512, cols] = (acc2[n, 0:128, :] * (0.25 * scale)).astype(BF)
            far = acc2[n, 256:384, :] * (0.25 * scale)
            mid = acc1[n, 768:1024, :] * (0.5 * scale)
            near = acc0[n, 1280:1536, :] * scale
            to_right[0:256, cols] = (near + twice(mid[:128] + twice(far[:64]))).astype(BF)
            to_right[256:384, cols] = (mid[128:] + twice(far[64:])).astype(BF)
            to_right[384:512, cols] = (acc2[n, 384:512, :] * (0.25 * scale)).astype(BF)
    oq_own[...] = oq[pl.ds(side * 2, 2)]
    oq_far[...] = oq[pl.ds((1 - side) * 2, 2)]
    near_out[...] = halos[1 - odd]
    wide_out[...] = halos[odd]


def main(where, kv_own, kv_got, near_got, wide_got, qg_own, qg_got, qg_first):
    rows, both = kv_own.shape
    width = both // 2
    oq_shape = jax.ShapeDtypeStruct((2, 2, width, PARENT), BF)
    halo_shape = jax.ShapeDtypeStruct((512, both), BF)
    operands = [kv_own, kv_got, near_got, wide_got, qg_own, qg_got]
    if qg_first:
        operands = operands[:2] + operands[4:] + operands[2:4]
    return pl.pallas_call(
        placed(functools.partial(main_kernel, qg_first), where),
        in_specs=[vmem()] * 6,
        out_specs=[vmem()] * 5,
        out_shape=[
            oq_shape,
            oq_shape,
            jax.ShapeDtypeStruct((2 * rows, both), F32),
            halo_shape,
            halo_shape,
        ],
        scratch_shapes=[
            pltpu.VMEM((2, 1536, HEAD), BF),
            pltpu.VMEM((2, HEAD, 1536), BF),
            pltpu.VMEM((2, 1024, HEAD), BF),
            pltpu.VMEM((2, HEAD, 1024), BF),
            pltpu.VMEM((2, 512, HEAD), BF),
            pltpu.VMEM((2, HEAD, 512), BF),
            pltpu.VMEM((1024, HEAD), BF),
            pltpu.VMEM((1024, HEAD), BF),
            pltpu.VMEM((2, 768, PARENT), F32),
            pltpu.VMEM((2, 384, PARENT), F32),
            pltpu.VMEM((384, PARENT), F32),
            pltpu.VMEM((2, 1536, HEAD), F32),
            pltpu.VMEM((2, 1024, HEAD), F32),
            pltpu.VMEM((2, 512, HEAD), F32),
            pltpu.VMEM((4, 2, width, PARENT), BF),
            pltpu.VMEM((2, 512, both), BF),
        ],
        compiler_params=pltpu.CompilerParams(vmem_limit_bytes=24 * 1024 * 1024),
        cost_estimate=light(),
    )(*operands)


def join_kernel(where, grad, near_got, wide_got, own, far):
    def fill(first, second, from_left, from_right):
        def parent(i):
            return grad[i * PARENT : (i + 1) * PARENT, :]

        def part(ref, start, stop):
            return ref[start:stop, :].astype(F32)

        first[0:256, :] = (
            parent(0) + part(from_left, 0, 256) + twice(twice(part(from_right, 384, 448)))
        ).astype(BF)
        first[256:512, :] = (
            parent(1) + twice(part(from_left, 256, 384) + twice(part(from_right, 448, 512)))
        ).astype(BF)
        second[0:256, :] = (
            parent(2) + twice(part(from_right, 256, 384) + twice(part(from_left, 384, 448)))
        ).astype(BF)
        second[256:512, :] = (
            parent(3) + part(from_right, 0, 256) + twice(twice(part(from_left, 448, 512)))
        ).astype(BF)

    for side in range(2):
        for odd in range(2):

            @pl.when((where[0] == side) & (where[3] == odd))
            def _(side=side, odd=odd):
                halves = (own, far) if side == 0 else (far, own)
                fill(*halves, *((wide_got, near_got) if odd == 0 else (near_got, wide_got)))


def join(where, grad, near_got, wide_got):
    shape = jax.ShapeDtypeStruct(near_got.shape, BF)
    return pl.pallas_call(
        placed(join_kernel, where),
        in_specs=[vmem(), vmem(), vmem()],
        out_specs=[vmem(), vmem()],
        out_shape=[shape, shape],
        compiler_params=small(),
        cost_estimate=light(),
    )(grad, near_got, wide_got)


def unpack_rows_kernel(where, *refs):
    ins, (first, second) = refs[:-2], refs[-2:]
    order = order_matrix(True)
    width = ins[0].shape[1] // 2
    side = where[0]
    blocks = [(side * CHUNKS + c, ins[c]) for c in range(CHUNKS)]
    blocks += [((1 - side) * CHUNKS + 1 - LATE_CHUNK, ins[CHUNKS])]
    for block, ref in blocks:
        at = pl.ds(pl.multiple_of(block * width, width), width)
        for i in range(2):
            rows = slice(i * PARENT, (i + 1) * PARENT)
            first[rows, at] = dot_nn(order, ref[rows, :width]).astype(BF)
            second[rows, at] = dot_nn(order, ref[rows, width:]).astype(BF)


def unpack_rows(where, own, got, shape):
    out = jax.ShapeDtypeStruct(shape, BF)
    return pl.pallas_call(
        placed(unpack_rows_kernel, where),
        in_specs=[vmem()] * (CHUNKS + 1),
        out_specs=[vmem(), vmem()],
        out_shape=[out, out],
        compiler_params=small(),
        cost_estimate=light(),
    )(*own, got)


def unpack_last_kernel(where, got, first_in, second_in, first, second, held, sems):
    del first_in, second_in
    order = order_matrix(True)
    width = got.shape[1] // 2
    block = (1 - where[0]) * CHUNKS + LATE_CHUNK
    at = pl.ds(pl.multiple_of(block * width, width), width)
    copies = []
    for i in range(2):
        rows = slice(i * PARENT, (i + 1) * PARENT)
        x = dot_nn(order, got[rows, :]).astype(BF)
        for m, ref in enumerate((first, second)):
            held[m, rows, :] = x[:, m * width : (m + 1) * width]
            copies.append(
                pltpu.make_async_copy(held.at[m, rows, :], ref.at[rows, at], sems.at[2 * i + m])
            )
            copies[-1].start()
    for copy in copies:
        copy.wait()


def unpack_last(where, got, first, second):
    out = jax.ShapeDtypeStruct(first.shape, BF)
    hbm = pl.BlockSpec(memory_space=pltpu.HBM)
    return pl.pallas_call(
        placed(unpack_last_kernel, where),
        in_specs=[vmem(), hbm, hbm],
        out_specs=[hbm, hbm],
        out_shape=[out, out],
        input_output_aliases={1: 0, 2: 1},
        scratch_shapes=[
            pltpu.VMEM((2, got.shape[0], got.shape[1] // 2), BF),
            pltpu.SemaphoreType.DMA((4,)),
        ],
        compiler_params=small(),
        cost_estimate=light(),
    )(got, first, second)


def unpack_columns_kernel(where, *refs):
    ins, (first, second) = refs[:-2], refs[-2:]
    order = order_matrix(True)
    width = ins[0].shape[2]
    for c in range(CHUNKS):
        for ref, side in ((ins[c], where[0]), (ins[CHUNKS + c], 1 - where[0])):
            at = pl.ds(pl.multiple_of((side * CHUNKS + c) * width, width), width)
            for i in range(2):
                rows = slice(i * PARENT, (i + 1) * PARENT)
                first[rows, at] = dot_nt(order, ref[i, 0]).astype(BF)
                second[rows, at] = dot_nt(order, ref[i, 1]).astype(BF)


def unpack_columns(where, own, got, shape):
    out = jax.ShapeDtypeStruct(shape, BF)
    return pl.pallas_call(
        placed(unpack_columns_kernel, where),
        in_specs=[vmem()] * (2 * CHUNKS),
        out_specs=[vmem(), vmem()],
        out_shape=[out, out],
        compiler_params=small(),
        cost_estimate=light(),
    )(*own, *got)


def on_device(queries, key_matrix, value_matrix, cotangent):
    axes = ("outer", "inner")
    count = lax.axis_size("outer") * lax.axis_size("inner")
    device = lax.axis_index("outer") * lax.axis_size("inner") + lax.axis_index("inner")
    where = (lax.axis_size("inner"), count)
    across = [(i, i ^ 1) for i in range(count)]
    near_edges = [(i, i ^ 2) for i in range(count) if i ^ 2 < count]
    wide_edges = [(i, i + 2 if i // 2 % 2 else i - 2) for i in range(count)]
    wide_edges = [(i, j) for i, j in wide_edges if 0 <= j < count]

    def swap(x):
        return lax.ppermute(x, axes, across)

    def beside(near, wide):
        near = lax.ppermute(near, axes, near_edges)
        return near, lax.ppermute(wide, axes, wide_edges)

    kv_far = [pack_cut(1 - device % 2, 0, key_matrix, value_matrix)]
    for c in range(1, CHUNKS):
        later, kv_far[0] = lax.optimization_barrier(((key_matrix, value_matrix), kv_far[0]))
        kv_far.append(pack_cut(1 - device % 2, c, *later))
    qg_far = pack(False, where, queries, cotangent)
    packed = pack(True, where, key_matrix, value_matrix, queries, cotangent)
    kv, qg = packed[:CHUNKS], packed[CHUNKS:]
    oq_own, oq_got, back = [], [], []
    for c in range(CHUNKS):
        got_kv = swap(kv_far[c])
        near, wide = halo(where, kv[c], got_kv)
        far = qg_far[c]
        if c > 0:
            near, wide, far = lax.optimization_barrier((near, wide, far))
        near, wide = beside(near, wide)
        own, far, grad, near, wide = main(where, kv[c], got_kv, near, wide, qg[c], swap(far), c == 0)
        oq_own.append(own)
        if c > 0:
            back[c - 1], near, wide, far = lax.optimization_barrier(
                (back[c - 1], near, wide, far)
            )
        back.append([grad, *beside(near, wide)])
        oq_got.append(swap(far))
    for c in range(CHUNKS):
        back[c], oq_got[c] = lax.optimization_barrier((back[c], oq_got[c]))
    kv_own, kv_got = [], []
    for c in range(CHUNKS):
        own, far = join(where, *back[c])
        kv_own.append(own)
        kv_got.append(swap(far))
    attended, query_grad = unpack_columns(where, oq_own, oq_got, queries.shape)
    key_grad, value_grad = unpack_rows(where, kv_own, kv_got[1 - LATE_CHUNK], queries.shape)
    key_grad, value_grad = unpack_last(where, kv_got[LATE_CHUNK], key_grad, value_grad)
    return attended, query_grad, key_grad, value_grad


def solution(mesh):
    spec = P(("outer", "inner"), None)
    return jax.shard_map(
        on_device,
        mesh=mesh,
        in_specs=(spec,) * 4,
        out_specs=(spec,) * 4,
        check_vma=False,
    )
```

```python
import functools
import math

import jax
import jax.numpy as jnp
from jax import lax
from jax.experimental import pallas as pl
from jax.experimental.pallas import tpu as pltpu
from jax.sharding import PartitionSpec as P

HEAD = 128
BLOCK = 128
PARENT = 256
LEVELS = 3
CHUNKS = 2
LATE_CHUNK = 1
INV_ROOT = HEAD**-0.5
TO_LOG2 = INV_ROOT * math.log2(math.e)
MASKED = -1e30
BF = jnp.bfloat16
F32 = jnp.float32


def dot_nt(a, b):
    return lax.dot_general(a, b, (((1,), (1,)), ((), ())), preferred_element_type=F32)


def dot_nn(a, b):
    return jnp.dot(a, b, preferred_element_type=F32)


def order_matrix(inverse):
    row = lax.broadcasted_iota(jnp.int32, (PARENT, PARENT), 0)
    col = lax.broadcasted_iota(jnp.int32, (PARENT, PARENT), 1)
    place, token = (col, row) if inverse else (row, col)
    slab = place // 64
    source = 4 * (place % 64) + 2 * (slab % 2) + slab // 2
    return jnp.where(source == token, 1.0, 0.0).astype(BF)


def pool1(x):
    return ((x[:BLOCK].astype(F32) + x[BLOCK:].astype(F32)) * 0.5).astype(BF)


def pool2(x):
    half = x[:BLOCK].astype(F32) + x[BLOCK:].astype(F32)
    return ((half[:64] + half[64:]) * 0.25).astype(BF)


def pool12(x):
    return ((x[:64].astype(F32) + x[64:].astype(F32)) * 0.5).astype(BF)


def twice(x, axis=0):
    return jnp.concatenate([x, x], axis=axis)


def pack_kernel(own, where, *refs):
    count = 4 if own else 2
    arrays, outs, (held, sems) = refs[:count], refs[count:-2], refs[-2:]
    rows, columns = arrays[0].shape
    half = columns // 2
    width = half // CHUNKS
    side = where[0] if own else 1 - where[0]
    at = pl.ds(pl.multiple_of(side * half, half), half)
    copies = [
        pltpu.make_async_copy(ref.at[:, at], held.at[m], sems.at[m]) for m, ref in enumerate(arrays)
    ]
    for copy in copies:
        copy.start()
    order = order_matrix(False)
    for m in range(count):
        copies[m].wait()
        first = m % 2 * width
        for i in range(rows // PARENT):
            at = slice(i * PARENT, (i + 1) * PARENT)
            x = dot_nn(order, held[m, at, :]).astype(BF)
            for c in range(CHUNKS):
                out = outs[m // 2 * CHUNKS + c]
                out[at, first : first + width] = x[:, c * width : (c + 1) * width]


def pack(own, where, *arrays):
    rows, columns = arrays[0].shape
    count = len(arrays)
    return pl.pallas_call(
        placed(functools.partial(pack_kernel, own), where),
        in_specs=[pl.BlockSpec(memory_space=pltpu.HBM)] * count,
        out_specs=[vmem()] * (count // 2 * CHUNKS),
        out_shape=[jax.ShapeDtypeStruct((rows, columns // CHUNKS), BF)] * (count // 2 * CHUNKS),
        scratch_shapes=[
            pltpu.VMEM((count, rows, columns // 2), BF),
            pltpu.SemaphoreType.DMA((count,)),
        ],
        compiler_params=small(),
        cost_estimate=light(),
    )(*arrays)


def pack_cut_kernel(a, b, out):
    order = order_matrix(False)
    width = a.shape[1]
    for m, ref in enumerate((a, b)):
        for i in range(a.shape[0] // PARENT):
            rows = slice(i * PARENT, (i + 1) * PARENT)
            out[rows, m * width : (m + 1) * width] = dot_nn(order, ref[rows, :]).astype(BF)


def pack_cut(side, chunk, a, b):
    rows, columns = a.shape
    width = columns // 2 // CHUNKS
    cut = [lax.dynamic_slice_in_dim(x, (side * CHUNKS + chunk) * width, width, 1) for x in (a, b)]
    return pl.pallas_call(
        pack_cut_kernel,
        in_specs=[vmem(), vmem()],
        out_specs=vmem(),
        out_shape=jax.ShapeDtypeStruct((rows, 2 * width), BF),
        compiler_params=small(),
        cost_estimate=light(),
    )(*cut)


def placed(kernel, grid):
    inner, count = grid

    def body(*refs):
        device = lax.axis_index("outer") * inner + lax.axis_index("inner")
        pair = device // 2
        left = jnp.where(pair > 0, 1, 0)
        right = jnp.where(pair < count // 2 - 1, 1, 0)
        kernel((device % 2, left, right, pair % 2), *refs)

    return body


def vmem():
    return pl.BlockSpec(memory_space=pltpu.VMEM)


def small():
    return pltpu.CompilerParams(vmem_limit_bytes=8 * 1024 * 1024)


def light():
    return pl.CostEstimate(flops=1000, bytes_accessed=1000, transcendentals=0)


def halo_kernel(where, own, got, near, wide):
    def fill(first, second, to_right, to_left):
        to_right[0:256, :] = second[256:512, :]
        to_right[256:384, :] = pool1(second[0:256, :])
        to_right[384:448, :] = pool2(first[0:256, :])
        to_right[448:512, :] = pool2(first[256:512, :])
        to_left[0:256, :] = first[0:256, :]
        to_left[256:384, :] = pool1(first[256:512, :])
        to_left[384:448, :] = pool2(second[0:256, :])
        to_left[448:512, :] = pool2(second[256:512, :])

    for side in range(2):
        for odd in range(2):

            @pl.when((where[0] == side) & (where[3] == odd))
            def _(side=side, odd=odd):
                halves = (own, got) if side == 0 else (got, own)
                fill(*halves, *((near, wide) if odd == 0 else (wide, near)))


def halo(where, own, got):
    shape = jax.ShapeDtypeStruct(own.shape, BF)
    return pl.pallas_call(
        placed(halo_kernel, where),
        in_specs=[vmem(), vmem()],
        out_specs=[vmem(), vmem()],
        out_shape=[shape, shape],
        compiler_params=small(),
        cost_estimate=light(),
    )(own, got)


def turn_kernel(where, own, got, raw_t, one, one_t):
    for side, ref in ((where[0], own), (1 - where[0], got)):
        for i in range(2):
            rows = slice(i * PARENT, (i + 1) * PARENT)
            at = pl.ds(pl.multiple_of((side * 2 + i) * PARENT, PARENT), PARENT)
            half = pl.ds(pl.multiple_of((side * 2 + i) * BLOCK, BLOCK), BLOCK)
            for n in range(2):
                x = ref[rows, n * HEAD : (n + 1) * HEAD]
                raw_t[n, :, at] = x.T
                x = pool1(x)
                one[n, half, :] = x
                one_t[n, :, half] = x.T


def turn(where, own, got):
    shapes = ((2, HEAD, 1024), (2, 512, HEAD), (2, HEAD, 512))
    return pl.pallas_call(
        placed(turn_kernel, where),
        in_specs=[vmem()] * 2,
        out_specs=[vmem()] * 3,
        out_shape=[jax.ShapeDtypeStruct(shape, BF) for shape in shapes],
        compiler_params=small(),
        cost_estimate=light(),
    )(own, got)


def swap64(x):
    return pltpu.roll(x, 64, 1)


def low_lanes(shape):
    return lax.broadcasted_iota(jnp.int32, shape, 1) < 64


def spread64(x, half):
    other = swap64(x)
    low = low_lanes(x.shape)
    return jnp.where(low, x, other) if half == 0 else jnp.where(low, other, x)


def far_forward(k, v_t, q, bias, p_ref):
    k0, k1, k2, k3 = k
    v0, v1, v2, v3 = v_t
    left, right = bias
    outer = dot_nt(jnp.concatenate([k0, k3], axis=0), q)
    first, last = outer[:BLOCK], outer[BLOCK:]
    mid_low = dot_nt(k2, q[:BLOCK])
    mid_high = dot_nt(k1, q[BLOCK:])
    if left is not None:
        first = first + left
        mid_high = mid_high + left
    if right is not None:
        last = last + right
        mid_low = mid_low + right
    mid = jnp.concatenate([mid_low, mid_high], axis=1)
    peak = jnp.max(jnp.maximum(jnp.maximum(first, last), mid), axis=0, keepdims=True)
    parts = [jnp.exp2((x - peak) * TO_LOG2) for x in (first, last, mid)]
    for n, x in enumerate(parts):
        p_ref[n * BLOCK : (n + 1) * BLOCK, :] = x
    total = jnp.sum(parts[0] + parts[1] + parts[2], axis=0, keepdims=True)
    pb = [x.astype(BF) for x in parts]
    mixed = dot_nn(
        jnp.concatenate([v0, v3], axis=1), jnp.concatenate(pb[:2], axis=0)
    ) + jnp.concatenate([dot_nn(v2, pb[2][:, :BLOCK]), dot_nn(v1, pb[2][:, BLOCK:])], axis=1)
    return peak, total, mixed


def far_backward(k_t, v, q, p_ref, factor, g, ec):
    k0, k1, k2, k3 = k_t
    v0, v1, v2, v3 = v
    e_out = p_ref[: 2 * BLOCK, :] * factor
    e_mid = p_ref[2 * BLOCK :, :] * factor
    eb_out, eb_mid = e_out.astype(BF), e_mid.astype(BF)
    p_out = dot_nt(jnp.concatenate([v0, v3], axis=0), g)
    p_mid = jnp.concatenate([dot_nt(v2, g[:BLOCK]), dot_nt(v1, g[BLOCK:])], axis=1)
    r_out = (e_out * (p_out - ec)).astype(BF)
    r_mid = (e_mid * (p_mid - ec)).astype(BF)
    dv03 = dot_nn(eb_out, g)
    dv2 = dot_nn(eb_mid[:, :BLOCK], g[:BLOCK])
    dv1 = dot_nn(eb_mid[:, BLOCK:], g[BLOCK:])
    dk03 = dot_nn(r_out, q)
    dk2 = dot_nn(r_mid[:, :BLOCK], q[:BLOCK])
    dk1 = dot_nn(r_mid[:, BLOCK:], q[BLOCK:])
    dq_t = dot_nn(jnp.concatenate([k0, k3], axis=1), r_out) + jnp.concatenate(
        [dot_nn(k2, r_mid[:, :BLOCK]), dot_nn(k1, r_mid[:, BLOCK:])], axis=1
    )
    return (dk03[:BLOCK], dk1, dk2, dk03[BLOCK:]), (dv03[:BLOCK], dv1, dv2, dv03[BLOCK:]), dq_t


def main_kernel(qg_first, where, kv_own, kv_got, *refs):
    turned, refs = refs[:3], refs[3:]
    if qg_first:
        refs = (*refs[2:4], *refs[:2], *refs[4:])
    one_chunk(where, turned, kv_own, kv_got, *refs)


def one_chunk(
    where, turned, kv_own, kv_got, near_got, wide_got, qg_own, qg_got,
    oq_own, oq_far, grad, near_out, wide_out,
    raw, raw_t, one, one_t, two, two_t, qs, gs, p0, p1, p2, acc0, acc1, acc2, oq, halos,
):
    side = where[0]
    odd = where[3]
    halos[1 - odd] = near_got[...]
    halos[odd] = wide_got[...]
    from_left, from_right = halos.at[0], halos.at[1]
    to_left, to_right = halos.at[0], halos.at[1]
    width = kv_own.shape[1] // 2
    left_bias = (1 - where[1]).astype(F32) * MASKED
    right_bias = (1 - where[2]).astype(F32) * MASKED
    own_at = pl.multiple_of(side * 512, 512)
    got_at = pl.multiple_of((1 - side) * 512, 512)
    for h in range(width // HEAD):
        kc = slice(h * HEAD, (h + 1) * HEAD)
        vc = slice(width + h * HEAD, width + (h + 1) * HEAD)
        for n, cols in ((0, kc), (1, vc)):
            raw[n, 0:256, :] = from_left[0:256, cols]
            raw[n, pl.ds(256 + own_at, 512), :] = kv_own[:, cols]
            raw[n, pl.ds(256 + got_at, 512), :] = kv_got[:, cols]
            raw[n, 1280:1536, :] = from_right[0:256, cols]
            raw_t[n, :, 256:1280] = turned[0][n]
            one[n, 256:768, :] = turned[1][n]
            one_t[n, :, 256:768] = turned[2][n]
            one[n, 0:128, :] = from_left[256:384, cols]
            one[n, 128:256, :] = pool1(raw[n, 0:256, :])
            one[n, 768:896, :] = pool1(raw[n, 1280:1536, :])
            one[n, 896:1024, :] = from_right[256:384, cols]
            two[n, 0:128, :] = from_left[384:512, cols]
            two[n, 128:192, :] = pool12(one[n, 0:128, :])
            two[n, 192:256, :] = pool2(raw[n, 0:256, :])
            two[n, 256:320, :] = pool2(raw[n, 1280:1536, :])
            two[n, 320:384, :] = pool12(one[n, 896:1024, :])
            two[n, 384:512, :] = from_right[384:512, cols]
            for i in (0, 5):
                rows = slice(i * PARENT, (i + 1) * PARENT)
                raw_t[n, :, rows] = raw[n, rows, :].T
            for i in (0, 1, 6, 7):
                rows = slice(i * BLOCK, (i + 1) * BLOCK)
                one_t[n, :, rows] = one[n, rows, :].T
            for i in range(4):
                rows = slice(i * BLOCK, (i + 1) * BLOCK)
                two_t[n, :, rows] = two[n, rows, :].T
        qs[pl.ds(own_at, 512), :] = qg_own[:, kc]
        qs[pl.ds(got_at, 512), :] = qg_got[:, kc]
        gs[pl.ds(own_at, 512), :] = qg_own[:, vc]
        gs[pl.ds(got_at, 512), :] = qg_got[:, vc]

        def blocks(ref, n, which):
            return [ref[n, b * BLOCK : (b + 1) * BLOCK, :] for b in which]

        def blocks_t(ref, n, which):
            return [ref[n, :, b * BLOCK : (b + 1) * BLOCK] for b in which]

        q_parents = [qs[i * PARENT : (i + 1) * PARENT, :] for i in range(4)]
        q1 = [
            jnp.concatenate([pool1(q_parents[2 * j]), pool1(q_parents[2 * j + 1])], axis=0)
            for j in range(2)
        ]
        q2 = jnp.concatenate([pool2(x) for x in q_parents], axis=0)
        which1 = [(0, 1, 4, 5), (2, 3, 6, 7)]
        bias1 = [(left_bias, None), (None, right_bias)]
        which2 = (0, 1, 2, 3)
        far1 = [
            far_forward(
                blocks(one, 0, which1[j]), blocks_t(one_t, 1, which1[j]), q1[j], bias1[j], p1.at[j]
            )
            for j in range(2)
        ]
        far2 = far_forward(
            blocks(two, 0, which2), blocks_t(two_t, 1, which2), q2, (left_bias, right_bias), p2
        )
        g1_t, ec1, f1 = [], [], []
        g2_t, ec2, low2 = [], [], []
        dq0 = []
        for i in range(4):
            rows = slice(i * PARENT, i * PARENT + 3 * PARENT)
            q = q_parents[i]
            g = gs[i * PARENT : (i + 1) * PARENT, :]
            s = dot_nt(raw[0, rows, :], q)
            pieces = [s[:PARENT], s[PARENT : 2 * PARENT], s[2 * PARENT :]]
            if i == 0:
                pieces[0] = pieces[0] + left_bias
            if i == 3:
                pieces[2] = pieces[2] + right_bias
            m0 = jnp.max(
                jnp.maximum(jnp.maximum(pieces[0], pieces[1]), pieces[2]), axis=0, keepdims=True
            )
            e = [jnp.exp2((x - m0) * TO_LOG2) for x in pieces]
            for n in range(3):
                p0[i % 2, n * PARENT : (n + 1) * PARENT, :] = e[n]
            z0 = jnp.sum(e[0] + e[1] + e[2], axis=0, keepdims=True)
            u0 = dot_nn(raw_t[1, :, rows], jnp.concatenate([x.astype(BF) for x in e], axis=0))
            j, half = i // 2, i % 2
            lanes = slice(half * BLOCK, (half + 1) * BLOCK)
            m1, z1, u1 = (x[:, lanes] for x in far1[j])
            lanes2 = slice(j * BLOCK, (j + 1) * BLOCK)
            m2, z2, u2 = (spread64(x[:, lanes2], half) for x in far2)
            m1w, m2w = twice(m1, 1), twice(m2, 1)
            m = jnp.maximum(jnp.maximum(m0, m1w), m2w)
            a0 = jnp.exp2((m0 - m) * TO_LOG2)
            a1 = 2.0 * jnp.exp2((m1w - m) * TO_LOG2)
            a2 = 4.0 * jnp.exp2((m2w - m) * TO_LOG2)
            z = a0 * z0 + a1 * twice(z1, 1) + a2 * twice(z2, 1)
            inv = 1.0 / z
            o = ((a0 * inv) * u0 + (a1 * inv) * twice(u1, 1) + (a2 * inv) * twice(u2, 1)).astype(BF)
            oq[i, 0, h * HEAD : (h + 1) * HEAD, :] = o
            lg = m * TO_LOG2 + jnp.log2(z)
            g_t = g.astype(F32).T
            dr = jnp.sum(o.astype(F32) * g_t, axis=0, keepdims=True)
            lg_a, lg_b = lg[:, :BLOCK], lg[:, BLOCK:]
            g_a, g_b = g_t[:, :BLOCK], g_t[:, BLOCK:]
            dr_a, dr_b = dr[:, :BLOCK], dr[:, BLOCK:]
            low = jnp.minimum(lg_a, lg_b)
            w_a, w_b = jnp.exp2(low - lg_a), jnp.exp2(low - lg_b)
            g1_t.append((w_a * g_a + w_b * g_b).astype(BF))
            ec1.append(w_a * dr_a + w_b * dr_b)
            f1.append(2.0 * jnp.exp2(m1 * TO_LOG2 - low))
            lower = jnp.minimum(low, swap64(low))
            w_a, w_b = jnp.exp2(lower - lg_a), jnp.exp2(lower - lg_b)
            part = w_a * g_a + w_b * g_b
            g2_t.append(part + swap64(part))
            part = w_a * dr_a + w_b * dr_b
            ec2.append(part + swap64(part))
            low2.append(lower)
            f0 = jnp.exp2(m0 * TO_LOG2 - lg)
            products = dot_nt(raw[1, rows, :], g)
            weights = p0[i % 2] * f0
            eb = weights.astype(BF)
            r = (weights * (products - dr)).astype(BF)
            for n, x in ((1, dot_nn(eb, g)), (0, dot_nn(r, q))):
                if i == 0:
                    acc0[n, rows, :] = x
                else:
                    old = slice(i * PARENT, (i + 2) * PARENT)
                    acc0[n, old, :] += x[: 2 * PARENT]
                    acc0[n, (i + 2) * PARENT : (i + 3) * PARENT, :] = x[2 * PARENT :]
            dq0.append(dot_nn(raw_t[0, :, rows], r))
        dq1 = []
        for j in range(2):
            pair = slice(2 * j, 2 * j + 2)
            g1 = jnp.concatenate([x.astype(F32).T.astype(BF) for x in g1_t[pair]], axis=0)
            dk, dv, dq = far_backward(
                blocks_t(one_t, 0, which1[j]), blocks(one, 1, which1[j]), q1[j], p1.at[j],
                jnp.concatenate(f1[pair], axis=1), g1, jnp.concatenate(ec1[pair], axis=1),
            )
            for n, b in enumerate(which1[j]):
                acc1[0, b * BLOCK : (b + 1) * BLOCK, :] = dk[n]
                acc1[1, b * BLOCK : (b + 1) * BLOCK, :] = dv[n]
            dq1.append(dq)

        def joined(parts):
            return jnp.concatenate(
                [
                    jnp.where(low_lanes(parts[0].shape), parts[2 * j], parts[2 * j + 1])
                    for j in range(2)
                ],
                axis=1,
            )

        g2 = joined(g2_t).T.astype(BF)
        f2 = 4.0 * jnp.exp2(far2[0] * TO_LOG2 - joined(low2))
        dk, dv, dq2 = far_backward(
            blocks_t(two_t, 0, which2), blocks(two, 1, which2), q2, p2, f2, g2, joined(ec2)
        )
        for n in range(4):
            acc2[0, n * BLOCK : (n + 1) * BLOCK, :] = dk[n]
            acc2[1, n * BLOCK : (n + 1) * BLOCK, :] = dv[n]
        for i in range(4):
            j, half = i // 2, i % 2
            d1 = dq1[j][:, half * BLOCK : (half + 1) * BLOCK]
            d2 = spread64(dq2[:, j * BLOCK : (j + 1) * BLOCK], half)
            coarse = 0.5 * d1 + 0.25 * d2
            oq[i, 1, h * HEAD : (h + 1) * HEAD, :] = ((dq0[i] + twice(coarse, 1)) * INV_ROOT).astype(BF)
        for n, cols, scale in ((0, kc, INV_ROOT), (1, vc, 1.0)):
            for i in range(4):
                rows = slice((i + 1) * PARENT, (i + 2) * PARENT)
                coarse = acc1[n, (i + 2) * BLOCK : (i + 3) * BLOCK, :] * (0.5 * scale)
                grad[i * PARENT : (i + 1) * PARENT, cols] = acc0[n, rows, :] * scale + twice(coarse)
            far = acc2[n, 128:256, :] * (0.25 * scale)
            mid = acc1[n, 0:256, :] * (0.5 * scale)
            near = acc0[n, 0:256, :] * scale
            to_left[0:256, cols] = (near + twice(mid[128:] + twice(far[64:]))).astype(BF)
            to_left[256:384, cols] = (mid[:128] + twice(far[:64])).astype(BF)
            to_left[384:512, cols] = (acc2[n, 0:128, :] * (0.25 * scale)).astype(BF)
            far = acc2[n, 256:384, :] * (0.25 * scale)
            mid = acc1[n, 768:1024, :] * (0.5 * scale)
            near = acc0[n, 1280:1536, :] * scale
            to_right[0:256, cols] = (near + twice(mid[:128] + twice(far[:64]))).astype(BF)
            to_right[256:384, cols] = (mid[128:] + twice(far[64:])).astype(BF)
            to_right[384:512, cols] = (acc2[n, 384:512, :] * (0.25 * scale)).astype(BF)
    oq_own[...] = oq[pl.ds(side * 2, 2)]
    oq_far[...] = oq[pl.ds((1 - side) * 2, 2)]
    near_out[...] = halos[1 - odd]
    wide_out[...] = halos[odd]


def main(where, turned, kv_own, kv_got, near_got, wide_got, qg_own, qg_got, qg_first):
    rows, both = kv_own.shape
    width = both // 2
    oq_shape = jax.ShapeDtypeStruct((2, 2, width, PARENT), BF)
    halo_shape = jax.ShapeDtypeStruct((512, both), BF)
    operands = [kv_own, kv_got, near_got, wide_got, qg_own, qg_got]
    if qg_first:
        operands = operands[:2] + operands[4:] + operands[2:4]
    operands[2:2] = turned
    return pl.pallas_call(
        placed(functools.partial(main_kernel, qg_first), where),
        in_specs=[vmem()] * 9,
        out_specs=[vmem()] * 5,
        out_shape=[
            oq_shape,
            oq_shape,
            jax.ShapeDtypeStruct((2 * rows, both), F32),
            halo_shape,
            halo_shape,
        ],
        scratch_shapes=[
            pltpu.VMEM((2, 1536, HEAD), BF),
            pltpu.VMEM((2, HEAD, 1536), BF),
            pltpu.VMEM((2, 1024, HEAD), BF),
            pltpu.VMEM((2, HEAD, 1024), BF),
            pltpu.VMEM((2, 512, HEAD), BF),
            pltpu.VMEM((2, HEAD, 512), BF),
            pltpu.VMEM((1024, HEAD), BF),
            pltpu.VMEM((1024, HEAD), BF),
            pltpu.VMEM((2, 768, PARENT), F32),
            pltpu.VMEM((2, 384, PARENT), F32),
            pltpu.VMEM((384, PARENT), F32),
            pltpu.VMEM((2, 1536, HEAD), F32),
            pltpu.VMEM((2, 1024, HEAD), F32),
            pltpu.VMEM((2, 512, HEAD), F32),
            pltpu.VMEM((4, 2, width, PARENT), BF),
            pltpu.VMEM((2, 512, both), BF),
        ],
        compiler_params=pltpu.CompilerParams(vmem_limit_bytes=24 * 1024 * 1024),
        cost_estimate=light(),
    )(*operands)


def join_kernel(where, grad, near_got, wide_got, own, far):
    def fill(first, second, from_left, from_right):
        def parent(i):
            return grad[i * PARENT : (i + 1) * PARENT, :]

        def part(ref, start, stop):
            return ref[start:stop, :].astype(F32)

        first[0:256, :] = (
            parent(0) + part(from_left, 0, 256) + twice(twice(part(from_right, 384, 448)))
        ).astype(BF)
        first[256:512, :] = (
            parent(1) + twice(part(from_left, 256, 384) + twice(part(from_right, 448, 512)))
        ).astype(BF)
        second[0:256, :] = (
            parent(2) + twice(part(from_right, 256, 384) + twice(part(from_left, 384, 448)))
        ).astype(BF)
        second[256:512, :] = (
            parent(3) + part(from_right, 0, 256) + twice(twice(part(from_left, 448, 512)))
        ).astype(BF)

    for side in range(2):
        for odd in range(2):

            @pl.when((where[0] == side) & (where[3] == odd))
            def _(side=side, odd=odd):
                halves = (own, far) if side == 0 else (far, own)
                fill(*halves, *((wide_got, near_got) if odd == 0 else (near_got, wide_got)))


def join(where, grad, near_got, wide_got):
    shape = jax.ShapeDtypeStruct(near_got.shape, BF)
    return pl.pallas_call(
        placed(join_kernel, where),
        in_specs=[vmem(), vmem(), vmem()],
        out_specs=[vmem(), vmem()],
        out_shape=[shape, shape],
        compiler_params=small(),
        cost_estimate=light(),
    )(grad, near_got, wide_got)


def unpack_rows_kernel(where, *refs):
    ins, (first, second) = refs[:-2], refs[-2:]
    order = order_matrix(True)
    width = ins[0].shape[1] // 2
    side = where[0]
    blocks = [(side * CHUNKS + c, ins[c]) for c in range(CHUNKS)]
    blocks += [((1 - side) * CHUNKS + 1 - LATE_CHUNK, ins[CHUNKS])]
    for block, ref in blocks:
        at = pl.ds(pl.multiple_of(block * width, width), width)
        for i in range(2):
            rows = slice(i * PARENT, (i + 1) * PARENT)
            first[rows, at] = dot_nn(order, ref[rows, :width]).astype(BF)
            second[rows, at] = dot_nn(order, ref[rows, width:]).astype(BF)


def unpack_rows(where, own, got, shape):
    out = jax.ShapeDtypeStruct(shape, BF)
    return pl.pallas_call(
        placed(unpack_rows_kernel, where),
        in_specs=[vmem()] * (CHUNKS + 1),
        out_specs=[vmem(), vmem()],
        out_shape=[out, out],
        compiler_params=small(),
        cost_estimate=light(),
    )(*own, got)


def unpack_last_kernel(where, got, first_in, second_in, first, second, held, sems):
    del first_in, second_in
    order = order_matrix(True)
    width = got.shape[1] // 2
    block = (1 - where[0]) * CHUNKS + LATE_CHUNK
    at = pl.ds(pl.multiple_of(block * width, width), width)
    copies = []
    for i in range(2):
        rows = slice(i * PARENT, (i + 1) * PARENT)
        x = dot_nn(order, got[rows, :]).astype(BF)
        for m, ref in enumerate((first, second)):
            held[m, rows, :] = x[:, m * width : (m + 1) * width]
            copies.append(
                pltpu.make_async_copy(held.at[m, rows, :], ref.at[rows, at], sems.at[2 * i + m])
            )
            copies[-1].start()
    for copy in copies:
        copy.wait()


def unpack_last(where, got, first, second):
    out = jax.ShapeDtypeStruct(first.shape, BF)
    hbm = pl.BlockSpec(memory_space=pltpu.HBM)
    return pl.pallas_call(
        placed(unpack_last_kernel, where),
        in_specs=[vmem(), hbm, hbm],
        out_specs=[hbm, hbm],
        out_shape=[out, out],
        input_output_aliases={1: 0, 2: 1},
        scratch_shapes=[
            pltpu.VMEM((2, got.shape[0], got.shape[1] // 2), BF),
            pltpu.SemaphoreType.DMA((4,)),
        ],
        compiler_params=small(),
        cost_estimate=light(),
    )(got, first, second)


def unpack_columns_kernel(where, *refs):
    ins, (first, second) = refs[:-2], refs[-2:]
    order = order_matrix(True)
    width = ins[0].shape[2]
    for c in range(CHUNKS):
        for ref, side in ((ins[c], where[0]), (ins[CHUNKS + c], 1 - where[0])):
            at = pl.ds(pl.multiple_of((side * CHUNKS + c) * width, width), width)
            for i in range(2):
                rows = slice(i * PARENT, (i + 1) * PARENT)
                first[rows, at] = dot_nt(order, ref[i, 0]).astype(BF)
                second[rows, at] = dot_nt(order, ref[i, 1]).astype(BF)


def unpack_columns(where, own, got, shape):
    out = jax.ShapeDtypeStruct(shape, BF)
    return pl.pallas_call(
        placed(unpack_columns_kernel, where),
        in_specs=[vmem()] * (2 * CHUNKS),
        out_specs=[vmem(), vmem()],
        out_shape=[out, out],
        compiler_params=small(),
        cost_estimate=light(),
    )(*own, *got)


def on_device(queries, key_matrix, value_matrix, cotangent):
    axes = ("outer", "inner")
    count = lax.axis_size("outer") * lax.axis_size("inner")
    device = lax.axis_index("outer") * lax.axis_size("inner") + lax.axis_index("inner")
    where = (lax.axis_size("inner"), count)
    across = [(i, i ^ 1) for i in range(count)]
    near_edges = [(i, i ^ 2) for i in range(count) if i ^ 2 < count]
    wide_edges = [(i, i + 2 if i // 2 % 2 else i - 2) for i in range(count)]
    wide_edges = [(i, j) for i, j in wide_edges if 0 <= j < count]

    def swap(x):
        return lax.ppermute(x, axes, across)

    def beside(near, wide):
        near = lax.ppermute(near, axes, near_edges)
        return near, lax.ppermute(wide, axes, wide_edges)

    kv_far = [pack_cut(1 - device % 2, 0, key_matrix, value_matrix)]
    for c in range(1, CHUNKS):
        later, kv_far[0] = lax.optimization_barrier(((key_matrix, value_matrix), kv_far[0]))
        kv_far.append(pack_cut(1 - device % 2, c, *later))
    qg_far = pack(False, where, queries, cotangent)
    packed = pack(True, where, key_matrix, value_matrix, queries, cotangent)
    kv, qg = packed[:CHUNKS], packed[CHUNKS:]
    oq_own, oq_got, back = [], [], []
    for c in range(CHUNKS):
        got_kv = swap(kv_far[c])
        near, wide = halo(where, kv[c], got_kv)
        far = qg_far[c]
        if c > 0:
            near, wide, far = lax.optimization_barrier((near, wide, far))
        near, wide = beside(near, wide)
        own, far, grad, near, wide = main(where, turn(where, kv[c], got_kv), kv[c], got_kv, near, wide, qg[c], swap(far), c == 0)
        oq_own.append(own)
        oq_got.append(swap(far))
        if c > 0:
            back[c - 1], near, wide = lax.optimization_barrier((back[c - 1], near, wide))
        back.append([grad, *beside(near, wide)])
    for c in range(CHUNKS):
        oq_got[c], back[c] = lax.optimization_barrier((oq_got[c], back[c]))
    kv_own, kv_got = [], []
    for c in range(CHUNKS):
        own, far = join(where, *back[c])
        kv_own.append(own)
        kv_got.append(swap(far))
    attended, query_grad = unpack_columns(where, oq_own, oq_got, queries.shape)
    key_grad, value_grad = unpack_rows(where, kv_own, kv_got[1 - LATE_CHUNK], queries.shape)
    key_grad, value_grad = unpack_last(where, kv_got[LATE_CHUNK], key_grad, value_grad)
    return attended, query_grad, key_grad, value_grad


def solution(mesh):
    spec = P(("outer", "inner"), None)
    return jax.shard_map(
        on_device,
        mesh=mesh,
        in_specs=(spec,) * 4,
        out_specs=(spec,) * 4,
        check_vma=False,
    )
```

```python
import functools
import math

import jax
import jax.numpy as jnp
from jax import lax
from jax.experimental import pallas as pl
from jax.experimental.pallas import tpu as pltpu
from jax.sharding import PartitionSpec as P

HEAD = 128
BLOCK = 128
PARENT = 256
LEVELS = 3
CHUNKS = 2
LATE_CHUNK = 1
INV_ROOT = HEAD**-0.5
TO_LOG2 = INV_ROOT * math.log2(math.e)
MASKED = -1e30
BF = jnp.bfloat16
F32 = jnp.float32


def dot_nt(a, b):
    return lax.dot_general(a, b, (((1,), (1,)), ((), ())), preferred_element_type=F32)


def dot_nn(a, b):
    return jnp.dot(a, b, preferred_element_type=F32)


def order_matrix(inverse):
    row = lax.broadcasted_iota(jnp.int32, (PARENT, PARENT), 0)
    col = lax.broadcasted_iota(jnp.int32, (PARENT, PARENT), 1)
    place, token = (col, row) if inverse else (row, col)
    slab = place // 64
    source = 4 * (place % 64) + 2 * (slab % 2) + slab // 2
    return jnp.where(source == token, 1.0, 0.0).astype(BF)


def pool1(x):
    return ((x[:BLOCK].astype(F32) + x[BLOCK:].astype(F32)) * 0.5).astype(BF)


def pool2(x):
    half = x[:BLOCK].astype(F32) + x[BLOCK:].astype(F32)
    return ((half[:64] + half[64:]) * 0.25).astype(BF)


def pool12(x):
    return ((x[:64].astype(F32) + x[64:].astype(F32)) * 0.5).astype(BF)


def twice(x, axis=0):
    return jnp.concatenate([x, x], axis=axis)


def pack_kernel(own, where, *refs):
    count = 4 if own else 2
    arrays, outs, (held, sems) = refs[:count], refs[count:-2], refs[-2:]
    rows, columns = arrays[0].shape
    half = columns // 2
    width = half // CHUNKS
    side = where[0] if own else 1 - where[0]
    at = pl.ds(pl.multiple_of(side * half, half), half)
    copies = [
        pltpu.make_async_copy(ref.at[:, at], held.at[m], sems.at[m]) for m, ref in enumerate(arrays)
    ]
    for copy in copies:
        copy.start()
    order = order_matrix(False)
    for m in range(count):
        copies[m].wait()
        first = m % 2 * width
        for i in range(rows // PARENT):
            at = slice(i * PARENT, (i + 1) * PARENT)
            x = dot_nn(order, held[m, at, :]).astype(BF)
            for c in range(CHUNKS):
                out = outs[m // 2 * CHUNKS + c]
                out[at, first : first + width] = x[:, c * width : (c + 1) * width]


def pack(own, where, *arrays):
    rows, columns = arrays[0].shape
    count = len(arrays)
    return pl.pallas_call(
        placed(functools.partial(pack_kernel, own), where),
        in_specs=[pl.BlockSpec(memory_space=pltpu.HBM)] * count,
        out_specs=[vmem()] * (count // 2 * CHUNKS),
        out_shape=[jax.ShapeDtypeStruct((rows, columns // CHUNKS), BF)] * (count // 2 * CHUNKS),
        scratch_shapes=[
            pltpu.VMEM((count, rows, columns // 2), BF),
            pltpu.SemaphoreType.DMA((count,)),
        ],
        compiler_params=small(),
        cost_estimate=light(),
    )(*arrays)


def pack_cut_kernel(a, b, out):
    order = order_matrix(False)
    width = a.shape[1]
    for m, ref in enumerate((a, b)):
        for i in range(a.shape[0] // PARENT):
            rows = slice(i * PARENT, (i + 1) * PARENT)
            out[rows, m * width : (m + 1) * width] = dot_nn(order, ref[rows, :]).astype(BF)


def pack_cut(side, chunk, a, b):
    rows, columns = a.shape
    width = columns // 2 // CHUNKS
    cut = [lax.dynamic_slice_in_dim(x, (side * CHUNKS + chunk) * width, width, 1) for x in (a, b)]
    return pl.pallas_call(
        pack_cut_kernel,
        in_specs=[vmem(), vmem()],
        out_specs=vmem(),
        out_shape=jax.ShapeDtypeStruct((rows, 2 * width), BF),
        compiler_params=small(),
        cost_estimate=light(),
    )(*cut)


def placed(kernel, grid):
    inner, count = grid

    def body(*refs):
        device = lax.axis_index("outer") * inner + lax.axis_index("inner")
        pair = device // 2
        left = jnp.where(pair > 0, 1, 0)
        right = jnp.where(pair < count // 2 - 1, 1, 0)
        kernel((device % 2, left, right, pair % 2), *refs)

    return body


def vmem():
    return pl.BlockSpec(memory_space=pltpu.VMEM)


def small():
    return pltpu.CompilerParams(vmem_limit_bytes=8 * 1024 * 1024)


def light():
    return pl.CostEstimate(flops=1000, bytes_accessed=1000, transcendentals=0)


def halo_kernel(where, own, got, near, wide):
    def fill(first, second, to_right, to_left):
        to_right[0:256, :] = second[256:512, :]
        to_right[256:384, :] = pool1(second[0:256, :])
        to_right[384:448, :] = pool2(first[0:256, :])
        to_right[448:512, :] = pool2(first[256:512, :])
        to_left[0:256, :] = first[0:256, :]
        to_left[256:384, :] = pool1(first[256:512, :])
        to_left[384:448, :] = pool2(second[0:256, :])
        to_left[448:512, :] = pool2(second[256:512, :])

    for side in range(2):
        for odd in range(2):

            @pl.when((where[0] == side) & (where[3] == odd))
            def _(side=side, odd=odd):
                halves = (own, got) if side == 0 else (got, own)
                fill(*halves, *((near, wide) if odd == 0 else (wide, near)))


def halo(where, own, got):
    shape = jax.ShapeDtypeStruct(own.shape, BF)
    return pl.pallas_call(
        placed(halo_kernel, where),
        in_specs=[vmem(), vmem()],
        out_specs=[vmem(), vmem()],
        out_shape=[shape, shape],
        compiler_params=small(),
        cost_estimate=light(),
    )(own, got)


def turn_kernel(where, own, got, raw_t, one, one_t):
    for side, ref in ((where[0], own), (1 - where[0], got)):
        for i in range(2):
            rows = slice(i * PARENT, (i + 1) * PARENT)
            at = pl.ds(pl.multiple_of((side * 2 + i) * PARENT, PARENT), PARENT)
            half = pl.ds(pl.multiple_of((side * 2 + i) * BLOCK, BLOCK), BLOCK)
            for n in range(2):
                x = ref[rows, n * HEAD : (n + 1) * HEAD]
                raw_t[n, :, at] = x.T
                x = pool1(x)
                one[n, half, :] = x
                one_t[n, :, half] = x.T


def turn(where, own, got):
    shapes = ((2, HEAD, 1024), (2, 512, HEAD), (2, HEAD, 512))
    return pl.pallas_call(
        placed(turn_kernel, where),
        in_specs=[vmem()] * 2,
        out_specs=[vmem()] * 3,
        out_shape=[jax.ShapeDtypeStruct(shape, BF) for shape in shapes],
        compiler_params=small(),
        cost_estimate=light(),
    )(own, got)


def swap64(x):
    return pltpu.roll(x, 64, 1)


def low_lanes(shape):
    return lax.broadcasted_iota(jnp.int32, shape, 1) < 64


def spread64(x, half):
    other = swap64(x)
    low = low_lanes(x.shape)
    return jnp.where(low, x, other) if half == 0 else jnp.where(low, other, x)


def far_forward(k, v_t, q, bias, p_ref):
    k0, k1, k2, k3 = k
    v0, v1, v2, v3 = v_t
    left, right = bias
    outer = dot_nt(jnp.concatenate([k0, k3], axis=0), q)
    first, last = outer[:BLOCK], outer[BLOCK:]
    mid_low = dot_nt(k2, q[:BLOCK])
    mid_high = dot_nt(k1, q[BLOCK:])
    if left is not None:
        first = first + left
        mid_high = mid_high + left
    if right is not None:
        last = last + right
        mid_low = mid_low + right
    mid = jnp.concatenate([mid_low, mid_high], axis=1)
    peak = jnp.max(jnp.maximum(jnp.maximum(first, last), mid), axis=0, keepdims=True)
    parts = [jnp.exp2((x - peak) * TO_LOG2) for x in (first, last, mid)]
    for n, x in enumerate(parts):
        p_ref[n * BLOCK : (n + 1) * BLOCK, :] = x
    total = jnp.sum(parts[0] + parts[1] + parts[2], axis=0, keepdims=True)
    pb = [x.astype(BF) for x in parts]
    mixed = dot_nn(
        jnp.concatenate([v0, v3], axis=1), jnp.concatenate(pb[:2], axis=0)
    ) + jnp.concatenate([dot_nn(v2, pb[2][:, :BLOCK]), dot_nn(v1, pb[2][:, BLOCK:])], axis=1)
    return peak, total, mixed


def far_backward(k_t, v, q, p_ref, factor, g, ec):
    k0, k1, k2, k3 = k_t
    v0, v1, v2, v3 = v
    e_out = p_ref[: 2 * BLOCK, :] * factor
    e_mid = p_ref[2 * BLOCK :, :] * factor
    eb_out, eb_mid = e_out.astype(BF), e_mid.astype(BF)
    p_out = dot_nt(jnp.concatenate([v0, v3], axis=0), g)
    p_mid = jnp.concatenate([dot_nt(v2, g[:BLOCK]), dot_nt(v1, g[BLOCK:])], axis=1)
    r_out = (e_out * (p_out - ec)).astype(BF)
    r_mid = (e_mid * (p_mid - ec)).astype(BF)
    dv03 = dot_nn(eb_out, g)
    dv2 = dot_nn(eb_mid[:, :BLOCK], g[:BLOCK])
    dv1 = dot_nn(eb_mid[:, BLOCK:], g[BLOCK:])
    dk03 = dot_nn(r_out, q)
    dk2 = dot_nn(r_mid[:, :BLOCK], q[:BLOCK])
    dk1 = dot_nn(r_mid[:, BLOCK:], q[BLOCK:])
    dq_t = dot_nn(jnp.concatenate([k0, k3], axis=1), r_out) + jnp.concatenate(
        [dot_nn(k2, r_mid[:, :BLOCK]), dot_nn(k1, r_mid[:, BLOCK:])], axis=1
    )
    return (dk03[:BLOCK], dk1, dk2, dk03[BLOCK:]), (dv03[:BLOCK], dv1, dv2, dv03[BLOCK:]), dq_t


def main_kernel(qg_first, where, kv_own, kv_got, *refs):
    turned, refs = refs[:3], refs[3:]
    if qg_first:
        refs = (*refs[2:4], *refs[:2], *refs[4:])
    one_chunk(where, turned, kv_own, kv_got, *refs)


def one_chunk(
    where, turned, kv_own, kv_got, near_got, wide_got, qg_own, qg_got,
    oq_own, oq_far, grad, near_out, wide_out,
    raw, raw_t, one, one_t, two, two_t, qs, gs, p0, p1, p2, acc0, acc1, acc2, oq, halos,
):
    side = where[0]
    odd = where[3]
    halos[1 - odd] = near_got[...]
    halos[odd] = wide_got[...]
    from_left, from_right = halos.at[0], halos.at[1]
    to_left, to_right = halos.at[0], halos.at[1]
    width = kv_own.shape[1] // 2
    left_bias = (1 - where[1]).astype(F32) * MASKED
    right_bias = (1 - where[2]).astype(F32) * MASKED
    own_at = pl.multiple_of(side * 512, 512)
    got_at = pl.multiple_of((1 - side) * 512, 512)
    for h in range(width // HEAD):
        kc = slice(h * HEAD, (h + 1) * HEAD)
        vc = slice(width + h * HEAD, width + (h + 1) * HEAD)
        for n, cols in ((0, kc), (1, vc)):
            raw[n, 0:256, :] = from_left[0:256, cols]
            raw[n, pl.ds(256 + own_at, 512), :] = kv_own[:, cols]
            raw[n, pl.ds(256 + got_at, 512), :] = kv_got[:, cols]
            raw[n, 1280:1536, :] = from_right[0:256, cols]
            raw_t[n, :, 256:1280] = turned[0][n]
            one[n, 256:768, :] = turned[1][n]
            one_t[n, :, 256:768] = turned[2][n]
            one[n, 0:128, :] = from_left[256:384, cols]
            one[n, 128:256, :] = pool1(raw[n, 0:256, :])
            one[n, 768:896, :] = pool1(raw[n, 1280:1536, :])
            one[n, 896:1024, :] = from_right[256:384, cols]
            two[n, 0:128, :] = from_left[384:512, cols]
            two[n, 128:192, :] = pool12(one[n, 0:128, :])
            two[n, 192:256, :] = pool2(raw[n, 0:256, :])
            two[n, 256:320, :] = pool2(raw[n, 1280:1536, :])
            two[n, 320:384, :] = pool12(one[n, 896:1024, :])
            two[n, 384:512, :] = from_right[384:512, cols]
            for i in (0, 5):
                rows = slice(i * PARENT, (i + 1) * PARENT)
                raw_t[n, :, rows] = raw[n, rows, :].T
            for i in (0, 1, 6, 7):
                rows = slice(i * BLOCK, (i + 1) * BLOCK)
                one_t[n, :, rows] = one[n, rows, :].T
            for i in range(4):
                rows = slice(i * BLOCK, (i + 1) * BLOCK)
                two_t[n, :, rows] = two[n, rows, :].T
        qs[pl.ds(own_at, 512), :] = qg_own[:, kc]
        qs[pl.ds(got_at, 512), :] = qg_got[:, kc]
        gs[pl.ds(own_at, 512), :] = qg_own[:, vc]
        gs[pl.ds(got_at, 512), :] = qg_got[:, vc]

        def blocks(ref, n, which):
            return [ref[n, b * BLOCK : (b + 1) * BLOCK, :] for b in which]

        def blocks_t(ref, n, which):
            return [ref[n, :, b * BLOCK : (b + 1) * BLOCK] for b in which]

        q_parents = [qs[i * PARENT : (i + 1) * PARENT, :] for i in range(4)]
        q1 = [
            jnp.concatenate([pool1(q_parents[2 * j]), pool1(q_parents[2 * j + 1])], axis=0)
            for j in range(2)
        ]
        q2 = jnp.concatenate([pool2(x) for x in q_parents], axis=0)
        which1 = [(0, 1, 4, 5), (2, 3, 6, 7)]
        bias1 = [(left_bias, None), (None, right_bias)]
        which2 = (0, 1, 2, 3)
        far1 = [
            far_forward(
                blocks(one, 0, which1[j]), blocks_t(one_t, 1, which1[j]), q1[j], bias1[j], p1.at[j]
            )
            for j in range(2)
        ]
        far2 = far_forward(
            blocks(two, 0, which2), blocks_t(two_t, 1, which2), q2, (left_bias, right_bias), p2
        )
        g1_t, ec1, f1 = [], [], []
        g2_t, ec2, low2 = [], [], []
        dq0 = []
        for i in range(4):
            rows = slice(i * PARENT, i * PARENT + 3 * PARENT)
            q = q_parents[i]
            g = gs[i * PARENT : (i + 1) * PARENT, :]
            s = dot_nt(raw[0, rows, :], q)
            pieces = [s[:PARENT], s[PARENT : 2 * PARENT], s[2 * PARENT :]]
            if i == 0:
                pieces[0] = pieces[0] + left_bias
            if i == 3:
                pieces[2] = pieces[2] + right_bias
            m0 = jnp.max(
                jnp.maximum(jnp.maximum(pieces[0], pieces[1]), pieces[2]), axis=0, keepdims=True
            )
            e = [jnp.exp2((x - m0) * TO_LOG2) for x in pieces]
            for n in range(3):
                p0[i % 2, n * PARENT : (n + 1) * PARENT, :] = e[n]
            z0 = jnp.sum(e[0] + e[1] + e[2], axis=0, keepdims=True)
            u0 = dot_nn(raw_t[1, :, rows], jnp.concatenate([x.astype(BF) for x in e], axis=0))
            j, half = i // 2, i % 2
            lanes = slice(half * BLOCK, (half + 1) * BLOCK)
            m1, z1, u1 = (x[:, lanes] for x in far1[j])
            lanes2 = slice(j * BLOCK, (j + 1) * BLOCK)
            m2, z2, u2 = (spread64(x[:, lanes2], half) for x in far2)
            m1w, m2w = twice(m1, 1), twice(m2, 1)
            m = jnp.maximum(jnp.maximum(m0, m1w), m2w)
            a0 = jnp.exp2((m0 - m) * TO_LOG2)
            a1 = 2.0 * jnp.exp2((m1w - m) * TO_LOG2)
            a2 = 4.0 * jnp.exp2((m2w - m) * TO_LOG2)
            z = a0 * z0 + a1 * twice(z1, 1) + a2 * twice(z2, 1)
            inv = 1.0 / z
            o = ((a0 * inv) * u0 + (a1 * inv) * twice(u1, 1) + (a2 * inv) * twice(u2, 1)).astype(BF)
            oq[i, 0, h * HEAD : (h + 1) * HEAD, :] = o
            lg = m * TO_LOG2 + jnp.log2(z)
            g_t = g.astype(F32).T
            dr = jnp.sum(o.astype(F32) * g_t, axis=0, keepdims=True)
            lg_a, lg_b = lg[:, :BLOCK], lg[:, BLOCK:]
            g_a, g_b = g_t[:, :BLOCK], g_t[:, BLOCK:]
            dr_a, dr_b = dr[:, :BLOCK], dr[:, BLOCK:]
            low = jnp.minimum(lg_a, lg_b)
            w_a, w_b = jnp.exp2(low - lg_a), jnp.exp2(low - lg_b)
            g1_t.append((w_a * g_a + w_b * g_b).astype(BF))
            ec1.append(w_a * dr_a + w_b * dr_b)
            f1.append(2.0 * jnp.exp2(m1 * TO_LOG2 - low))
            lower = jnp.minimum(low, swap64(low))
            w_a, w_b = jnp.exp2(lower - lg_a), jnp.exp2(lower - lg_b)
            part = w_a * g_a + w_b * g_b
            g2_t.append(part + swap64(part))
            part = w_a * dr_a + w_b * dr_b
            ec2.append(part + swap64(part))
            low2.append(lower)
            f0 = jnp.exp2(m0 * TO_LOG2 - lg)
            products = dot_nt(raw[1, rows, :], g)
            weights = p0[i % 2] * f0
            eb = weights.astype(BF)
            r = (weights * (products - dr)).astype(BF)
            for n, x in ((1, dot_nn(eb, g)), (0, dot_nn(r, q))):
                if i == 0:
                    acc0[n, rows, :] = x
                else:
                    old = slice(i * PARENT, (i + 2) * PARENT)
                    acc0[n, old, :] += x[: 2 * PARENT]
                    acc0[n, (i + 2) * PARENT : (i + 3) * PARENT, :] = x[2 * PARENT :]
            dq0.append(dot_nn(raw_t[0, :, rows], r))
        dq1 = []
        for j in range(2):
            pair = slice(2 * j, 2 * j + 2)
            g1 = jnp.concatenate([x.astype(F32).T.astype(BF) for x in g1_t[pair]], axis=0)
            dk, dv, dq = far_backward(
                blocks_t(one_t, 0, which1[j]), blocks(one, 1, which1[j]), q1[j], p1.at[j],
                jnp.concatenate(f1[pair], axis=1), g1, jnp.concatenate(ec1[pair], axis=1),
            )
            for n, b in enumerate(which1[j]):
                acc1[0, b * BLOCK : (b + 1) * BLOCK, :] = dk[n]
                acc1[1, b * BLOCK : (b + 1) * BLOCK, :] = dv[n]
            dq1.append(dq)

        def joined(parts):
            return jnp.concatenate(
                [
                    jnp.where(low_lanes(parts[0].shape), parts[2 * j], parts[2 * j + 1])
                    for j in range(2)
                ],
                axis=1,
            )

        g2 = joined(g2_t).T.astype(BF)
        f2 = 4.0 * jnp.exp2(far2[0] * TO_LOG2 - joined(low2))
        dk, dv, dq2 = far_backward(
            blocks_t(two_t, 0, which2), blocks(two, 1, which2), q2, p2, f2, g2, joined(ec2)
        )
        for n in range(4):
            acc2[0, n * BLOCK : (n + 1) * BLOCK, :] = dk[n]
            acc2[1, n * BLOCK : (n + 1) * BLOCK, :] = dv[n]
        for i in range(4):
            j, half = i // 2, i % 2
            d1 = dq1[j][:, half * BLOCK : (half + 1) * BLOCK]
            d2 = spread64(dq2[:, j * BLOCK : (j + 1) * BLOCK], half)
            coarse = 0.5 * d1 + 0.25 * d2
            oq[i, 1, h * HEAD : (h + 1) * HEAD, :] = ((dq0[i] + twice(coarse, 1)) * INV_ROOT).astype(BF)
        for n, cols, scale in ((0, kc, INV_ROOT), (1, vc, 1.0)):
            for i in range(4):
                rows = slice((i + 1) * PARENT, (i + 2) * PARENT)
                coarse = acc1[n, (i + 2) * BLOCK : (i + 3) * BLOCK, :] * (0.5 * scale)
                grad[i * PARENT : (i + 1) * PARENT, cols] = acc0[n, rows, :] * scale + twice(coarse)
            far = acc2[n, 128:256, :] * (0.25 * scale)
            mid = acc1[n, 0:256, :] * (0.5 * scale)
            near = acc0[n, 0:256, :] * scale
            to_left[0:256, cols] = (near + twice(mid[128:] + twice(far[64:]))).astype(BF)
            to_left[256:384, cols] = (mid[:128] + twice(far[:64])).astype(BF)
            to_left[384:512, cols] = (acc2[n, 0:128, :] * (0.25 * scale)).astype(BF)
            far = acc2[n, 256:384, :] * (0.25 * scale)
            mid = acc1[n, 768:1024, :] * (0.5 * scale)
            near = acc0[n, 1280:1536, :] * scale
            to_right[0:256, cols] = (near + twice(mid[:128] + twice(far[:64]))).astype(BF)
            to_right[256:384, cols] = (mid[128:] + twice(far[64:])).astype(BF)
            to_right[384:512, cols] = (acc2[n, 384:512, :] * (0.25 * scale)).astype(BF)
    oq_own[...] = oq[pl.ds(side * 2, 2)]
    oq_far[...] = oq[pl.ds((1 - side) * 2, 2)]
    near_out[...] = halos[1 - odd]
    wide_out[...] = halos[odd]


def main(where, turned, kv_own, kv_got, near_got, wide_got, qg_own, qg_got, qg_first):
    rows, both = kv_own.shape
    width = both // 2
    oq_shape = jax.ShapeDtypeStruct((2, 2, width, PARENT), BF)
    halo_shape = jax.ShapeDtypeStruct((512, both), BF)
    operands = [kv_own, kv_got, near_got, wide_got, qg_own, qg_got]
    if qg_first:
        operands = operands[:2] + operands[4:] + operands[2:4]
    operands[2:2] = turned
    return pl.pallas_call(
        placed(functools.partial(main_kernel, qg_first), where),
        in_specs=[vmem()] * 9,
        out_specs=[vmem()] * 5,
        out_shape=[
            oq_shape,
            oq_shape,
            jax.ShapeDtypeStruct((2 * rows, both), F32),
            halo_shape,
            halo_shape,
        ],
        scratch_shapes=[
            pltpu.VMEM((2, 1536, HEAD), BF),
            pltpu.VMEM((2, HEAD, 1536), BF),
            pltpu.VMEM((2, 1024, HEAD), BF),
            pltpu.VMEM((2, HEAD, 1024), BF),
            pltpu.VMEM((2, 512, HEAD), BF),
            pltpu.VMEM((2, HEAD, 512), BF),
            pltpu.VMEM((1024, HEAD), BF),
            pltpu.VMEM((1024, HEAD), BF),
            pltpu.VMEM((2, 768, PARENT), F32),
            pltpu.VMEM((2, 384, PARENT), F32),
            pltpu.VMEM((384, PARENT), F32),
            pltpu.VMEM((2, 1536, HEAD), F32),
            pltpu.VMEM((2, 1024, HEAD), F32),
            pltpu.VMEM((2, 512, HEAD), F32),
            pltpu.VMEM((4, 2, width, PARENT), BF),
            pltpu.VMEM((2, 512, both), BF),
        ],
        compiler_params=pltpu.CompilerParams(vmem_limit_bytes=24 * 1024 * 1024),
        cost_estimate=light(),
    )(*operands)


def join_kernel(where, grad, near_got, wide_got, own, far):
    def fill(first, second, from_left, from_right):
        def parent(i):
            return grad[i * PARENT : (i + 1) * PARENT, :]

        def part(ref, start, stop):
            return ref[start:stop, :].astype(F32)

        first[0:256, :] = (
            parent(0) + part(from_left, 0, 256) + twice(twice(part(from_right, 384, 448)))
        ).astype(BF)
        first[256:512, :] = (
            parent(1) + twice(part(from_left, 256, 384) + twice(part(from_right, 448, 512)))
        ).astype(BF)
        second[0:256, :] = (
            parent(2) + twice(part(from_right, 256, 384) + twice(part(from_left, 384, 448)))
        ).astype(BF)
        second[256:512, :] = (
            parent(3) + part(from_right, 0, 256) + twice(twice(part(from_left, 448, 512)))
        ).astype(BF)

    for side in range(2):
        for odd in range(2):

            @pl.when((where[0] == side) & (where[3] == odd))
            def _(side=side, odd=odd):
                halves = (own, far) if side == 0 else (far, own)
                fill(*halves, *((wide_got, near_got) if odd == 0 else (near_got, wide_got)))


def join(where, grad, near_got, wide_got):
    shape = jax.ShapeDtypeStruct(near_got.shape, BF)
    return pl.pallas_call(
        placed(join_kernel, where),
        in_specs=[vmem(), vmem(), vmem()],
        out_specs=[vmem(), vmem()],
        out_shape=[shape, shape],
        compiler_params=small(),
        cost_estimate=light(),
    )(grad, near_got, wide_got)


def unpack_rows_kernel(where, *refs):
    ins, (first, second) = refs[:-2], refs[-2:]
    order = order_matrix(True)
    width = ins[0].shape[1] // 2
    side = where[0]
    blocks = [(side * CHUNKS + c, ins[c]) for c in range(CHUNKS)]
    blocks += [((1 - side) * CHUNKS + 1 - LATE_CHUNK, ins[CHUNKS])]
    for block, ref in blocks:
        at = pl.ds(pl.multiple_of(block * width, width), width)
        for i in range(2):
            rows = slice(i * PARENT, (i + 1) * PARENT)
            first[rows, at] = dot_nn(order, ref[rows, :width]).astype(BF)
            second[rows, at] = dot_nn(order, ref[rows, width:]).astype(BF)


def unpack_rows(where, own, got, shape):
    out = jax.ShapeDtypeStruct(shape, BF)
    return pl.pallas_call(
        placed(unpack_rows_kernel, where),
        in_specs=[vmem()] * (CHUNKS + 1),
        out_specs=[vmem(), vmem()],
        out_shape=[out, out],
        compiler_params=small(),
        cost_estimate=light(),
    )(*own, got)


def unpack_last_kernel(where, got, first_in, second_in, first, second, held, sems):
    del first_in, second_in
    order = order_matrix(True)
    width = got.shape[1] // 2
    block = (1 - where[0]) * CHUNKS + LATE_CHUNK
    at = pl.ds(pl.multiple_of(block * width, width), width)
    copies = []
    for i in range(2):
        rows = slice(i * PARENT, (i + 1) * PARENT)
        x = dot_nn(order, got[rows, :]).astype(BF)
        for m, ref in enumerate((first, second)):
            held[m, rows, :] = x[:, m * width : (m + 1) * width]
            copies.append(
                pltpu.make_async_copy(held.at[m, rows, :], ref.at[rows, at], sems.at[2 * i + m])
            )
            copies[-1].start()
    for copy in copies:
        copy.wait()


def unpack_last(where, got, first, second):
    out = jax.ShapeDtypeStruct(first.shape, BF)
    hbm = pl.BlockSpec(memory_space=pltpu.HBM)
    return pl.pallas_call(
        placed(unpack_last_kernel, where),
        in_specs=[vmem(), hbm, hbm],
        out_specs=[hbm, hbm],
        out_shape=[out, out],
        input_output_aliases={1: 0, 2: 1},
        scratch_shapes=[
            pltpu.VMEM((2, got.shape[0], got.shape[1] // 2), BF),
            pltpu.SemaphoreType.DMA((4,)),
        ],
        compiler_params=small(),
        cost_estimate=light(),
    )(got, first, second)


def unpack_columns_kernel(where, *refs):
    ins, (first, second) = refs[:-2], refs[-2:]
    order = order_matrix(True)
    width = ins[0].shape[2]
    for c in range(CHUNKS):
        for ref, side in ((ins[c], where[0]), (ins[CHUNKS + c], 1 - where[0])):
            at = pl.ds(pl.multiple_of((side * CHUNKS + c) * width, width), width)
            for i in range(2):
                rows = slice(i * PARENT, (i + 1) * PARENT)
                first[rows, at] = dot_nt(order, ref[i, 0]).astype(BF)
                second[rows, at] = dot_nt(order, ref[i, 1]).astype(BF)


def unpack_columns(where, own, got, shape):
    out = jax.ShapeDtypeStruct(shape, BF)
    return pl.pallas_call(
        placed(unpack_columns_kernel, where),
        in_specs=[vmem()] * (2 * CHUNKS),
        out_specs=[vmem(), vmem()],
        out_shape=[out, out],
        compiler_params=small(),
        cost_estimate=light(),
    )(*own, *got)


def on_device(queries, key_matrix, value_matrix, cotangent):
    axes = ("outer", "inner")
    count = lax.axis_size("outer") * lax.axis_size("inner")
    device = lax.axis_index("outer") * lax.axis_size("inner") + lax.axis_index("inner")
    where = (lax.axis_size("inner"), count)
    across = [(i, i ^ 1) for i in range(count)]
    near_edges = [(i, i ^ 2) for i in range(count) if i ^ 2 < count]
    wide_edges = [(i, i + 2 if i // 2 % 2 else i - 2) for i in range(count)]
    wide_edges = [(i, j) for i, j in wide_edges if 0 <= j < count]

    def swap(x):
        return lax.ppermute(x, axes, across)

    def beside(near, wide):
        near = lax.ppermute(near, axes, near_edges)
        return near, lax.ppermute(wide, axes, wide_edges)

    kv_far = [pack_cut(1 - device % 2, 0, key_matrix, value_matrix)]
    for c in range(1, CHUNKS):
        later, kv_far[0] = lax.optimization_barrier(((key_matrix, value_matrix), kv_far[0]))
        kv_far.append(pack_cut(1 - device % 2, c, *later))
    qg_far = pack(False, where, queries, cotangent)
    packed = pack(True, where, key_matrix, value_matrix, queries, cotangent)
    kv, qg = packed[:CHUNKS], packed[CHUNKS:]
    oq_own, oq_got, back, turned, halos, kv_got = [], [], [], [], [], []
    for c in range(CHUNKS):
        got_kv = swap(kv_far[c])
        if c > 0:
            got_kv, turned[0] = lax.optimization_barrier((got_kv, turned[0]))
        turned.append(turn(where, kv[c], got_kv))
        near, wide = halo(where, kv[c], got_kv)
        far = qg_far[c]
        if c > 0:
            near, wide, far, turned[c] = lax.optimization_barrier((near, wide, far, turned[c]))
        near, wide = beside(near, wide)
        halos.append((near, wide, swap(far)))
        kv_got.append(got_kv)
    for c in range(CHUNKS):
        near, wide, got_qg = halos[c]
        own, far, grad, near, wide = main(
            where, turned[c], kv[c], kv_got[c], near, wide, qg[c], got_qg, c == 0
        )
        oq_own.append(own)
        oq_got.append(swap(far))
        if c > 0:
            back[c - 1], near, wide = lax.optimization_barrier((back[c - 1], near, wide))
        back.append([grad, *beside(near, wide)])
    for c in range(CHUNKS):
        oq_got[c], back[c] = lax.optimization_barrier((oq_got[c], back[c]))
    kv_own, kv_got = [], []
    for c in range(CHUNKS):
        own, far = join(where, *back[c])
        kv_own.append(own)
        kv_got.append(swap(far))
    attended, query_grad = unpack_columns(where, oq_own, oq_got, queries.shape)
    key_grad, value_grad = unpack_rows(where, kv_own, kv_got[1 - LATE_CHUNK], queries.shape)
    key_grad, value_grad = unpack_last(where, kv_got[LATE_CHUNK], key_grad, value_grad)
    return attended, query_grad, key_grad, value_grad


def solution(mesh):
    spec = P(("outer", "inner"), None)
    return jax.shard_map(
        on_device,
        mesh=mesh,
        in_specs=(spec,) * 4,
        out_specs=(spec,) * 4,
        check_vma=False,
    )
```

```python
import functools
import math

import jax
import jax.numpy as jnp
from jax import lax
from jax.experimental import pallas as pl
from jax.experimental.pallas import tpu as pltpu
from jax.sharding import PartitionSpec as P

HEAD = 128
BLOCK = 128
PARENT = 256
LEVELS = 3
CHUNKS = 2
LATE_CHUNK = 1
INV_ROOT = HEAD**-0.5
TO_LOG2 = INV_ROOT * math.log2(math.e)
MASKED = -1e30
BF = jnp.bfloat16
F32 = jnp.float32


def dot_nt(a, b):
    return lax.dot_general(a, b, (((1,), (1,)), ((), ())), preferred_element_type=F32)


def dot_nn(a, b):
    return jnp.dot(a, b, preferred_element_type=F32)


def order_matrix(inverse):
    row = lax.broadcasted_iota(jnp.int32, (PARENT, PARENT), 0)
    col = lax.broadcasted_iota(jnp.int32, (PARENT, PARENT), 1)
    place, token = (col, row) if inverse else (row, col)
    slab = place // 64
    source = 4 * (place % 64) + 2 * (slab % 2) + slab // 2
    return jnp.where(source == token, 1.0, 0.0).astype(BF)


def pool1(x):
    return ((x[:BLOCK].astype(F32) + x[BLOCK:].astype(F32)) * 0.5).astype(BF)


def pool2(x):
    half = x[:BLOCK].astype(F32) + x[BLOCK:].astype(F32)
    return ((half[:64] + half[64:]) * 0.25).astype(BF)


def pool12(x):
    return ((x[:64].astype(F32) + x[64:].astype(F32)) * 0.5).astype(BF)


def twice(x, axis=0):
    return jnp.concatenate([x, x], axis=axis)


def pack_kernel(own, where, *refs):
    count = 4 if own else 2
    arrays, outs, (held, sems) = refs[:count], refs[count:-2], refs[-2:]
    rows, columns = arrays[0].shape
    half = columns // 2
    width = half // CHUNKS
    side = where[0] if own else 1 - where[0]
    at = pl.ds(pl.multiple_of(side * half, half), half)
    copies = [
        pltpu.make_async_copy(ref.at[:, at], held.at[m], sems.at[m]) for m, ref in enumerate(arrays)
    ]
    for copy in copies:
        copy.start()
    order = order_matrix(False)
    for m in range(count):
        copies[m].wait()
        first = m % 2 * width
        for i in range(rows // PARENT):
            at = slice(i * PARENT, (i + 1) * PARENT)
            x = dot_nn(order, held[m, at, :]).astype(BF)
            for c in range(CHUNKS):
                out = outs[m // 2 * CHUNKS + c]
                out[at, first : first + width] = x[:, c * width : (c + 1) * width]


def pack(own, where, *arrays):
    rows, columns = arrays[0].shape
    count = len(arrays)
    return pl.pallas_call(
        placed(functools.partial(pack_kernel, own), where),
        in_specs=[pl.BlockSpec(memory_space=pltpu.HBM)] * count,
        out_specs=[vmem()] * (count // 2 * CHUNKS),
        out_shape=[jax.ShapeDtypeStruct((rows, columns // CHUNKS), BF)] * (count // 2 * CHUNKS),
        scratch_shapes=[
            pltpu.VMEM((count, rows, columns // 2), BF),
            pltpu.SemaphoreType.DMA((count,)),
        ],
        compiler_params=small(),
        cost_estimate=light(),
    )(*arrays)


def pack_cut_kernel(a, b, out):
    order = order_matrix(False)
    width = a.shape[1]
    for m, ref in enumerate((a, b)):
        for i in range(a.shape[0] // PARENT):
            rows = slice(i * PARENT, (i + 1) * PARENT)
            out[rows, m * width : (m + 1) * width] = dot_nn(order, ref[rows, :]).astype(BF)


def pack_cut(side, chunk, a, b):
    rows, columns = a.shape
    width = columns // 2 // CHUNKS
    cut = [lax.dynamic_slice_in_dim(x, (side * CHUNKS + chunk) * width, width, 1) for x in (a, b)]
    return pl.pallas_call(
        pack_cut_kernel,
        in_specs=[vmem(), vmem()],
        out_specs=vmem(),
        out_shape=jax.ShapeDtypeStruct((rows, 2 * width), BF),
        compiler_params=small(),
        cost_estimate=light(),
    )(*cut)


def placed(kernel, grid):
    inner, count = grid

    def body(*refs):
        device = lax.axis_index("outer") * inner + lax.axis_index("inner")
        pair = device // 2
        left = jnp.where(pair > 0, 1, 0)
        right = jnp.where(pair < count // 2 - 1, 1, 0)
        kernel((device % 2, left, right, pair % 2), *refs)

    return body


def vmem():
    return pl.BlockSpec(memory_space=pltpu.VMEM)


def small():
    return pltpu.CompilerParams(vmem_limit_bytes=8 * 1024 * 1024)


def light():
    return pl.CostEstimate(flops=1000, bytes_accessed=1000, transcendentals=0)


def halo_kernel(where, own, got, near, wide):
    def fill(first, second, to_right, to_left):
        to_right[0:256, :] = second[256:512, :]
        to_right[256:384, :] = pool1(second[0:256, :])
        to_right[384:448, :] = pool2(first[0:256, :])
        to_right[448:512, :] = pool2(first[256:512, :])
        to_left[0:256, :] = first[0:256, :]
        to_left[256:384, :] = pool1(first[256:512, :])
        to_left[384:448, :] = pool2(second[0:256, :])
        to_left[448:512, :] = pool2(second[256:512, :])

    for side in range(2):
        for odd in range(2):

            @pl.when((where[0] == side) & (where[3] == odd))
            def _(side=side, odd=odd):
                halves = (own, got) if side == 0 else (got, own)
                fill(*halves, *((near, wide) if odd == 0 else (wide, near)))


def halo(where, own, got):
    shape = jax.ShapeDtypeStruct(own.shape, BF)
    return pl.pallas_call(
        placed(halo_kernel, where),
        in_specs=[vmem(), vmem()],
        out_specs=[vmem(), vmem()],
        out_shape=[shape, shape],
        compiler_params=small(),
        cost_estimate=light(),
    )(own, got)


def turn_kernel(where, own, got, raw_t, one, one_t):
    for side, ref in ((where[0], own), (1 - where[0], got)):
        for i in range(2):
            rows = slice(i * PARENT, (i + 1) * PARENT)
            at = pl.ds(pl.multiple_of((side * 2 + i) * PARENT, PARENT), PARENT)
            half = pl.ds(pl.multiple_of((side * 2 + i) * BLOCK, BLOCK), BLOCK)
            for n in range(2):
                x = ref[rows, n * HEAD : (n + 1) * HEAD]
                raw_t[n, :, at] = x.T
                x = pool1(x)
                one[n, half, :] = x
                one_t[n, :, half] = x.T


def turn(where, own, got):
    shapes = ((2, HEAD, 1024), (2, 512, HEAD), (2, HEAD, 512))
    return pl.pallas_call(
        placed(turn_kernel, where),
        in_specs=[vmem()] * 2,
        out_specs=[vmem()] * 3,
        out_shape=[jax.ShapeDtypeStruct(shape, BF) for shape in shapes],
        compiler_params=small(),
        cost_estimate=light(),
    )(own, got)


def swap64(x):
    return pltpu.roll(x, 64, 1)


def low_lanes(shape):
    return lax.broadcasted_iota(jnp.int32, shape, 1) < 64


def spread64(x, half):
    other = swap64(x)
    low = low_lanes(x.shape)
    return jnp.where(low, x, other) if half == 0 else jnp.where(low, other, x)


def far_forward(k, v_t, q, bias, p_ref):
    k0, k1, k2, k3 = k
    v0, v1, v2, v3 = v_t
    left, right = bias
    outer = dot_nt(jnp.concatenate([k0, k3], axis=0), q)
    first, last = outer[:BLOCK], outer[BLOCK:]
    mid_low = dot_nt(k2, q[:BLOCK])
    mid_high = dot_nt(k1, q[BLOCK:])
    if left is not None:
        first = first + left
        mid_high = mid_high + left
    if right is not None:
        last = last + right
        mid_low = mid_low + right
    mid = jnp.concatenate([mid_low, mid_high], axis=1)
    peak = jnp.max(jnp.maximum(jnp.maximum(first, last), mid), axis=0, keepdims=True)
    parts = [jnp.exp2((x - peak) * TO_LOG2) for x in (first, last, mid)]
    for n, x in enumerate(parts):
        p_ref[n * BLOCK : (n + 1) * BLOCK, :] = x
    total = jnp.sum(parts[0] + parts[1] + parts[2], axis=0, keepdims=True)
    pb = [x.astype(BF) for x in parts]
    mixed = dot_nn(
        jnp.concatenate([v0, v3], axis=1), jnp.concatenate(pb[:2], axis=0)
    ) + jnp.concatenate([dot_nn(v2, pb[2][:, :BLOCK]), dot_nn(v1, pb[2][:, BLOCK:])], axis=1)
    return peak, total, mixed


def far_backward(k_t, v, q, p_ref, factor, g, ec):
    k0, k1, k2, k3 = k_t
    v0, v1, v2, v3 = v
    e_out = p_ref[: 2 * BLOCK, :] * factor
    e_mid = p_ref[2 * BLOCK :, :] * factor
    eb_out, eb_mid = e_out.astype(BF), e_mid.astype(BF)
    p_out = dot_nt(jnp.concatenate([v0, v3], axis=0), g)
    p_mid = jnp.concatenate([dot_nt(v2, g[:BLOCK]), dot_nt(v1, g[BLOCK:])], axis=1)
    r_out = (e_out * (p_out - ec)).astype(BF)
    r_mid = (e_mid * (p_mid - ec)).astype(BF)
    dv03 = dot_nn(eb_out, g)
    dv2 = dot_nn(eb_mid[:, :BLOCK], g[:BLOCK])
    dv1 = dot_nn(eb_mid[:, BLOCK:], g[BLOCK:])
    dk03 = dot_nn(r_out, q)
    dk2 = dot_nn(r_mid[:, :BLOCK], q[:BLOCK])
    dk1 = dot_nn(r_mid[:, BLOCK:], q[BLOCK:])
    dq_t = dot_nn(jnp.concatenate([k0, k3], axis=1), r_out) + jnp.concatenate(
        [dot_nn(k2, r_mid[:, :BLOCK]), dot_nn(k1, r_mid[:, BLOCK:])], axis=1
    )
    return (dk03[:BLOCK], dk1, dk2, dk03[BLOCK:]), (dv03[:BLOCK], dv1, dv2, dv03[BLOCK:]), dq_t


def main_kernel(qg_first, where, kv_own, kv_got, *refs):
    turned, refs = refs[:3], refs[3:]
    if qg_first:
        refs = (*refs[2:4], *refs[:2], *refs[4:])
    one_chunk(where, turned, kv_own, kv_got, *refs)


def one_chunk(
    where, turned, kv_own, kv_got, near_got, wide_got, qg_own, qg_got,
    oq_own, oq_far, grad, near_out, wide_out,
    raw, raw_t, one, one_t, two, two_t, qs, gs, p0, p1, p2, acc0, acc1, acc2, oq, halos,
):
    side = where[0]
    odd = where[3]
    halos[1 - odd] = near_got[...]
    halos[odd] = wide_got[...]
    from_left, from_right = halos.at[0], halos.at[1]
    to_left, to_right = halos.at[0], halos.at[1]
    width = kv_own.shape[1] // 2
    left_bias = (1 - where[1]).astype(F32) * MASKED
    right_bias = (1 - where[2]).astype(F32) * MASKED
    own_at = pl.multiple_of(side * 512, 512)
    got_at = pl.multiple_of((1 - side) * 512, 512)
    for h in range(width // HEAD):
        kc = slice(h * HEAD, (h + 1) * HEAD)
        vc = slice(width + h * HEAD, width + (h + 1) * HEAD)
        for n, cols in ((0, kc), (1, vc)):
            raw[n, 0:256, :] = from_left[0:256, cols]
            raw[n, pl.ds(256 + own_at, 512), :] = kv_own[:, cols]
            raw[n, pl.ds(256 + got_at, 512), :] = kv_got[:, cols]
            raw[n, 1280:1536, :] = from_right[0:256, cols]
            raw_t[n, :, 256:1280] = turned[0][n]
            one[n, 256:768, :] = turned[1][n]
            one_t[n, :, 256:768] = turned[2][n]
            one[n, 0:128, :] = from_left[256:384, cols]
            one[n, 128:256, :] = pool1(raw[n, 0:256, :])
            one[n, 768:896, :] = pool1(raw[n, 1280:1536, :])
            one[n, 896:1024, :] = from_right[256:384, cols]
            two[n, 0:128, :] = from_left[384:512, cols]
            two[n, 128:192, :] = pool12(one[n, 0:128, :])
            two[n, 192:256, :] = pool2(raw[n, 0:256, :])
            two[n, 256:320, :] = pool2(raw[n, 1280:1536, :])
            two[n, 320:384, :] = pool12(one[n, 896:1024, :])
            two[n, 384:512, :] = from_right[384:512, cols]
            for i in (0, 5):
                rows = slice(i * PARENT, (i + 1) * PARENT)
                raw_t[n, :, rows] = raw[n, rows, :].T
            for i in (0, 1, 6, 7):
                rows = slice(i * BLOCK, (i + 1) * BLOCK)
                one_t[n, :, rows] = one[n, rows, :].T
            for i in range(4):
                rows = slice(i * BLOCK, (i + 1) * BLOCK)
                two_t[n, :, rows] = two[n, rows, :].T
        qs[pl.ds(own_at, 512), :] = qg_own[:, kc]
        qs[pl.ds(got_at, 512), :] = qg_got[:, kc]
        gs[pl.ds(own_at, 512), :] = qg_own[:, vc]
        gs[pl.ds(got_at, 512), :] = qg_got[:, vc]

        def blocks(ref, n, which):
            return [ref[n, b * BLOCK : (b + 1) * BLOCK, :] for b in which]

        def blocks_t(ref, n, which):
            return [ref[n, :, b * BLOCK : (b + 1) * BLOCK] for b in which]

        q_parents = [qs[i * PARENT : (i + 1) * PARENT, :] for i in range(4)]
        q1 = [
            jnp.concatenate([pool1(q_parents[2 * j]), pool1(q_parents[2 * j + 1])], axis=0)
            for j in range(2)
        ]
        q2 = jnp.concatenate([pool2(x) for x in q_parents], axis=0)
        which1 = [(0, 1, 4, 5), (2, 3, 6, 7)]
        bias1 = [(left_bias, None), (None, right_bias)]
        which2 = (0, 1, 2, 3)
        far1 = [
            far_forward(
                blocks(one, 0, which1[j]), blocks_t(one_t, 1, which1[j]), q1[j], bias1[j], p1.at[j]
            )
            for j in range(2)
        ]
        far2 = far_forward(
            blocks(two, 0, which2), blocks_t(two_t, 1, which2), q2, (left_bias, right_bias), p2
        )
        g1_t, ec1, f1 = [], [], []
        g2_t, ec2, low2 = [], [], []
        dq0 = []
        for i in range(4):
            rows = slice(i * PARENT, i * PARENT + 3 * PARENT)
            q = q_parents[i]
            g = gs[i * PARENT : (i + 1) * PARENT, :]
            s = dot_nt(raw[0, rows, :], q)
            pieces = [s[:PARENT], s[PARENT : 2 * PARENT], s[2 * PARENT :]]
            if i == 0:
                pieces[0] = pieces[0] + left_bias
            if i == 3:
                pieces[2] = pieces[2] + right_bias
            m0 = jnp.max(
                jnp.maximum(jnp.maximum(pieces[0], pieces[1]), pieces[2]), axis=0, keepdims=True
            )
            e = [jnp.exp2((x - m0) * TO_LOG2) for x in pieces]
            for n in range(3):
                p0[i % 2, n * PARENT : (n + 1) * PARENT, :] = e[n]
            z0 = jnp.sum(e[0] + e[1] + e[2], axis=0, keepdims=True)
            u0 = dot_nn(raw_t[1, :, rows], jnp.concatenate([x.astype(BF) for x in e], axis=0))
            j, half = i // 2, i % 2
            lanes = slice(half * BLOCK, (half + 1) * BLOCK)
            m1, z1, u1 = (x[:, lanes] for x in far1[j])
            lanes2 = slice(j * BLOCK, (j + 1) * BLOCK)
            m2, z2, u2 = (spread64(x[:, lanes2], half) for x in far2)
            m1w, m2w = twice(m1, 1), twice(m2, 1)
            m = jnp.maximum(jnp.maximum(m0, m1w), m2w)
            a0 = jnp.exp2((m0 - m) * TO_LOG2)
            a1 = 2.0 * jnp.exp2((m1w - m) * TO_LOG2)
            a2 = 4.0 * jnp.exp2((m2w - m) * TO_LOG2)
            z = a0 * z0 + a1 * twice(z1, 1) + a2 * twice(z2, 1)
            inv = 1.0 / z
            o = ((a0 * inv) * u0 + (a1 * inv) * twice(u1, 1) + (a2 * inv) * twice(u2, 1)).astype(BF)
            oq[i, 0, h * HEAD : (h + 1) * HEAD, :] = o
            lg = m * TO_LOG2 + jnp.log2(z)
            g_t = g.astype(F32).T
            dr = jnp.sum(o.astype(F32) * g_t, axis=0, keepdims=True)
            lg_a, lg_b = lg[:, :BLOCK], lg[:, BLOCK:]
            g_a, g_b = g_t[:, :BLOCK], g_t[:, BLOCK:]
            dr_a, dr_b = dr[:, :BLOCK], dr[:, BLOCK:]
            low = jnp.minimum(lg_a, lg_b)
            w_a, w_b = jnp.exp2(low - lg_a), jnp.exp2(low - lg_b)
            g1_t.append((w_a * g_a + w_b * g_b).astype(BF))
            ec1.append(w_a * dr_a + w_b * dr_b)
            f1.append(2.0 * jnp.exp2(m1 * TO_LOG2 - low))
            lower = jnp.minimum(low, swap64(low))
            w_a, w_b = jnp.exp2(lower - lg_a), jnp.exp2(lower - lg_b)
            part = w_a * g_a + w_b * g_b
            g2_t.append(part + swap64(part))
            part = w_a * dr_a + w_b * dr_b
            ec2.append(part + swap64(part))
            low2.append(lower)
            f0 = jnp.exp2(m0 * TO_LOG2 - lg)
            products = dot_nt(raw[1, rows, :], g)
            weights = p0[i % 2] * f0
            eb = weights.astype(BF)
            r = (weights * (products - dr)).astype(BF)
            for n, x in ((1, dot_nn(eb, g)), (0, dot_nn(r, q))):
                if i == 0:
                    acc0[n, rows, :] = x
                else:
                    old = slice(i * PARENT, (i + 2) * PARENT)
                    acc0[n, old, :] += x[: 2 * PARENT]
                    acc0[n, (i + 2) * PARENT : (i + 3) * PARENT, :] = x[2 * PARENT :]
            dq0.append(dot_nn(raw_t[0, :, rows], r))
        dq1 = []
        for j in range(2):
            pair = slice(2 * j, 2 * j + 2)
            g1 = jnp.concatenate([x.astype(F32).T.astype(BF) for x in g1_t[pair]], axis=0)
            dk, dv, dq = far_backward(
                blocks_t(one_t, 0, which1[j]), blocks(one, 1, which1[j]), q1[j], p1.at[j],
                jnp.concatenate(f1[pair], axis=1), g1, jnp.concatenate(ec1[pair], axis=1),
            )
            for n, b in enumerate(which1[j]):
                acc1[0, b * BLOCK : (b + 1) * BLOCK, :] = dk[n]
                acc1[1, b * BLOCK : (b + 1) * BLOCK, :] = dv[n]
            dq1.append(dq)

        def joined(parts):
            return jnp.concatenate(
                [
                    jnp.where(low_lanes(parts[0].shape), parts[2 * j], parts[2 * j + 1])
                    for j in range(2)
                ],
                axis=1,
            )

        g2 = joined(g2_t).T.astype(BF)
        f2 = 4.0 * jnp.exp2(far2[0] * TO_LOG2 - joined(low2))
        dk, dv, dq2 = far_backward(
            blocks_t(two_t, 0, which2), blocks(two, 1, which2), q2, p2, f2, g2, joined(ec2)
        )
        for n in range(4):
            acc2[0, n * BLOCK : (n + 1) * BLOCK, :] = dk[n]
            acc2[1, n * BLOCK : (n + 1) * BLOCK, :] = dv[n]
        for i in range(4):
            j, half = i // 2, i % 2
            d1 = dq1[j][:, half * BLOCK : (half + 1) * BLOCK]
            d2 = spread64(dq2[:, j * BLOCK : (j + 1) * BLOCK], half)
            coarse = 0.5 * d1 + 0.25 * d2
            oq[i, 1, h * HEAD : (h + 1) * HEAD, :] = ((dq0[i] + twice(coarse, 1)) * INV_ROOT).astype(BF)
        for n, cols, scale in ((0, kc, INV_ROOT), (1, vc, 1.0)):
            for i in range(4):
                rows = slice((i + 1) * PARENT, (i + 2) * PARENT)
                coarse = acc1[n, (i + 2) * BLOCK : (i + 3) * BLOCK, :] * (0.5 * scale)
                grad[i * PARENT : (i + 1) * PARENT, cols] = acc0[n, rows, :] * scale + twice(coarse)
            far = acc2[n, 128:256, :] * (0.25 * scale)
            mid = acc1[n, 0:256, :] * (0.5 * scale)
            near = acc0[n, 0:256, :] * scale
            to_left[0:256, cols] = (near + twice(mid[128:] + twice(far[64:]))).astype(BF)
            to_left[256:384, cols] = (mid[:128] + twice(far[:64])).astype(BF)
            to_left[384:512, cols] = (acc2[n, 0:128, :] * (0.25 * scale)).astype(BF)
            far = acc2[n, 256:384, :] * (0.25 * scale)
            mid = acc1[n, 768:1024, :] * (0.5 * scale)
            near = acc0[n, 1280:1536, :] * scale
            to_right[0:256, cols] = (near + twice(mid[:128] + twice(far[:64]))).astype(BF)
            to_right[256:384, cols] = (mid[128:] + twice(far[64:])).astype(BF)
            to_right[384:512, cols] = (acc2[n, 384:512, :] * (0.25 * scale)).astype(BF)
    oq_own[...] = oq[pl.ds(side * 2, 2)]
    oq_far[...] = oq[pl.ds((1 - side) * 2, 2)]
    near_out[...] = halos[1 - odd]
    wide_out[...] = halos[odd]


def main(where, turned, kv_own, kv_got, near_got, wide_got, qg_own, qg_got, qg_first):
    rows, both = kv_own.shape
    width = both // 2
    oq_shape = jax.ShapeDtypeStruct((2, 2, width, PARENT), BF)
    halo_shape = jax.ShapeDtypeStruct((512, both), BF)
    operands = [kv_own, kv_got, near_got, wide_got, qg_own, qg_got]
    if qg_first:
        operands = operands[:2] + operands[4:] + operands[2:4]
    operands[2:2] = turned
    return pl.pallas_call(
        placed(functools.partial(main_kernel, qg_first), where),
        in_specs=[vmem()] * 9,
        out_specs=[vmem()] * 5,
        out_shape=[
            oq_shape,
            oq_shape,
            jax.ShapeDtypeStruct((2 * rows, both), F32),
            halo_shape,
            halo_shape,
        ],
        scratch_shapes=[
            pltpu.VMEM((2, 1536, HEAD), BF),
            pltpu.VMEM((2, HEAD, 1536), BF),
            pltpu.VMEM((2, 1024, HEAD), BF),
            pltpu.VMEM((2, HEAD, 1024), BF),
            pltpu.VMEM((2, 512, HEAD), BF),
            pltpu.VMEM((2, HEAD, 512), BF),
            pltpu.VMEM((1024, HEAD), BF),
            pltpu.VMEM((1024, HEAD), BF),
            pltpu.VMEM((2, 768, PARENT), F32),
            pltpu.VMEM((2, 384, PARENT), F32),
            pltpu.VMEM((384, PARENT), F32),
            pltpu.VMEM((2, 1536, HEAD), F32),
            pltpu.VMEM((2, 1024, HEAD), F32),
            pltpu.VMEM((2, 512, HEAD), F32),
            pltpu.VMEM((4, 2, width, PARENT), BF),
            pltpu.VMEM((2, 512, both), BF),
        ],
        compiler_params=pltpu.CompilerParams(vmem_limit_bytes=24 * 1024 * 1024),
        cost_estimate=light(),
    )(*operands)


def join_kernel(where, grad, near_got, wide_got, own, far):
    def fill(first, second, from_left, from_right):
        def parent(i):
            return grad[i * PARENT : (i + 1) * PARENT, :]

        def part(ref, start, stop):
            return ref[start:stop, :].astype(F32)

        first[0:256, :] = (
            parent(0) + part(from_left, 0, 256) + twice(twice(part(from_right, 384, 448)))
        ).astype(BF)
        first[256:512, :] = (
            parent(1) + twice(part(from_left, 256, 384) + twice(part(from_right, 448, 512)))
        ).astype(BF)
        second[0:256, :] = (
            parent(2) + twice(part(from_right, 256, 384) + twice(part(from_left, 384, 448)))
        ).astype(BF)
        second[256:512, :] = (
            parent(3) + part(from_right, 0, 256) + twice(twice(part(from_left, 448, 512)))
        ).astype(BF)

    for side in range(2):
        for odd in range(2):

            @pl.when((where[0] == side) & (where[3] == odd))
            def _(side=side, odd=odd):
                halves = (own, far) if side == 0 else (far, own)
                fill(*halves, *((wide_got, near_got) if odd == 0 else (near_got, wide_got)))


def join(where, grad, near_got, wide_got):
    shape = jax.ShapeDtypeStruct(near_got.shape, BF)
    return pl.pallas_call(
        placed(join_kernel, where),
        in_specs=[vmem(), vmem(), vmem()],
        out_specs=[vmem(), vmem()],
        out_shape=[shape, shape],
        compiler_params=small(),
        cost_estimate=light(),
    )(grad, near_got, wide_got)


def unpack_rows_kernel(where, *refs):
    ins, (first, second) = refs[:-2], refs[-2:]
    order = order_matrix(True)
    width = ins[0].shape[1] // 2
    side = where[0]
    blocks = [(side * CHUNKS + c, ins[c]) for c in range(CHUNKS)]
    blocks += [((1 - side) * CHUNKS + 1 - LATE_CHUNK, ins[CHUNKS])]
    for block, ref in blocks:
        at = pl.ds(pl.multiple_of(block * width, width), width)
        for i in range(2):
            rows = slice(i * PARENT, (i + 1) * PARENT)
            first[rows, at] = dot_nn(order, ref[rows, :width]).astype(BF)
            second[rows, at] = dot_nn(order, ref[rows, width:]).astype(BF)


def unpack_rows(where, own, got, shape):
    out = jax.ShapeDtypeStruct(shape, BF)
    return pl.pallas_call(
        placed(unpack_rows_kernel, where),
        in_specs=[vmem()] * (CHUNKS + 1),
        out_specs=[vmem(), vmem()],
        out_shape=[out, out],
        compiler_params=small(),
        cost_estimate=light(),
    )(*own, got)


def unpack_last_kernel(where, got, first_in, second_in, first, second, held, sems):
    del first_in, second_in
    order = order_matrix(True)
    width = got.shape[1] // 2
    block = (1 - where[0]) * CHUNKS + LATE_CHUNK
    at = pl.ds(pl.multiple_of(block * width, width), width)
    copies = []
    for i in range(2):
        rows = slice(i * PARENT, (i + 1) * PARENT)
        x = dot_nn(order, got[rows, :]).astype(BF)
        for m, ref in enumerate((first, second)):
            held[m, rows, :] = x[:, m * width : (m + 1) * width]
            copies.append(
                pltpu.make_async_copy(held.at[m, rows, :], ref.at[rows, at], sems.at[2 * i + m])
            )
            copies[-1].start()
    for copy in copies:
        copy.wait()


def unpack_last(where, got, first, second):
    out = jax.ShapeDtypeStruct(first.shape, BF)
    hbm = pl.BlockSpec(memory_space=pltpu.HBM)
    return pl.pallas_call(
        placed(unpack_last_kernel, where),
        in_specs=[vmem(), hbm, hbm],
        out_specs=[hbm, hbm],
        out_shape=[out, out],
        input_output_aliases={1: 0, 2: 1},
        scratch_shapes=[
            pltpu.VMEM((2, got.shape[0], got.shape[1] // 2), BF),
            pltpu.SemaphoreType.DMA((4,)),
        ],
        compiler_params=small(),
        cost_estimate=light(),
    )(got, first, second)


def unpack_columns_kernel(where, *refs):
    ins, (first, second) = refs[:-2], refs[-2:]
    order = order_matrix(True)
    width = ins[0].shape[2]
    for c in range(CHUNKS):
        for ref, side in ((ins[c], where[0]), (ins[CHUNKS + c], 1 - where[0])):
            at = pl.ds(pl.multiple_of((side * CHUNKS + c) * width, width), width)
            for i in range(2):
                rows = slice(i * PARENT, (i + 1) * PARENT)
                first[rows, at] = dot_nt(order, ref[i, 0]).astype(BF)
                second[rows, at] = dot_nt(order, ref[i, 1]).astype(BF)


def unpack_columns(where, own, got, shape):
    out = jax.ShapeDtypeStruct(shape, BF)
    return pl.pallas_call(
        placed(unpack_columns_kernel, where),
        in_specs=[vmem()] * (2 * CHUNKS),
        out_specs=[vmem(), vmem()],
        out_shape=[out, out],
        compiler_params=small(),
        cost_estimate=light(),
    )(*own, *got)


def on_device(queries, key_matrix, value_matrix, cotangent):
    axes = ("outer", "inner")
    count = lax.axis_size("outer") * lax.axis_size("inner")
    device = lax.axis_index("outer") * lax.axis_size("inner") + lax.axis_index("inner")
    where = (lax.axis_size("inner"), count)
    across = [(i, i ^ 1) for i in range(count)]
    near_edges = [(i, i ^ 2) for i in range(count) if i ^ 2 < count]
    wide_edges = [(i, i + 2 if i // 2 % 2 else i - 2) for i in range(count)]
    wide_edges = [(i, j) for i, j in wide_edges if 0 <= j < count]

    def swap(x):
        return lax.ppermute(x, axes, across)

    def beside(near, wide):
        near = lax.ppermute(near, axes, near_edges)
        return near, lax.ppermute(wide, axes, wide_edges)

    kv_far = [pack_cut(1 - device % 2, 0, key_matrix, value_matrix)]
    for c in range(1, CHUNKS):
        later, kv_far[0] = lax.optimization_barrier(((key_matrix, value_matrix), kv_far[0]))
        kv_far.append(pack_cut(1 - device % 2, c, *later))
    qg_far = pack(False, where, queries, cotangent)
    packed = pack(True, where, key_matrix, value_matrix, queries, cotangent)
    kv, qg = packed[:CHUNKS], packed[CHUNKS:]
    oq_own, oq_got, back, turned, halos, kv_got = [], [], [], [], [], []
    for c in range(CHUNKS):
        got_kv = swap(kv_far[c])
        if c > 0:
            far, turned[0] = lax.optimization_barrier((qg_far[c], turned[0]))
            got_kv, turned[0] = lax.optimization_barrier((got_kv, turned[0]))
        turned.append(turn(where, kv[c], got_kv))
        near, wide = halo(where, kv[c], got_kv)
        if c == 0:
            far = qg_far[c]
        else:
            near, wide, turned[c] = lax.optimization_barrier((near, wide, turned[c]))
        near, wide = beside(near, wide)
        halos.append((near, wide, swap(far)))
        kv_got.append(got_kv)
    for c in range(CHUNKS):
        near, wide, got_qg = halos[c]
        own, far, grad, near, wide = main(
            where, turned[c], kv[c], kv_got[c], near, wide, qg[c], got_qg, c == 0
        )
        oq_own.append(own)
        oq_got.append(swap(far))
        if c > 0:
            back[c - 1], near, wide = lax.optimization_barrier((back[c - 1], near, wide))
        back.append([grad, *beside(near, wide)])
    for c in range(CHUNKS):
        oq_got[c], back[c] = lax.optimization_barrier((oq_got[c], back[c]))
    kv_own, kv_got = [], []
    for c in range(CHUNKS):
        own, far = join(where, *back[c])
        kv_own.append(own)
        kv_got.append(swap(far))
    attended, query_grad = unpack_columns(where, oq_own, oq_got, queries.shape)
    key_grad, value_grad = unpack_rows(where, kv_own, kv_got[1 - LATE_CHUNK], queries.shape)
    key_grad, value_grad = unpack_last(where, kv_got[LATE_CHUNK], key_grad, value_grad)
    return attended, query_grad, key_grad, value_grad


def solution(mesh):
    spec = P(("outer", "inner"), None)
    return jax.shard_map(
        on_device,
        mesh=mesh,
        in_specs=(spec,) * 4,
        out_specs=(spec,) * 4,
        check_vma=False,
    )
```
